128 devices in a mesh: batch: 8 (over y, core), blk: 16 (over x, z).
Axes of the slice: x: 4, y: 4, z: 4, core: 2. Of those that a mesh axis runs over, the one named last changes fastest.
Arguments:
- inputs: bfloat16 [8, 2048, 768], P('batch', 'blk'), may hold values from -6 to 6
- queries: bfloat16 [8, 2048, 768], P('batch', 'blk'), may hold values from -6 to 6
- lengths: int32 [8], P('batch'), may hold values from 1921 to 2048, as said below
- latent_array: bfloat16 [256, 1280], P('blk'), may hold values from -6 to 6
- latent_mats: bfloat16 [10, 1280, 1280], P(None, 'blk'), may hold values from -0.15625 to 0.15625
- out_mats: bfloat16 [2, 1280, 1280], P(None, 'blk'), may hold values from -0.75 to 0.75
- byte_mats: bfloat16 [3, 768, 1280], P(None, 'blk'), may hold values from -0.21875 to 0.21875
- dec_out: bfloat16 [1280, 768], P('blk'), may hold values from -0.75 to 0.75
- latent_gains: float32 [5, 1280], replicated, may hold values from 0.5 to 1.5
- byte_gains: float32 [2, 768], replicated, may hold values from 0.5 to 1.5
- cotangent: bfloat16 [8, 2048, 768], P('batch', 'blk'), may hold values from -6 to 6
Outputs:
- result: bfloat16 [8, 2048, 768], P('batch', 'blk')
- grad_inputs: float32 [8, 2048, 768], P('batch', 'blk')
- grad_queries: float32 [8, 2048, 768], P('batch', 'blk')
- grad_latent_array: float32 [256, 1280], P('batch', 'blk')
- grad_latent_mats: float32 [10, 1280, 1280], P(None, 'batch', 'blk')
- grad_out_mats: float32 [2, 1280, 1280], P(None, 'batch', 'blk')
- grad_byte_mats: float32 [3, 768, 1280], P(None, 'batch', 'blk')
- grad_dec_out: float32 [1280, 768], P('batch', 'blk')
- grad_latent_gains: float32 [5, 1280], replicated
- grad_byte_gains: float32 [2, 768], replicated
The draws below stay inside these ranges and needn't reach their ends.
Inputs may be any that keep to these rules, and one draw needn't show every extreme that they name: `lengths`: byte positions at or past a sequence's length are padding whose keys are masked; every draw has a sequence of length 2048.
All inputs are finite; a program needn't handle non-finite values.
Results may differ from the reference program's by a relative error of at most 0.025.
Values may be sent and summed in bfloat16 or wider, within the bound.
No kernel may reach another device: no remote copies, remote signals or barrier semaphores. Data moves between devices by JAX's collectives and lax.ppermute only.
A program may use at most 256 MiB of HBM per device.

```python
import jax
import jax.numpy as jnp
from jax import lax

D_IN = 768
D_LAT = 1280
HEADS = 8
LATENTS = 256
LEN_DEV = 128
LEN = 2048
SEQS = 8


def draw_lengths(key, part):
    key = jax.random.fold_in(key, 11)
    first_key, second_key = jax.random.split(key)
    drawn = jax.random.randint(first_key, (SEQS,), LEN - LEN_DEV + 1, LEN + 1, dtype=jnp.int32)
    chosen = jax.random.randint(second_key, (), 0, SEQS, dtype=jnp.int32)
    return jnp.where(jnp.arange(SEQS, dtype=jnp.int32) == chosen, LEN, drawn).astype(jnp.int32)


def steps_of(key, dims, shards, low, high):
    loudness = 1.0
    for dim, shards_of in shards:
        draws = jax.random.uniform(jax.random.fold_in(jax.random.fold_in(key, 6), dim), (shards_of,), jnp.float32, low / len(shards), high / len(shards))
        loudness = loudness * jnp.repeat(jnp.exp(draws), dims[dim] // shards_of).reshape((-1,) + (1,) * (len(dims) - 1 - dim))
    return loudness


def gaussian(rng, shape, scale, reach, pieces=(), kind=jnp.bfloat16):
    array = scale * jax.random.normal(rng, shape, jnp.float32)
    if pieces:
        array = array * steps_of(rng, shape, pieces, -0.22, 0.18)
    return jnp.clip(array, -reach, reach).astype(kind)


def setup_inputs(seed: int = 0) -> dict:
    splits = jax.random.split(jax.random.key(seed), 12)
    inputs = gaussian(splits[0], (SEQS, LEN, D_IN), 1.0, 6.0, ((0, 8), (1, 16)))
    queries = gaussian(splits[1], (SEQS, LEN, D_IN), 1.0, 6.0, ((0, 8), (1, 16)))
    lengths = draw_lengths(jax.random.fold_in(splits[11], 71), 0)
    latent_array = gaussian(splits[3], (LATENTS, D_LAT), 1.0, 6.0, ((0, 16),))
    latent_mats = gaussian(splits[4], (10, D_LAT, D_LAT), D_LAT ** -0.5, 0.15625, ((1, 16),))
    out_mats = gaussian(splits[5], (2, D_LAT, D_LAT), (max(D_LAT // 20, 8)) ** -0.5, 0.75, ((1, 16),))
    byte_mats = gaussian(splits[6], (3, D_IN, D_LAT), D_IN ** -0.5, 0.21875, ((1, 16),))
    dec_out = gaussian(splits[7], (D_LAT, D_IN), (max(D_LAT // 20, 8)) ** -0.5, 0.75, ((0, 16),))
    latent_gains = jnp.clip(1.0 + 0.1 * jax.random.normal(splits[8], (5, D_LAT), jnp.float32), 0.5, 1.5)
    byte_gains = jnp.clip(1.0 + 0.1 * jax.random.normal(splits[9], (2, D_IN), jnp.float32), 0.5, 1.5)
    cotangent = gaussian(splits[10], (SEQS, LEN, D_IN), 1.0, 6.0, ((0, 8), (1, 16)))
    return dict(inputs=inputs, queries=queries, lengths=lengths, latent_array=latent_array, latent_mats=latent_mats, out_mats=out_mats, byte_mats=byte_mats, dec_out=dec_out, latent_gains=latent_gains, byte_gains=byte_gains, cotangent=cotangent)


EPSILON = 1e-05
HIGHEST = lax.Precision.HIGHEST

@jax.custom_vjp
def low(v):
    return lax.optimization_barrier(v.astype(jnp.bfloat16)).astype(jnp.float32)

@jax.custom_vjp
def low_back(v):
    return v

def low_keep(v):
    return (low(v), None)

def low_pass(kept, grad):
    return (grad,)

def back_keep(v):
    return (v, None)

def back_low(kept, grad):
    return (low(grad),)
low.defvjp(low_keep, low_pass)
low_back.defvjp(back_keep, back_low)

def matmul_high(left_op, right_op):
    return jnp.dot(left_op, right_op, precision=HIGHEST, preferred_element_type=jnp.float32)

def linear(lowered, weight):
    return low_back(matmul_high(lowered, weight))

def layer_norm(values, gain_vec):
    center = values - lax.optimization_barrier(jnp.mean(values, axis=-1, keepdims=True))
    spread = lax.optimization_barrier(jnp.mean(center * center, axis=-1, keepdims=True))
    return center * lax.rsqrt(spread + EPSILON) * gain_vec

def attend(query_lin, key_lin, value_lin, valid_keys):
    rows_query = query_lin.shape[0]
    rows_key = key_lin.shape[0]
    query_heads = low(query_lin).reshape(rows_query, HEADS, -1)
    key_heads = low(key_lin).reshape(rows_key, HEADS, -1)
    value_heads = low(value_lin).reshape(rows_key, HEADS, -1)
    scale_factor = query_heads.shape[-1] ** (-0.5)
    scores = low_back(jnp.einsum('mhe,nhe->hmn', query_heads, key_heads, precision=HIGHEST) * scale_factor)
    scores = jnp.where(valid_keys[None, None, :], scores, -1e+30)
    row_peak = lax.optimization_barrier(jnp.max(scores, axis=-1, keepdims=True))
    exponent = jnp.exp(scores - row_peak)
    probability = exponent / lax.optimization_barrier(jnp.sum(exponent, axis=-1, keepdims=True))
    mixture = jnp.einsum('hmn,nhe->mhe', low(probability), value_heads, precision=HIGHEST)
    return low_back(mixture.reshape(rows_query, -1))

def forward_one(byte_in, byte_query, seq_length, latent_array, latent_mats, out_mats, byte_mats, dec_out, latent_gains, byte_gains):
    positions = jnp.arange(byte_in.shape[0], dtype=jnp.int32)
    valid_keys = positions < seq_length
    normed_in = low(layer_norm(byte_in, byte_gains[0]))
    enc_keys = linear(normed_in, byte_mats[0])
    enc_values = linear(normed_in, byte_mats[1])
    latent_zero = latent_array
    normed_q = low(layer_norm(latent_zero, latent_gains[0]))
    enc_mix = attend(linear(normed_q, latent_mats[0]), enc_keys, enc_values, valid_keys)
    latent_one = latent_zero + linear(low(enc_mix), out_mats[0])
    normed_f1 = low(layer_norm(latent_one, latent_gains[1]))
    latent_two = latent_one + linear(low(jax.nn.gelu(linear(normed_f1, latent_mats[1]))), latent_mats[2])
    normed_s = low(layer_norm(latent_two, latent_gains[2]))
    every_latent = jnp.ones((latent_two.shape[0],), bool)
    self_mix = attend(linear(normed_s, latent_mats[3]), linear(normed_s, latent_mats[4]), linear(normed_s, latent_mats[5]), every_latent)
    latent_three = latent_two + linear(low(self_mix), out_mats[1])
    normed_f2 = low(layer_norm(latent_three, latent_gains[3]))
    latent_four = latent_three + linear(low(jax.nn.gelu(linear(normed_f2, latent_mats[6]))), latent_mats[7])
    normed_c = low(layer_norm(latent_four, latent_gains[4]))
    normed_d = low(layer_norm(byte_query, byte_gains[1]))
    dec_mix = attend(linear(normed_d, byte_mats[2]), linear(normed_c, latent_mats[8]), linear(normed_c, latent_mats[9]), every_latent)
    return byte_query + linear(low(dec_mix), dec_out)

def reference(inputs, queries, lengths, latent_array, latent_mats, out_mats, byte_mats, dec_out, latent_gains, byte_gains, cotangent):

    def whole(all_inputs, all_queries, lat_array, lat_mats, lat_outs, byte_weights, dec_weight, lat_gains, bgains):

        def single(item):
            byte_in, byte_query, seq_length = item
            return forward_one(byte_in, byte_query, seq_length, lat_array, lat_mats, lat_outs, byte_weights, dec_weight, lat_gains, bgains)
        return lax.map(jax.checkpoint(single), (all_inputs, all_queries, lengths))
    primals = (inputs.astype(jnp.float32), queries.astype(jnp.float32), latent_array.astype(jnp.float32), latent_mats.astype(jnp.float32), out_mats.astype(jnp.float32), byte_mats.astype(jnp.float32), dec_out.astype(jnp.float32), latent_gains.astype(jnp.float32), byte_gains.astype(jnp.float32))
    output, pull_back = jax.vjp(whole, *primals)
    grads = pull_back(cotangent.astype(jnp.float32))
    return (output.astype(jnp.bfloat16), grads[0], grads[1], grads[2], grads[3], grads[4], grads[5], grads[6], grads[7], grads[8])
```

```python
import jax
import jax.numpy as jnp
from jax import lax
from jax.experimental import pallas as pl
from jax.experimental.pallas import tpu as pltpu
from jax.sharding import Mesh, PartitionSpec as P

F32, BF = jnp.float32, jnp.bfloat16
D, DI, R, N, H, E = 1280, 768, 256, 128, 8, 160
NX, NZ, NJ, NI = 4, 4, 16, 8
SCALE = E**-0.5
EPS = 1e-5
MIB = 1 << 20
AXES = ("y", "core", "x", "z")
BATCH = ("y", "core")
BLK = ("x", "z")
WIN = [128 * (E * h // 128) for h in range(H)]
OFF = [E * h - WIN[h] for h in range(H)]
SQUARE = [("o", 0), ("l", 1), ("l", 2), ("l", 3), ("l", 4), ("l", 5), ("o", 1), ("l", 6), ("l", 7), ("l", 8), ("l", 9)]
ROWS_I = 128
DEC_ROW, BQ_ROW = 880, 960


def dot(a, b, ca=1, cb=0):
    return lax.dot_general(a, b, (((ca,), (cb,)), ((), ())), preferred_element_type=F32)


def dot_nt(a, b):
    return dot(a, b, 1, 1)


def dot_tn(a, b):
    return dot(a, b, 0, 0)


def half(v):
    return v.astype(BF)


def norm(v):
    c = v - jnp.mean(v, axis=-1, keepdims=True)
    inv = lax.rsqrt(jnp.mean(c * c, axis=-1, keepdims=True) + EPS)
    return c * inv, inv


def norm_back(g, gain, n, inv):
    gg = jnp.sum(g * n, axis=0, keepdims=True)
    inner = g * gain
    m1 = jnp.mean(inner, axis=-1, keepdims=True)
    m2 = jnp.mean(inner * n, axis=-1, keepdims=True)
    return inv * (inner - m1 - n * m2), gg


C0, C1 = 0.7978845608028654, 0.044715


def gelu(x):
    return 0.5 * x * (1.0 + jnp.tanh(C0 * (x + C1 * x * x * x)))


def gelu_slope(x):
    t = jnp.tanh(C0 * (x + C1 * x * x * x))
    return 0.5 * (1.0 + t) + 0.5 * x * (1.0 - t * t) * (C0 * (1.0 + 3.0 * C1 * x * x))


def lanes(width):
    return lax.broadcasted_iota(jnp.int32, (1, width), 1)


def head_mask(h):
    lane = lanes(256)
    return jnp.where((lane >= OFF[h]) & (lane < OFF[h] + E), 1.0, 0.0).astype(F32)


def pieces(row, count):
    out = []
    done = 0
    while done < count:
        i, r0 = divmod(row + done, ROWS_I)
        n = min(count - done, ROWS_I - r0)
        out.append((i, r0, done, n))
        done += n
    return out


def split3(v):
    hi = half(v).astype(F32)
    mid = half(v - hi).astype(F32)
    lo = half(v - hi - mid).astype(F32)
    return hi, mid, lo


def pack3(v):
    hi, mid, lo = split3(v)
    return half(hi + pltpu.roll(mid, 16, 1) + pltpu.roll(lo, 32, 1))


def unpack3(v, axis):
    return v + pltpu.roll(v, 112, axis) + pltpu.roll(v, 96, axis)


def as_rows(parts, count):
    row = lax.broadcasted_iota(jnp.int32, (count, 128), 0)
    out = jnp.zeros((count, 128), F32)
    for r, part in parts:
        out = jnp.where(row == r, part, out)
    return out


def call(body, outs, args, scratch=(), vmem=48, flops=0, name=None):
    spaces = {"v": pltpu.VMEM, "a": pl.ANY, "s": pltpu.SMEM}
    return pl.pallas_call(
        body,
        out_shape=[jax.ShapeDtypeStruct(s, t) for s, t, _ in outs],
        in_specs=[pl.BlockSpec(memory_space=spaces[m]) for _, m in args],
        out_specs=[pl.BlockSpec(memory_space=spaces[m]) for _, _, m in outs],
        scratch_shapes=list(scratch),
        compiler_params=pltpu.CompilerParams(vmem_limit_bytes=vmem * MIB),
        cost_estimate=pl.CostEstimate(flops=int(flops), bytes_accessed=4 * MIB, transcendentals=0),
        name=name,
    )(*[a for a, _ in args])


DMA = pltpu.SemaphoreType.DMA


def pack_body(sc, lm, om, bm, do, la, g0, wsh, sem):
    i, core = sc[0], sc[4]
    cols = pl.ds(pl.multiple_of(core * 640, 128), 640)
    first = [
        pltpu.make_async_copy(bm.at[0, :, cols], g0.at[0:48, :], sem.at[8]),
        pltpu.make_async_copy(bm.at[1, :, cols], g0.at[48:96, :], sem.at[9]),
        pltpu.make_async_copy(lm.at[0, :, cols], g0.at[96:176, :], sem.at[10]),
        pltpu.make_async_copy(la.at[:, cols], g0.at[176:192, :], sem.at[11]),
    ]
    for c in first:
        c.start()
    blocks = [(80 * k, 80, (om if s == "o" else lm), n, D) for k, (s, n) in enumerate(SQUARE)]
    blocks += [(DEC_ROW, 80, do, None, DI), (BQ_ROW, 48, bm, 2, D)]
    for k in range(NI):
        lo, hi = ROWS_I * k, ROWS_I * (k + 1)

        @pl.when(i == k)
        def _(lo=lo, hi=hi):
            cs = []
            for row, count, ref, n, width in blocks:
                a, b = max(lo, row), min(hi, row + count)
                if a < b:
                    src = ref.at[a - row : b - row, :] if n is None else ref.at[n, a - row : b - row, :]
                    dst = wsh.at[a - lo : b - lo, :] if width == D else wsh.at[a - lo : b - lo, 0:width]
                    cs.append(pltpu.make_async_copy(src, dst, sem.at[len(cs)]))
            for c in cs:
                c.start()
            for c in cs:
                c.wait()

    for c in first:
        c.wait()


def enc_body(sc, t0, t1, t2, t3, u0, u1, u2, u3, x_in, bg, lg, g_out, nb_o, k_o, v_o, q_o, z_o, pay, gs, acc, sem):
    x, z, core = sc[2], sc[3], sc[4]
    copies = []
    for side, group in enumerate(((t0, t1, t2, t3), (u0, u1, u2, u3))):
        c = core if side == 0 else 1 - core
        col = pl.ds(pl.multiple_of(c * 640, 128), 640)
        for e in range(4):
            for d in range(4):
                xs = jnp.where(c == 0, (x + 4 - d) & 3, (x + 4 - e) & 3)
                zs = jnp.where(c == 0, (z + 4 - e) & 3, (z + 4 - d) & 3)
                copies.append(
                    pltpu.make_async_copy(group[e].at[d], gs.at[xs * 4 + zs, :, col], sem.at[len(copies)])
                )
    for c in copies:
        c.start()
    n_in, _ = norm(x_in[...].astype(F32))
    nb = half(n_in * bg[0:1, :])
    nb_o[...] = nb
    for c in copies:
        c.wait()
    save = pltpu.make_async_copy(gs, g_out, sem.at[32])
    save.start()
    k_o[...] = half(dot(nb, gs[:, 0:48, :].reshape(DI, D)))
    v_o[...] = half(dot(nb, gs[:, 48:96, :].reshape(DI, D)))
    z0b = gs[:, 176:192, :].reshape(R, D)
    z_o[...] = z0b
    nq, _ = norm(z0b.astype(F32))
    q_o[...] = half(dot(half(nq * lg[0:1, :]), gs[:, 96:176, :].reshape(D, D)))
    acc[...] = jnp.zeros_like(acc)
    valid = lanes(N) + sc[1] * N < sc[5]
    lane = lanes(128)
    stats = jnp.zeros((R, 128), F32)
    for h in range(H):
        w = slice(WIN[h], WIN[h] + 256)
        mk = head_mask(h)
        s = dot_nt(q_o[:, w] * half(mk), k_o[:, w]) * SCALE
        s = jnp.where(valid, s, -1e30)
        m = jnp.max(s, axis=-1, keepdims=True)
        p = jnp.exp(s - m)
        acc[:, w] += dot(half(p), v_o[:, w]) * mk
        stats = jnp.where(lane == h, m, stats)
        stats = jnp.where(lane == 8 + h, jnp.sum(p, axis=-1, keepdims=True), stats)
    pay[:, 0:D] = half(acc[...])
    pay[:, D : D + 128] = pack3(stats)
    save.wait()


def combine_body(rcv, out):
    st = unpack3(rcv[:, :, D : D + 128].astype(F32), 2)
    peak = jnp.max(st, axis=0, keepdims=True)
    w = jnp.exp(st - peak)
    total = jnp.sum(w * pltpu.roll(st, 120, 2), axis=0, keepdims=True)
    coef = w / total
    lane = lax.broadcasted_iota(jnp.int32, (1, 1, 128), 2)
    for t in range(10):
        h0, h1 = 128 * t // E, (128 * t + 127) // E
        c = coef[:, :, h0 : h0 + 1]
        if h1 != h0:
            c = jnp.where(lane >= E * h1 - 128 * t, coef[:, :, h1 : h1 + 1], c)
        o = jnp.sum(rcv[:, :, 128 * t : 128 * t + 128].astype(F32) * c, axis=0)
        out[:, 128 * t : 128 * t + 128] = half(o)
    lse = jnp.where(lanes(128) < 8, (peak + jnp.log(total))[0], 0.0)
    out[:, D : D + 128] = pack3(lse)


class Ring:
    def __init__(self, w, slots, sem, order):
        self.w, self.slots, self.sem, self.order = w, slots, sem, order
        self.n = slots.shape[0]
        self.pos = {m: k for k, m in enumerate(order)}

    def copies(self, m):
        s = self.pos[m] % self.n
        return [
            pltpu.make_async_copy(
                self.w.at[i, :, r0 : r0 + n, :], self.slots.at[s, :, d0 : d0 + n, :], self.sem.at[s, k]
            )
            for k, (i, r0, d0, n) in enumerate(pieces(80 * m, 80))
        ]

    def start(self, m):
        for c in self.copies(m):
            c.start()

    def begin(self):
        for m in self.order[: self.n]:
            self.start(m)

    def get(self, m):
        for c in self.copies(m):
            c.wait()
        return self.slots[self.pos[m] % self.n].reshape(D, D)

    def done(self, m):
        k = self.pos[m] + self.n
        if k < len(self.order):
            self.start(self.order[k])


def lat_forward_body(e, z0b, lg, w, kd, vd, z_h, h_h, a_h, slots, zs, hs, qs, acc, wsem, ssem):
    ring = Ring(w, slots, wsem, list(range(11)))
    ring.begin()
    saves = []

    def save(src, dst):
        c = pltpu.make_async_copy(src, dst, ssem.at[len(saves)])
        c.start()
        saves.append(c)

    def mul(a, m):
        out = dot(a, ring.get(m))
        ring.done(m)
        return out

    z1 = z0b[...].astype(F32) + mul(e[:, 0:D], 0)
    zs[0] = z1
    save(zs.at[0], z_h.at[0])
    h1 = mul(half(norm(z1)[0] * lg[1:2, :]), 1)
    hs[0] = h1
    save(hs.at[0], h_h.at[0])
    zs[1] = zs[0] + mul(half(gelu(h1)), 2)
    save(zs.at[1], z_h.at[1])
    s_b = half(norm(zs[1])[0] * lg[2:3, :])
    for k in range(3):
        qs[k] = half(mul(s_b, 3 + k))
        save(qs.at[k], a_h.at[k])
    acc[...] = jnp.zeros_like(acc)
    for h in range(H):
        win = slice(WIN[h], WIN[h] + 256)
        mk = head_mask(h)
        s = dot_nt(qs[0, :, win] * half(mk), qs[1, :, win]) * SCALE
        p = jnp.exp(s - jnp.max(s, axis=-1, keepdims=True))
        p = p / jnp.sum(p, axis=-1, keepdims=True)
        acc[:, win] += dot(half(p), qs[2, :, win]) * mk
    qs[3] = half(acc[...])
    save(qs.at[3], a_h.at[3])
    zs[2] = zs[1] + mul(qs[3], 6)
    save(zs.at[2], z_h.at[2])
    h2 = mul(half(norm(zs[2])[0] * lg[3:4, :]), 7)
    hs[1] = h2
    save(hs.at[1], h_h.at[1])
    zs[3] = zs[2] + mul(half(gelu(h2)), 8)
    save(zs.at[3], z_h.at[3])
    c_b = half(norm(zs[3])[0] * lg[4:5, :])
    kd[...] = half(mul(c_b, 9))
    vd[...] = half(mul(c_b, 10))
    for c in saves:
        c.wait()


def lat_backward_body(
    sc, e, gkv, lg, w, z_h, h_h, a_h, gmix, pack_o, g1c_o, gains_o, slots, zs, hs, qs, gs, acc, acc2, acc3, pack, wsem, ssem
):
    order = [9, 10, 8, 7, 6, 3, 4, 5, 2, 1, 0]
    ring = Ring(w, slots, wsem, order)
    loads = {}
    for k in (3, 2, 1, 0):
        loads["z", k] = pltpu.make_async_copy(z_h.at[k], zs.at[k], ssem.at[k])
        if k in (3, 2):
            loads["h", k - 2] = pltpu.make_async_copy(h_h.at[k - 2], hs.at[k - 2], ssem.at[k + 2])
    for k in range(4):
        loads["a", k] = pltpu.make_async_copy(a_h.at[k], qs.at[k], ssem.at[6 + k])
    loads["z", 3].start()
    ring.begin()
    loads["h", 1].start()
    loads["z", 2].start()
    for k in range(4):
        loads["a", k].start()
    for key in (("z", 1), ("h", 0), ("z", 0)):
        loads[key].start()
    pack[...] = jnp.zeros_like(pack)
    src = sc[1] * 80
    start = jnp.minimum((src >> 7) * 128, 1024)
    start = pl.multiple_of(start, 128)
    offset = src - start

    def window(target):
        v = gs[:, pl.ds(start, 256)]
        return pltpu.roll(v, (target - offset + 256) & 255, 1)

    lane = lanes(256)

    def weight_grad(a_b, g, m):
        gs[...] = g
        base = 128 * (80 * m // 128)
        to = 80 * m - base
        wide = 128 if to + 80 <= 128 else 256
        v = jnp.where((lane >= to) & (lane < to + 80), window(to), 0.0)
        pack[:, base : base + wide] += dot_tn(a_b, half(v[:, 0:wide]))

    def mul(g_b, m):
        out = dot_nt(g_b, ring.get(m))
        ring.done(m)
        return out

    gain_rows = []

    def gain(k, gg):
        for t in range(10):
            gain_rows.append((10 * (k - 1) + t, gg[:, 128 * t : 128 * t + 128]))

    gk = gkv[:, 0:D]
    gv = gkv[:, D : 2 * D]
    loads["z", 3].wait()
    n, inv = norm(zs[3])
    c_b = half(n * lg[4:5, :])
    weight_grad(c_b, gk.astype(F32), 9)
    weight_grad(c_b, gv.astype(F32), 10)
    gn = mul(gk, 9) + mul(gv, 10)
    g4, gg = norm_back(gn, lg[4:5, :], n, inv)
    gain(4, gg)
    acc[...] = g4
    loads["h", 1].wait()
    weight_grad(half(gelu(hs[1])), g4, 8)
    gh = mul(half(g4), 8) * gelu_slope(hs[1])
    loads["z", 2].wait()
    n, inv = norm(zs[2])
    weight_grad(half(n * lg[3:4, :]), gh, 7)
    g3, gg = norm_back(mul(half(gh), 7), lg[3:4, :], n, inv)
    gain(3, gg)
    acc[...] += g3
    g3 = acc[...]
    for k in range(4):
        loads["a", k].wait()
    weight_grad(qs[3], g3, 6)
    qs[4] = half(mul(half(g3), 6))
    acc2[...] = jnp.zeros_like(acc2)
    for k in range(2):
        acc3[k] = jnp.zeros_like(acc2)
    for h in range(H):
        win = slice(WIN[h], WIN[h] + 256)
        mk = head_mask(h)
        mkb = half(mk)
        s = dot_nt(qs[0, :, win] * mkb, qs[1, :, win]) * SCALE
        p = jnp.exp(s - jnp.max(s, axis=-1, keepdims=True))
        p = p / jnp.sum(p, axis=-1, keepdims=True)
        dp = dot_nt(qs[4, :, win] * mkb, qs[2, :, win])
        ds = half(p * (dp - jnp.sum(p * dp, axis=-1, keepdims=True)))
        acc2[:, win] += dot(ds, qs[1, :, win]) * mk
        acc3[0, :, win] += dot_tn(ds, qs[0, :, win]) * mk
        acc3[1, :, win] += dot_tn(half(p), qs[4, :, win]) * mk
    loads["z", 1].wait()
    n, inv = norm(zs[1])
    s_b = half(n * lg[2:3, :])
    gq = acc2[...] * SCALE
    weight_grad(s_b, gq, 3)
    gn = mul(half(gq), 3)
    gk = acc3[0] * SCALE
    weight_grad(s_b, gk, 4)
    gn = gn + mul(half(gk), 4)
    weight_grad(s_b, acc3[1], 5)
    gn = gn + mul(half(acc3[1]), 5)
    g2, gg = norm_back(gn, lg[2:3, :], n, inv)
    gain(2, gg)
    acc[...] += g2
    g2 = acc[...]
    loads["h", 0].wait()
    weight_grad(half(gelu(hs[0])), g2, 2)
    gh = mul(half(g2), 2) * gelu_slope(hs[0])
    loads["z", 0].wait()
    n, inv = norm(zs[0])
    weight_grad(half(n * lg[1:2, :]), gh, 1)
    g1, gg = norm_back(mul(half(gh), 1), lg[1:2, :], n, inv)
    gain(1, gg)
    acc[...] += g1
    g1 = acc[...]
    weight_grad(e[:, 0:D], g1, 0)
    g1c_o[...] = half(window(0)[:, 0:128])
    gmix[...] = half(mul(half(g1), 0))
    gains_o[...] = as_rows(gain_rows, 48)
    pack_o[...] = half(pack[...])


def dec_body(qin, cot, bg, kd, vd, w, res, gqin, pay, gain_o, mix_o, nd_o, gq_o, dec, bq, acc, gq, gkv, sem):
    copies = []
    for i, r0, d0, n in pieces(DEC_ROW, 80):
        copies.append(
            pltpu.make_async_copy(w.at[i, :, r0 : r0 + n, 0:DI], dec.at[:, d0 : d0 + n, :], sem.at[len(copies)])
        )
    for i, r0, d0, n in pieces(BQ_ROW, 48):
        copies.append(
            pltpu.make_async_copy(w.at[i, :, r0 : r0 + n, :], bq.at[:, d0 : d0 + n, :], sem.at[len(copies)])
        )
    for c in copies:
        c.start()
    x = qin[...].astype(F32)
    n, inv = norm(x)
    nd = half(n * bg[1:2, :])
    nd_o[...] = nd
    for c in copies:
        c.wait()
    wq = bq[...].reshape(DI, D)
    wd = dec[...].reshape(D, DI)
    gq_o[...] = half(dot(nd, wq))
    gq[...] = dot_nt(cot[...], wd)
    gm = half(gq[...])
    mix_o[...] = gm
    acc[...] = jnp.zeros_like(acc)
    gq[...] = jnp.zeros_like(gq)
    gkv[...] = jnp.zeros_like(gkv)
    for h in range(H):
        win = slice(WIN[h], WIN[h] + 256)
        mk = head_mask(h)
        mkb = half(mk)
        qw, gw, kw, vw = gq_o[:, win], mix_o[:, win], kd[:, win], vd[:, win]
        s = dot_nt(qw * mkb, kw) * SCALE
        p = jnp.exp(s - jnp.max(s, axis=-1, keepdims=True))
        p = p / jnp.sum(p, axis=-1, keepdims=True)
        pb = half(p)
        acc[:, win] += dot(pb, vw) * mk
        dp = dot_nt(gw * mkb, vw)
        ds = half(p * (dp - jnp.sum(p * dp, axis=-1, keepdims=True)))
        gq[:, win] += dot(ds, kw) * mk
        gkv[0, :, win] += dot_tn(ds, qw) * mk
        gkv[1, :, win] += dot_tn(pb, gw) * mk
    pay[:, 0:D] = half(gkv[0] * SCALE)
    pay[:, D : 2 * D] = half(gkv[1])
    mix = half(acc[...])
    mix_o[...] = mix
    res[...] = half(x + dot(mix, wd))
    gqb = half(gq[...] * SCALE)
    gq_o[...] = gqb
    gin, gg = norm_back(dot_nt(gqb, wq), bg[1:2, :], n, inv)
    gqin[...] = cot[...].astype(F32) + gin
    gain_o[...] = gg


def sum_rows_body(rcv, out):
    s = half(jnp.sum(rcv[...].astype(F32), axis=0))
    for k in range(NJ):
        out[k] = s


def dec_weights_body(mix, cot, nd, gq, out):
    g = half(dot_tn(mix[...], cot[...]))
    for i in range(NI):
        for t in range(6):
            out[i, 160 * t : 160 * t + 160, :] = g[160 * i : 160 * i + 160, 128 * t : 128 * t + 128]
    g = half(dot_tn(nd[...], gq[...]))
    for i in range(NI):
        for t in range(10):
            r = 960 + 96 * t
            out[i, r : r + 96, :] = g[96 * i : 96 * i + 96, 128 * t : 128 * t + 128]


def dec_spread_body(chunk, out, td, tb):
    fill = jnp.zeros((96, 128), F32)
    for t in range(6):
        v = jnp.concatenate([chunk[160 * t : 160 * t + 160, :].astype(F32), fill], axis=0)
        td[128 * t : 128 * t + 128, :] = v.T
    fill = jnp.zeros((32, 128), F32)
    for t in range(10):
        v = jnp.concatenate([chunk[960 + 96 * t : 960 + 96 * t + 96, :].astype(F32), fill], axis=0)
        tb[128 * t : 128 * t + 128, :] = v.T
    for j in range(NJ):
        out[j, 0:48, :] = half(td[48 * j : 48 * j + 48, 0:128])
        out[j, 48:96, :] = half(td[48 * j : 48 * j + 48, 128:256])
        out[j, 96:176, :] = half(tb[80 * j : 80 * j + 80, :])


def dec_finish_body(rcv, dec_o, bq_o):
    s = jnp.sum(rcv[...].astype(F32), axis=0)
    fill = jnp.zeros((80, 128), F32)
    a = jnp.concatenate([s[0:48], fill], axis=0).T
    b = jnp.concatenate([s[48:96], fill], axis=0).T
    dec_o[0:128, :] = a[:, 0:48]
    dec_o[128:160, :] = b[0:32, 0:48]
    c = jnp.concatenate([s[96:176], fill[0:48]], axis=0).T
    bq_o[...] = c[0:96, 0:80]


def enc_back_body(sc, gmix, e, q, k, v, x_in, bg, gd, g_all, gin_o, pay, wkv, gq, gkt, gvt, sem):
    load = pltpu.make_async_copy(g_all.at[:, 0:96, :], wkv, sem)
    load.start()
    lse = unpack3(e[:, D : D + 128].astype(F32), 1)
    valid = lanes(N) + sc[1] * N < sc[5]
    gq[...] = jnp.zeros_like(gq)
    for h in range(H):
        win = slice(WIN[h], WIN[h] + 256)
        mk = head_mask(h)
        mkb = half(mk)
        qw, gw, kw, vw = q[:, win], gmix[:, win], k[:, win], v[:, win]
        rd = jnp.sum(gw.astype(F32) * e[:, win].astype(F32) * mk, axis=-1, keepdims=True)
        s = dot_nt(qw * mkb, kw) * SCALE
        p = jnp.where(valid, jnp.exp(jnp.where(valid, s, -1e30) - lse[:, h : h + 1]), 0.0)
        dp = dot_nt(gw * mkb, vw)
        ds = half(p * (dp - rd))
        gq[:, win] += dot(ds, kw) * mk
        o = OFF[h]
        gkt[E * h : E * h + E, :] = half(dot_tn(qw, ds)[o : o + E, :] * SCALE)
        gvt[E * h : E * h + E, :] = half(dot_tn(gw, half(p))[o : o + E, :])
    for t in range(10):
        pay[:, 16 * t : 16 * t + 16, :] = half(gq[:, 128 * t : 128 * t + 128] * SCALE).reshape(NJ, 16, 128)
    pay[:, 160:240, :] = gkt[...].reshape(NJ, 80, 128)
    pay[:, 240:320, :] = gvt[...].reshape(NJ, 80, 128)
    n, inv = norm(x_in[...].astype(F32))
    load.wait()
    gnt = dot(wkv[:, 0:48, :].reshape(DI, D), gkt[...]) + dot(wkv[:, 48:96, :].reshape(DI, D), gvt[...])
    gin, gg = norm_back(gnt.T, bg[0:1, :], n, inv)
    gin_o[...] = gin
    rows = [(t, gg[:, 128 * t : 128 * t + 128]) for t in range(6)]
    rows += [(6 + t, gd[:, 128 * t : 128 * t + 128]) for t in range(6)]
    g = as_rows(rows, 16)
    hi = half(g)
    lo = half(g - hi.astype(F32))
    for j in range(NJ):
        pay[j, 320:336, :] = hi
        pay[j, 336:352, :] = lo


def tail_one_body(rcv, nf, lat_gain, g1c, out, left):
    gq = half(jnp.sum(rcv[:, 0:160, :].astype(F32), axis=0))
    left[...] = jnp.zeros_like(left)
    for s in range(NJ):
        left[0:80, 128 * s : 128 * s + 128] = rcv[s, 160:240, :]
        left[128:208, 128 * s : 128 * s + 128] = rcv[s, 240:320, :]
    wt = half(dot(left[...], nf[...]).T)
    b = jnp.sum(rcv[:, 320:352, :].astype(F32), axis=0)
    g = jnp.concatenate([b[0:16] + b[16:32], lat_gain[...]], axis=0)
    hi = half(g)
    lo = half(g - hi.astype(F32))
    for i in range(NI):
        out[i, 0:160, :] = gq
        out[i, 160:256, :] = wt[96 * i : 96 * i + 96, 0:128]
        out[i, 256:352, :] = wt[96 * i : 96 * i + 96, 128:256]
        out[i, 352:416, :] = hi
        out[i, 416:480, :] = lo
        out[i, 480:512, :] = g1c[32 * i : 32 * i + 32, :]


def tail_two_body(sc, rcv, z0b, lg, g_all, pay, wkv_o, byte_o, lat_o, g1s_o, w0, sem):
    load = pltpu.make_async_copy(g_all.at[:, 96:176, :], w0, sem)
    load.start()
    sums = jnp.sum(rcv[...].astype(F32), axis=0)
    wkv_o[0] = sums[160:256, 0:80]
    wkv_o[1] = sums[256:352, 0:80]
    g = sums[352:416] + sums[416:480]
    for t in range(6):
        for b in range(2):
            byte_o[b : b + 1, 128 * t : 128 * t + 128] = g[6 * b + t : 6 * b + t + 1, :]
    for t in range(10):
        for b in range(4):
            r = 16 + 10 * b + t
            lat_o[b : b + 1, 128 * t : 128 * t + 128] = g[r : r + 1, :]
    g1s_o[...] = sums[480:512]
    sg = jnp.concatenate([sums[16 * t : 16 * t + 16, :] for t in range(10)], axis=1)
    n, inv = norm(z0b[pl.ds(pl.multiple_of(sc[1] * 16, 16), 16), :].astype(F32))
    load.wait()
    gz, gg = norm_back(dot_nt(half(sg), w0[...].reshape(D, D)), lg[0:1, :], n, inv)
    g = as_rows([(t, gg[:, 128 * t : 128 * t + 128]) for t in range(10)], 16)
    hi = half(g)
    lo = half(g - hi.astype(F32))
    for j in range(NJ):
        s = min(128 * (80 * j // 128), 1024)
        o = 80 * j - s
        a, b = gz[:, s : s + 256], sg[:, s : s + 256]
        if o:
            a, b = pltpu.roll(a, 256 - o, 1), pltpu.roll(b, 256 - o, 1)
        pay[j, 0:16, :] = half(a[:, 0:128])
        pay[j, 16:32, :] = half(b[:, 0:128])
        pay[j, 32:48, :] = hi
        pay[j, 48:64, :] = lo


def tail_three_body(sc, rcv, z0b, lg, g1s, lat, pack, arr_o, lm_o, om_o, gain_o, w0):
    i = sc[0]
    nq = half(norm(z0b[...].astype(F32))[0] * lg[0:1, :])
    w0[...] = dot_tn(nq, rcv[:, 16:32, :].reshape(R, 128))
    lm_o[0] = w0[pl.ds(pl.multiple_of(i * 160, 32), 160), :][:, 0:80]
    gz = jnp.concatenate([rcv[2 * i, 0:16, :].astype(F32), rcv[2 * i + 1, 0:16, :].astype(F32)], axis=0)
    arr_o[...] = (gz + g1s[...])[:, 0:80]
    g = jnp.sum(rcv[:, 32:64, :].astype(F32), axis=0)
    g = g[0:16] + g[16:32]
    for t in range(10):
        gain_o[0:1, 128 * t : 128 * t + 128] = g[t : t + 1, :]
    gain_o[1:5, :] = lat[...]
    for m, (kind, n) in enumerate(SQUARE):
        base = 128 * (80 * m // 128)
        o = 80 * m - base
        wide = 128 if o + 80 <= 128 else 256
        v = pack[:, base : base + wide].astype(F32)
        if o:
            v = pltpu.roll(v, wide - o, 1)
        if kind == "l":
            lm_o[n] = v[:, 0:80]
        else:
            om_o[n] = v[:, 0:80]


def line(y, c, x, z):
    return ((y % 4) * 2 + c) * NJ + (x % 4) * NZ + (z % 4)


EVERY = [(y, c, x, z) for y in range(4) for c in range(2) for x in range(NX) for z in range(NZ)]


def along(stage, d):
    out = []
    for y, c, x, z in EVERY:
        on_x = (c == 0) == (stage == 0)
        out.append((line(y, c, x, z), line(y, c, x + d, z) if on_x else line(y, c, x, z + d)))
    return out


SWAP = [(line(y, c, x, z), line(y, 1 - c, x, z)) for y, c, x, z in EVERY]


def exchange(v, axes):
    flat = v.reshape(v.shape[0] * v.shape[1], v.shape[2])
    return lax.all_to_all(flat, axes, split_axis=0, concat_axis=0, tiled=True).reshape(v.shape)


def shards(inputs, queries, lengths, latent_array, latent_mats, out_mats, byte_mats, dec_out, lg, bg, cotangent):
    y, core, x, z = (lax.axis_index(a) for a in AXES)
    i, j = y * 2 + core, x * NZ + z
    sc = jnp.stack([i, j, x, z, core, lengths[0]]).astype(jnp.int32)
    xin, qin, cot = inputs[0], queries[0], cotangent[0]

    g0, wsh = call(
        pack_body,
        [((192, 640), BF, "a"), ((ROWS_I, D), BF, "a")],
        [(sc, "s"), (latent_mats, "a"), (out_mats, "a"), (byte_mats, "a"), (dec_out, "a"), (latent_array, "a")],
        [DMA((12,))],
        vmem=16,
        name="pack",
    )
    w = lax.all_gather(wsh, AXES, axis=0, tiled=True).reshape(NI, NJ, ROWS_I, D)

    s1 = jnp.stack([g0] + [lax.ppermute(g0, AXES, along(0, d)) for d in (1, 2, 3)])
    own = [s1] + [lax.ppermute(s1, AXES, along(1, d)) for d in (1, 2, 3)]
    sib = [lax.ppermute(v, AXES, SWAP) for v in own]
    g_all, nb, k_b, v_b, q_b, z0b, pay = call(
        enc_body,
        [
            ((NJ, 192, D), BF, "a"),
            ((N, DI), BF, "v"),
            ((N, D), BF, "v"),
            ((N, D), BF, "v"),
            ((R, D), BF, "v"),
            ((R, D), BF, "v"),
            ((R, D + 128), BF, "v"),
        ],
        [(sc, "s")] + [(v, "a") for v in own + sib] + [(xin, "v"), (bg, "v"), (lg, "v")],
        [pltpu.VMEM((NJ, 192, D), BF), pltpu.VMEM((R, D), F32), DMA((33,))],
        flops=3e9,
        name="enc",
    )
    rcv = exchange(pay.reshape(NJ, 16, D + 128), BLK)
    (mine,) = call(combine_body, [((16, D + 128), BF, "v")], [(rcv, "v")], name="combine")
    e = lax.all_gather(mine, BLK, axis=0, tiled=True)
    nf = lax.all_gather(nb, BLK, axis=0, tiled=True)

    big = (NJ, 80, D)
    kd, vd, z_h, h_h, a_h = call(
        lat_forward_body,
        [
            ((R, D), BF, "v"),
            ((R, D), BF, "v"),
            ((4, R, D), F32, "a"),
            ((2, R, D), F32, "a"),
            ((4, R, D), BF, "a"),
        ],
        [(e, "v"), (z0b, "v"), (lg, "v"), (w, "a")],
        [
            pltpu.VMEM((5,) + big, BF),
            pltpu.VMEM((4, R, D), F32),
            pltpu.VMEM((2, R, D), F32),
            pltpu.VMEM((4, R, D), BF),
            pltpu.VMEM((R, D), F32),
            DMA((5, 2)),
            DMA((10,)),
        ],
        vmem=56,
        flops=1.2e10,
        name="lat_forward",
    )
    res, gqin, dpay, gd, mix, nd, gq = call(
        dec_body,
        [
            ((N, DI), BF, "v"),
            ((N, DI), F32, "v"),
            ((R, 2 * D), BF, "v"),
            ((1, DI), F32, "v"),
            ((N, D), BF, "v"),
            ((N, DI), BF, "v"),
            ((N, D), BF, "v"),
        ],
        [(qin, "v"), (cot, "v"), (bg, "v"), (kd, "v"), (vd, "v"), (w, "a")],
        [
            pltpu.VMEM((NJ, 80, DI), BF),
            pltpu.VMEM((NJ, 48, D), BF),
            pltpu.VMEM((N, D), F32),
            pltpu.VMEM((N, D), F32),
            pltpu.VMEM((2, R, D), F32),
            DMA((3,)),
        ],
        flops=3e9,
        name="dec",
    )
    rows = exchange(dpay.reshape(NJ, 16, 2 * D), BLK)
    (dup,) = call(sum_rows_body, [((NJ, 16, 2 * D), BF, "v")], [(rows, "v")], name="sum_rows")
    gkv = exchange(dup, BLK).reshape(R, 2 * D)
    (dw,) = call(
        dec_weights_body,
        [((NI, 1920, 128), BF, "v")],
        [(mix, "v"), (cot, "v"), (nd, "v"), (gq, "v")],
        flops=5e8,
        name="dec_weights",
    )
    dw = lax.psum_scatter(dw.reshape(NI * 1920, 128), BATCH, scatter_dimension=0, tiled=True)
    (dspread,) = call(
        dec_spread_body,
        [((NJ, 176, 128), BF, "v")],
        [(dw, "v")],
        [pltpu.VMEM((DI, 256), F32), pltpu.VMEM((D, 128), F32)],
        name="dec_spread",
    )
    dwr = exchange(dspread, BLK)
    dec_grad, bq_grad = call(
        dec_finish_body, [((160, 48), F32, "v"), ((96, 80), F32, "v")], [(dwr, "v")], name="dec_finish"
    )

    gmix, pack, g1c, lat_gain = call(
        lat_backward_body,
        [((R, D), BF, "v"), ((D, 896), BF, "v"), ((R, 128), BF, "v"), ((48, 128), F32, "v")],
        [(sc, "s"), (e, "v"), (gkv, "v"), (lg, "v"), (w, "a"), (z_h, "a"), (h_h, "a"), (a_h, "a")],
        [
            pltpu.VMEM((4,) + big, BF),
            pltpu.VMEM((4, R, D), F32),
            pltpu.VMEM((2, R, D), F32),
            pltpu.VMEM((5, R, D), BF),
            pltpu.VMEM((R, D), F32),
            pltpu.VMEM((R, D), F32),
            pltpu.VMEM((R, D), F32),
            pltpu.VMEM((2, R, D), F32),
            pltpu.VMEM((D, 896), F32),
            DMA((4, 2)),
            DMA((10,)),
        ],
        vmem=58,
        flops=1.6e10,
        name="lat_backward",
    )
    pack = lax.psum_scatter(pack, BATCH, scatter_dimension=0, tiled=True)
    gin, epay = call(
        enc_back_body,
        [((N, DI), F32, "v"), ((NJ, 352, 128), BF, "v")],
        [(sc, "s"), (gmix, "v"), (e, "v"), (q_b, "v"), (k_b, "v"), (v_b, "v"), (xin, "v"), (bg, "v"), (gd, "v"), (g_all, "a")],
        [
            pltpu.VMEM((NJ, 96, D), BF),
            pltpu.VMEM((R, D), F32),
            pltpu.VMEM((D, N), BF),
            pltpu.VMEM((D, N), BF),
            DMA,
        ],
        flops=2e9,
        name="enc_back",
    )
    r1 = exchange(epay, BLK)
    (p2,) = call(
        tail_one_body,
        [((NI, 512, 128), BF, "v")],
        [(r1, "v"), (nf, "v"), (lat_gain, "v"), (g1c, "v")],
        [pltpu.VMEM((256, 2048), BF)],
        name="tail_one",
    )
    r2 = exchange(p2, BATCH)
    p3, wkv, byte_gain, lat4, g1s = call(
        tail_two_body,
        [
            ((NJ, 64, 128), BF, "v"),
            ((2, 96, 80), F32, "v"),
            ((2, DI), F32, "v"),
            ((4, D), F32, "v"),
            ((32, 128), F32, "v"),
        ],
        [(sc, "s"), (r2, "v"), (z0b, "v"), (lg, "v"), (g_all, "a")],
        [pltpu.VMEM(big, BF), DMA],
        name="tail_two",
    )
    r3 = exchange(p3, BLK)
    arr, lm, om, lat_gains = call(
        tail_three_body,
        [((32, 80), F32, "v"), ((10, 160, 80), F32, "v"), ((2, 160, 80), F32, "v"), ((5, D), F32, "v")],
        [(sc, "s"), (r3, "v"), (z0b, "v"), (lg, "v"), (g1s, "v"), (lat4, "v"), (pack, "v")],
        [pltpu.VMEM((D, 128), F32)],
        name="tail_three",
    )
    byte_grads = jnp.concatenate([wkv, bq_grad[None]], axis=0)
    return (res[None], gin[None], gqin[None], arr, lm, om, byte_grads, dec_grad, lat_gains, byte_gain)


def solution(mesh):
    grid = Mesh(mesh.devices.reshape(4, 2, NX, NZ), AXES)
    return jax.shard_map(
        shards,
        mesh=grid,
        in_specs=(
            P(BATCH, BLK, None),
            P(BATCH, BLK, None),
            P(BATCH),
            P(BLK, None),
            P(None, BLK, None),
            P(None, BLK, None),
            P(None, BLK, None),
            P(BLK, None),
            P(),
            P(),
            P(BATCH, BLK, None),
        ),
        out_specs=(
            P(BATCH, BLK, None),
            P(BATCH, BLK, None),
            P(BATCH, BLK, None),
            P(BATCH, BLK),
            P(None, BATCH, BLK),
            P(None, BATCH, BLK),
            P(None, BATCH, BLK),
            P(BATCH, BLK),
            P(),
            P(),
        ),
        check_vma=False,
    )
```

```python
import jax
import jax.numpy as jnp
from jax import lax
from jax.experimental import pallas as pl
from jax.experimental.pallas import tpu as pltpu
from jax.sharding import Mesh, PartitionSpec as P

F32, BF = jnp.float32, jnp.bfloat16
D, DI, R, N, H, E = 1280, 768, 256, 128, 8, 160
NX, NZ, NJ, NI = 4, 4, 16, 8
SCALE = E**-0.5
EPS = 1e-5
MIB = 1 << 20
AXES = ("y", "core", "x", "z")
BATCH = ("y", "core")
BLK = ("x", "z")
WIN = [128 * (E * h // 128) for h in range(H)]
OFF = [E * h - WIN[h] for h in range(H)]
SQUARE = [("o", 0), ("l", 1), ("l", 2), ("l", 3), ("l", 4), ("l", 5), ("o", 1), ("l", 6), ("l", 7), ("l", 8), ("l", 9)]
EARLY = 3
ROWS_I = 96
DEC_ROW, BQ_ROW = 640, 720


def dot(a, b, ca=1, cb=0):
    return lax.dot_general(a, b, (((ca,), (cb,)), ((), ())), preferred_element_type=F32)


def dot_nt(a, b):
    return dot(a, b, 1, 1)


def dot_tn(a, b):
    return dot(a, b, 0, 0)


def half(v):
    return v.astype(BF)


def norm(v):
    c = v - jnp.mean(v, axis=-1, keepdims=True)
    inv = lax.rsqrt(jnp.mean(c * c, axis=-1, keepdims=True) + EPS)
    return c * inv, inv


def norm_back(g, gain, n, inv):
    gg = jnp.sum(g * n, axis=0, keepdims=True)
    inner = g * gain
    m1 = jnp.mean(inner, axis=-1, keepdims=True)
    m2 = jnp.mean(inner * n, axis=-1, keepdims=True)
    return inv * (inner - m1 - n * m2), gg


C0, C1 = 0.7978845608028654, 0.044715


def gelu(x):
    return 0.5 * x * (1.0 + jnp.tanh(C0 * (x + C1 * x * x * x)))


def gelu_slope(x):
    t = jnp.tanh(C0 * (x + C1 * x * x * x))
    return 0.5 * (1.0 + t) + 0.5 * x * (1.0 - t * t) * (C0 * (1.0 + 3.0 * C1 * x * x))


def lanes(width):
    return lax.broadcasted_iota(jnp.int32, (1, width), 1)


def head_mask(h):
    lane = lanes(256)
    return jnp.where((lane >= OFF[h]) & (lane < OFF[h] + E), 1.0, 0.0).astype(F32)


def pieces(row, count):
    out = []
    done = 0
    while done < count:
        i, r0 = divmod(row + done, ROWS_I)
        n = min(count - done, ROWS_I - r0)
        out.append((i, r0, done, n))
        done += n
    return out


def split3(v):
    hi = half(v).astype(F32)
    mid = half(v - hi).astype(F32)
    lo = half(v - hi - mid).astype(F32)
    return hi, mid, lo


def pack3(v):
    hi, mid, lo = split3(v)
    return half(hi + pltpu.roll(mid, 16, 1) + pltpu.roll(lo, 32, 1))


def unpack3(v, axis):
    return v + pltpu.roll(v, 112, axis) + pltpu.roll(v, 96, axis)


def as_rows(parts, count):
    row = lax.broadcasted_iota(jnp.int32, (count, 128), 0)
    out = jnp.zeros((count, 128), F32)
    for r, part in parts:
        out = jnp.where(row == r, part, out)
    return out


def call(body, outs, args, scratch=(), vmem=48, flops=0, name=None):
    spaces = {"v": pltpu.VMEM, "a": pl.ANY, "s": pltpu.SMEM, "h": pltpu.HBM}
    return pl.pallas_call(
        body,
        out_shape=[jax.ShapeDtypeStruct(s, t) for s, t, _ in outs],
        in_specs=[pl.BlockSpec(memory_space=spaces[m]) for _, m in args],
        out_specs=[pl.BlockSpec(memory_space=spaces[m]) for _, _, m in outs],
        scratch_shapes=list(scratch),
        compiler_params=pltpu.CompilerParams(vmem_limit_bytes=vmem * MIB),
        cost_estimate=pl.CostEstimate(flops=int(flops), bytes_accessed=4 * MIB, transcendentals=0),
        name=name,
    )(*[a for a, _ in args])


DMA = pltpu.SemaphoreType.DMA


def pack_body(sc, lm, om, bm, do, la, g0, g1, wsh, sem):
    i, core = sc[0], sc[4]
    cols = pl.ds(pl.multiple_of(core * 640, 128), 640)
    first = [
        (bm.at[0, :, cols], g0.at[0:48, :]),
        (bm.at[1, :, cols], g0.at[48:96, :]),
        (lm.at[0, :, cols], g0.at[96:176, :]),
        (la.at[:, cols], g0.at[176:192, :]),
        (om.at[0, :, cols], g1.at[0:80, :]),
        (lm.at[1, :, cols], g1.at[80:160, :]),
        (lm.at[2, :, cols], g1.at[160:240, :]),
    ]
    first = [pltpu.make_async_copy(a, b, sem.at[8 + k]) for k, (a, b) in enumerate(first)]
    for c in first:
        c.start()
    blocks = [(80 * k, 80, (om if s == "o" else lm), n, D) for k, (s, n) in enumerate(SQUARE[EARLY:])]
    blocks += [(DEC_ROW, 80, do, None, DI), (BQ_ROW, 48, bm, 2, D)]
    for k in range(NI):
        lo, hi = ROWS_I * k, ROWS_I * (k + 1)

        @pl.when(i == k)
        def _(lo=lo, hi=hi):
            cs = []
            for row, count, ref, n, width in blocks:
                a, b = max(lo, row), min(hi, row + count)
                if a < b:
                    src = ref.at[a - row : b - row, :] if n is None else ref.at[n, a - row : b - row, :]
                    dst = wsh.at[a - lo : b - lo, :] if width == D else wsh.at[a - lo : b - lo, 0:width]
                    cs.append(pltpu.make_async_copy(src, dst, sem.at[len(cs)]))
            for c in cs:
                c.start()
            for c in cs:
                c.wait()

    for c in first:
        c.wait()


def pieces_from(sc, groups):
    x, z, core = sc[2], sc[3], sc[4]
    out = []
    for side in range(2):
        c = core if side == 0 else 1 - core
        col = pl.ds(pl.multiple_of(c * 640, 128), 640)
        for e in range(4):
            for d in range(4):
                xs = jnp.where(c == 0, (x + 4 - d) & 3, (x + 4 - e) & 3)
                zs = jnp.where(c == 0, (z + 4 - e) & 3, (z + 4 - d) & 3)
                out.append((xs * 4 + zs, col, groups[4 * side + e].at[d]))
    return out


def enc_body(sc, t0, t1, t2, t3, u0, u1, u2, u3, x_in, bg, lg, g_out, nb_o, k_o, v_o, q_o, pay, gs, acc, sem):
    copies = [
        pltpu.make_async_copy(src, gs.at[pos, :, col], sem.at[k])
        for k, (pos, col, src) in enumerate(pieces_from(sc, (t0, t1, t2, t3, u0, u1, u2, u3)))
    ]
    for c in copies:
        c.start()
    n_in, _ = norm(x_in[...].astype(F32))
    nb = half(n_in * bg[0:1, :])
    nb_o[...] = nb
    for c in copies:
        c.wait()
    save = pltpu.make_async_copy(gs, g_out, sem.at[32])
    save.start()
    k_o[...] = half(dot(nb, gs[:, 0:48, :].reshape(DI, D)))
    v_o[...] = half(dot(nb, gs[:, 48:96, :].reshape(DI, D)))
    z0b = gs[:, 176:192, :].reshape(R, D)
    nq, _ = norm(z0b.astype(F32))
    q_o[...] = half(dot(half(nq * lg[0:1, :]), gs[:, 96:176, :].reshape(D, D)))
    acc[...] = jnp.zeros_like(acc)
    valid = lanes(N) + sc[1] * N < sc[5]
    lane = lanes(128)
    stats = jnp.zeros((R, 128), F32)
    for h in range(H):
        w = slice(WIN[h], WIN[h] + 256)
        mk = head_mask(h)
        s = dot_nt(q_o[:, w] * half(mk), k_o[:, w]) * SCALE
        s = jnp.where(valid, s, -1e30)
        m = jnp.max(s, axis=-1, keepdims=True)
        p = jnp.exp(s - m)
        acc[:, w] += dot(half(p), v_o[:, w]) * mk
        stats = jnp.where(lane == h, m, stats)
        stats = jnp.where(lane == 8 + h, jnp.sum(p, axis=-1, keepdims=True), stats)
    pay[:, 0:D] = half(acc[...])
    pay[:, D : D + 128] = pack3(stats)
    save.wait()


def combine_body(rcv, out):
    st = unpack3(rcv[:, :, D : D + 128].astype(F32), 2)
    peak = jnp.max(st, axis=0, keepdims=True)
    w = jnp.exp(st - peak)
    total = jnp.sum(w * pltpu.roll(st, 120, 2), axis=0, keepdims=True)
    coef = w / total
    lane = lax.broadcasted_iota(jnp.int32, (1, 1, 128), 2)
    for t in range(10):
        h0, h1 = 128 * t // E, (128 * t + 127) // E
        c = coef[:, :, h0 : h0 + 1]
        if h1 != h0:
            c = jnp.where(lane >= E * h1 - 128 * t, coef[:, :, h1 : h1 + 1], c)
        o = jnp.sum(rcv[:, :, 128 * t : 128 * t + 128].astype(F32) * c, axis=0)
        out[:, 128 * t : 128 * t + 128] = half(o)
    lse = jnp.where(lanes(128) < 8, (peak + jnp.log(total))[0], 0.0)
    out[:, D : D + 128] = pack3(lse)


class Ring:
    def __init__(self, w, early, slots, sem, order):
        self.w, self.early, self.slots, self.sem, self.order = w, early, slots, sem, order
        self.n = slots.shape[0]
        self.pos = {m: k for k, m in enumerate(order)}

    def copies(self, m):
        s = self.pos[m] % self.n
        if m < EARLY:
            return [pltpu.make_async_copy(self.early.at[:, 80 * m : 80 * m + 80, :], self.slots.at[s], self.sem.at[s, 0])]
        return [
            pltpu.make_async_copy(
                self.w.at[i, :, r0 : r0 + n, :], self.slots.at[s, :, d0 : d0 + n, :], self.sem.at[s, k]
            )
            for k, (i, r0, d0, n) in enumerate(pieces(80 * (m - EARLY), 80))
        ]

    def start(self, m):
        for c in self.copies(m):
            c.start()

    def begin(self):
        for m in self.order[: self.n]:
            self.start(m)

    def get(self, m):
        for c in self.copies(m):
            c.wait()
        return self.slots[self.pos[m] % self.n].reshape(D, D)

    def done(self, m):
        k = self.pos[m] + self.n
        if k < len(self.order):
            self.start(self.order[k])


def lat_first_body(
    sc, e, g_all, lg, t0, t1, t2, t3, u0, u1, u2, u3, z_h, h_h, g1_h, z0b, gs, zs, hs, sem, ssem
):
    got = pieces_from(sc, (t0, t1, t2, t3, u0, u1, u2, u3))
    load = pltpu.make_async_copy(g_all.at[:, 176:192, :], z0b, ssem.at[4])
    load.start()
    copies = [
        [
            pltpu.make_async_copy(src.at[80 * m : 80 * m + 80, :], gs.at[pos, 80 * m : 80 * m + 80, col], sem.at[m, k])
            for k, (pos, col, src) in enumerate(got)
        ]
        for m in range(EARLY)
    ]
    for group in copies:
        for c in group:
            c.start()

    def mul(a, m):
        for c in copies[m]:
            c.wait()
        return dot(a, gs[:, 80 * m : 80 * m + 80, :].reshape(D, D))

    load.wait()
    z1 = z0b[...].reshape(R, D).astype(F32) + mul(e[:, 0:D], 0)
    zs[0] = z1
    saves = [pltpu.make_async_copy(zs.at[0], z_h.at[0], ssem.at[0])]
    saves[-1].start()
    h1 = mul(half(norm(z1)[0] * lg[1:2, :]), 1)
    hs[...] = h1
    saves.append(pltpu.make_async_copy(hs, h_h, ssem.at[1]))
    saves[-1].start()
    z2 = zs[0] + mul(half(gelu(h1)), 2)
    saves.append(pltpu.make_async_copy(gs, g1_h, ssem.at[3]))
    saves[-1].start()
    zs[1] = z2
    saves.append(pltpu.make_async_copy(zs.at[1], z_h.at[1], ssem.at[2]))
    saves[-1].start()
    for c in saves:
        c.wait()


def forward_body(
    qin, cot, bg, lg, zin, w,
    res, gqin, gain_o, pay, mix_o, nd_o, gq_o, z_h, h_h, a_h,
    slots, zs, hs, qs, acc, kd, vd, dec, bq, dacc, gq, gkv, wsem, ssem, lsem,
):
    load = pltpu.make_async_copy(zin.at[1], zs.at[0], lsem.at[3])
    load.start()
    ring = Ring(w, None, slots, wsem, list(range(EARLY, 11)))
    ring.begin()
    copies = []
    for i, r0, d0, n in pieces(BQ_ROW, 48):
        copies.append(pltpu.make_async_copy(w.at[i, :, r0 : r0 + n, :], bq.at[:, d0 : d0 + n, :], lsem.at[0]))
    for i, r0, d0, n in pieces(DEC_ROW, 80):
        copies.append(
            pltpu.make_async_copy(w.at[i, :, r0 : r0 + n, 0:DI], dec.at[:, d0 : d0 + n, :], lsem.at[len(copies)])
        )
    for c in copies:
        c.start()
    saves = []

    def save(src, dst):
        c = pltpu.make_async_copy(src, dst, ssem.at[len(saves)])
        c.start()
        saves.append(c)

    def mul(a, m):
        out = dot(a, ring.get(m))
        ring.done(m)
        return out

    load.wait()
    s_b = half(norm(zs[0])[0] * lg[2:3, :])
    for k in range(3):
        qs[k] = half(mul(s_b, 3 + k))
        save(qs.at[k], a_h.at[k])
    acc[...] = jnp.zeros_like(acc)
    for h in range(H):
        win = slice(WIN[h], WIN[h] + 256)
        mk = head_mask(h)
        s = dot_nt(qs[0, :, win] * half(mk), qs[1, :, win]) * SCALE
        p = jnp.exp(s - jnp.max(s, axis=-1, keepdims=True))
        p = p / jnp.sum(p, axis=-1, keepdims=True)
        acc[:, win] += dot(half(p), qs[2, :, win]) * mk
    qs[3] = half(acc[...])
    save(qs.at[3], a_h.at[3])
    zs[1] = zs[0] + mul(qs[3], 6)
    save(zs.at[1], z_h.at[0])
    h2 = mul(half(norm(zs[1])[0] * lg[3:4, :]), 7)
    hs[...] = h2
    save(hs, h_h)
    zs[2] = zs[1] + mul(half(gelu(h2)), 8)
    save(zs.at[2], z_h.at[1])
    c_b = half(norm(zs[2])[0] * lg[4:5, :])
    kd[...] = half(mul(c_b, 9))
    vd[...] = half(mul(c_b, 10))

    x = qin[...].astype(F32)
    n, inv = norm(x)
    nd = half(n * bg[1:2, :])
    nd_o[...] = nd
    for c in copies:
        c.wait()
    wq = bq[...].reshape(DI, D)
    wd = dec[...].reshape(D, DI)
    gq_o[...] = half(dot(nd, wq))
    mix_o[...] = half(dot_nt(cot[...], wd))
    dacc[...] = jnp.zeros_like(dacc)
    gq[...] = jnp.zeros_like(gq)
    gkv[...] = jnp.zeros_like(gkv)
    for h in range(H):
        win = slice(WIN[h], WIN[h] + 256)
        mk = head_mask(h)
        mkb = half(mk)
        qw, gw, kw, vw = gq_o[:, win], mix_o[:, win], kd[:, win], vd[:, win]
        s = dot_nt(qw * mkb, kw) * SCALE
        p = jnp.exp(s - jnp.max(s, axis=-1, keepdims=True))
        p = p / jnp.sum(p, axis=-1, keepdims=True)
        pb = half(p)
        dacc[:, win] += dot(pb, vw) * mk
        dp = dot_nt(gw * mkb, vw)
        ds = half(p * (dp - jnp.sum(p * dp, axis=-1, keepdims=True)))
        gq[:, win] += dot(ds, kw) * mk
        gkv[0, :, win] += dot_tn(ds, qw) * mk
        gkv[1, :, win] += dot_tn(pb, gw) * mk
    pay[:, 0:D] = half(gkv[0] * SCALE)
    pay[:, D : 2 * D] = half(gkv[1])
    mix = half(dacc[...])
    mix_o[...] = mix
    res[...] = half(x + dot(mix, wd))
    gqb = half(gq[...] * SCALE)
    gq_o[...] = gqb
    gin, gg = norm_back(dot_nt(gqb, wq), bg[1:2, :], n, inv)
    gqin[...] = cot[...].astype(F32) + gin
    gain_o[...] = gg
    for c in saves:
        c.wait()


def lat_backward_body(
    sc, e, gkv, lg, w, g1_h, za_h, ha_h, zb_h, hb_h, a_h, gmix, pack_o, g1c_o, gains_o, slots, zs, hs, qs, gs, acc, acc2, acc3, pack, wsem, ssem
):
    order = [9, 10, 8, 7, 6, 3, 4, 5, 2, 1, 0]
    ring = Ring(w, g1_h, slots, wsem, order)
    z_src = (za_h.at[0], za_h.at[1], zb_h.at[0], zb_h.at[1])
    h_src = (ha_h, hb_h)
    loads = {}
    for k in (3, 2, 1, 0):
        loads["z", k] = pltpu.make_async_copy(z_src[k], zs.at[k], ssem.at[k])
        if k in (3, 2):
            loads["h", k - 2] = pltpu.make_async_copy(h_src[k - 2], hs.at[k - 2], ssem.at[k + 2])
    for k in range(4):
        loads["a", k] = pltpu.make_async_copy(a_h.at[k], qs.at[k], ssem.at[6 + k])
    loads["z", 3].start()
    ring.begin()
    loads["h", 1].start()
    loads["z", 2].start()
    for k in range(4):
        loads["a", k].start()
    for key in (("z", 1), ("h", 0), ("z", 0)):
        loads[key].start()
    pack[...] = jnp.zeros_like(pack)
    src = sc[1] * 80
    start = jnp.minimum((src >> 7) * 128, 1024)
    start = pl.multiple_of(start, 128)
    offset = src - start

    def window(target):
        v = gs[:, pl.ds(start, 256)]
        return pltpu.roll(v, (target - offset + 256) & 255, 1)

    lane = lanes(256)

    def weight_grad(a_b, g, m):
        gs[...] = g
        base = 128 * (80 * m // 128)
        to = 80 * m - base
        wide = 128 if to + 80 <= 128 else 256
        v = jnp.where((lane >= to) & (lane < to + 80), window(to), 0.0)
        pack[:, base : base + wide] += dot_tn(a_b, half(v[:, 0:wide]))

    def mul(g_b, m):
        out = dot_nt(g_b, ring.get(m))
        ring.done(m)
        return out

    gain_rows = []

    def gain(k, gg):
        for t in range(10):
            gain_rows.append((10 * (k - 1) + t, gg[:, 128 * t : 128 * t + 128]))

    gk = gkv[:, 0:D]
    gv = gkv[:, D : 2 * D]
    loads["z", 3].wait()
    n, inv = norm(zs[3])
    c_b = half(n * lg[4:5, :])
    weight_grad(c_b, gk.astype(F32), 9)
    weight_grad(c_b, gv.astype(F32), 10)
    gn = mul(gk, 9) + mul(gv, 10)
    g4, gg = norm_back(gn, lg[4:5, :], n, inv)
    gain(4, gg)
    acc[...] = g4
    loads["h", 1].wait()
    weight_grad(half(gelu(hs[1])), g4, 8)
    gh = mul(half(g4), 8) * gelu_slope(hs[1])
    loads["z", 2].wait()
    n, inv = norm(zs[2])
    weight_grad(half(n * lg[3:4, :]), gh, 7)
    g3, gg = norm_back(mul(half(gh), 7), lg[3:4, :], n, inv)
    gain(3, gg)
    acc[...] += g3
    g3 = acc[...]
    for k in range(4):
        loads["a", k].wait()
    weight_grad(qs[3], g3, 6)
    qs[4] = half(mul(half(g3), 6))
    acc2[...] = jnp.zeros_like(acc2)
    for k in range(2):
        acc3[k] = jnp.zeros_like(acc2)
    for h in range(H):
        win = slice(WIN[h], WIN[h] + 256)
        mk = head_mask(h)
        mkb = half(mk)
        s = dot_nt(qs[0, :, win] * mkb, qs[1, :, win]) * SCALE
        p = jnp.exp(s - jnp.max(s, axis=-1, keepdims=True))
        p = p / jnp.sum(p, axis=-1, keepdims=True)
        dp = dot_nt(qs[4, :, win] * mkb, qs[2, :, win])
        ds = half(p * (dp - jnp.sum(p * dp, axis=-1, keepdims=True)))
        acc2[:, win] += dot(ds, qs[1, :, win]) * mk
        acc3[0, :, win] += dot_tn(ds, qs[0, :, win]) * mk
        acc3[1, :, win] += dot_tn(half(p), qs[4, :, win]) * mk
    loads["z", 1].wait()
    n, inv = norm(zs[1])
    s_b = half(n * lg[2:3, :])
    gq = acc2[...] * SCALE
    weight_grad(s_b, gq, 3)
    gn = mul(half(gq), 3)
    gk = acc3[0] * SCALE
    weight_grad(s_b, gk, 4)
    gn = gn + mul(half(gk), 4)
    weight_grad(s_b, acc3[1], 5)
    gn = gn + mul(half(acc3[1]), 5)
    g2, gg = norm_back(gn, lg[2:3, :], n, inv)
    gain(2, gg)
    acc[...] += g2
    g2 = acc[...]
    loads["h", 0].wait()
    weight_grad(half(gelu(hs[0])), g2, 2)
    gh = mul(half(g2), 2) * gelu_slope(hs[0])
    loads["z", 0].wait()
    n, inv = norm(zs[0])
    weight_grad(half(n * lg[1:2, :]), gh, 1)
    g1, gg = norm_back(mul(half(gh), 1), lg[1:2, :], n, inv)
    gain(1, gg)
    acc[...] += g1
    g1 = acc[...]
    weight_grad(e[:, 0:D], g1, 0)
    g1c_o[...] = half(window(0)[:, 0:128])
    gmix[...] = half(mul(half(g1), 0))
    gains_o[...] = as_rows(gain_rows, 48)
    pack_o[...] = half(pack[...])


def sum_rows_body(rcv, out):
    s = half(jnp.sum(rcv[...].astype(F32), axis=0))
    for k in range(NJ):
        out[k] = s


def dec_weights_body(mix, cot, nd, gq, out, buf, sem):
    g = half(dot_tn(mix[...], cot[...]))
    for i in range(NI):
        for t in range(6):
            buf[i, 160 * t : 160 * t + 160, :] = g[160 * i : 160 * i + 160, 128 * t : 128 * t + 128]
    one = pltpu.make_async_copy(buf.at[:, 0:960, :], out.at[:, 0:960, :], sem.at[0])
    one.start()
    g = half(dot_tn(nd[...], gq[...]))
    for i in range(NI):
        for t in range(10):
            r = 960 + 96 * t
            buf[i, r : r + 96, :] = g[96 * i : 96 * i + 96, 128 * t : 128 * t + 128]
    two = pltpu.make_async_copy(buf.at[:, 960:1920, :], out.at[:, 960:1920, :], sem.at[1])
    two.start()
    one.wait()
    two.wait()


def dec_spread_body(chunk, out, td, tb):
    fill = jnp.zeros((96, 128), F32)
    for t in range(6):
        v = jnp.concatenate([chunk[160 * t : 160 * t + 160, :].astype(F32), fill], axis=0)
        td[128 * t : 128 * t + 128, :] = v.T
    fill = jnp.zeros((32, 128), F32)
    for t in range(10):
        v = jnp.concatenate([chunk[960 + 96 * t : 960 + 96 * t + 96, :].astype(F32), fill], axis=0)
        tb[128 * t : 128 * t + 128, :] = v.T
    for j in range(NJ):
        out[j, 0:48, :] = half(td[48 * j : 48 * j + 48, 0:128])
        out[j, 48:96, :] = half(td[48 * j : 48 * j + 48, 128:256])
        out[j, 96:176, :] = half(tb[80 * j : 80 * j + 80, :])


def dec_finish_body(rcv, dec_o, bq_o):
    s = jnp.sum(rcv[...].astype(F32), axis=0)
    fill = jnp.zeros((80, 128), F32)
    a = jnp.concatenate([s[0:48], fill], axis=0).T
    b = jnp.concatenate([s[48:96], fill], axis=0).T
    dec_o[0:128, :] = a[:, 0:48]
    dec_o[128:160, :] = b[0:32, 0:48]
    c = jnp.concatenate([s[96:176], fill[0:48]], axis=0).T
    bq_o[...] = c[0:96, 0:80]


def enc_back_body(sc, x_in, bg, lg, gd, gmix_h, e_h, q_h, k_h, v_h, g_all, gin_o, pay, gmix, e, q, k, v, wkv, gq, gkt, gvt, sem):
    pairs = [(gmix_h, gmix), (q_h, q), (k_h, k), (v_h, v), (e_h, e), (g_all, wkv)]
    loads = [pltpu.make_async_copy(a, b, sem.at[n]) for n, (a, b) in enumerate(pairs)]
    for c in loads:
        c.start()
    for c in loads[:5]:
        c.wait()
    lse = unpack3(e[:, D : D + 128].astype(F32), 1)
    valid = lanes(N) + sc[1] * N < sc[5]
    gq[...] = jnp.zeros_like(gq)
    for h in range(H):
        win = slice(WIN[h], WIN[h] + 256)
        mk = head_mask(h)
        mkb = half(mk)
        qw, gw, kw, vw = q[:, win], gmix[:, win], k[:, win], v[:, win]
        rd = jnp.sum(gw.astype(F32) * e[:, win].astype(F32) * mk, axis=-1, keepdims=True)
        s = dot_nt(qw * mkb, kw) * SCALE
        p = jnp.where(valid, jnp.exp(jnp.where(valid, s, -1e30) - lse[:, h : h + 1]), 0.0)
        dp = dot_nt(gw * mkb, vw)
        ds = half(p * (dp - rd))
        gq[:, win] += dot(ds, kw) * mk
        o = OFF[h]
        gkt[E * h : E * h + E, :] = half(dot_tn(qw, ds)[o : o + E, :] * SCALE)
        gvt[E * h : E * h + E, :] = half(dot_tn(gw, half(p))[o : o + E, :])
    pay[:, 320:400, :] = gkt[...].reshape(NJ, 80, 128)
    pay[:, 400:480, :] = gvt[...].reshape(NJ, 80, 128)
    loads[5].wait()
    gqs = gq[...] * SCALE
    gqt = half(gqs.T)
    pay[:, 160:240, :] = gqt[:, 0:128].reshape(NJ, 80, 128)
    pay[:, 240:320, :] = gqt[:, 128:256].reshape(NJ, 80, 128)
    n, inv = norm(wkv[:, 176:192, :].reshape(R, D).astype(F32))
    gz, g0 = norm_back(dot_nt(half(gqs), wkv[:, 96:176, :].reshape(D, D)), lg[0:1, :], n, inv)
    gzt = half(gz.T)
    pay[:, 0:80, :] = gzt[:, 0:128].reshape(NJ, 80, 128)
    pay[:, 80:160, :] = gzt[:, 128:256].reshape(NJ, 80, 128)
    n, inv = norm(x_in[...].astype(F32))
    gnt = dot(wkv[:, 0:48, :].reshape(DI, D), gkt[...]) + dot(wkv[:, 48:96, :].reshape(DI, D), gvt[...])
    gin, gg = norm_back(gnt.T, bg[0:1, :], n, inv)
    gin_o[...] = gin
    rows = [(t, gg[:, 128 * t : 128 * t + 128]) for t in range(6)]
    rows += [(6 + t, gd[:, 128 * t : 128 * t + 128]) for t in range(6)]
    rows += [(16 + t, g0[:, 128 * t : 128 * t + 128]) for t in range(10)]
    g = half(as_rows(rows, 32))
    for j in range(NJ):
        pay[j, 480:512, :] = g


def tail_one_body(rcv, nf_h, g_all, lg, lat_gain, g1c, out, nf, z0b, left, sem):
    loads = [
        pltpu.make_async_copy(nf_h, nf, sem.at[0]),
        pltpu.make_async_copy(g_all.at[:, 176:192, :], z0b, sem.at[1]),
    ]
    for c in loads:
        c.start()
    sums = jnp.sum(rcv[:, 0:320, :].astype(F32), axis=0)
    fill = jnp.zeros((48, 128), F32)
    left[...] = jnp.zeros_like(left)
    for s in range(NJ):
        left[0:80, 128 * s : 128 * s + 128] = rcv[s, 320:400, :]
        left[128:208, 128 * s : 128 * s + 128] = rcv[s, 400:480, :]
    loads[1].wait()
    nq = half(norm(z0b[...].reshape(R, D).astype(F32))[0] * lg[0:1, :])
    a = jnp.concatenate([sums[160:240], fill], axis=0).T
    b = jnp.concatenate([sums[240:320], fill], axis=0).T
    w0 = half(dot_tn(nq, half(jnp.concatenate([a, b], axis=0))))
    a = jnp.concatenate([sums[0:80], fill], axis=0).T
    b = jnp.concatenate([sums[80:160], fill], axis=0).T
    gz = half(jnp.concatenate([a, b], axis=0) + g1c[...].astype(F32))
    gains = jnp.sum(rcv[:, 480:512, :].astype(F32), axis=0)
    gains = half(jnp.concatenate([gains, lat_gain[...]], axis=0))
    loads[0].wait()
    wt = half(dot(left[...], nf[...]).T)
    for i in range(NI):
        out[i, 0:160, :] = w0[160 * i : 160 * i + 160, :]
        out[i, 160:192, :] = gz[32 * i : 32 * i + 32, :]
        out[i, 192:288, :] = wt[96 * i : 96 * i + 96, 0:128]
        out[i, 288:384, :] = wt[96 * i : 96 * i + 96, 128:256]
        out[i, 384:464, :] = gains


def tail_two_body(rcv, pack, arr_o, lm_o, om_o, wkv_o, lat_o, byte_o):
    sums = jnp.sum(rcv[...].astype(F32), axis=0)
    lm_o[0] = sums[0:160, 0:80]
    arr_o[...] = sums[160:192, 0:80]
    wkv_o[0] = sums[192:288, 0:80]
    wkv_o[1] = sums[288:384, 0:80]
    g = sums[384:464]
    for t in range(6):
        for b in range(2):
            byte_o[b : b + 1, 128 * t : 128 * t + 128] = g[6 * b + t : 6 * b + t + 1, :]
    for t in range(10):
        for b in range(5):
            r = 16 + t if b == 0 else 32 + 10 * (b - 1) + t
            lat_o[b : b + 1, 128 * t : 128 * t + 128] = g[r : r + 1, :]
    for m, (kind, n) in enumerate(SQUARE):
        base = 128 * (80 * m // 128)
        o = 80 * m - base
        wide = 128 if o + 80 <= 128 else 256
        v = pack[:, base : base + wide].astype(F32)
        if o:
            v = pltpu.roll(v, wide - o, 1)
        if kind == "l":
            lm_o[n] = v[:, 0:80]
        else:
            om_o[n] = v[:, 0:80]


def line(y, c, x, z):
    return ((y % 4) * 2 + c) * NJ + (x % 4) * NZ + (z % 4)


EVERY = [(y, c, x, z) for y in range(4) for c in range(2) for x in range(NX) for z in range(NZ)]


def along(stage, d):
    out = []
    for y, c, x, z in EVERY:
        on_x = (c == 0) == (stage == 0)
        out.append((line(y, c, x, z), line(y, c, x + d, z) if on_x else line(y, c, x, z + d)))
    return out


SWAP = [(line(y, c, x, z), line(y, 1 - c, x, z)) for y, c, x, z in EVERY]


def exchange(v, axes):
    flat = v.reshape(v.shape[0] * v.shape[1], v.shape[2])
    return lax.all_to_all(flat, axes, split_axis=0, concat_axis=0, tiled=True).reshape(v.shape)


def shards(inputs, queries, lengths, latent_array, latent_mats, out_mats, byte_mats, dec_out, lg, bg, cotangent):
    y, core, x, z = (lax.axis_index(a) for a in AXES)
    i, j = y * 2 + core, x * NZ + z
    sc = jnp.stack([i, j, x, z, core, lengths[0]]).astype(jnp.int32)
    xin, qin, cot = inputs[0], queries[0], cotangent[0]

    g0, g1, wsh = call(
        pack_body,
        [((192, 640), BF, "h"), ((240, 640), BF, "h"), ((ROWS_I, D), BF, "h")],
        [(sc, "s"), (latent_mats, "h"), (out_mats, "h"), (byte_mats, "h"), (dec_out, "h"), (latent_array, "h")],
        [DMA((15,))],
        vmem=16,
        name="pack",
    )
    w = lax.all_gather(wsh, AXES, axis=0, tiled=True).reshape(NI, NJ, ROWS_I, D)

    def step(v, stage):
        return [lax.ppermute(v, AXES, along(stage, d)) for d in (1, 2, 3)]

    s0 = jnp.stack([g0] + step(g0, 0))
    own0 = [s0] + step(s0, 1)
    g1, _ = lax.optimization_barrier((g1, s0))
    sib0 = [lax.ppermute(v, AXES, SWAP) for v in own0]
    s1 = jnp.stack([g1] + step(g1, 0))
    s1, *_ = lax.optimization_barrier((s1, *own0[1:]))
    own1 = [s1] + step(s1, 1)
    sib1 = [lax.ppermute(v, AXES, SWAP) for v in own1]

    g_all, nb, k_b, v_b, q_b, pay = call(
        enc_body,
        [
            ((NJ, 192, D), BF, "h"),
            ((N, DI), BF, "v"),
            ((N, D), BF, "v"),
            ((N, D), BF, "v"),
            ((R, D), BF, "v"),
            ((R, D + 128), BF, "v"),
        ],
        [(sc, "s")] + [(v, "h") for v in own0 + sib0] + [(xin, "v"), (bg, "v"), (lg, "v")],
        [pltpu.VMEM((NJ, 192, D), BF), pltpu.VMEM((R, D), F32), DMA((33,))],
        flops=3e9,
        name="enc",
    )
    rcv = exchange(pay.reshape(NJ, 16, D + 128), BLK)
    (mine,) = call(combine_body, [((16, D + 128), BF, "v")], [(rcv, "v")], name="combine")
    e = lax.all_gather(mine, BLK, axis=0, tiled=True)
    nf = lax.all_gather(nb, BLK, axis=0, tiled=True)

    big = (NJ, 80, D)
    za, ha, g1_all = call(
        lat_first_body,
        [((2, R, D), F32, "h"), ((R, D), F32, "h"), ((NJ, 240, D), BF, "h")],
        [(sc, "s"), (e, "v"), (g_all, "h"), (lg, "v")] + [(v, "h") for v in own1 + sib1],
        [
            pltpu.VMEM((NJ, 16, D), BF),
            pltpu.VMEM((NJ, 240, D), BF),
            pltpu.VMEM((2, R, D), F32),
            pltpu.VMEM((R, D), F32),
            DMA((EARLY, 32)),
            DMA((5,)),
        ],
        flops=4e9,
        name="lat_first",
    )
    res, gqin, gd, dpay, mix, nd, gq, zb, hb, a_h = call(
        forward_body,
        [
            ((N, DI), BF, "v"),
            ((N, DI), F32, "v"),
            ((1, DI), F32, "v"),
            ((R, 2 * D), BF, "v"),
            ((N, D), BF, "v"),
            ((N, DI), BF, "v"),
            ((N, D), BF, "v"),
            ((2, R, D), F32, "h"),
            ((R, D), F32, "h"),
            ((4, R, D), BF, "h"),
        ],
        [(qin, "v"), (cot, "v"), (bg, "v"), (lg, "v"), (za, "h"), (w, "h")],
        [
            pltpu.VMEM((5,) + big, BF),
            pltpu.VMEM((3, R, D), F32),
            pltpu.VMEM((R, D), F32),
            pltpu.VMEM((4, R, D), BF),
            pltpu.VMEM((R, D), F32),
            pltpu.VMEM((R, D), BF),
            pltpu.VMEM((R, D), BF),
            pltpu.VMEM((NJ, 80, DI), BF),
            pltpu.VMEM((NJ, 48, D), BF),
            pltpu.VMEM((N, D), F32),
            pltpu.VMEM((N, D), F32),
            pltpu.VMEM((2, R, D), F32),
            DMA((5, 2)),
            DMA((8,)),
            DMA((4,)),
        ],
        vmem=58,
        flops=1.2e10,
        name="forward",
    )
    rows = exchange(dpay.reshape(NJ, 16, 2 * D), BLK)
    (dup,) = call(sum_rows_body, [((NJ, 16, 2 * D), BF, "v")], [(rows, "v")], name="sum_rows")
    gkv = exchange(dup, BLK).reshape(R, 2 * D)
    (dw,) = call(
        dec_weights_body,
        [((NI, 1920, 128), BF, "h")],
        [(mix, "v"), (cot, "v"), (nd, "v"), (gq, "v")],
        [pltpu.VMEM((NI, 1920, 128), BF), DMA((2,))],
        flops=5e8,
        name="dec_weights",
    )
    dw = lax.psum_scatter(dw.reshape(NI * 1920, 128), BATCH, scatter_dimension=0, tiled=True)
    (dspread,) = call(
        dec_spread_body,
        [((NJ, 176, 128), BF, "v")],
        [(dw, "v")],
        [pltpu.VMEM((DI, 256), F32), pltpu.VMEM((D, 128), F32)],
        name="dec_spread",
    )

    gmix, pack, g1c, lat_gain = call(
        lat_backward_body,
        [((R, D), BF, "v"), ((D, 896), BF, "v"), ((R, 128), BF, "v"), ((48, 128), F32, "v")],
        [(sc, "s"), (e, "v"), (gkv, "v"), (lg, "v")] + [(v, "h") for v in (w, g1_all, za, ha, zb, hb, a_h)],
        [
            pltpu.VMEM((4,) + big, BF),
            pltpu.VMEM((4, R, D), F32),
            pltpu.VMEM((2, R, D), F32),
            pltpu.VMEM((5, R, D), BF),
            pltpu.VMEM((R, D), F32),
            pltpu.VMEM((R, D), F32),
            pltpu.VMEM((R, D), F32),
            pltpu.VMEM((2, R, D), F32),
            pltpu.VMEM((D, 896), F32),
            DMA((4, 2)),
            DMA((10,)),
        ],
        vmem=58,
        flops=1.6e10,
        name="lat_backward",
    )
    pack = lax.psum_scatter(pack, BATCH, scatter_dimension=0, tiled=True)
    gin, epay = call(
        enc_back_body,
        [((N, DI), F32, "v"), ((NJ, 512, 128), BF, "v")],
        [(sc, "s"), (xin, "v"), (bg, "v"), (lg, "v"), (gd, "v")]
        + [(v, "h") for v in (gmix, e, q_b, k_b, v_b, g_all)],
        [
            pltpu.VMEM((R, D), BF),
            pltpu.VMEM((R, D + 128), BF),
            pltpu.VMEM((R, D), BF),
            pltpu.VMEM((N, D), BF),
            pltpu.VMEM((N, D), BF),
            pltpu.VMEM((NJ, 192, D), BF),
            pltpu.VMEM((R, D), F32),
            pltpu.VMEM((D, N), BF),
            pltpu.VMEM((D, N), BF),
            DMA((6,)),
        ],
        flops=3e9,
        name="enc_back",
    )
    r1 = exchange(epay, BLK)
    (p2,) = call(
        tail_one_body,
        [((NI, 464, 128), BF, "v")],
        [(r1, "v"), (nf, "h"), (g_all, "h"), (lg, "v"), (lat_gain, "v"), (g1c, "v")],
        [pltpu.VMEM((NJ * N, DI), BF), pltpu.VMEM((NJ, 16, D), BF), pltpu.VMEM((256, 2048), BF), DMA((2,))],
        name="tail_one",
    )
    p2, dspread = lax.optimization_barrier((p2, dspread))
    r2 = exchange(p2, BATCH)
    dwr = exchange(dspread, BLK)
    dec_grad, bq_grad = call(
        dec_finish_body, [((160, 48), F32, "v"), ((96, 80), F32, "v")], [(dwr, "v")], name="dec_finish"
    )
    arr, lm, om, wkv, lat_gains, byte_gain = call(
        tail_two_body,
        [
            ((32, 80), F32, "v"),
            ((10, 160, 80), F32, "v"),
            ((2, 160, 80), F32, "v"),
            ((2, 96, 80), F32, "v"),
            ((5, D), F32, "v"),
            ((2, DI), F32, "v"),
        ],
        [(r2, "v"), (pack, "v")],
        name="tail_two",
    )
    byte_grads = jnp.concatenate([wkv, bq_grad[None]], axis=0)
    return (res[None], gin[None], gqin[None], arr, lm, om, byte_grads, dec_grad, lat_gains, byte_gain)


def solution(mesh):
    grid = Mesh(mesh.devices.reshape(4, 2, NX, NZ), AXES)
    return jax.shard_map(
        shards,
        mesh=grid,
        in_specs=(
            P(BATCH, BLK, None),
            P(BATCH, BLK, None),
            P(BATCH),
            P(BLK, None),
            P(None, BLK, None),
            P(None, BLK, None),
            P(None, BLK, None),
            P(BLK, None),
            P(),
            P(),
            P(BATCH, BLK, None),
        ),
        out_specs=(
            P(BATCH, BLK, None),
            P(BATCH, BLK, None),
            P(BATCH, BLK, None),
            P(BATCH, BLK),
            P(None, BATCH, BLK),
            P(None, BATCH, BLK),
            P(None, BATCH, BLK),
            P(BATCH, BLK),
            P(),
            P(),
        ),
        check_vma=False,
    )
```

```python
import jax
import jax.numpy as jnp
from jax import lax
from jax.experimental import pallas as pl
from jax.experimental.pallas import tpu as pltpu
from jax.sharding import Mesh, PartitionSpec as P

F32, BF = jnp.float32, jnp.bfloat16
D, DI, R, N, H, E = 1280, 768, 256, 128, 8, 160
NX, NZ, NJ, NI = 4, 4, 16, 8
SCALE = E**-0.5
EPS = 1e-5
MIB = 1 << 20
AXES = ("y", "core", "x", "z")
BATCH = ("y", "core")
BLK = ("x", "z")
WIN = [128 * (E * h // 128) for h in range(H)]
OFF = [E * h - WIN[h] for h in range(H)]
SQUARE = [("o", 0), ("l", 1), ("l", 2), ("l", 3), ("l", 4), ("l", 5), ("o", 1), ("l", 6), ("l", 7), ("l", 8), ("l", 9)]
ROWS_I = 128
DEC_ROW, BQ_ROW = 880, 960
PLACE = {9: (0, 0), 10: (0, 80), 8: (0, 160), 3: (1, 0), 4: (1, 80), 5: (1, 160), 7: (2, 0), 6: (2, 80), 2: (2, 160), 1: (3, 0), 0: (3, 80)}


def dot(a, b, ca=1, cb=0):
    return lax.dot_general(a, b, (((ca,), (cb,)), ((), ())), preferred_element_type=F32)


def dot_nt(a, b):
    return dot(a, b, 1, 1)


def dot_tn(a, b):
    return dot(a, b, 0, 0)


def half(v):
    return v.astype(BF)


def norm(v):
    c = v - jnp.mean(v, axis=-1, keepdims=True)
    inv = lax.rsqrt(jnp.mean(c * c, axis=-1, keepdims=True) + EPS)
    return c * inv, inv


def norm_back(g, gain, n, inv):
    gg = jnp.sum(g * n, axis=0, keepdims=True)
    inner = g * gain
    m1 = jnp.mean(inner, axis=-1, keepdims=True)
    m2 = jnp.mean(inner * n, axis=-1, keepdims=True)
    return inv * (inner - m1 - n * m2), gg


C0, C1 = 0.7978845608028654, 0.044715


def gelu(x):
    return 0.5 * x * (1.0 + jnp.tanh(C0 * (x + C1 * x * x * x)))


def gelu_slope(x):
    t = jnp.tanh(C0 * (x + C1 * x * x * x))
    return 0.5 * (1.0 + t) + 0.5 * x * (1.0 - t * t) * (C0 * (1.0 + 3.0 * C1 * x * x))


def lanes(width):
    return lax.broadcasted_iota(jnp.int32, (1, width), 1)


def head_mask(h):
    lane = lanes(256)
    return jnp.where((lane >= OFF[h]) & (lane < OFF[h] + E), 1.0, 0.0).astype(F32)


def pieces(row, count):
    out = []
    done = 0
    while done < count:
        i, r0 = divmod(row + done, ROWS_I)
        n = min(count - done, ROWS_I - r0)
        out.append((i, r0, done, n))
        done += n
    return out


def split3(v):
    hi = half(v).astype(F32)
    mid = half(v - hi).astype(F32)
    lo = half(v - hi - mid).astype(F32)
    return hi, mid, lo


def pack3(v):
    hi, mid, lo = split3(v)
    return half(hi + pltpu.roll(mid, 16, 1) + pltpu.roll(lo, 32, 1))


def unpack3(v, axis):
    return v + pltpu.roll(v, 112, axis) + pltpu.roll(v, 96, axis)


def as_rows(parts, count):
    row = lax.broadcasted_iota(jnp.int32, (count, 128), 0)
    out = jnp.zeros((count, 128), F32)
    for r, part in parts:
        out = jnp.where(row == r, part, out)
    return out


def call(body, outs, args, scratch=(), vmem=48, flops=0, name=None):
    spaces = {"v": pltpu.VMEM, "a": pl.ANY, "s": pltpu.SMEM, "h": pltpu.HBM}
    return pl.pallas_call(
        body,
        out_shape=[jax.ShapeDtypeStruct(s, t) for s, t, _ in outs],
        in_specs=[pl.BlockSpec(memory_space=spaces[m]) for _, m in args],
        out_specs=[pl.BlockSpec(memory_space=spaces[m]) for _, _, m in outs],
        scratch_shapes=list(scratch),
        compiler_params=pltpu.CompilerParams(vmem_limit_bytes=vmem * MIB),
        cost_estimate=pl.CostEstimate(flops=int(flops), bytes_accessed=4 * MIB, transcendentals=0),
        name=name,
    )(*[a for a, _ in args])


DMA = pltpu.SemaphoreType.DMA


def pack_body(sc, lm, om, bm, do, la, g0, wsh, sem):
    i, core = sc[0], sc[4]
    cols = pl.ds(pl.multiple_of(core * 640, 128), 640)
    first = [
        (bm.at[0, :, cols], g0.at[0:48, :]),
        (bm.at[1, :, cols], g0.at[48:96, :]),
        (lm.at[0, :, cols], g0.at[96:176, :]),
        (la.at[:, cols], g0.at[176:192, :]),
    ]
    first = [pltpu.make_async_copy(a, b, sem.at[8 + k]) for k, (a, b) in enumerate(first)]
    for c in first:
        c.start()
    blocks = [(80 * k, 80, (om if s == "o" else lm), n, D) for k, (s, n) in enumerate(SQUARE)]
    blocks += [(DEC_ROW, 80, do, None, DI), (BQ_ROW, 48, bm, 2, D)]
    for k in range(NI):
        lo, hi = ROWS_I * k, ROWS_I * (k + 1)

        @pl.when(i == k)
        def _(lo=lo, hi=hi):
            cs = []
            for row, count, ref, n, width in blocks:
                a, b = max(lo, row), min(hi, row + count)
                if a < b:
                    src = ref.at[a - row : b - row, :] if n is None else ref.at[n, a - row : b - row, :]
                    dst = wsh.at[a - lo : b - lo, :] if width == D else wsh.at[a - lo : b - lo, 0:width]
                    cs.append(pltpu.make_async_copy(src, dst, sem.at[len(cs)]))
            for c in cs:
                c.start()
            for c in cs:
                c.wait()

    for c in first:
        c.wait()


def pieces_from(sc, groups):
    x, z, core = sc[2], sc[3], sc[4]
    out = []
    for side in range(2):
        c = core if side == 0 else 1 - core
        col = pl.ds(pl.multiple_of(c * 640, 128), 640)
        for e in range(4):
            for d in range(4):
                xs = jnp.where(c == 0, (x + 4 - d) & 3, (x + 4 - e) & 3)
                zs = jnp.where(c == 0, (z + 4 - e) & 3, (z + 4 - d) & 3)
                out.append((xs * 4 + zs, col, groups[4 * side + e].at[d]))
    return out


def enc_body(sc, t0, t1, t2, t3, u0, u1, u2, u3, x_in, bg, lg, g_out, nb_o, k_o, v_o, q_o, pay, gs, acc, sem):
    copies = [
        pltpu.make_async_copy(src, gs.at[pos, :, col], sem.at[k])
        for k, (pos, col, src) in enumerate(pieces_from(sc, (t0, t1, t2, t3, u0, u1, u2, u3)))
    ]
    for c in copies:
        c.start()
    n_in, _ = norm(x_in[...].astype(F32))
    nb = half(n_in * bg[0:1, :])
    nb_o[...] = nb
    for c in copies:
        c.wait()
    save = pltpu.make_async_copy(gs, g_out, sem.at[32])
    save.start()
    k_o[...] = half(dot(nb, gs[:, 0:48, :].reshape(DI, D)))
    v_o[...] = half(dot(nb, gs[:, 48:96, :].reshape(DI, D)))
    z0b = gs[:, 176:192, :].reshape(R, D)
    nq, _ = norm(z0b.astype(F32))
    q_o[...] = half(dot(half(nq * lg[0:1, :]), gs[:, 96:176, :].reshape(D, D)))
    acc[...] = jnp.zeros_like(acc)
    valid = lanes(N) + sc[1] * N < sc[5]
    lane = lanes(128)
    stats = jnp.zeros((R, 128), F32)
    for h in range(H):
        w = slice(WIN[h], WIN[h] + 256)
        mk = head_mask(h)
        s = dot_nt(q_o[:, w] * half(mk), k_o[:, w]) * SCALE
        s = jnp.where(valid, s, -1e30)
        m = jnp.max(s, axis=-1, keepdims=True)
        p = jnp.exp(s - m)
        acc[:, w] += dot(half(p), v_o[:, w]) * mk
        stats = jnp.where(lane == h, m, stats)
        stats = jnp.where(lane == 8 + h, jnp.sum(p, axis=-1, keepdims=True), stats)
    pay[:, 0:D] = half(acc[...])
    pay[:, D : D + 128] = pack3(stats)
    save.wait()


def combine_body(rcv, out):
    st = unpack3(rcv[:, :, D : D + 128].astype(F32), 2)
    peak = jnp.max(st, axis=0, keepdims=True)
    w = jnp.exp(st - peak)
    total = jnp.sum(w * pltpu.roll(st, 120, 2), axis=0, keepdims=True)
    coef = w / total
    lane = lax.broadcasted_iota(jnp.int32, (1, 1, 128), 2)
    for t in range(10):
        h0, h1 = 128 * t // E, (128 * t + 127) // E
        c = coef[:, :, h0 : h0 + 1]
        if h1 != h0:
            c = jnp.where(lane >= E * h1 - 128 * t, coef[:, :, h1 : h1 + 1], c)
        o = jnp.sum(rcv[:, :, 128 * t : 128 * t + 128].astype(F32) * c, axis=0)
        out[:, 128 * t : 128 * t + 128] = half(o)
    lse = jnp.where(lanes(128) < 8, (peak + jnp.log(total))[0], 0.0)
    out[:, D : D + 128] = pack3(lse)


class Ring:
    def __init__(self, w, slots, sem, order):
        self.w, self.slots, self.sem, self.order = w, slots, sem, order
        self.n = slots.shape[0]
        self.pos = {m: k for k, m in enumerate(order)}

    def copies(self, m):
        s = self.pos[m] % self.n
        return [
            pltpu.make_async_copy(
                self.w.at[i, :, r0 : r0 + n, :], self.slots.at[s, :, d0 : d0 + n, :], self.sem.at[s, k]
            )
            for k, (i, r0, d0, n) in enumerate(pieces(80 * m, 80))
        ]

    def start(self, m):
        for c in self.copies(m):
            c.start()

    def begin(self):
        for m in self.order[: self.n]:
            self.start(m)

    def get(self, m):
        for c in self.copies(m):
            c.wait()
        return self.slots[self.pos[m] % self.n].reshape(D, D)

    def done(self, m):
        k = self.pos[m] + self.n
        if k < len(self.order):
            self.start(self.order[k])


def forward_body(
    qin, cot, bg, lg, e_h, g_all, w,
    res, gqin, gain_o, pay, mix_o, nd_o, gq_o, z_h, h_h, a_h,
    slots, e, z0b, zs, hs, qs, acc, kd, vd, dec, bq, dacc, gq, gkv, wsem, ssem, lsem,
):
    first = [
        pltpu.make_async_copy(e_h.at[:, 0:D], e, lsem.at[3]),
        pltpu.make_async_copy(g_all.at[:, 176:192, :], z0b, lsem.at[4]),
    ]
    for c in first:
        c.start()
    ring = Ring(w, slots, wsem, list(range(11)))
    ring.begin()
    copies = []
    for i, r0, d0, n in pieces(BQ_ROW, 48):
        copies.append(pltpu.make_async_copy(w.at[i, :, r0 : r0 + n, :], bq.at[:, d0 : d0 + n, :], lsem.at[0]))
    for i, r0, d0, n in pieces(DEC_ROW, 80):
        copies.append(
            pltpu.make_async_copy(w.at[i, :, r0 : r0 + n, 0:DI], dec.at[:, d0 : d0 + n, :], lsem.at[len(copies)])
        )
    for c in copies:
        c.start()
    saves = []

    def save(src, dst):
        c = pltpu.make_async_copy(src, dst, ssem.at[len(saves)])
        c.start()
        saves.append(c)

    def mul(a, m):
        out = dot(a, ring.get(m))
        ring.done(m)
        return out

    for c in first:
        c.wait()
    z1 = z0b[...].reshape(R, D).astype(F32) + mul(e[...], 0)
    zs[0] = z1
    save(zs.at[0], z_h.at[0])
    h1 = mul(half(norm(z1)[0] * lg[1:2, :]), 1)
    hs[0] = h1
    save(hs.at[0], h_h.at[0])
    zs[1] = zs[0] + mul(half(gelu(h1)), 2)
    save(zs.at[1], z_h.at[1])
    s_b = half(norm(zs[1])[0] * lg[2:3, :])
    for k in range(3):
        qs[k] = half(mul(s_b, 3 + k))
        save(qs.at[k], a_h.at[k])
    acc[...] = jnp.zeros_like(acc)
    for h in range(H):
        win = slice(WIN[h], WIN[h] + 256)
        mk = head_mask(h)
        s = dot_nt(qs[0, :, win] * half(mk), qs[1, :, win]) * SCALE
        p = jnp.exp(s - jnp.max(s, axis=-1, keepdims=True))
        p = p / jnp.sum(p, axis=-1, keepdims=True)
        acc[:, win] += dot(half(p), qs[2, :, win]) * mk
    qs[3] = half(acc[...])
    save(qs.at[3], a_h.at[3])
    zs[2] = zs[1] + mul(qs[3], 6)
    save(zs.at[2], z_h.at[2])
    h2 = mul(half(norm(zs[2])[0] * lg[3:4, :]), 7)
    hs[1] = h2
    save(hs.at[1], h_h.at[1])
    zs[3] = zs[2] + mul(half(gelu(h2)), 8)
    save(zs.at[3], z_h.at[3])
    c_b = half(norm(zs[3])[0] * lg[4:5, :])
    kd[...] = half(mul(c_b, 9))
    vd[...] = half(mul(c_b, 10))

    x = qin[...].astype(F32)
    n, inv = norm(x)
    nd = half(n * bg[1:2, :])
    nd_o[...] = nd
    for c in copies:
        c.wait()
    wq = bq[...].reshape(DI, D)
    wd = dec[...].reshape(D, DI)
    gq_o[...] = half(dot(nd, wq))
    mix_o[...] = half(dot_nt(cot[...], wd))
    dacc[...] = jnp.zeros_like(dacc)
    gq[...] = jnp.zeros_like(gq)
    gkv[...] = jnp.zeros_like(gkv)
    for h in range(H):
        win = slice(WIN[h], WIN[h] + 256)
        mk = head_mask(h)
        mkb = half(mk)
        qw, gw, kw, vw = gq_o[:, win], mix_o[:, win], kd[:, win], vd[:, win]
        s = dot_nt(qw * mkb, kw) * SCALE
        p = jnp.exp(s - jnp.max(s, axis=-1, keepdims=True))
        p = p / jnp.sum(p, axis=-1, keepdims=True)
        pb = half(p)
        dacc[:, win] += dot(pb, vw) * mk
        dp = dot_nt(gw * mkb, vw)
        ds = half(p * (dp - jnp.sum(p * dp, axis=-1, keepdims=True)))
        gq[:, win] += dot(ds, kw) * mk
        gkv[0, :, win] += dot_tn(ds, qw) * mk
        gkv[1, :, win] += dot_tn(pb, gw) * mk
    pay[:, 0:D] = half(gkv[0] * SCALE)
    pay[:, D : 2 * D] = half(gkv[1])
    mix = half(dacc[...])
    mix_o[...] = mix
    res[...] = half(x + dot(mix, wd))
    gqb = half(gq[...] * SCALE)
    gq_o[...] = gqb
    gin, gg = norm_back(dot_nt(gqb, wq), bg[1:2, :], n, inv)
    gqin[...] = cot[...].astype(F32) + gin
    gain_o[...] = gg
    for c in saves:
        c.wait()


def prepare_body(lg, z_h, h_h, a_h, n_h, i_h, s_h, act_h, p_h, zs, hs, qs, ns, vs, ss, acts, ps, sem, osem):
    loads = {}
    for k in range(4):
        loads["z", k] = pltpu.make_async_copy(z_h.at[k], zs.at[k], sem.at[k])
    for k in range(2):
        loads["h", k] = pltpu.make_async_copy(h_h.at[k], hs.at[k], sem.at[4 + k])
    loads["q"] = pltpu.make_async_copy(a_h.at[0:2], qs, sem.at[6])
    for c in loads.values():
        c.start()
    saves = []

    def save(src, dst):
        c = pltpu.make_async_copy(src, dst, osem.at[len(saves)])
        c.start()
        saves.append(c)

    for k, a in ((3, 0), (2, 2), (1, 1), (0, 4)):
        loads["z", k].wait()
        n, inv = norm(zs[k])
        ns[k] = n
        save(ns.at[k], n_h.at[k])
        vs[k] = jnp.broadcast_to(inv, (R, 128))
        acts[a] = half(n * lg[k + 1 : k + 2, :])
        save(acts.at[a], act_h.at[a])
    save(vs, i_h)
    for k, a in ((1, 3), (0, 5)):
        loads["h", k].wait()
        x = hs[k]
        t = jnp.tanh(C0 * (x + C1 * x * x * x))
        acts[a] = half(0.5 * x * (1.0 + t))
        save(acts.at[a], act_h.at[a])
        ss[k] = 0.5 * (1.0 + t) + 0.5 * x * (1.0 - t * t) * (C0 * (1.0 + 3.0 * C1 * x * x))
        save(ss.at[k], s_h.at[k])
    loads["q"].wait()
    for h in range(H):
        win = slice(WIN[h], WIN[h] + 256)
        s = dot_nt(qs[0, :, win] * half(head_mask(h)), qs[1, :, win]) * SCALE
        p = jnp.exp(s - jnp.max(s, axis=-1, keepdims=True))
        ps[h] = p / jnp.sum(p, axis=-1, keepdims=True)
    save(ps, p_h)
    for c in saves:
        c.wait()


def lat_backward_body(
    sc, gkv, lg, w, e_h, n_h, i_h, s_h, act_h, a_h, p_h, gmix, pack_o, g1c_o, gains_o,
    slots, ns, vs, ss, acts, qs, ps, acc, acc2, acc3, gh, gw, wsem, lsem,
):
    order = [9, 10, 8, 7, 6, 3, 4, 5, 2, 1, 0]
    ring = Ring(w, slots, wsem, order)
    todo = [
        (n_h.at[3], ns.at[3]),
        (i_h, vs),
        (act_h.at[0], acts.at[0]),
        (s_h.at[1], ss.at[1]),
        (act_h.at[3], acts.at[1]),
        (n_h.at[2], ns.at[2]),
        (act_h.at[2], acts.at[3]),
        (a_h.at[3], acts.at[4]),
        (p_h, ps),
        (a_h.at[0:3], qs.at[0:3]),
        (n_h.at[1], ns.at[1]),
        (act_h.at[1], acts.at[2]),
        (s_h.at[0], ss.at[0]),
        (act_h.at[5], acts.at[5]),
        (n_h.at[0], ns.at[0]),
        (act_h.at[4], acts.at[6]),
        (e_h.at[:, 0:D], acts.at[7]),
    ]
    loads = [pltpu.make_async_copy(a, b, lsem.at[k]) for k, (a, b) in enumerate(todo)]
    for c in loads[:2]:
        c.start()
    ring.start(order[0])
    ring.start(order[1])
    for c in loads[2:6]:
        c.start()
    for m in order[2 : ring.n]:
        ring.start(m)
    for c in loads[6:]:
        c.start()

    def ready(*ks):
        for k in ks:
            loads[k].wait()

    src = sc[1] * 80
    start = pl.multiple_of(jnp.minimum((src >> 7) * 128, 1024), 128)
    offset = src - start
    lane = lanes(256)

    def put(ref, to):
        v = pltpu.roll(ref[:, pl.ds(start, 256)].astype(F32), (to - offset + 256) & 255, 1)
        return jnp.where((lane >= to) & (lane < to + 80), v, 0.0)

    def weight_grad(window, first, count):
        a = acts[first : first + count].reshape(count * R, D)
        pack_o[:, 256 * window : 256 * window + 256] = half(dot_tn(a, gw[first : first + count].reshape(count * R, 256)))

    def mul(g_b, m):
        out = dot_nt(g_b, ring.get(m))
        ring.done(m)
        return out

    gain_rows = []

    def back(g, k):
        out, gg = norm_back(g, lg[k + 1 : k + 2, :], ns[k], vs[k][:, 0:1])
        for t in range(10):
            gain_rows.append((10 * k + t, gg[:, 128 * t : 128 * t + 128]))
        return out

    ready(0, 1)
    gn = mul(gkv[:, 0:D], 9) + mul(gkv[:, D : 2 * D], 10)
    acc[...] = back(gn, 3)
    gw[0] = half(put(gkv.at[:, 0:D], 0) + put(gkv.at[:, D : 2 * D], 80))
    gw[1] = half(put(acc, 160))
    ready(2, 3, 4)
    gh[...] = half(mul(half(acc[...]), 8) * ss[1])
    weight_grad(0, 0, 2)
    ready(5)
    gw[3] = half(put(gh, 0))
    acc[...] += back(mul(gh[...], 7), 2)
    gw[4] = half(put(acc, 80))
    qs[3] = half(mul(half(acc[...]), 6))
    acc2[...] = jnp.zeros_like(acc2)
    acc3[...] = jnp.zeros_like(acc3)
    ready(6, 7, 8, 9)
    for h in range(H):
        win = slice(WIN[h], WIN[h] + 256)
        mk = head_mask(h)
        p = ps[h]
        dp = dot_nt(qs[3, :, win] * half(mk), qs[2, :, win])
        ds = half(p * (dp - jnp.sum(p * dp, axis=-1, keepdims=True)) * SCALE)
        acc2[:, win] += dot(ds, qs[1, :, win]) * mk
        acc3[0, :, win] += dot_tn(ds, qs[0, :, win]) * mk
        acc3[1, :, win] += dot_tn(half(p), qs[3, :, win]) * mk
    gw[2] = half(put(acc2, 0) + put(acc3.at[0], 80) + put(acc3.at[1], 160))
    gn = mul(half(acc2[...]), 3)
    gn = gn + mul(half(acc3[0]), 4)
    gn = gn + mul(half(acc3[1]), 5)
    ready(10, 11)
    weight_grad(1, 2, 1)
    acc[...] += back(gn, 1)
    gw[5] = half(put(acc, 160))
    ready(12, 13)
    gh[...] = half(mul(half(acc[...]), 2) * ss[0])
    weight_grad(2, 3, 3)
    gw[6] = half(put(gh, 0))
    ready(14, 15, 16)
    acc[...] += back(mul(gh[...], 1), 0)
    gw[7] = half(put(acc, 80))
    g1c_o[...] = half(put(acc, 0)[:, 0:128])
    gmix[...] = half(mul(half(acc[...]), 0))
    weight_grad(3, 6, 2)
    gains_o[...] = as_rows(gain_rows, 48)


def sum_rows_body(rcv, out):
    s = half(jnp.sum(rcv[...].astype(F32), axis=0))
    for k in range(NJ):
        out[k] = s


def dec_weights_body(mix, cot, nd, gq, out, buf, sem):
    g = half(dot_tn(mix[...], cot[...]))
    for i in range(NI):
        for t in range(6):
            buf[i, 160 * t : 160 * t + 160, :] = g[160 * i : 160 * i + 160, 128 * t : 128 * t + 128]
    one = pltpu.make_async_copy(buf.at[:, 0:960, :], out.at[:, 0:960, :], sem.at[0])
    one.start()
    g = half(dot_tn(nd[...], gq[...]))
    for i in range(NI):
        for t in range(10):
            r = 960 + 96 * t
            buf[i, r : r + 96, :] = g[96 * i : 96 * i + 96, 128 * t : 128 * t + 128]
    two = pltpu.make_async_copy(buf.at[:, 960:1920, :], out.at[:, 960:1920, :], sem.at[1])
    two.start()
    one.wait()
    two.wait()


def spread(chunk, pay, td, tb):
    fill = jnp.zeros((96, 128), F32)
    for t in range(6):
        v = jnp.concatenate([chunk[160 * t : 160 * t + 160, :].astype(F32), fill], axis=0)
        td[128 * t : 128 * t + 128, :] = v.T
    fill = jnp.zeros((32, 128), F32)
    for t in range(10):
        v = jnp.concatenate([chunk[960 + 96 * t : 960 + 96 * t + 96, :].astype(F32), fill], axis=0)
        tb[128 * t : 128 * t + 128, :] = v.T
    for j in range(NJ):
        pay[j, 512:560, :] = half(td[48 * j : 48 * j + 48, 0:128])
        pay[j, 560:608, :] = half(td[48 * j : 48 * j + 48, 128:256])
        pay[j, 608:688, :] = half(tb[80 * j : 80 * j + 80, :])


def unspread(s, dec_o, bq_o):
    fill = jnp.zeros((80, 128), F32)
    a = jnp.concatenate([s[0:48], fill], axis=0).T
    b = jnp.concatenate([s[48:96], fill], axis=0).T
    dec_o[0:128, :] = a[:, 0:48]
    dec_o[128:160, :] = b[0:32, 0:48]
    c = jnp.concatenate([s[96:176], fill[0:48]], axis=0).T
    bq_o[...] = c[0:96, 0:80]


def enc_back_body(
    sc, x_in, bg, lg, gd, gmix_h, e_h, q_h, k_h, v_h, g_all, dw_h, gin_o, pay,
    gmix, e, q, k, v, wkv, gq, gkt, gvt, dw, td, tb, sem,
):
    pairs = [(gmix_h, gmix), (q_h, q), (k_h, k), (v_h, v), (e_h, e), (g_all, wkv), (dw_h, dw)]
    loads = [pltpu.make_async_copy(a, b, sem.at[n]) for n, (a, b) in enumerate(pairs)]
    for c in loads:
        c.start()
    for c in loads[:5]:
        c.wait()
    lse = unpack3(e[:, D : D + 128].astype(F32), 1)
    valid = lanes(N) + sc[1] * N < sc[5]
    gq[...] = jnp.zeros_like(gq)
    for h in range(H):
        win = slice(WIN[h], WIN[h] + 256)
        mk = head_mask(h)
        mkb = half(mk)
        qw, gw, kw, vw = q[:, win], gmix[:, win], k[:, win], v[:, win]
        rd = jnp.sum(gw.astype(F32) * e[:, win].astype(F32) * mk, axis=-1, keepdims=True)
        s = dot_nt(qw * mkb, kw) * SCALE
        p = jnp.where(valid, jnp.exp(jnp.where(valid, s, -1e30) - lse[:, h : h + 1]), 0.0)
        dp = dot_nt(gw * mkb, vw)
        ds = half(p * (dp - rd))
        gq[:, win] += dot(ds, kw) * mk
        o = OFF[h]
        gkt[E * h : E * h + E, :] = half(dot_tn(qw, ds)[o : o + E, :] * SCALE)
        gvt[E * h : E * h + E, :] = half(dot_tn(gw, half(p))[o : o + E, :])
    pay[:, 320:400, :] = gkt[...].reshape(NJ, 80, 128)
    pay[:, 400:480, :] = gvt[...].reshape(NJ, 80, 128)
    loads[5].wait()
    gqs = gq[...] * SCALE
    gqt = half(gqs.T)
    pay[:, 160:240, :] = gqt[:, 0:128].reshape(NJ, 80, 128)
    pay[:, 240:320, :] = gqt[:, 128:256].reshape(NJ, 80, 128)
    n, inv = norm(wkv[:, 176:192, :].reshape(R, D).astype(F32))
    gz, g0 = norm_back(dot_nt(half(gqs), wkv[:, 96:176, :].reshape(D, D)), lg[0:1, :], n, inv)
    gzt = half(gz.T)
    pay[:, 0:80, :] = gzt[:, 0:128].reshape(NJ, 80, 128)
    pay[:, 80:160, :] = gzt[:, 128:256].reshape(NJ, 80, 128)
    n, inv = norm(x_in[...].astype(F32))
    gnt = dot(wkv[:, 0:48, :].reshape(DI, D), gkt[...]) + dot(wkv[:, 48:96, :].reshape(DI, D), gvt[...])
    gin, gg = norm_back(gnt.T, bg[0:1, :], n, inv)
    gin_o[...] = gin
    rows = [(t, gg[:, 128 * t : 128 * t + 128]) for t in range(6)]
    rows += [(6 + t, gd[:, 128 * t : 128 * t + 128]) for t in range(6)]
    rows += [(16 + t, g0[:, 128 * t : 128 * t + 128]) for t in range(10)]
    g = half(as_rows(rows, 32))
    for j in range(NJ):
        pay[j, 480:512, :] = g
    loads[6].wait()
    spread(dw, pay, td, tb)


def tail_one_body(rcv, nf_h, g_all, lg, lat_gain, g1c, out, dec_o, bq_o, nf, z0b, left, sem):
    loads = [
        pltpu.make_async_copy(nf_h, nf, sem.at[0]),
        pltpu.make_async_copy(g_all.at[:, 176:192, :], z0b, sem.at[1]),
    ]
    for c in loads:
        c.start()
    sums = jnp.sum(rcv[:, 0:320, :].astype(F32), axis=0)
    fill = jnp.zeros((48, 128), F32)
    left[...] = jnp.zeros_like(left)
    for s in range(NJ):
        left[0:80, 128 * s : 128 * s + 128] = rcv[s, 320:400, :]
        left[128:208, 128 * s : 128 * s + 128] = rcv[s, 400:480, :]
    loads[1].wait()
    nq = half(norm(z0b[...].reshape(R, D).astype(F32))[0] * lg[0:1, :])
    a = jnp.concatenate([sums[160:240], fill], axis=0).T
    b = jnp.concatenate([sums[240:320], fill], axis=0).T
    w0 = half(dot_tn(nq, half(jnp.concatenate([a, b], axis=0))))
    a = jnp.concatenate([sums[0:80], fill], axis=0).T
    b = jnp.concatenate([sums[80:160], fill], axis=0).T
    gz = half(jnp.concatenate([a, b], axis=0) + g1c[...].astype(F32))
    gains = jnp.sum(rcv[:, 480:512, :].astype(F32), axis=0)
    gains = half(jnp.concatenate([gains, lat_gain[...]], axis=0))
    loads[0].wait()
    wt = half(dot(left[...], nf[...]).T)
    for i in range(NI):
        out[i, 0:160, :] = w0[160 * i : 160 * i + 160, :]
        out[i, 160:192, :] = gz[32 * i : 32 * i + 32, :]
        out[i, 192:288, :] = wt[96 * i : 96 * i + 96, 0:128]
        out[i, 288:384, :] = wt[96 * i : 96 * i + 96, 128:256]
        out[i, 384:464, :] = gains
    unspread(jnp.sum(rcv[:, 512:688, :].astype(F32), axis=0), dec_o, bq_o)


def tail_two_body(rcv, pack, arr_o, lm_o, om_o, wkv_o, lat_o, byte_o):
    sums = jnp.sum(rcv[...].astype(F32), axis=0)
    lm_o[0] = sums[0:160, 0:80]
    arr_o[...] = sums[160:192, 0:80]
    wkv_o[0] = sums[192:288, 0:80]
    wkv_o[1] = sums[288:384, 0:80]
    g = sums[384:464]
    for t in range(6):
        for b in range(2):
            byte_o[b : b + 1, 128 * t : 128 * t + 128] = g[6 * b + t : 6 * b + t + 1, :]
    for t in range(10):
        for b in range(5):
            r = 16 + t if b == 0 else 32 + 10 * (b - 1) + t
            lat_o[b : b + 1, 128 * t : 128 * t + 128] = g[r : r + 1, :]
    for m, (kind, n) in enumerate(SQUARE):
        window, o = PLACE[m]
        v = pack[:, 256 * window : 256 * window + 256].astype(F32)
        if o:
            v = pltpu.roll(v, 256 - o, 1)
        if kind == "l":
            lm_o[n] = v[:, 0:80]
        else:
            om_o[n] = v[:, 0:80]


def line(y, c, x, z):
    return ((y % 4) * 2 + c) * NJ + (x % 4) * NZ + (z % 4)


EVERY = [(y, c, x, z) for y in range(4) for c in range(2) for x in range(NX) for z in range(NZ)]


def along(stage, d):
    out = []
    for y, c, x, z in EVERY:
        on_x = (c == 0) == (stage == 0)
        out.append((line(y, c, x, z), line(y, c, x + d, z) if on_x else line(y, c, x, z + d)))
    return out


SWAP = [(line(y, c, x, z), line(y, 1 - c, x, z)) for y, c, x, z in EVERY]


def exchange(v, axes):
    flat = v.reshape(v.shape[0] * v.shape[1], v.shape[2])
    return lax.all_to_all(flat, axes, split_axis=0, concat_axis=0, tiled=True).reshape(v.shape)


def shards(inputs, queries, lengths, latent_array, latent_mats, out_mats, byte_mats, dec_out, lg, bg, cotangent):
    y, core, x, z = (lax.axis_index(a) for a in AXES)
    i, j = y * 2 + core, x * NZ + z
    sc = jnp.stack([i, j, x, z, core, lengths[0]]).astype(jnp.int32)
    xin, qin, cot = inputs[0], queries[0], cotangent[0]

    g0, wsh = call(
        pack_body,
        [((192, 640), BF, "h"), ((ROWS_I, D), BF, "h")],
        [(sc, "s"), (latent_mats, "h"), (out_mats, "h"), (byte_mats, "h"), (dec_out, "h"), (latent_array, "h")],
        [DMA((12,))],
        vmem=60,
        name="pack",
    )
    w = lax.all_gather(wsh, AXES, axis=0, tiled=True).reshape(NI, NJ, ROWS_I, D)

    def step(v, stage):
        return [lax.ppermute(v, AXES, along(stage, d)) for d in (1, 2, 3)]

    s0 = jnp.stack([g0] + step(g0, 0))
    own = [s0] + step(s0, 1)
    sib = [lax.ppermute(v, AXES, SWAP) for v in own]
    g_all, nb, k_b, v_b, q_b, pay = call(
        enc_body,
        [
            ((NJ, 192, D), BF, "h"),
            ((N, DI), BF, "v"),
            ((N, D), BF, "v"),
            ((N, D), BF, "v"),
            ((R, D), BF, "v"),
            ((R, D + 128), BF, "v"),
        ],
        [(sc, "s")] + [(v, "h") for v in own + sib] + [(xin, "v"), (bg, "v"), (lg, "v")],
        [pltpu.VMEM((NJ, 192, D), BF), pltpu.VMEM((R, D), F32), DMA((33,))],
        vmem=60,
        flops=3e9,
        name="enc",
    )
    rcv = exchange(pay.reshape(NJ, 16, D + 128), BLK)
    (mine,) = call(combine_body, [((16, D + 128), BF, "v")], [(rcv, "v")], name="combine")
    e = lax.all_gather(mine, BLK, axis=0, tiled=True)
    nf = lax.all_gather(nb, BLK, axis=0, tiled=True)

    big = (NJ, 80, D)
    res, gqin, gd, dpay, mix, nd, gq, z_h, h_h, a_h = call(
        forward_body,
        [
            ((N, DI), BF, "v"),
            ((N, DI), F32, "v"),
            ((1, DI), F32, "v"),
            ((R, 2 * D), BF, "v"),
            ((N, D), BF, "v"),
            ((N, DI), BF, "v"),
            ((N, D), BF, "v"),
            ((4, R, D), F32, "h"),
            ((2, R, D), F32, "h"),
            ((4, R, D), BF, "h"),
        ],
        [(qin, "v"), (cot, "v"), (bg, "v"), (lg, "v"), (e, "h"), (g_all, "h"), (w, "h")],
        [
            pltpu.VMEM((5,) + big, BF),
            pltpu.VMEM((R, D), BF),
            pltpu.VMEM((NJ, 16, D), BF),
            pltpu.VMEM((4, R, D), F32),
            pltpu.VMEM((2, R, D), F32),
            pltpu.VMEM((4, R, D), BF),
            pltpu.VMEM((R, D), F32),
            pltpu.VMEM((R, D), BF),
            pltpu.VMEM((R, D), BF),
            pltpu.VMEM((NJ, 80, DI), BF),
            pltpu.VMEM((NJ, 48, D), BF),
            pltpu.VMEM((N, D), F32),
            pltpu.VMEM((N, D), F32),
            pltpu.VMEM((2, R, D), F32),
            DMA((5, 2)),
            DMA((10,)),
            DMA((5,)),
        ],
        vmem=58,
        flops=1.5e10,
        name="forward",
    )
    rows = exchange(dpay.reshape(NJ, 16, 2 * D), BLK)
    n_h, i_h, s_h, act_h, p_h = call(
        prepare_body,
        [
            ((4, R, D), F32, "h"),
            ((4, R, 128), F32, "h"),
            ((2, R, D), F32, "h"),
            ((6, R, D), BF, "h"),
            ((H, R, R), F32, "h"),
        ],
        [(lg, "v"), (z_h, "h"), (h_h, "h"), (a_h, "h")],
        [
            pltpu.VMEM((4, R, D), F32),
            pltpu.VMEM((2, R, D), F32),
            pltpu.VMEM((2, R, D), BF),
            pltpu.VMEM((4, R, D), F32),
            pltpu.VMEM((4, R, 128), F32),
            pltpu.VMEM((2, R, D), F32),
            pltpu.VMEM((6, R, D), BF),
            pltpu.VMEM((H, R, R), F32),
            DMA((7,)),
            DMA((14,)),
        ],
        vmem=60,
        flops=5e9,
        name="prepare",
    )
    (dup,) = call(sum_rows_body, [((NJ, 16, 2 * D), BF, "v")], [(rows, "v")], name="sum_rows")
    gkv = exchange(dup, BLK).reshape(R, 2 * D)
    mix, _, nf = lax.optimization_barrier((mix, dup, nf))
    (dw,) = call(
        dec_weights_body,
        [((NI, 1920, 128), BF, "h")],
        [(mix, "v"), (cot, "v"), (nd, "v"), (gq, "v")],
        [pltpu.VMEM((NI, 1920, 128), BF), DMA((2,))],
        vmem=60,
        flops=4e9,
        name="dec_weights",
    )
    dw = lax.psum_scatter(dw.reshape(NI * 1920, 128), BATCH, scatter_dimension=0, tiled=True)

    gmix, pack, g1c, lat_gain = call(
        lat_backward_body,
        [((R, D), BF, "v"), ((D, 1024), BF, "v"), ((R, 128), BF, "v"), ((48, 128), F32, "v")],
        [(sc, "s"), (gkv, "v"), (lg, "v")] + [(v, "h") for v in (w, e, n_h, i_h, s_h, act_h, a_h, p_h)],
        [
            pltpu.VMEM((4,) + big, BF),
            pltpu.VMEM((4, R, D), F32),
            pltpu.VMEM((4, R, 128), F32),
            pltpu.VMEM((2, R, D), F32),
            pltpu.VMEM((8, R, D), BF),
            pltpu.VMEM((4, R, D), BF),
            pltpu.VMEM((H, R, R), F32),
            pltpu.VMEM((R, D), F32),
            pltpu.VMEM((R, D), F32),
            pltpu.VMEM((2, R, D), F32),
            pltpu.VMEM((R, D), BF),
            pltpu.VMEM((8, R, 256), BF),
            DMA((4, 2)),
            DMA((17,)),
        ],
        vmem=58,
        flops=1.6e10,
        name="lat_backward",
    )
    pack = lax.psum_scatter(pack, BATCH, scatter_dimension=0, tiled=True)
    gin, epay = call(
        enc_back_body,
        [((N, DI), F32, "v"), ((NJ, 688, 128), BF, "v")],
        [(sc, "s"), (xin, "v"), (bg, "v"), (lg, "v"), (gd, "v")]
        + [(v, "h") for v in (gmix, e, q_b, k_b, v_b, g_all, dw)],
        [
            pltpu.VMEM((R, D), BF),
            pltpu.VMEM((R, D + 128), BF),
            pltpu.VMEM((R, D), BF),
            pltpu.VMEM((N, D), BF),
            pltpu.VMEM((N, D), BF),
            pltpu.VMEM((NJ, 192, D), BF),
            pltpu.VMEM((R, D), F32),
            pltpu.VMEM((D, N), BF),
            pltpu.VMEM((D, N), BF),
            pltpu.VMEM((1920, 128), BF),
            pltpu.VMEM((DI, 256), F32),
            pltpu.VMEM((D, 128), F32),
            DMA((7,)),
        ],
        vmem=56,
        flops=3e9,
        name="enc_back",
    )
    r1 = exchange(epay, BLK)
    p2, dec_grad, bq_grad = call(
        tail_one_body,
        [((NI, 464, 128), BF, "v"), ((160, 48), F32, "v"), ((96, 80), F32, "v")],
        [(r1, "v"), (nf, "h"), (g_all, "h"), (lg, "v"), (lat_gain, "v"), (g1c, "v")],
        [pltpu.VMEM((NJ * N, DI), BF), pltpu.VMEM((NJ, 16, D), BF), pltpu.VMEM((256, 2048), BF), DMA((2,))],
        name="tail_one",
    )
    r2 = exchange(p2, BATCH)
    arr, lm, om, wkv, lat_gains, byte_gain = call(
        tail_two_body,
        [
            ((32, 80), F32, "v"),
            ((10, 160, 80), F32, "v"),
            ((2, 160, 80), F32, "v"),
            ((2, 96, 80), F32, "v"),
            ((5, D), F32, "v"),
            ((2, DI), F32, "v"),
        ],
        [(r2, "v"), (pack, "v")],
        name="tail_two",
    )
    byte_grads = jnp.concatenate([wkv, bq_grad[None]], axis=0)
    return (res[None], gin[None], gqin[None], arr, lm, om, byte_grads, dec_grad, lat_gains, byte_gain)


def solution(mesh):
    grid = Mesh(mesh.devices.reshape(4, 2, NX, NZ), AXES)
    return jax.shard_map(
        shards,
        mesh=grid,
        in_specs=(
            P(BATCH, BLK, None),
            P(BATCH, BLK, None),
            P(BATCH),
            P(BLK, None),
            P(None, BLK, None),
            P(None, BLK, None),
            P(None, BLK, None),
            P(BLK, None),
            P(),
            P(),
            P(BATCH, BLK, None),
        ),
        out_specs=(
            P(BATCH, BLK, None),
            P(BATCH, BLK, None),
            P(BATCH, BLK, None),
            P(BATCH, BLK),
            P(None, BATCH, BLK),
            P(None, BATCH, BLK),
            P(None, BATCH, BLK),
            P(BATCH, BLK),
            P(),
            P(),
        ),
        check_vma=False,
    )
```

```python
import jax
import jax.numpy as jnp
from jax import lax
from jax.experimental import pallas as pl
from jax.experimental.pallas import tpu as pltpu
from jax.sharding import Mesh, PartitionSpec as P

F32, BF = jnp.float32, jnp.bfloat16
D, DI, R, N, H, E = 1280, 768, 256, 128, 8, 160
NX, NZ, NJ, NI = 4, 4, 16, 8
SCALE = E**-0.5
EPS = 1e-5
MIB = 1 << 20
AXES = ("y", "core", "x", "z")
BATCH = ("y", "core")
BLK = ("x", "z")
WIN = [128 * (E * h // 128) for h in range(H)]
OFF = [E * h - WIN[h] for h in range(H)]
SQUARE = [("o", 0), ("l", 1), ("l", 2), ("l", 3), ("l", 4), ("l", 5), ("o", 1), ("l", 6), ("l", 7), ("l", 8), ("l", 9)]
ROWS_I = 128
DEC_ROW, BQ_ROW = 880, 960
PLACE = {9: (0, 0), 10: (0, 80), 8: (0, 160), 3: (1, 0), 4: (1, 80), 5: (1, 160), 7: (2, 0), 6: (2, 80), 2: (2, 160), 1: (3, 0), 0: (3, 80)}


def dot(a, b, ca=1, cb=0):
    return lax.dot_general(a, b, (((ca,), (cb,)), ((), ())), preferred_element_type=F32)


def dot_nt(a, b):
    return dot(a, b, 1, 1)


def dot_tn(a, b):
    return dot(a, b, 0, 0)


def half(v):
    return v.astype(BF)


def norm(v):
    c = v - jnp.mean(v, axis=-1, keepdims=True)
    inv = lax.rsqrt(jnp.mean(c * c, axis=-1, keepdims=True) + EPS)
    return c * inv, inv


def norm_back(g, gain, n, inv):
    gg = jnp.sum(g * n, axis=0, keepdims=True)
    inner = g * gain
    m1 = jnp.mean(inner, axis=-1, keepdims=True)
    m2 = jnp.mean(inner * n, axis=-1, keepdims=True)
    return inv * (inner - m1 - n * m2), gg


C0, C1 = 0.7978845608028654, 0.044715


def gelu(x):
    return 0.5 * x * (1.0 + jnp.tanh(C0 * (x + C1 * x * x * x)))


def gelu_slope(x):
    t = jnp.tanh(C0 * (x + C1 * x * x * x))
    return 0.5 * (1.0 + t) + 0.5 * x * (1.0 - t * t) * (C0 * (1.0 + 3.0 * C1 * x * x))


def lanes(width):
    return lax.broadcasted_iota(jnp.int32, (1, width), 1)


def head_mask(h):
    lane = lanes(256)
    return jnp.where((lane >= OFF[h]) & (lane < OFF[h] + E), 1.0, 0.0).astype(F32)


def pieces(row, count):
    out = []
    done = 0
    while done < count:
        i, r0 = divmod(row + done, ROWS_I)
        n = min(count - done, ROWS_I - r0)
        out.append((i, r0, done, n))
        done += n
    return out


def split3(v):
    hi = half(v).astype(F32)
    mid = half(v - hi).astype(F32)
    lo = half(v - hi - mid).astype(F32)
    return hi, mid, lo


def pack3(v):
    hi, mid, lo = split3(v)
    return half(hi + pltpu.roll(mid, 16, 1) + pltpu.roll(lo, 32, 1))


def unpack3(v, axis):
    return v + pltpu.roll(v, 112, axis) + pltpu.roll(v, 96, axis)


def as_rows(parts, count):
    row = lax.broadcasted_iota(jnp.int32, (count, 128), 0)
    out = jnp.zeros((count, 128), F32)
    for r, part in parts:
        out = jnp.where(row == r, part, out)
    return out


def call(body, outs, args, scratch=(), vmem=48, flops=0, name=None):
    spaces = {"v": pltpu.VMEM, "a": pl.ANY, "s": pltpu.SMEM, "h": pltpu.HBM}
    return pl.pallas_call(
        body,
        out_shape=[jax.ShapeDtypeStruct(s, t) for s, t, _ in outs],
        in_specs=[pl.BlockSpec(memory_space=spaces[m]) for _, m in args],
        out_specs=[pl.BlockSpec(memory_space=spaces[m]) for _, _, m in outs],
        scratch_shapes=list(scratch),
        compiler_params=pltpu.CompilerParams(vmem_limit_bytes=vmem * MIB),
        cost_estimate=pl.CostEstimate(flops=int(flops), bytes_accessed=4 * MIB, transcendentals=0),
        name=name,
    )(*[a for a, _ in args])


DMA = pltpu.SemaphoreType.DMA


def pack_body(sc, lm, om, bm, do, la, g0, wsh, buf, sem):
    i, core = sc[0], sc[4]
    cols = pl.ds(pl.multiple_of(core * 640, 128), 640)
    first = [
        (bm.at[0, :, cols], g0.at[0:48, :]),
        (bm.at[1, :, cols], g0.at[48:96, :]),
        (lm.at[0, :, cols], g0.at[96:176, :]),
        (la.at[:, cols], g0.at[176:192, :]),
    ]
    first = [pltpu.make_async_copy(a, b, sem.at[8 + k]) for k, (a, b) in enumerate(first)]
    for c in first:
        c.start()
    blocks = [(80 * k, 80, (om if s == "o" else lm), n, D) for k, (s, n) in enumerate(SQUARE)]
    blocks += [(DEC_ROW, 80, do, None, DI), (BQ_ROW, 48, bm, 2, D)]
    for k in range(NI):
        lo, hi = ROWS_I * k, ROWS_I * (k + 1)

        @pl.when(i == k)
        def _(lo=lo, hi=hi):
            cs = []
            for row, count, ref, n, width in blocks:
                a, b = max(lo, row), min(hi, row + count)
                if a < b:
                    src = ref.at[a - row : b - row, :] if n is None else ref.at[n, a - row : b - row, :]
                    dst = buf.at[a - lo : b - lo, :] if width == D else buf.at[a - lo : b - lo, 0:width]
                    cs.append(pltpu.make_async_copy(src, dst, sem.at[len(cs)]))
            for c in cs:
                c.start()
            for c in cs:
                c.wait()

    out = pltpu.make_async_copy(buf, wsh, sem.at[12])
    out.start()
    for c in first:
        c.wait()
    out.wait()


def pieces_from(sc, groups):
    x, z, core = sc[2], sc[3], sc[4]
    out = []
    for side in range(2):
        c = core if side == 0 else 1 - core
        col = pl.ds(pl.multiple_of(c * 640, 128), 640)
        for e in range(4):
            for d in range(4):
                xs = jnp.where(c == 0, (x + 4 - d) & 3, (x + 4 - e) & 3)
                zs = jnp.where(c == 0, (z + 4 - e) & 3, (z + 4 - d) & 3)
                out.append((xs * 4 + zs, col, groups[4 * side + e].at[d]))
    return out


def enc_body(sc, t0, t1, t2, t3, u0, u1, u2, u3, x_in, bg, lg, g_out, nb_o, k_o, v_o, q_o, pay, gs, acc, sem):
    copies = [
        pltpu.make_async_copy(src, gs.at[pos, :, col], sem.at[k])
        for k, (pos, col, src) in enumerate(pieces_from(sc, (t0, t1, t2, t3, u0, u1, u2, u3)))
    ]
    for c in copies:
        c.start()
    n_in, _ = norm(x_in[...].astype(F32))
    nb = half(n_in * bg[0:1, :])
    nb_o[...] = nb
    for c in copies:
        c.wait()
    save = pltpu.make_async_copy(gs, g_out, sem.at[32])
    save.start()
    k_o[...] = half(dot(nb, gs[:, 0:48, :].reshape(DI, D)))
    v_o[...] = half(dot(nb, gs[:, 48:96, :].reshape(DI, D)))
    z0b = gs[:, 176:192, :].reshape(R, D)
    nq, _ = norm(z0b.astype(F32))
    q_o[...] = half(dot(half(nq * lg[0:1, :]), gs[:, 96:176, :].reshape(D, D)))
    acc[...] = jnp.zeros_like(acc)
    valid = lanes(N) + sc[1] * N < sc[5]
    lane = lanes(128)
    stats = jnp.zeros((R, 128), F32)
    for h in range(H):
        w = slice(WIN[h], WIN[h] + 256)
        mk = head_mask(h)
        s = dot_nt(q_o[:, w] * half(mk), k_o[:, w]) * SCALE
        s = jnp.where(valid, s, -1e30)
        m = jnp.max(s, axis=-1, keepdims=True)
        p = jnp.exp(s - m)
        acc[:, w] += dot(half(p), v_o[:, w]) * mk
        stats = jnp.where(lane == h, m, stats)
        stats = jnp.where(lane == 8 + h, jnp.sum(p, axis=-1, keepdims=True), stats)
    pay[:, 0:D] = half(acc[...])
    pay[:, D : D + 128] = pack3(stats)
    save.wait()


def combine_body(rcv, out):
    st = unpack3(rcv[:, :, D : D + 128].astype(F32), 2)
    peak = jnp.max(st, axis=0, keepdims=True)
    w = jnp.exp(st - peak)
    total = jnp.sum(w * pltpu.roll(st, 120, 2), axis=0, keepdims=True)
    coef = w / total
    lane = lax.broadcasted_iota(jnp.int32, (1, 1, 128), 2)
    for t in range(10):
        h0, h1 = 128 * t // E, (128 * t + 127) // E
        c = coef[:, :, h0 : h0 + 1]
        if h1 != h0:
            c = jnp.where(lane >= E * h1 - 128 * t, coef[:, :, h1 : h1 + 1], c)
        o = jnp.sum(rcv[:, :, 128 * t : 128 * t + 128].astype(F32) * c, axis=0)
        out[:, 128 * t : 128 * t + 128] = half(o)
    lse = jnp.where(lanes(128) < 8, (peak + jnp.log(total))[0], 0.0)
    out[:, D : D + 128] = pack3(lse)


class Ring:
    def __init__(self, w, slots, sem, order):
        self.w, self.slots, self.sem, self.order = w, slots, sem, order
        self.n = slots.shape[0]
        self.pos = {m: k for k, m in enumerate(order)}

    def copies(self, m):
        s = self.pos[m] % self.n
        return [
            pltpu.make_async_copy(
                self.w.at[i, :, r0 : r0 + n, :], self.slots.at[s, :, d0 : d0 + n, :], self.sem.at[s, k]
            )
            for k, (i, r0, d0, n) in enumerate(pieces(80 * m, 80))
        ]

    def start(self, m):
        for c in self.copies(m):
            c.start()

    def begin(self):
        for m in self.order[: self.n]:
            self.start(m)

    def get(self, m):
        for c in self.copies(m):
            c.wait()
        return self.slots[self.pos[m] % self.n].reshape(D, D)

    def done(self, m):
        k = self.pos[m] + self.n
        if k < len(self.order):
            self.start(self.order[k])


def forward_body(
    qin, cot, bg, lg, e_h, g_all, w,
    res, gqin, gain_o, pay, mix_o, nd_o, gq_o, z_h, h_h, a_h,
    slots, e, z0b, zs, hs, qs, acc, kd, vd, dec, bq, dacc, gq, gkv, wsem, ssem, lsem,
):
    first = [
        pltpu.make_async_copy(e_h.at[:, 0:D], e, lsem.at[3]),
        pltpu.make_async_copy(g_all.at[:, 176:192, :], z0b, lsem.at[4]),
    ]
    for c in first:
        c.start()
    ring = Ring(w, slots, wsem, list(range(11)))
    ring.begin()
    copies = []
    for i, r0, d0, n in pieces(BQ_ROW, 48):
        copies.append(pltpu.make_async_copy(w.at[i, :, r0 : r0 + n, :], bq.at[:, d0 : d0 + n, :], lsem.at[0]))
    for i, r0, d0, n in pieces(DEC_ROW, 80):
        copies.append(
            pltpu.make_async_copy(w.at[i, :, r0 : r0 + n, 0:DI], dec.at[:, d0 : d0 + n, :], lsem.at[len(copies)])
        )
    for c in copies:
        c.start()
    saves = []

    def save(src, dst):
        c = pltpu.make_async_copy(src, dst, ssem.at[len(saves)])
        c.start()
        saves.append(c)

    def mul(a, m):
        out = dot(a, ring.get(m))
        ring.done(m)
        return out

    for c in first:
        c.wait()
    z1 = z0b[...].reshape(R, D).astype(F32) + mul(e[...], 0)
    zs[0] = z1
    save(zs.at[0], z_h.at[0])
    h1 = mul(half(norm(z1)[0] * lg[1:2, :]), 1)
    hs[0] = h1
    save(hs.at[0], h_h.at[0])
    zs[1] = zs[0] + mul(half(gelu(h1)), 2)
    save(zs.at[1], z_h.at[1])
    s_b = half(norm(zs[1])[0] * lg[2:3, :])
    for k in range(3):
        qs[k] = half(mul(s_b, 3 + k))
        save(qs.at[k], a_h.at[k])
    acc[...] = jnp.zeros_like(acc)
    for h in range(H):
        win = slice(WIN[h], WIN[h] + 256)
        mk = head_mask(h)
        s = dot_nt(qs[0, :, win] * half(mk), qs[1, :, win]) * SCALE
        p = jnp.exp(s - jnp.max(s, axis=-1, keepdims=True))
        p = p / jnp.sum(p, axis=-1, keepdims=True)
        acc[:, win] += dot(half(p), qs[2, :, win]) * mk
    qs[3] = half(acc[...])
    save(qs.at[3], a_h.at[3])
    zs[2] = zs[1] + mul(qs[3], 6)
    save(zs.at[2], z_h.at[2])
    h2 = mul(half(norm(zs[2])[0] * lg[3:4, :]), 7)
    hs[1] = h2
    save(hs.at[1], h_h.at[1])
    zs[3] = zs[2] + mul(half(gelu(h2)), 8)
    save(zs.at[3], z_h.at[3])
    c_b = half(norm(zs[3])[0] * lg[4:5, :])
    kd[...] = half(mul(c_b, 9))
    vd[...] = half(mul(c_b, 10))

    x = qin[...].astype(F32)
    n, inv = norm(x)
    nd = half(n * bg[1:2, :])
    nd_o[...] = nd
    for c in copies:
        c.wait()
    wq = bq[...].reshape(DI, D)
    wd = dec[...].reshape(D, DI)
    gq_o[...] = half(dot(nd, wq))
    mix_o[...] = half(dot_nt(cot[...], wd))
    dacc[...] = jnp.zeros_like(dacc)
    gq[...] = jnp.zeros_like(gq)
    gkv[...] = jnp.zeros_like(gkv)
    for h in range(H):
        win = slice(WIN[h], WIN[h] + 256)
        mk = head_mask(h)
        mkb = half(mk)
        qw, gw, kw, vw = gq_o[:, win], mix_o[:, win], kd[:, win], vd[:, win]
        s = dot_nt(qw * mkb, kw) * SCALE
        p = jnp.exp(s - jnp.max(s, axis=-1, keepdims=True))
        p = p / jnp.sum(p, axis=-1, keepdims=True)
        pb = half(p)
        dacc[:, win] += dot(pb, vw) * mk
        dp = dot_nt(gw * mkb, vw)
        ds = half(p * (dp - jnp.sum(p * dp, axis=-1, keepdims=True)))
        gq[:, win] += dot(ds, kw) * mk
        gkv[0, :, win] += dot_tn(ds, qw) * mk
        gkv[1, :, win] += dot_tn(pb, gw) * mk
    pay[:, 0:D] = half(gkv[0] * SCALE)
    pay[:, D : 2 * D] = half(gkv[1])
    mix = half(dacc[...])
    mix_o[...] = mix
    res[...] = half(x + dot(mix, wd))
    gqb = half(gq[...] * SCALE)
    gq_o[...] = gqb
    gin, gg = norm_back(dot_nt(gqb, wq), bg[1:2, :], n, inv)
    gqin[...] = cot[...].astype(F32) + gin
    gain_o[...] = gg
    for c in saves:
        c.wait()


def prepare_body(lg, z_h, h_h, a_h, n_h, i_h, s_h, act_h, p_h, mark, zs, hs, qs, ns, vs, ss, acts, ps, sem, osem):
    loads = {}
    for k in range(4):
        loads["z", k] = pltpu.make_async_copy(z_h.at[k], zs.at[k], sem.at[k])
    for k in range(2):
        loads["h", k] = pltpu.make_async_copy(h_h.at[k], hs.at[k], sem.at[4 + k])
    loads["q"] = pltpu.make_async_copy(a_h.at[0:2], qs, sem.at[6])
    for c in loads.values():
        c.start()
    saves = []

    def save(src, dst):
        c = pltpu.make_async_copy(src, dst, osem.at[len(saves)])
        c.start()
        saves.append(c)

    for k, a in ((3, 0), (2, 2), (1, 1), (0, 4)):
        loads["z", k].wait()
        n, inv = norm(zs[k])
        ns[k] = half(n)
        save(ns.at[k], n_h.at[k])
        vs[k] = jnp.broadcast_to(inv, (R, 128))
        acts[a] = half(n * lg[k + 1 : k + 2, :])
        save(acts.at[a], act_h.at[a])
    save(vs, i_h)
    for k, a in ((1, 3), (0, 5)):
        loads["h", k].wait()
        x = hs[k]
        t = jnp.tanh(C0 * (x + C1 * x * x * x))
        acts[a] = half(0.5 * x * (1.0 + t))
        save(acts.at[a], act_h.at[a])
        ss[k] = 0.5 * (1.0 + t) + 0.5 * x * (1.0 - t * t) * (C0 * (1.0 + 3.0 * C1 * x * x))
        save(ss.at[k], s_h.at[k])
    loads["q"].wait()
    for h in range(H):
        win = slice(WIN[h], WIN[h] + 256)
        s = dot_nt(qs[0, :, win] * half(head_mask(h)), qs[1, :, win]) * SCALE
        p = jnp.exp(s - jnp.max(s, axis=-1, keepdims=True))
        ps[h] = half(p / jnp.sum(p, axis=-1, keepdims=True))
    save(ps, p_h)
    mark[...] = vs[0, 0:8, :]
    for c in saves:
        c.wait()


def lat_backward_body(
    sc, gkv, lg, w, e_h, n_h, i_h, s_h, act_h, a_h, p_h, gmix, pack_o, g1c_o, gains_o,
    slots, ns, vs, ss, acts, qs, ps, acc, acc2, acc3, gh, gw, wsem, lsem,
):
    order = [9, 10, 8, 7, 6, 3, 4, 5, 2, 1, 0]
    ring = Ring(w, slots, wsem, order)
    todo = [
        (n_h.at[3], ns.at[3]),
        (i_h, vs),
        (act_h.at[0], acts.at[0]),
        (s_h.at[1], ss.at[1]),
        (act_h.at[3], acts.at[1]),
        (n_h.at[2], ns.at[2]),
        (act_h.at[2], acts.at[3]),
        (a_h.at[3], acts.at[4]),
        (p_h, ps),
        (a_h.at[0:3], qs.at[0:3]),
        (n_h.at[1], ns.at[1]),
        (act_h.at[1], acts.at[2]),
        (s_h.at[0], ss.at[0]),
        (act_h.at[5], acts.at[5]),
        (n_h.at[0], ns.at[0]),
        (act_h.at[4], acts.at[6]),
        (e_h.at[:, 0:D], acts.at[7]),
    ]
    loads = [pltpu.make_async_copy(a, b, lsem.at[k]) for k, (a, b) in enumerate(todo)]
    after = {9: (5, 6, 7), 10: (8,), 8: (9,), 7: (10, 11), 6: (12, 13), 3: (14, 15, 16)}
    ring.start(9)
    ring.start(10)
    for c in loads[:2]:
        c.start()
    ring.start(8)
    for c in loads[2:5]:
        c.start()
    for m in order[3 : ring.n]:
        ring.start(m)

    def ready(*ks):
        for k in ks:
            loads[k].wait()

    src = sc[1] * 80
    start = pl.multiple_of(jnp.minimum((src >> 7) * 128, 1024), 128)
    offset = src - start
    lane = lanes(256)

    def put(ref, to):
        v = pltpu.roll(ref[:, pl.ds(start, 256)].astype(F32), (to - offset + 256) & 255, 1)
        return jnp.where((lane >= to) & (lane < to + 80), v, 0.0)

    def weight_grad(window, first, count):
        a = acts[first : first + count].reshape(count * R, D)
        pack_o[:, 256 * window : 256 * window + 256] = half(dot_tn(a, gw[first : first + count].reshape(count * R, 256)))

    def mul(g_b, m):
        out = dot_nt(g_b, ring.get(m))
        ring.done(m)
        for k in after.get(m, ()):
            loads[k].start()
        return out

    gain_rows = []

    def back(g, k):
        out, gg = norm_back(g, lg[k + 1 : k + 2, :], ns[k].astype(F32), vs[k][:, 0:1])
        for t in range(10):
            gain_rows.append((10 * k + t, gg[:, 128 * t : 128 * t + 128]))
        return out

    ready(0, 1)
    gn = mul(gkv[:, 0:D], 9) + mul(gkv[:, D : 2 * D], 10)
    acc[...] = back(gn, 3)
    gw[0] = half(put(gkv.at[:, 0:D], 0) + put(gkv.at[:, D : 2 * D], 80))
    gw[1] = half(put(acc, 160))
    ready(2, 3, 4)
    gh[...] = half(mul(half(acc[...]), 8) * ss[1])
    weight_grad(0, 0, 2)
    ready(5)
    gw[3] = half(put(gh, 0))
    acc[...] += back(mul(gh[...], 7), 2)
    gw[4] = half(put(acc, 80))
    qs[3] = half(mul(half(acc[...]), 6))
    acc2[...] = jnp.zeros_like(acc2)
    acc3[...] = jnp.zeros_like(acc3)
    ready(6, 7, 8, 9)
    for h in range(H):
        win = slice(WIN[h], WIN[h] + 256)
        mk = head_mask(h)
        pb = ps[h]
        p = pb.astype(F32)
        dp = dot_nt(qs[3, :, win] * half(mk), qs[2, :, win])
        ds = half(p * (dp - jnp.sum(p * dp, axis=-1, keepdims=True)) * SCALE)
        acc2[:, win] += dot(ds, qs[1, :, win]) * mk
        acc3[0, :, win] += dot_tn(ds, qs[0, :, win]) * mk
        acc3[1, :, win] += dot_tn(pb, qs[3, :, win]) * mk
    gw[2] = half(put(acc2, 0) + put(acc3.at[0], 80) + put(acc3.at[1], 160))
    gn = mul(half(acc2[...]), 3)
    gn = gn + mul(half(acc3[0]), 4)
    gn = gn + mul(half(acc3[1]), 5)
    ready(10, 11)
    weight_grad(1, 2, 1)
    acc[...] += back(gn, 1)
    gw[5] = half(put(acc, 160))
    ready(12, 13)
    gh[...] = half(mul(half(acc[...]), 2) * ss[0])
    weight_grad(2, 3, 3)
    gw[6] = half(put(gh, 0))
    ready(14, 15, 16)
    acc[...] += back(mul(gh[...], 1), 0)
    gw[7] = half(put(acc, 80))
    g1c_o[...] = half(put(acc, 0)[:, 0:128])
    gmix[...] = half(mul(half(acc[...]), 0))
    weight_grad(3, 6, 2)
    gains_o[...] = as_rows(gain_rows, 48)


def sum_rows_body(rcv, dw, out):
    s = half(jnp.sum(rcv[...].astype(F32), axis=0))
    for k in range(NJ):
        out[k] = s


def dec_weights_body(mix, cot, nd, gq, mark, out, buf, sem):
    g = half(dot_tn(mix[...], cot[...]))
    for i in range(NI):
        for t in range(6):
            buf[i, 160 * t : 160 * t + 160, :] = g[160 * i : 160 * i + 160, 128 * t : 128 * t + 128]
    one = pltpu.make_async_copy(buf.at[:, 0:960, :], out.at[:, 0:960, :], sem.at[0])
    one.start()
    g = half(dot_tn(nd[...], gq[...]))
    for i in range(NI):
        for t in range(10):
            r = 960 + 96 * t
            buf[i, r : r + 96, :] = g[96 * i : 96 * i + 96, 128 * t : 128 * t + 128]
    two = pltpu.make_async_copy(buf.at[:, 960:1920, :], out.at[:, 960:1920, :], sem.at[1])
    two.start()
    one.wait()
    two.wait()


def spread(chunk, pay, td, tb):
    fill = jnp.zeros((96, 128), F32)
    for t in range(6):
        v = jnp.concatenate([chunk[160 * t : 160 * t + 160, :].astype(F32), fill], axis=0)
        td[128 * t : 128 * t + 128, :] = v.T
    fill = jnp.zeros((32, 128), F32)
    for t in range(10):
        v = jnp.concatenate([chunk[960 + 96 * t : 960 + 96 * t + 96, :].astype(F32), fill], axis=0)
        tb[128 * t : 128 * t + 128, :] = v.T
    for j in range(NJ):
        pay[j, 512:560, :] = half(td[48 * j : 48 * j + 48, 0:128])
        pay[j, 560:608, :] = half(td[48 * j : 48 * j + 48, 128:256])
        pay[j, 608:688, :] = half(tb[80 * j : 80 * j + 80, :])


def unspread(s, dec_o, bq_o):
    fill = jnp.zeros((80, 128), F32)
    a = jnp.concatenate([s[0:48], fill], axis=0).T
    b = jnp.concatenate([s[48:96], fill], axis=0).T
    dec_o[0:128, :] = a[:, 0:48]
    dec_o[128:160, :] = b[0:32, 0:48]
    c = jnp.concatenate([s[96:176], fill[0:48]], axis=0).T
    bq_o[...] = c[0:96, 0:80]


def enc_back_body(
    sc, x_in, bg, lg, gd, gmix_h, e_h, q_h, k_h, v_h, g_all, dw_h, gin_o, pay,
    gmix, e, q, k, v, wkv, gq, gkt, gvt, dw, td, tb, sem,
):
    pairs = [(gmix_h, gmix), (q_h, q), (k_h, k), (v_h, v), (e_h, e), (g_all, wkv), (dw_h, dw)]
    loads = [pltpu.make_async_copy(a, b, sem.at[n]) for n, (a, b) in enumerate(pairs)]
    for c in loads:
        c.start()
    for c in loads[:5]:
        c.wait()
    lse = unpack3(e[:, D : D + 128].astype(F32), 1)
    valid = lanes(N) + sc[1] * N < sc[5]
    gq[...] = jnp.zeros_like(gq)
    for h in range(H):
        win = slice(WIN[h], WIN[h] + 256)
        mk = head_mask(h)
        mkb = half(mk)
        qw, gw, kw, vw = q[:, win], gmix[:, win], k[:, win], v[:, win]
        rd = jnp.sum(gw.astype(F32) * e[:, win].astype(F32) * mk, axis=-1, keepdims=True)
        s = dot_nt(qw * mkb, kw) * SCALE
        p = jnp.where(valid, jnp.exp(jnp.where(valid, s, -1e30) - lse[:, h : h + 1]), 0.0)
        dp = dot_nt(gw * mkb, vw)
        ds = half(p * (dp - rd))
        gq[:, win] += dot(ds, kw) * mk
        o = OFF[h]
        gkt[E * h : E * h + E, :] = half(dot_tn(qw, ds)[o : o + E, :] * SCALE)
        gvt[E * h : E * h + E, :] = half(dot_tn(gw, half(p))[o : o + E, :])
    pay[:, 320:400, :] = gkt[...].reshape(NJ, 80, 128)
    pay[:, 400:480, :] = gvt[...].reshape(NJ, 80, 128)
    loads[5].wait()
    gqs = gq[...] * SCALE
    gqt = half(gqs.T)
    pay[:, 160:240, :] = gqt[:, 0:128].reshape(NJ, 80, 128)
    pay[:, 240:320, :] = gqt[:, 128:256].reshape(NJ, 80, 128)
    n, inv = norm(wkv[:, 176:192, :].reshape(R, D).astype(F32))
    gz, g0 = norm_back(dot_nt(half(gqs), wkv[:, 96:176, :].reshape(D, D)), lg[0:1, :], n, inv)
    gzt = half(gz.T)
    pay[:, 0:80, :] = gzt[:, 0:128].reshape(NJ, 80, 128)
    pay[:, 80:160, :] = gzt[:, 128:256].reshape(NJ, 80, 128)
    n, inv = norm(x_in[...].astype(F32))
    gnt = dot(wkv[:, 0:48, :].reshape(DI, D), gkt[...]) + dot(wkv[:, 48:96, :].reshape(DI, D), gvt[...])
    gin, gg = norm_back(gnt.T, bg[0:1, :], n, inv)
    gin_o[...] = gin
    rows = [(t, gg[:, 128 * t : 128 * t + 128]) for t in range(6)]
    rows += [(6 + t, gd[:, 128 * t : 128 * t + 128]) for t in range(6)]
    rows += [(16 + t, g0[:, 128 * t : 128 * t + 128]) for t in range(10)]
    g = half(as_rows(rows, 32))
    for j in range(NJ):
        pay[j, 480:512, :] = g
    loads[6].wait()
    spread(dw, pay, td, tb)


def tail_one_body(rcv, nf_h, g_all, lg, lat_gain, g1c, out, dec_o, bq_o, nf, z0b, left, sem):
    loads = [
        pltpu.make_async_copy(nf_h, nf, sem.at[0]),
        pltpu.make_async_copy(g_all.at[:, 176:192, :], z0b, sem.at[1]),
    ]
    for c in loads:
        c.start()
    sums = jnp.sum(rcv[:, 0:320, :].astype(F32), axis=0)
    fill = jnp.zeros((48, 128), F32)
    left[...] = jnp.zeros_like(left)
    for s in range(NJ):
        left[0:80, 128 * s : 128 * s + 128] = rcv[s, 320:400, :]
        left[128:208, 128 * s : 128 * s + 128] = rcv[s, 400:480, :]
    loads[1].wait()
    nq = half(norm(z0b[...].reshape(R, D).astype(F32))[0] * lg[0:1, :])
    a = jnp.concatenate([sums[160:240], fill], axis=0).T
    b = jnp.concatenate([sums[240:320], fill], axis=0).T
    w0 = half(dot_tn(nq, half(jnp.concatenate([a, b], axis=0))))
    a = jnp.concatenate([sums[0:80], fill], axis=0).T
    b = jnp.concatenate([sums[80:160], fill], axis=0).T
    gz = half(jnp.concatenate([a, b], axis=0) + g1c[...].astype(F32))
    gains = jnp.sum(rcv[:, 480:512, :].astype(F32), axis=0)
    gains = half(jnp.concatenate([gains, lat_gain[...]], axis=0))
    loads[0].wait()
    wt = half(dot(left[...], nf[...]).T)
    for i in range(NI):
        out[i, 0:160, :] = w0[160 * i : 160 * i + 160, :]
        out[i, 160:192, :] = gz[32 * i : 32 * i + 32, :]
        out[i, 192:288, :] = wt[96 * i : 96 * i + 96, 0:128]
        out[i, 288:384, :] = wt[96 * i : 96 * i + 96, 128:256]
        out[i, 384:464, :] = gains
    unspread(jnp.sum(rcv[:, 512:688, :].astype(F32), axis=0), dec_o, bq_o)


def tail_two_body(rcv, pack, arr_o, lm_o, om_o, wkv_o, lat_o, byte_o):
    sums = jnp.sum(rcv[...].astype(F32), axis=0)
    lm_o[0] = sums[0:160, 0:80]
    arr_o[...] = sums[160:192, 0:80]
    wkv_o[0] = sums[192:288, 0:80]
    wkv_o[1] = sums[288:384, 0:80]
    g = sums[384:464]
    for t in range(6):
        for b in range(2):
            byte_o[b : b + 1, 128 * t : 128 * t + 128] = g[6 * b + t : 6 * b + t + 1, :]
    for t in range(10):
        for b in range(5):
            r = 16 + t if b == 0 else 32 + 10 * (b - 1) + t
            lat_o[b : b + 1, 128 * t : 128 * t + 128] = g[r : r + 1, :]
    for m, (kind, n) in enumerate(SQUARE):
        window, o = PLACE[m]
        v = pack[:, 256 * window : 256 * window + 256].astype(F32)
        if o:
            v = pltpu.roll(v, 256 - o, 1)
        if kind == "l":
            lm_o[n] = v[:, 0:80]
        else:
            om_o[n] = v[:, 0:80]


def line(y, c, x, z):
    return ((y % 4) * 2 + c) * NJ + (x % 4) * NZ + (z % 4)


EVERY = [(y, c, x, z) for y in range(4) for c in range(2) for x in range(NX) for z in range(NZ)]


def along(stage, d):
    out = []
    for y, c, x, z in EVERY:
        on_x = (c == 0) == (stage == 0)
        out.append((line(y, c, x, z), line(y, c, x + d, z) if on_x else line(y, c, x, z + d)))
    return out


SWAP = [(line(y, c, x, z), line(y, 1 - c, x, z)) for y, c, x, z in EVERY]


def exchange(v, axes):
    flat = v.reshape(v.shape[0] * v.shape[1], v.shape[2])
    return lax.all_to_all(flat, axes, split_axis=0, concat_axis=0, tiled=True).reshape(v.shape)


def shards(inputs, queries, lengths, latent_array, latent_mats, out_mats, byte_mats, dec_out, lg, bg, cotangent):
    y, core, x, z = (lax.axis_index(a) for a in AXES)
    i, j = y * 2 + core, x * NZ + z
    sc = jnp.stack([i, j, x, z, core, lengths[0]]).astype(jnp.int32)
    xin, qin, cot = inputs[0], queries[0], cotangent[0]

    g0, wsh = call(
        pack_body,
        [((192, 640), BF, "v"), ((ROWS_I, D), BF, "h")],
        [(sc, "s"), (latent_mats, "h"), (out_mats, "h"), (byte_mats, "h"), (dec_out, "h"), (latent_array, "h")],
        [pltpu.VMEM((ROWS_I, D), BF), DMA((13,))],
        vmem=60,
        name="pack",
    )
    w = lax.all_gather(wsh, AXES, axis=0, tiled=True).reshape(NI, NJ, ROWS_I, D)

    def step(v, stage):
        return [lax.ppermute(v, AXES, along(stage, d)) for d in (1, 2, 3)]

    s0 = jnp.stack([g0] + step(g0, 0))
    own = [s0] + step(s0, 1)
    sib = [lax.ppermute(v, AXES, SWAP) for v in own]
    g_all, nb, k_b, v_b, q_b, pay = call(
        enc_body,
        [
            ((NJ, 192, D), BF, "h"),
            ((N, DI), BF, "v"),
            ((N, D), BF, "v"),
            ((N, D), BF, "v"),
            ((R, D), BF, "v"),
            ((R, D + 128), BF, "v"),
        ],
        [(sc, "s")] + [(v, "a") for v in own + sib] + [(xin, "v"), (bg, "v"), (lg, "v")],
        [pltpu.VMEM((NJ, 192, D), BF), pltpu.VMEM((R, D), F32), DMA((33,))],
        vmem=60,
        flops=3e9,
        name="enc",
    )
    rcv = exchange(pay.reshape(NJ, 16, D + 128), BLK)
    (mine,) = call(combine_body, [((16, D + 128), BF, "v")], [(rcv, "v")], name="combine")
    e = lax.all_gather(mine, BLK, axis=0, tiled=True)

    big = (NJ, 80, D)
    res, gqin, gd, dpay, mix, nd, gq, z_h, h_h, a_h = call(
        forward_body,
        [
            ((N, DI), BF, "v"),
            ((N, DI), F32, "v"),
            ((1, DI), F32, "v"),
            ((R, 2 * D), BF, "v"),
            ((N, D), BF, "v"),
            ((N, DI), BF, "v"),
            ((N, D), BF, "v"),
            ((4, R, D), F32, "h"),
            ((2, R, D), F32, "h"),
            ((4, R, D), BF, "h"),
        ],
        [(qin, "v"), (cot, "v"), (bg, "v"), (lg, "v"), (e, "h"), (g_all, "h"), (w, "h")],
        [
            pltpu.VMEM((5,) + big, BF),
            pltpu.VMEM((R, D), BF),
            pltpu.VMEM((NJ, 16, D), BF),
            pltpu.VMEM((4, R, D), F32),
            pltpu.VMEM((2, R, D), F32),
            pltpu.VMEM((4, R, D), BF),
            pltpu.VMEM((R, D), F32),
            pltpu.VMEM((R, D), BF),
            pltpu.VMEM((R, D), BF),
            pltpu.VMEM((NJ, 80, DI), BF),
            pltpu.VMEM((NJ, 48, D), BF),
            pltpu.VMEM((N, D), F32),
            pltpu.VMEM((N, D), F32),
            pltpu.VMEM((2, R, D), F32),
            DMA((5, 2)),
            DMA((10,)),
            DMA((5,)),
        ],
        vmem=58,
        flops=1.5e10,
        name="forward",
    )
    rows = exchange(dpay.reshape(NJ, 16, 2 * D), BLK)
    n_h, i_h, s_h, act_h, p_h, mark = call(
        prepare_body,
        [
            ((4, R, D), BF, "h"),
            ((4, R, 128), F32, "h"),
            ((2, R, D), F32, "h"),
            ((6, R, D), BF, "h"),
            ((H, R, R), BF, "h"),
            ((8, 128), F32, "v"),
        ],
        [(lg, "v"), (z_h, "h"), (h_h, "h"), (a_h, "h")],
        [
            pltpu.VMEM((4, R, D), F32),
            pltpu.VMEM((2, R, D), F32),
            pltpu.VMEM((2, R, D), BF),
            pltpu.VMEM((4, R, D), BF),
            pltpu.VMEM((4, R, 128), F32),
            pltpu.VMEM((2, R, D), F32),
            pltpu.VMEM((6, R, D), BF),
            pltpu.VMEM((H, R, R), BF),
            DMA((7,)),
            DMA((14,)),
        ],
        vmem=60,
        flops=5e9,
        name="prepare",
    )
    (dw,) = call(
        dec_weights_body,
        [((NI, 1920, 128), BF, "h")],
        [(mix, "v"), (cot, "v"), (nd, "v"), (gq, "v"), (mark, "h")],
        [pltpu.VMEM((NI, 1920, 128), BF), DMA((2,))],
        vmem=60,
        flops=4e9,
        name="dec_weights",
    )
    (dup,) = call(
        sum_rows_body,
        [((NJ, 16, 2 * D), BF, "v")],
        [(rows, "v"), (dw, "h")],
        vmem=60,
        name="sum_rows",
    )
    gkv = exchange(dup, BLK).reshape(R, 2 * D)
    nb, _ = lax.optimization_barrier((nb, dup))
    nf = lax.all_gather(nb, BLK, axis=0, tiled=True)
    dw = lax.psum_scatter(dw.reshape(NI * 1920, 128), BATCH, scatter_dimension=0, tiled=True)

    gmix, pack, g1c, lat_gain = call(
        lat_backward_body,
        [((R, D), BF, "v"), ((D, 1024), BF, "v"), ((R, 128), BF, "v"), ((48, 128), F32, "v")],
        [(sc, "s"), (gkv, "v"), (lg, "v")] + [(v, "h") for v in (w, e, n_h, i_h, s_h, act_h, a_h, p_h)],
        [
            pltpu.VMEM((5,) + big, BF),
            pltpu.VMEM((4, R, D), BF),
            pltpu.VMEM((4, R, 128), F32),
            pltpu.VMEM((2, R, D), F32),
            pltpu.VMEM((8, R, D), BF),
            pltpu.VMEM((4, R, D), BF),
            pltpu.VMEM((H, R, R), BF),
            pltpu.VMEM((R, D), F32),
            pltpu.VMEM((R, D), F32),
            pltpu.VMEM((2, R, D), F32),
            pltpu.VMEM((R, D), BF),
            pltpu.VMEM((8, R, 256), BF),
            DMA((5, 2)),
            DMA((17,)),
        ],
        vmem=60,
        flops=1.6e10,
        name="lat_backward",
    )
    pack = lax.psum_scatter(pack, BATCH, scatter_dimension=0, tiled=True)
    gin, epay = call(
        enc_back_body,
        [((N, DI), F32, "v"), ((NJ, 688, 128), BF, "v")],
        [(sc, "s"), (xin, "v"), (bg, "v"), (lg, "v"), (gd, "v")]
        + [(v, "h") for v in (gmix, e, q_b, k_b, v_b, g_all, dw)],
        [
            pltpu.VMEM((R, D), BF),
            pltpu.VMEM((R, D + 128), BF),
            pltpu.VMEM((R, D), BF),
            pltpu.VMEM((N, D), BF),
            pltpu.VMEM((N, D), BF),
            pltpu.VMEM((NJ, 192, D), BF),
            pltpu.VMEM((R, D), F32),
            pltpu.VMEM((D, N), BF),
            pltpu.VMEM((D, N), BF),
            pltpu.VMEM((1920, 128), BF),
            pltpu.VMEM((DI, 256), F32),
            pltpu.VMEM((D, 128), F32),
            DMA((7,)),
        ],
        vmem=56,
        flops=3e9,
        name="enc_back",
    )
    r1 = exchange(epay, BLK)
    p2, dec_grad, bq_grad = call(
        tail_one_body,
        [((NI, 464, 128), BF, "v"), ((160, 48), F32, "v"), ((96, 80), F32, "v")],
        [(r1, "v"), (nf, "h"), (g_all, "h"), (lg, "v"), (lat_gain, "v"), (g1c, "v")],
        [pltpu.VMEM((NJ * N, DI), BF), pltpu.VMEM((NJ, 16, D), BF), pltpu.VMEM((256, 2048), BF), DMA((2,))],
        name="tail_one",
    )
    r2 = exchange(p2, BATCH)
    arr, lm, om, wkv, lat_gains, byte_gain = call(
        tail_two_body,
        [
            ((32, 80), F32, "v"),
            ((10, 160, 80), F32, "v"),
            ((2, 160, 80), F32, "v"),
            ((2, 96, 80), F32, "v"),
            ((5, D), F32, "v"),
            ((2, DI), F32, "v"),
        ],
        [(r2, "v"), (pack, "v")],
        name="tail_two",
    )
    byte_grads = jnp.concatenate([wkv, bq_grad[None]], axis=0)
    return (res[None], gin[None], gqin[None], arr, lm, om, byte_grads, dec_grad, lat_gains, byte_gain)


def solution(mesh):
    grid = Mesh(mesh.devices.reshape(4, 2, NX, NZ), AXES)
    return jax.shard_map(
        shards,
        mesh=grid,
        in_specs=(
            P(BATCH, BLK, None),
            P(BATCH, BLK, None),
            P(BATCH),
            P(BLK, None),
            P(None, BLK, None),
            P(None, BLK, None),
            P(None, BLK, None),
            P(BLK, None),
            P(),
            P(),
            P(BATCH, BLK, None),
        ),
        out_specs=(
            P(BATCH, BLK, None),
            P(BATCH, BLK, None),
            P(BATCH, BLK, None),
            P(BATCH, BLK),
            P(None, BATCH, BLK),
            P(None, BATCH, BLK),
            P(None, BATCH, BLK),
            P(BATCH, BLK),
            P(),
            P(),
        ),
        check_vma=False,
    )
```

```python
import jax
import jax.numpy as jnp
from jax import lax
from jax.experimental import pallas as pl
from jax.experimental.pallas import tpu as pltpu
from jax.sharding import Mesh, PartitionSpec as P

F32, BF = jnp.float32, jnp.bfloat16
D, DI, R, N, H, E = 1280, 768, 256, 128, 8, 160
NX, NZ, NJ, NI = 4, 4, 16, 8
SCALE = E**-0.5
EPS = 1e-5
MIB = 1 << 20
AXES = ("y", "core", "x", "z")
BATCH = ("y", "core")
BLK = ("x", "z")
WIN = [128 * (E * h // 128) for h in range(H)]
OFF = [E * h - WIN[h] for h in range(H)]
SQUARE = [("o", 0), ("l", 1), ("l", 2), ("l", 3), ("l", 4), ("l", 5), ("o", 1), ("l", 6), ("l", 7), ("l", 8), ("l", 9)]
ROWS_I = 128
DEC_ROW, BQ_ROW = 880, 960
PLACE = {9: (0, 0), 10: (0, 80), 8: (0, 160), 3: (1, 0), 4: (1, 80), 5: (1, 160), 7: (2, 0), 6: (2, 80), 2: (2, 160), 1: (3, 0), 0: (3, 80)}


def dot(a, b, ca=1, cb=0):
    return lax.dot_general(a, b, (((ca,), (cb,)), ((), ())), preferred_element_type=F32)


def dot_nt(a, b):
    return dot(a, b, 1, 1)


def dot_tn(a, b):
    return dot(a, b, 0, 0)


def half(v):
    return v.astype(BF)


def norm(v):
    c = v - jnp.mean(v, axis=-1, keepdims=True)
    inv = lax.rsqrt(jnp.mean(c * c, axis=-1, keepdims=True) + EPS)
    return c * inv, inv


def norm_back(g, gain, n, inv):
    gg = jnp.sum(g * n, axis=0, keepdims=True)
    inner = g * gain
    m1 = jnp.mean(inner, axis=-1, keepdims=True)
    m2 = jnp.mean(inner * n, axis=-1, keepdims=True)
    return inv * (inner - m1 - n * m2), gg


C0, C1 = 0.7978845608028654, 0.044715


def gelu(x):
    return 0.5 * x * (1.0 + jnp.tanh(C0 * (x + C1 * x * x * x)))


def gelu_slope(x):
    t = jnp.tanh(C0 * (x + C1 * x * x * x))
    return 0.5 * (1.0 + t) + 0.5 * x * (1.0 - t * t) * (C0 * (1.0 + 3.0 * C1 * x * x))


def lanes(width):
    return lax.broadcasted_iota(jnp.int32, (1, width), 1)


def head_mask(h):
    lane = lanes(256)
    return jnp.where((lane >= OFF[h]) & (lane < OFF[h] + E), 1.0, 0.0).astype(F32)


def pieces(row, count):
    out = []
    done = 0
    while done < count:
        i, r0 = divmod(row + done, ROWS_I)
        n = min(count - done, ROWS_I - r0)
        out.append((i, r0, done, n))
        done += n
    return out


def split3(v):
    hi = half(v).astype(F32)
    mid = half(v - hi).astype(F32)
    lo = half(v - hi - mid).astype(F32)
    return hi, mid, lo


def pack3(v):
    hi, mid, lo = split3(v)
    return half(hi + pltpu.roll(mid, 16, 1) + pltpu.roll(lo, 32, 1))


def unpack3(v, axis):
    return v + pltpu.roll(v, 112, axis) + pltpu.roll(v, 96, axis)


def as_rows(parts, count):
    row = lax.broadcasted_iota(jnp.int32, (count, 128), 0)
    out = jnp.zeros((count, 128), F32)
    for r, part in parts:
        out = jnp.where(row == r, part, out)
    return out


def call(body, outs, args, scratch=(), vmem=48, flops=0, name=None):
    spaces = {"v": pltpu.VMEM, "a": pl.ANY, "s": pltpu.SMEM, "h": pltpu.HBM}
    return pl.pallas_call(
        body,
        out_shape=[jax.ShapeDtypeStruct(s, t) for s, t, _ in outs],
        in_specs=[pl.BlockSpec(memory_space=spaces[m]) for _, m in args],
        out_specs=[pl.BlockSpec(memory_space=spaces[m]) for _, _, m in outs],
        scratch_shapes=list(scratch),
        compiler_params=pltpu.CompilerParams(vmem_limit_bytes=vmem * MIB),
        cost_estimate=pl.CostEstimate(flops=int(flops), bytes_accessed=4 * MIB, transcendentals=0),
        name=name,
    )(*[a for a, _ in args])


DMA = pltpu.SemaphoreType.DMA


def pack_body(sc, lm, om, bm, do, la, g0, wsh, buf, sem):
    i, core = sc[0], sc[4]
    cols = pl.ds(pl.multiple_of(core * 640, 128), 640)
    first = [
        (bm.at[0, :, cols], g0.at[0:48, :]),
        (bm.at[1, :, cols], g0.at[48:96, :]),
        (lm.at[0, :, cols], g0.at[96:176, :]),
        (la.at[:, cols], g0.at[176:192, :]),
    ]
    first = [pltpu.make_async_copy(a, b, sem.at[8 + k]) for k, (a, b) in enumerate(first)]
    for c in first:
        c.start()
    blocks = [(80 * k, 80, (om if s == "o" else lm), n, D) for k, (s, n) in enumerate(SQUARE)]
    blocks += [(DEC_ROW, 80, do, None, DI), (BQ_ROW, 48, bm, 2, D)]
    for k in range(NI):
        lo, hi = ROWS_I * k, ROWS_I * (k + 1)

        @pl.when(i == k)
        def _(lo=lo, hi=hi):
            cs = []
            for row, count, ref, n, width in blocks:
                a, b = max(lo, row), min(hi, row + count)
                if a < b:
                    src = ref.at[a - row : b - row, :] if n is None else ref.at[n, a - row : b - row, :]
                    dst = buf.at[a - lo : b - lo, :] if width == D else buf.at[a - lo : b - lo, 0:width]
                    cs.append(pltpu.make_async_copy(src, dst, sem.at[len(cs)]))
            for c in cs:
                c.start()
            for c in cs:
                c.wait()

    out = pltpu.make_async_copy(buf, wsh, sem.at[12])
    out.start()
    for c in first:
        c.wait()
    out.wait()


def pieces_from(sc, groups):
    x, z, core = sc[2], sc[3], sc[4]
    out = []
    for side in range(2):
        c = core if side == 0 else 1 - core
        col = pl.ds(pl.multiple_of(c * 640, 128), 640)
        for e in range(4):
            for d in range(4):
                xs = jnp.where(c == 0, (x + 4 - d) & 3, (x + 4 - e) & 3)
                zs = jnp.where(c == 0, (z + 4 - e) & 3, (z + 4 - d) & 3)
                out.append((xs * 4 + zs, col, groups[4 * side + e].at[d]))
    return out


def enc_body(sc, t0, t1, t2, t3, u0, u1, u2, u3, x_in, bg, lg, g_out, nb_o, k_o, v_o, q_o, pay, gs, acc, sem):
    copies = [
        pltpu.make_async_copy(src, gs.at[pos, :, col], sem.at[k])
        for k, (pos, col, src) in enumerate(pieces_from(sc, (t0, t1, t2, t3, u0, u1, u2, u3)))
    ]
    for c in copies:
        c.start()
    n_in, _ = norm(x_in[...].astype(F32))
    nb = half(n_in * bg[0:1, :])
    nb_o[...] = nb
    for c in copies:
        c.wait()
    save = pltpu.make_async_copy(gs, g_out, sem.at[32])
    save.start()
    k_o[...] = half(dot(nb, gs[:, 0:48, :].reshape(DI, D)))
    v_o[...] = half(dot(nb, gs[:, 48:96, :].reshape(DI, D)))
    z0b = gs[:, 176:192, :].reshape(R, D)
    nq, _ = norm(z0b.astype(F32))
    q_o[...] = half(dot(half(nq * lg[0:1, :]), gs[:, 96:176, :].reshape(D, D)))
    acc[...] = jnp.zeros_like(acc)
    valid = lanes(N) + sc[1] * N < sc[5]
    lane = lanes(128)
    stats = jnp.zeros((R, 128), F32)
    for h in range(H):
        w = slice(WIN[h], WIN[h] + 256)
        mk = head_mask(h)
        s = dot_nt(q_o[:, w] * half(mk), k_o[:, w]) * SCALE
        s = jnp.where(valid, s, -1e30)
        m = jnp.max(s, axis=-1, keepdims=True)
        p = jnp.exp(s - m)
        acc[:, w] += dot(half(p), v_o[:, w]) * mk
        stats = jnp.where(lane == h, m, stats)
        stats = jnp.where(lane == 8 + h, jnp.sum(p, axis=-1, keepdims=True), stats)
    pay[:, 0:D] = half(acc[...])
    pay[:, D : D + 128] = pack3(stats)
    save.wait()


def combine_body(rcv, out):
    st = unpack3(rcv[:, :, D : D + 128].astype(F32), 2)
    peak = jnp.max(st, axis=0, keepdims=True)
    w = jnp.exp(st - peak)
    total = jnp.sum(w * pltpu.roll(st, 120, 2), axis=0, keepdims=True)
    coef = w / total
    lane = lax.broadcasted_iota(jnp.int32, (1, 1, 128), 2)
    for t in range(10):
        h0, h1 = 128 * t // E, (128 * t + 127) // E
        c = coef[:, :, h0 : h0 + 1]
        if h1 != h0:
            c = jnp.where(lane >= E * h1 - 128 * t, coef[:, :, h1 : h1 + 1], c)
        o = jnp.sum(rcv[:, :, 128 * t : 128 * t + 128].astype(F32) * c, axis=0)
        out[:, 128 * t : 128 * t + 128] = half(o)
    lse = jnp.where(lanes(128) < 8, (peak + jnp.log(total))[0], 0.0)
    out[:, D : D + 128] = pack3(lse)


class Ring:
    def __init__(self, w, slots, sem, order):
        self.w, self.slots, self.sem, self.order = w, slots, sem, order
        self.n = slots.shape[0]
        self.pos = {m: k for k, m in enumerate(order)}

    def copies(self, m):
        s = self.pos[m] % self.n
        return [
            pltpu.make_async_copy(
                self.w.at[i, :, r0 : r0 + n, :], self.slots.at[s, :, d0 : d0 + n, :], self.sem.at[s, k]
            )
            for k, (i, r0, d0, n) in enumerate(pieces(80 * m, 80))
        ]

    def start(self, m):
        for c in self.copies(m):
            c.start()

    def begin(self):
        for m in self.order[: self.n]:
            self.start(m)

    def get(self, m):
        for c in self.copies(m):
            c.wait()
        return self.slots[self.pos[m] % self.n].reshape(D, D)

    def done(self, m):
        k = self.pos[m] + self.n
        if k < len(self.order):
            self.start(self.order[k])


def forward_body(
    qin, cot, bg, lg, e_h, g_all, w,
    res, gqin, gain_o, pay, mix_o, nd_o, gq_o, z_h, h_h, a_h,
    slots, e, z0b, zs, hs, qs, acc, kd, vd, dec, bq, dacc, gq, gkv, wsem, ssem, lsem,
):
    first = [
        pltpu.make_async_copy(e_h.at[:, 0:D], e, lsem.at[3]),
        pltpu.make_async_copy(g_all.at[:, 176:192, :], z0b, lsem.at[4]),
    ]
    for c in first:
        c.start()
    ring = Ring(w, slots, wsem, list(range(11)))
    ring.begin()
    copies = []
    for i, r0, d0, n in pieces(BQ_ROW, 48):
        copies.append(pltpu.make_async_copy(w.at[i, :, r0 : r0 + n, :], bq.at[:, d0 : d0 + n, :], lsem.at[0]))
    for i, r0, d0, n in pieces(DEC_ROW, 80):
        copies.append(
            pltpu.make_async_copy(w.at[i, :, r0 : r0 + n, 0:DI], dec.at[:, d0 : d0 + n, :], lsem.at[len(copies)])
        )
    for c in copies:
        c.start()
    saves = []

    def save(src, dst):
        c = pltpu.make_async_copy(src, dst, ssem.at[len(saves)])
        c.start()
        saves.append(c)

    def mul(a, m):
        out = dot(a, ring.get(m))
        ring.done(m)
        return out

    for c in first:
        c.wait()
    z1 = z0b[...].reshape(R, D).astype(F32) + mul(e[...], 0)
    zs[0] = z1
    save(zs.at[0], z_h.at[0])
    h1 = mul(half(norm(z1)[0] * lg[1:2, :]), 1)
    hs[0] = h1
    save(hs.at[0], h_h.at[0])
    zs[1] = zs[0] + mul(half(gelu(h1)), 2)
    save(zs.at[1], z_h.at[1])
    s_b = half(norm(zs[1])[0] * lg[2:3, :])
    for k in range(3):
        qs[k] = half(mul(s_b, 3 + k))
        save(qs.at[k], a_h.at[k])
    acc[...] = jnp.zeros_like(acc)
    for h in range(H):
        win = slice(WIN[h], WIN[h] + 256)
        mk = head_mask(h)
        s = dot_nt(qs[0, :, win] * half(mk), qs[1, :, win]) * SCALE
        p = jnp.exp(s - jnp.max(s, axis=-1, keepdims=True))
        p = p / jnp.sum(p, axis=-1, keepdims=True)
        acc[:, win] += dot(half(p), qs[2, :, win]) * mk
    qs[3] = half(acc[...])
    save(qs.at[3], a_h.at[3])
    zs[2] = zs[1] + mul(qs[3], 6)
    save(zs.at[2], z_h.at[2])
    h2 = mul(half(norm(zs[2])[0] * lg[3:4, :]), 7)
    hs[1] = h2
    save(hs.at[1], h_h.at[1])
    zs[3] = zs[2] + mul(half(gelu(h2)), 8)
    save(zs.at[3], z_h.at[3])
    c_b = half(norm(zs[3])[0] * lg[4:5, :])
    kd[...] = half(mul(c_b, 9))
    vd[...] = half(mul(c_b, 10))

    x = qin[...].astype(F32)
    n, inv = norm(x)
    nd = half(n * bg[1:2, :])
    nd_o[...] = nd
    for c in copies:
        c.wait()
    wq = bq[...].reshape(DI, D)
    wd = dec[...].reshape(D, DI)
    gq_o[...] = half(dot(nd, wq))
    mix_o[...] = half(dot_nt(cot[...], wd))
    dacc[...] = jnp.zeros_like(dacc)
    gq[...] = jnp.zeros_like(gq)
    gkv[...] = jnp.zeros_like(gkv)
    for h in range(H):
        win = slice(WIN[h], WIN[h] + 256)
        mk = head_mask(h)
        mkb = half(mk)
        qw, gw, kw, vw = gq_o[:, win], mix_o[:, win], kd[:, win], vd[:, win]
        s = dot_nt(qw * mkb, kw) * SCALE
        p = jnp.exp(s - jnp.max(s, axis=-1, keepdims=True))
        p = p / jnp.sum(p, axis=-1, keepdims=True)
        pb = half(p)
        dacc[:, win] += dot(pb, vw) * mk
        dp = dot_nt(gw * mkb, vw)
        ds = half(p * (dp - jnp.sum(p * dp, axis=-1, keepdims=True)))
        gq[:, win] += dot(ds, kw) * mk
        gkv[0, :, win] += dot_tn(ds, qw) * mk
        gkv[1, :, win] += dot_tn(pb, gw) * mk
    pay[:, 0:D] = half(gkv[0] * SCALE)
    pay[:, D : 2 * D] = half(gkv[1])
    mix = half(dacc[...])
    mix_o[...] = mix
    res[...] = half(x + dot(mix, wd))
    gqb = half(gq[...] * SCALE)
    gq_o[...] = gqb
    gin, gg = norm_back(dot_nt(gqb, wq), bg[1:2, :], n, inv)
    gqin[...] = cot[...].astype(F32) + gin
    gain_o[...] = gg
    for c in saves:
        c.wait()


def prepare_body(lg, z_h, h_h, a_h, n_h, i_h, s_h, act_h, p_h, mark, zs, hs, qs, ns, vs, ss, acts, ps, sem, osem):
    loads = {}
    for k in range(4):
        loads["z", k] = pltpu.make_async_copy(z_h.at[k], zs.at[k], sem.at[k])
    for k in range(2):
        loads["h", k] = pltpu.make_async_copy(h_h.at[k], hs.at[k], sem.at[4 + k])
    loads["q"] = pltpu.make_async_copy(a_h.at[0:2], qs, sem.at[6])
    for c in loads.values():
        c.start()
    saves = []

    def save(src, dst):
        c = pltpu.make_async_copy(src, dst, osem.at[len(saves)])
        c.start()
        saves.append(c)

    for k, a in ((3, 0), (2, 2), (1, 1), (0, 4)):
        loads["z", k].wait()
        n, inv = norm(zs[k])
        ns[k] = half(n)
        save(ns.at[k], n_h.at[k])
        vs[k] = jnp.broadcast_to(inv, (R, 128))
        acts[a] = half(n * lg[k + 1 : k + 2, :])
        save(acts.at[a], act_h.at[a])
    save(vs, i_h)
    for k, a in ((1, 3), (0, 5)):
        loads["h", k].wait()
        x = hs[k]
        t = jnp.tanh(C0 * (x + C1 * x * x * x))
        acts[a] = half(0.5 * x * (1.0 + t))
        save(acts.at[a], act_h.at[a])
        ss[k] = 0.5 * (1.0 + t) + 0.5 * x * (1.0 - t * t) * (C0 * (1.0 + 3.0 * C1 * x * x))
        save(ss.at[k], s_h.at[k])
    loads["q"].wait()
    for h in range(H):
        win = slice(WIN[h], WIN[h] + 256)
        s = dot_nt(qs[0, :, win] * half(head_mask(h)), qs[1, :, win]) * SCALE
        p = jnp.exp(s - jnp.max(s, axis=-1, keepdims=True))
        ps[h] = half(p / jnp.sum(p, axis=-1, keepdims=True))
    save(ps, p_h)
    mark[...] = vs[0, 0:8, :]
    for c in saves:
        c.wait()


def lat_backward_body(
    sc, gkv, lg, w, e_h, n_h, i_h, s_h, act_h, a_h, p_h, gmix, pack_o, g1c_o, gains_o,
    slots, ns, vs, ss, acts, qs, ps, acc, acc2, acc3, gh, gw, wsem, lsem,
):
    order = [9, 10, 8, 7, 6, 3, 4, 5, 2, 1, 0]
    ring = Ring(w, slots, wsem, order)
    todo = [
        (n_h.at[3], ns.at[3]),
        (i_h, vs),
        (act_h.at[0], acts.at[0]),
        (s_h.at[1], ss.at[1]),
        (act_h.at[3], acts.at[1]),
        (n_h.at[2], ns.at[2]),
        (act_h.at[2], acts.at[3]),
        (a_h.at[3], acts.at[4]),
        (p_h, ps),
        (a_h.at[0:3], qs.at[0:3]),
        (n_h.at[1], ns.at[1]),
        (act_h.at[1], acts.at[2]),
        (s_h.at[0], ss.at[0]),
        (act_h.at[5], acts.at[5]),
        (n_h.at[0], ns.at[0]),
        (act_h.at[4], acts.at[6]),
        (e_h.at[:, 0:D], acts.at[7]),
    ]
    loads = [pltpu.make_async_copy(a, b, lsem.at[k]) for k, (a, b) in enumerate(todo)]
    after = {9: (5, 6, 7), 10: (8,), 8: (9,), 7: (10, 11), 6: (12, 13), 3: (14, 15, 16)}
    ring.start(9)
    ring.start(10)
    for c in loads[:2]:
        c.start()
    ring.start(8)
    for c in loads[2:5]:
        c.start()
    for m in order[3 : ring.n]:
        ring.start(m)

    def ready(*ks):
        for k in ks:
            loads[k].wait()

    src = sc[1] * 80
    start = pl.multiple_of(jnp.minimum((src >> 7) * 128, 1024), 128)
    offset = src - start
    lane = lanes(256)

    def put(ref, to):
        v = pltpu.roll(ref[:, pl.ds(start, 256)].astype(F32), (to - offset + 256) & 255, 1)
        return jnp.where((lane >= to) & (lane < to + 80), v, 0.0)

    def weight_grad(window, first, count):
        a = acts[first : first + count].reshape(count * R, D)
        pack_o[:, 256 * window : 256 * window + 256] = half(dot_tn(a, gw[first : first + count].reshape(count * R, 256)))

    def mul(g_b, m):
        out = dot_nt(g_b, ring.get(m))
        ring.done(m)
        for k in after.get(m, ()):
            loads[k].start()
        return out

    gain_rows = []

    def back(g, k):
        out, gg = norm_back(g, lg[k + 1 : k + 2, :], ns[k].astype(F32), vs[k][:, 0:1])
        for t in range(10):
            gain_rows.append((10 * k + t, gg[:, 128 * t : 128 * t + 128]))
        return out

    ready(0, 1)
    gn = mul(gkv[:, 0:D], 9) + mul(gkv[:, D : 2 * D], 10)
    acc[...] = back(gn, 3)
    gw[0] = half(put(gkv.at[:, 0:D], 0) + put(gkv.at[:, D : 2 * D], 80))
    gw[1] = half(put(acc, 160))
    ready(2, 3, 4)
    gh[...] = half(mul(half(acc[...]), 8) * ss[1])
    weight_grad(0, 0, 2)
    ready(5)
    gw[3] = half(put(gh, 0))
    acc[...] += back(mul(gh[...], 7), 2)
    gw[4] = half(put(acc, 80))
    qs[3] = half(mul(half(acc[...]), 6))
    acc2[...] = jnp.zeros_like(acc2)
    acc3[...] = jnp.zeros_like(acc3)
    ready(6, 7, 8, 9)
    for h in range(H):
        win = slice(WIN[h], WIN[h] + 256)
        mk = head_mask(h)
        pb = ps[h]
        p = pb.astype(F32)
        dp = dot_nt(qs[3, :, win] * half(mk), qs[2, :, win])
        ds = half(p * (dp - jnp.sum(p * dp, axis=-1, keepdims=True)) * SCALE)
        acc2[:, win] += dot(ds, qs[1, :, win]) * mk
        acc3[0, :, win] += dot_tn(ds, qs[0, :, win]) * mk
        acc3[1, :, win] += dot_tn(pb, qs[3, :, win]) * mk
    gw[2] = half(put(acc2, 0) + put(acc3.at[0], 80) + put(acc3.at[1], 160))
    gn = mul(half(acc2[...]), 3)
    gn = gn + mul(half(acc3[0]), 4)
    gn = gn + mul(half(acc3[1]), 5)
    ready(10, 11)
    weight_grad(1, 2, 1)
    acc[...] += back(gn, 1)
    gw[5] = half(put(acc, 160))
    ready(12, 13)
    gh[...] = half(mul(half(acc[...]), 2) * ss[0])
    weight_grad(2, 3, 3)
    gw[6] = half(put(gh, 0))
    ready(14, 15, 16)
    acc[...] += back(mul(gh[...], 1), 0)
    gw[7] = half(put(acc, 80))
    g1c_o[...] = half(put(acc, 0)[:, 0:128])
    gmix[...] = half(mul(half(acc[...]), 0))
    weight_grad(3, 6, 2)
    gains_o[...] = as_rows(gain_rows, 48)


def sum_rows_body(rcv, mark, out):
    s = half(jnp.sum(rcv[...].astype(F32), axis=0))
    for k in range(NJ):
        out[k] = s


def dec_weights_body(mix, cot, nd, gq, out, buf, sem):
    g = half(dot_tn(mix[...], cot[...]))
    for i in range(NI):
        for t in range(6):
            buf[i, 160 * t : 160 * t + 160, :] = g[160 * i : 160 * i + 160, 128 * t : 128 * t + 128]
    one = pltpu.make_async_copy(buf.at[:, 0:960, :], out.at[:, 0:960, :], sem.at[0])
    one.start()
    g = half(dot_tn(nd[...], gq[...]))
    for i in range(NI):
        for t in range(10):
            r = 960 + 96 * t
            buf[i, r : r + 96, :] = g[96 * i : 96 * i + 96, 128 * t : 128 * t + 128]
    two = pltpu.make_async_copy(buf.at[:, 960:1920, :], out.at[:, 960:1920, :], sem.at[1])
    two.start()
    one.wait()
    two.wait()


def spread(chunk, pay, td, tb):
    fill = jnp.zeros((96, 128), F32)
    for t in range(6):
        v = jnp.concatenate([chunk[160 * t : 160 * t + 160, :].astype(F32), fill], axis=0)
        td[128 * t : 128 * t + 128, :] = v.T
    fill = jnp.zeros((32, 128), F32)
    for t in range(10):
        v = jnp.concatenate([chunk[960 + 96 * t : 960 + 96 * t + 96, :].astype(F32), fill], axis=0)
        tb[128 * t : 128 * t + 128, :] = v.T
    for j in range(NJ):
        tail = pltpu.roll(td[48 * j : 48 * j + 48, 128:256], 96, 1)
        pay[j, 512:560, :] = half(tb[80 * j : 80 * j + 48, :] + tail)
        pay[j, 560:592, :] = half(tb[80 * j + 48 : 80 * j + 80, :])
        pay[j, 592:640, :] = half(td[48 * j : 48 * j + 48, 0:128])


def enc_back_body(
    sc, x_in, bg, lg, gd, gmix_h, e_h, q_h, k_h, v_h, g_all, dw_h, gin_o, pay,
    gmix, e, q, k, v, wkv, gq, gkt, gvt, dw, td, tb, sem,
):
    pairs = [(gmix_h, gmix), (q_h, q), (k_h, k), (v_h, v), (e_h, e), (g_all, wkv), (dw_h, dw)]
    loads = [pltpu.make_async_copy(a, b, sem.at[n]) for n, (a, b) in enumerate(pairs)]
    for c in loads:
        c.start()
    for c in loads[:5]:
        c.wait()
    lse = unpack3(e[:, D : D + 128].astype(F32), 1)
    valid = lanes(N) + sc[1] * N < sc[5]
    gq[...] = jnp.zeros_like(gq)
    for h in range(H):
        win = slice(WIN[h], WIN[h] + 256)
        mk = head_mask(h)
        mkb = half(mk)
        qw, gw, kw, vw = q[:, win], gmix[:, win], k[:, win], v[:, win]
        rd = jnp.sum(gw.astype(F32) * e[:, win].astype(F32) * mk, axis=-1, keepdims=True)
        s = dot_nt(qw * mkb, kw) * SCALE
        p = jnp.where(valid, jnp.exp(jnp.where(valid, s, -1e30) - lse[:, h : h + 1]), 0.0)
        dp = dot_nt(gw * mkb, vw)
        ds = half(p * (dp - rd))
        gq[:, win] += dot(ds, kw) * mk
        o = OFF[h]
        gkt[E * h : E * h + E, :] = half(dot_tn(qw, ds)[o : o + E, :] * SCALE)
        gvt[E * h : E * h + E, :] = half(dot_tn(gw, half(p))[o : o + E, :])
    pay[:, 320:400, :] = gkt[...].reshape(NJ, 80, 128)
    pay[:, 400:480, :] = gvt[...].reshape(NJ, 80, 128)
    loads[5].wait()
    gqs = gq[...] * SCALE
    gqt = half(gqs.T)
    pay[:, 160:240, :] = gqt[:, 0:128].reshape(NJ, 80, 128)
    pay[:, 240:320, :] = gqt[:, 128:256].reshape(NJ, 80, 128)
    n, inv = norm(wkv[:, 176:192, :].reshape(R, D).astype(F32))
    gz, g0 = norm_back(dot_nt(half(gqs), wkv[:, 96:176, :].reshape(D, D)), lg[0:1, :], n, inv)
    gzt = half(gz.T)
    pay[:, 0:80, :] = gzt[:, 0:128].reshape(NJ, 80, 128)
    pay[:, 80:160, :] = gzt[:, 128:256].reshape(NJ, 80, 128)
    n, inv = norm(x_in[...].astype(F32))
    gnt = dot(wkv[:, 0:48, :].reshape(DI, D), gkt[...]) + dot(wkv[:, 48:96, :].reshape(DI, D), gvt[...])
    gin, gg = norm_back(gnt.T, bg[0:1, :], n, inv)
    gin_o[...] = gin
    rows = [(t, gg[:, 128 * t : 128 * t + 128]) for t in range(6)]
    rows += [(6 + t, gd[:, 128 * t : 128 * t + 128]) for t in range(6)]
    rows += [(16 + t, g0[:, 128 * t : 128 * t + 128]) for t in range(10)]
    g = half(as_rows(rows, 32))
    for j in range(NJ):
        pay[j, 480:512, :] = g
    loads[6].wait()
    spread(dw, pay, td, tb)


def tail_one_body(rcv, nf_h, g_all, lg, lat_gain, g1c, out, dec_o, bq_o, nf, z0b, left, sem):
    loads = [
        pltpu.make_async_copy(nf_h, nf, sem.at[0]),
        pltpu.make_async_copy(g_all.at[:, 176:192, :], z0b, sem.at[1]),
    ]
    for c in loads:
        c.start()
    sums = jnp.sum(rcv[:, 0:320, :].astype(F32), axis=0)
    fill = jnp.zeros((48, 128), F32)
    left[...] = jnp.zeros_like(left)
    for s in range(NJ):
        left[0:80, 128 * s : 128 * s + 128] = rcv[s, 320:400, :]
        left[128:208, 128 * s : 128 * s + 128] = rcv[s, 400:480, :]
    loads[1].wait()
    nq = half(norm(z0b[...].reshape(R, D).astype(F32))[0] * lg[0:1, :])
    a = jnp.concatenate([sums[160:240], fill], axis=0).T
    b = jnp.concatenate([sums[240:320], fill], axis=0).T
    w0 = dot_tn(nq, half(jnp.concatenate([a, b], axis=0)))
    a = jnp.concatenate([sums[0:80], fill], axis=0).T
    b = jnp.concatenate([sums[80:160], fill], axis=0).T
    gz = half(jnp.concatenate([a, b], axis=0) + g1c[...].astype(F32))
    gains = jnp.sum(rcv[:, 480:512, :].astype(F32), axis=0)
    gains = half(jnp.concatenate([gains, lat_gain[...]], axis=0))
    loads[0].wait()
    wt = dot(left[...], nf[...]).T
    lane = lanes(128)
    key, value = wt[:, 0:128], wt[:, 128:256]
    one = half(jnp.where(lane < 80, key, pltpu.roll(value, 80, 1)))
    other = pltpu.roll(value, 32, 1)
    for i in range(NI):
        r = 96 * i
        beside = jnp.concatenate([other[r : r + 96, :], jnp.zeros((64, 128), F32)], axis=0)
        out[i, 0:160, :] = half(jnp.where(lane < 80, w0[160 * i : 160 * i + 160, :], beside))
        out[i, 160:192, :] = gz[32 * i : 32 * i + 32, :]
        out[i, 192:288, :] = one[r : r + 96, :]
        out[i, 288:368, :] = gains
    s = jnp.sum(rcv[:, 512:640, :].astype(F32), axis=0)
    bq_o[...] = s[0:80, 0:96]
    dec_o[:, 0:128] = s[80:128]
    dec_o[:, 128:160] = pltpu.roll(s[0:48], 32, 1)[:, 0:32]


def tail_two_body(rcv, pack, bq, arr_o, lm_o, om_o, bm_o, lat_o, byte_o):
    sums = jnp.sum(rcv[...].astype(F32), axis=0)
    lm_o[0] = sums[0:160, 0:80]
    arr_o[...] = sums[160:192, 0:80]
    lane = lanes(128)
    value = jnp.where(lane < 48, pltpu.roll(sums[192:288], 48, 1), pltpu.roll(sums[0:96], 96, 1))
    fill = jnp.zeros((32, 128), F32)
    bm_o[0] = jnp.concatenate([sums[192:288], fill], axis=0).T[0:80, 0:96]
    bm_o[1] = jnp.concatenate([value, fill], axis=0).T[0:80, 0:96]
    bm_o[2] = bq[...]
    g = sums[288:368]
    for t in range(6):
        for b in range(2):
            byte_o[b : b + 1, 128 * t : 128 * t + 128] = g[6 * b + t : 6 * b + t + 1, :]
    for t in range(10):
        for b in range(5):
            r = 16 + t if b == 0 else 32 + 10 * (b - 1) + t
            lat_o[b : b + 1, 128 * t : 128 * t + 128] = g[r : r + 1, :]
    for m, (kind, n) in enumerate(SQUARE):
        window, o = PLACE[m]
        v = pack[:, 256 * window : 256 * window + 256].astype(F32)
        if o:
            v = pltpu.roll(v, 256 - o, 1)
        if kind == "l":
            lm_o[n] = v[:, 0:80]
        else:
            om_o[n] = v[:, 0:80]


def line(y, c, x, z):
    return ((y % 4) * 2 + c) * NJ + (x % 4) * NZ + (z % 4)


EVERY = [(y, c, x, z) for y in range(4) for c in range(2) for x in range(NX) for z in range(NZ)]


def along(stage, d):
    out = []
    for y, c, x, z in EVERY:
        on_x = (c == 0) == (stage == 0)
        out.append((line(y, c, x, z), line(y, c, x + d, z) if on_x else line(y, c, x, z + d)))
    return out


SWAP = [(line(y, c, x, z), line(y, 1 - c, x, z)) for y, c, x, z in EVERY]


def exchange(v, axes):
    flat = v.reshape(v.shape[0] * v.shape[1], v.shape[2])
    return lax.all_to_all(flat, axes, split_axis=0, concat_axis=0, tiled=True).reshape(v.shape)


def shards(inputs, queries, lengths, latent_array, latent_mats, out_mats, byte_mats, dec_out, lg, bg, cotangent):
    y, core, x, z = (lax.axis_index(a) for a in AXES)
    i, j = y * 2 + core, x * NZ + z
    sc = jnp.stack([i, j, x, z, core, lengths[0]]).astype(jnp.int32)
    xin, qin, cot = inputs[0], queries[0], cotangent[0]

    g0, wsh = call(
        pack_body,
        [((192, 640), BF, "v"), ((ROWS_I, D), BF, "h")],
        [(sc, "s"), (latent_mats, "h"), (out_mats, "h"), (byte_mats, "h"), (dec_out, "h"), (latent_array, "h")],
        [pltpu.VMEM((ROWS_I, D), BF), DMA((13,))],
        vmem=60,
        name="pack",
    )
    w = lax.all_gather(wsh, AXES, axis=0, tiled=True).reshape(NI, NJ, ROWS_I, D)

    def step(v, stage):
        return [lax.ppermute(v, AXES, along(stage, d)) for d in (1, 2, 3)]

    s0 = jnp.stack([g0] + step(g0, 0))
    own = [s0] + step(s0, 1)
    sib = [lax.ppermute(v, AXES, SWAP) for v in own]
    g_all, nb, k_b, v_b, q_b, pay = call(
        enc_body,
        [
            ((NJ, 192, D), BF, "h"),
            ((N, DI), BF, "v"),
            ((N, D), BF, "v"),
            ((N, D), BF, "v"),
            ((R, D), BF, "v"),
            ((R, D + 128), BF, "v"),
        ],
        [(sc, "s")] + [(v, "a") for v in own + sib] + [(xin, "v"), (bg, "v"), (lg, "v")],
        [pltpu.VMEM((NJ, 192, D), BF), pltpu.VMEM((R, D), F32), DMA((33,))],
        vmem=60,
        flops=3e9,
        name="enc",
    )
    rcv = exchange(pay.reshape(NJ, 16, D + 128), BLK)
    (mine,) = call(combine_body, [((16, D + 128), BF, "v")], [(rcv, "v")], name="combine")
    e = lax.all_gather(mine, BLK, axis=0, tiled=True)

    big = (NJ, 80, D)
    res, gqin, gd, dpay, mix, nd, gq, z_h, h_h, a_h = call(
        forward_body,
        [
            ((N, DI), BF, "v"),
            ((N, DI), F32, "v"),
            ((1, DI), F32, "v"),
            ((R, 2 * D), BF, "v"),
            ((N, D), BF, "v"),
            ((N, DI), BF, "v"),
            ((N, D), BF, "v"),
            ((4, R, D), F32, "h"),
            ((2, R, D), F32, "h"),
            ((4, R, D), BF, "h"),
        ],
        [(qin, "v"), (cot, "v"), (bg, "v"), (lg, "v"), (e, "h"), (g_all, "h"), (w, "h")],
        [
            pltpu.VMEM((4,) + big, BF),
            pltpu.VMEM((R, D), BF),
            pltpu.VMEM((NJ, 16, D), BF),
            pltpu.VMEM((4, R, D), F32),
            pltpu.VMEM((2, R, D), F32),
            pltpu.VMEM((4, R, D), BF),
            pltpu.VMEM((R, D), F32),
            pltpu.VMEM((R, D), BF),
            pltpu.VMEM((R, D), BF),
            pltpu.VMEM((NJ, 80, DI), BF),
            pltpu.VMEM((NJ, 48, D), BF),
            pltpu.VMEM((N, D), F32),
            pltpu.VMEM((N, D), F32),
            pltpu.VMEM((2, R, D), F32),
            DMA((4, 2)),
            DMA((10,)),
            DMA((5,)),
        ],
        vmem=54,
        flops=1.5e10,
        name="forward",
    )
    rows = exchange(dpay.reshape(NJ, 16, 2 * D), BLK)
    n_h, i_h, s_h, act_h, p_h, mark = call(
        prepare_body,
        [
            ((4, R, D), BF, "h"),
            ((4, R, 128), F32, "h"),
            ((2, R, D), F32, "h"),
            ((6, R, D), BF, "h"),
            ((H, R, R), BF, "h"),
            ((8, 128), F32, "v"),
        ],
        [(lg, "v"), (z_h, "h"), (h_h, "h"), (a_h, "h")],
        [
            pltpu.VMEM((4, R, D), F32),
            pltpu.VMEM((2, R, D), F32),
            pltpu.VMEM((2, R, D), BF),
            pltpu.VMEM((4, R, D), BF),
            pltpu.VMEM((4, R, 128), F32),
            pltpu.VMEM((2, R, D), F32),
            pltpu.VMEM((6, R, D), BF),
            pltpu.VMEM((H, R, R), BF),
            DMA((7,)),
            DMA((14,)),
        ],
        vmem=36,
        flops=5e9,
        name="prepare",
    )
    (dw,) = call(
        dec_weights_body,
        [((NI, 1920, 128), BF, "h")],
        [(mix, "v"), (cot, "v"), (nd, "v"), (gq, "v")],
        [pltpu.VMEM((NI, 1920, 128), BF), DMA((2,))],
        vmem=60,
        flops=4e9,
        name="dec_weights",
    )
    (dup,) = call(
        sum_rows_body, [((NJ, 16, 2 * D), BF, "v")], [(rows, "v"), (mark, "h")], vmem=12, name="sum_rows"
    )
    gkv = exchange(dup, BLK).reshape(R, 2 * D)
    nb, _ = lax.optimization_barrier((nb, dup))
    nf = lax.all_gather(nb, BLK, axis=0, tiled=True)
    dw = lax.psum_scatter(dw.reshape(NI * 1920, 128), BATCH, scatter_dimension=0, tiled=True)

    gmix, pack, g1c, lat_gain = call(
        lat_backward_body,
        [((R, D), BF, "v"), ((D, 1024), BF, "v"), ((R, 128), BF, "v"), ((48, 128), F32, "v")],
        [(sc, "s"), (gkv, "v"), (lg, "v")] + [(v, "h") for v in (w, e, n_h, i_h, s_h, act_h, a_h, p_h)],
        [
            pltpu.VMEM((5,) + big, BF),
            pltpu.VMEM((4, R, D), BF),
            pltpu.VMEM((4, R, 128), F32),
            pltpu.VMEM((2, R, D), F32),
            pltpu.VMEM((8, R, D), BF),
            pltpu.VMEM((4, R, D), BF),
            pltpu.VMEM((H, R, R), BF),
            pltpu.VMEM((R, D), F32),
            pltpu.VMEM((R, D), F32),
            pltpu.VMEM((2, R, D), F32),
            pltpu.VMEM((R, D), BF),
            pltpu.VMEM((8, R, 256), BF),
            DMA((5, 2)),
            DMA((17,)),
        ],
        vmem=60,
        flops=8e10,
        name="lat_backward",
    )
    pack = lax.psum_scatter(pack, BATCH, scatter_dimension=0, tiled=True)
    gin, epay = call(
        enc_back_body,
        [((N, DI), F32, "v"), ((NJ, 640, 128), BF, "v")],
        [(sc, "s"), (xin, "v"), (bg, "v"), (lg, "v"), (gd, "v")]
        + [(v, "h") for v in (gmix, e, q_b, k_b, v_b, g_all, dw)],
        [
            pltpu.VMEM((R, D), BF),
            pltpu.VMEM((R, D + 128), BF),
            pltpu.VMEM((R, D), BF),
            pltpu.VMEM((N, D), BF),
            pltpu.VMEM((N, D), BF),
            pltpu.VMEM((NJ, 192, D), BF),
            pltpu.VMEM((R, D), F32),
            pltpu.VMEM((D, N), BF),
            pltpu.VMEM((D, N), BF),
            pltpu.VMEM((1920, 128), BF),
            pltpu.VMEM((DI, 256), F32),
            pltpu.VMEM((D, 128), F32),
            DMA((7,)),
        ],
        vmem=58,
        flops=3e9,
        name="enc_back",
    )
    r1 = exchange(epay, BLK)
    p2, dec_grad, bq_grad = call(
        tail_one_body,
        [((NI, 368, 128), BF, "v"), ((48, 160), F32, "v"), ((80, 96), F32, "v")],
        [(r1, "v"), (nf, "h"), (g_all, "h"), (lg, "v"), (lat_gain, "v"), (g1c, "v")],
        [pltpu.VMEM((NJ * N, DI), BF), pltpu.VMEM((NJ, 16, D), BF), pltpu.VMEM((256, 2048), BF), DMA((2,))],
        name="tail_one",
    )
    r2 = exchange(p2, BATCH)
    arr, lm, om, byte_grads, lat_gains, byte_gain = call(
        tail_two_body,
        [
            ((32, 80), F32, "v"),
            ((10, 160, 80), F32, "v"),
            ((2, 160, 80), F32, "v"),
            ((3, 80, 96), F32, "v"),
            ((5, D), F32, "v"),
            ((2, DI), F32, "v"),
        ],
        [(r2, "v"), (pack, "v"), (bq_grad, "v")],
        name="tail_two",
    )
    byte_grads = jnp.swapaxes(byte_grads, 1, 2)
    return (res[None], gin[None], gqin[None], arr, lm, om, byte_grads, dec_grad.T, lat_gains, byte_gain)


def solution(mesh):
    grid = Mesh(mesh.devices.reshape(4, 2, NX, NZ), AXES)
    return jax.shard_map(
        shards,
        mesh=grid,
        in_specs=(
            P(BATCH, BLK, None),
            P(BATCH, BLK, None),
            P(BATCH),
            P(BLK, None),
            P(None, BLK, None),
            P(None, BLK, None),
            P(None, BLK, None),
            P(BLK, None),
            P(),
            P(),
            P(BATCH, BLK, None),
        ),
        out_specs=(
            P(BATCH, BLK, None),
            P(BATCH, BLK, None),
            P(BATCH, BLK, None),
            P(BATCH, BLK),
            P(None, BATCH, BLK),
            P(None, BATCH, BLK),
            P(None, BATCH, BLK),
            P(BATCH, BLK),
            P(),
            P(),
        ),
        check_vma=False,
    )
```

```python
import jax
import jax.numpy as jnp
from jax import lax
from jax.experimental import pallas as pl
from jax.experimental.pallas import tpu as pltpu
from jax.sharding import Mesh, PartitionSpec as P

F32, BF = jnp.float32, jnp.bfloat16
D, DI, R, N, H, E = 1280, 768, 256, 128, 8, 160
NX, NZ, NJ, NI = 4, 4, 16, 8
SCALE = E**-0.5
EPS = 1e-5
MIB = 1 << 20
AXES = ("y", "core", "x", "z")
BATCH = ("y", "core")
BLK = ("x", "z")
WIN = [128 * (E * h // 128) for h in range(H)]
OFF = [E * h - WIN[h] for h in range(H)]
SQUARE = [("o", 0), ("l", 1), ("l", 2), ("l", 3), ("l", 4), ("l", 5), ("o", 1), ("l", 6), ("l", 7), ("l", 8), ("l", 9)]
ROWS_I = 128
DEC_ROW, BQ_ROW = 880, 960
PLACE = {9: (0, 0), 10: (0, 80), 8: (0, 160), 3: (1, 0), 4: (1, 80), 5: (1, 160), 7: (2, 0), 6: (2, 80), 2: (2, 160), 1: (3, 0), 0: (3, 80)}


def dot(a, b, ca=1, cb=0):
    return lax.dot_general(a, b, (((ca,), (cb,)), ((), ())), preferred_element_type=F32)


def dot_nt(a, b):
    return dot(a, b, 1, 1)


def dot_tn(a, b):
    return dot(a, b, 0, 0)


def half(v):
    return v.astype(BF)


def norm(v):
    c = v - jnp.mean(v, axis=-1, keepdims=True)
    inv = lax.rsqrt(jnp.mean(c * c, axis=-1, keepdims=True) + EPS)
    return c * inv, inv


def norm_back(g, gain, n, inv):
    gg = jnp.sum(g * n, axis=0, keepdims=True)
    inner = g * gain
    m1 = jnp.mean(inner, axis=-1, keepdims=True)
    m2 = jnp.mean(inner * n, axis=-1, keepdims=True)
    return inv * (inner - m1 - n * m2), gg


C0, C1 = 0.7978845608028654, 0.044715


def gelu(x):
    return 0.5 * x * (1.0 + jnp.tanh(C0 * (x + C1 * x * x * x)))


def gelu_slope(x):
    t = jnp.tanh(C0 * (x + C1 * x * x * x))
    return 0.5 * (1.0 + t) + 0.5 * x * (1.0 - t * t) * (C0 * (1.0 + 3.0 * C1 * x * x))


def lanes(width):
    return lax.broadcasted_iota(jnp.int32, (1, width), 1)


def head_mask(h):
    lane = lanes(256)
    return jnp.where((lane >= OFF[h]) & (lane < OFF[h] + E), 1.0, 0.0).astype(F32)


def pieces(row, count):
    out = []
    done = 0
    while done < count:
        i, r0 = divmod(row + done, ROWS_I)
        n = min(count - done, ROWS_I - r0)
        out.append((i, r0, done, n))
        done += n
    return out


def split3(v):
    hi = half(v).astype(F32)
    mid = half(v - hi).astype(F32)
    lo = half(v - hi - mid).astype(F32)
    return hi, mid, lo


def pack3(v):
    hi, mid, lo = split3(v)
    return half(hi + pltpu.roll(mid, 16, 1) + pltpu.roll(lo, 32, 1))


def unpack3(v, axis):
    return v + pltpu.roll(v, 112, axis) + pltpu.roll(v, 96, axis)


def as_rows(parts, count):
    row = lax.broadcasted_iota(jnp.int32, (count, 128), 0)
    out = jnp.zeros((count, 128), F32)
    for r, part in parts:
        out = jnp.where(row == r, part, out)
    return out


def call(body, outs, args, scratch=(), vmem=48, flops=0, name=None):
    spaces = {"v": pltpu.VMEM, "a": pl.ANY, "s": pltpu.SMEM, "h": pltpu.HBM}
    return pl.pallas_call(
        body,
        out_shape=[jax.ShapeDtypeStruct(s, t) for s, t, _ in outs],
        in_specs=[pl.BlockSpec(memory_space=spaces[m]) for _, m in args],
        out_specs=[pl.BlockSpec(memory_space=spaces[m]) for _, _, m in outs],
        scratch_shapes=list(scratch),
        compiler_params=pltpu.CompilerParams(vmem_limit_bytes=vmem * MIB),
        cost_estimate=pl.CostEstimate(flops=int(flops), bytes_accessed=4 * MIB, transcendentals=0),
        name=name,
    )(*[a for a, _ in args])


DMA = pltpu.SemaphoreType.DMA


def pack_body(sc, lm, om, bm, do, la, g0, wsh, buf, sem):
    i, core = sc[0], sc[4]
    cols = pl.ds(pl.multiple_of(core * 640, 128), 640)
    first = [
        (bm.at[0, :, cols], g0.at[0:48, :]),
        (bm.at[1, :, cols], g0.at[48:96, :]),
        (lm.at[0, :, cols], g0.at[96:176, :]),
        (la.at[:, cols], g0.at[176:192, :]),
    ]
    first = [pltpu.make_async_copy(a, b, sem.at[8 + k]) for k, (a, b) in enumerate(first)]
    for c in first:
        c.start()
    blocks = [(80 * k, 80, (om if s == "o" else lm), n, D) for k, (s, n) in enumerate(SQUARE)]
    blocks += [(DEC_ROW, 80, do, None, DI), (BQ_ROW, 48, bm, 2, D)]
    for k in range(NI):
        lo, hi = ROWS_I * k, ROWS_I * (k + 1)

        @pl.when(i == k)
        def _(lo=lo, hi=hi):
            cs = []
            for row, count, ref, n, width in blocks:
                a, b = max(lo, row), min(hi, row + count)
                if a < b:
                    src = ref.at[a - row : b - row, :] if n is None else ref.at[n, a - row : b - row, :]
                    dst = buf.at[a - lo : b - lo, :] if width == D else buf.at[a - lo : b - lo, 0:width]
                    cs.append(pltpu.make_async_copy(src, dst, sem.at[len(cs)]))
            for c in cs:
                c.start()
            for c in cs:
                c.wait()

    out = pltpu.make_async_copy(buf, wsh, sem.at[12])
    out.start()
    for c in first:
        c.wait()
    out.wait()


def pieces_from(sc, groups):
    x, z, core = sc[2], sc[3], sc[4]
    out = []
    for side in range(2):
        c = core if side == 0 else 1 - core
        col = pl.ds(pl.multiple_of(c * 640, 128), 640)
        for e in range(4):
            for d in range(4):
                xs = jnp.where(c == 0, (x + 4 - d) & 3, (x + 4 - e) & 3)
                zs = jnp.where(c == 0, (z + 4 - e) & 3, (z + 4 - d) & 3)
                out.append((xs * 4 + zs, col, groups[4 * side + e].at[d]))
    return out


def enc_body(sc, t0, t1, t2, t3, u0, u1, u2, u3, x_in, bg, lg, g_out, nb_o, k_o, v_o, q_o, pay, gs, acc, sem):
    copies = [
        pltpu.make_async_copy(src, gs.at[pos, :, col], sem.at[k])
        for k, (pos, col, src) in enumerate(pieces_from(sc, (t0, t1, t2, t3, u0, u1, u2, u3)))
    ]
    for c in copies:
        c.start()
    n_in, _ = norm(x_in[...].astype(F32))
    nb = half(n_in * bg[0:1, :])
    nb_o[...] = nb
    for c in copies:
        c.wait()
    save = pltpu.make_async_copy(gs, g_out, sem.at[32])
    save.start()
    k_o[...] = half(dot(nb, gs[:, 0:48, :].reshape(DI, D)))
    v_o[...] = half(dot(nb, gs[:, 48:96, :].reshape(DI, D)))
    z0b = gs[:, 176:192, :].reshape(R, D)
    nq, _ = norm(z0b.astype(F32))
    q_o[...] = half(dot(half(nq * lg[0:1, :]), gs[:, 96:176, :].reshape(D, D)))
    acc[...] = jnp.zeros_like(acc)
    valid = lanes(N) + sc[1] * N < sc[5]
    lane = lanes(128)
    stats = jnp.zeros((R, 128), F32)
    for h in range(H):
        w = slice(WIN[h], WIN[h] + 256)
        mk = head_mask(h)
        s = dot_nt(q_o[:, w] * half(mk), k_o[:, w]) * SCALE
        s = jnp.where(valid, s, -1e30)
        m = jnp.max(s, axis=-1, keepdims=True)
        p = jnp.exp(s - m)
        acc[:, w] += dot(half(p), v_o[:, w]) * mk
        stats = jnp.where(lane == h, m, stats)
        stats = jnp.where(lane == 8 + h, jnp.sum(p, axis=-1, keepdims=True), stats)
    pay[:, 0:D] = half(acc[...])
    pay[:, D : D + 128] = pack3(stats)
    save.wait()


def combine_body(rcv, out):
    st = unpack3(rcv[:, :, D : D + 128].astype(F32), 2)
    peak = jnp.max(st, axis=0, keepdims=True)
    w = jnp.exp(st - peak)
    total = jnp.sum(w * pltpu.roll(st, 120, 2), axis=0, keepdims=True)
    coef = w / total
    lane = lax.broadcasted_iota(jnp.int32, (1, 1, 128), 2)
    for t in range(10):
        h0, h1 = 128 * t // E, (128 * t + 127) // E
        c = coef[:, :, h0 : h0 + 1]
        if h1 != h0:
            c = jnp.where(lane >= E * h1 - 128 * t, coef[:, :, h1 : h1 + 1], c)
        o = jnp.sum(rcv[:, :, 128 * t : 128 * t + 128].astype(F32) * c, axis=0)
        out[:, 128 * t : 128 * t + 128] = half(o)
    lse = jnp.where(lanes(128) < 8, (peak + jnp.log(total))[0], 0.0)
    out[:, D : D + 128] = pack3(lse)


class Ring:
    def __init__(self, w, slots, sem, order):
        self.w, self.slots, self.sem, self.order = w, slots, sem, order
        self.n = slots.shape[0]
        self.pos = {m: k for k, m in enumerate(order)}

    def copies(self, m):
        s = self.pos[m] % self.n
        return [
            pltpu.make_async_copy(
                self.w.at[i, :, r0 : r0 + n, :], self.slots.at[s, :, d0 : d0 + n, :], self.sem.at[s, k]
            )
            for k, (i, r0, d0, n) in enumerate(pieces(80 * m, 80))
        ]

    def start(self, m):
        for c in self.copies(m):
            c.start()

    def begin(self):
        for m in self.order[: self.n]:
            self.start(m)

    def get(self, m):
        for c in self.copies(m):
            c.wait()
        return self.slots[self.pos[m] % self.n].reshape(D, D)

    def done(self, m):
        k = self.pos[m] + self.n
        if k < len(self.order):
            self.start(self.order[k])


def forward_body(
    qin, cot, bg, lg, e_h, g_all, w,
    res, gqin, gain_o, pay, mix_o, nd_o, gq_o, z_h, h_h, a_h,
    slots, e, z0b, zs, zb, hs, qs, acc, kd, vd, dec, bq, dacc, gq, gkv, wsem, ssem, lsem,
):
    first = [
        pltpu.make_async_copy(e_h.at[:, 0:D], e, lsem.at[3]),
        pltpu.make_async_copy(g_all.at[:, 176:192, :], z0b, lsem.at[4]),
    ]
    for c in first:
        c.start()
    ring = Ring(w, slots, wsem, list(range(11)))
    ring.begin()
    copies = []
    for i, r0, d0, n in pieces(BQ_ROW, 48):
        copies.append(pltpu.make_async_copy(w.at[i, :, r0 : r0 + n, :], bq.at[:, d0 : d0 + n, :], lsem.at[0]))
    for i, r0, d0, n in pieces(DEC_ROW, 80):
        copies.append(
            pltpu.make_async_copy(w.at[i, :, r0 : r0 + n, 0:DI], dec.at[:, d0 : d0 + n, :], lsem.at[len(copies)])
        )
    for c in copies:
        c.start()
    saves = []

    def save(src, dst):
        c = pltpu.make_async_copy(src, dst, ssem.at[len(saves)])
        c.start()
        saves.append(c)

    def keep(k):
        zb[k] = half(zs[k])
        save(zb.at[k], z_h.at[k])

    def mul(a, m):
        out = dot(a, ring.get(m))
        ring.done(m)
        return out

    for c in first:
        c.wait()
    z1 = z0b[...].reshape(R, D).astype(F32) + mul(e[...], 0)
    zs[0] = z1
    keep(0)
    h1 = mul(half(norm(z1)[0] * lg[1:2, :]), 1)
    hs[0] = half(h1)
    save(hs.at[0], h_h.at[0])
    zs[1] = zs[0] + mul(half(gelu(h1)), 2)
    keep(1)
    s_b = half(norm(zs[1])[0] * lg[2:3, :])
    for k in range(3):
        qs[k] = half(mul(s_b, 3 + k))
        save(qs.at[k], a_h.at[k])
    acc[...] = jnp.zeros_like(acc)
    for h in range(H):
        win = slice(WIN[h], WIN[h] + 256)
        mk = head_mask(h)
        s = dot_nt(qs[0, :, win] * half(mk), qs[1, :, win]) * SCALE
        p = jnp.exp(s - jnp.max(s, axis=-1, keepdims=True))
        p = p / jnp.sum(p, axis=-1, keepdims=True)
        acc[:, win] += dot(half(p), qs[2, :, win]) * mk
    qs[3] = half(acc[...])
    save(qs.at[3], a_h.at[3])
    zs[2] = zs[1] + mul(qs[3], 6)
    keep(2)
    h2 = mul(half(norm(zs[2])[0] * lg[3:4, :]), 7)
    hs[1] = half(h2)
    save(hs.at[1], h_h.at[1])
    zs[3] = zs[2] + mul(half(gelu(h2)), 8)
    keep(3)
    c_b = half(norm(zs[3])[0] * lg[4:5, :])
    kd[...] = half(mul(c_b, 9))
    vd[...] = half(mul(c_b, 10))

    x = qin[...].astype(F32)
    n, inv = norm(x)
    nd = half(n * bg[1:2, :])
    nd_o[...] = nd
    for c in copies:
        c.wait()
    wq = bq[...].reshape(DI, D)
    wd = dec[...].reshape(D, DI)
    gq_o[...] = half(dot(nd, wq))
    mix_o[...] = half(dot_nt(cot[...], wd))
    dacc[...] = jnp.zeros_like(dacc)
    gq[...] = jnp.zeros_like(gq)
    gkv[...] = jnp.zeros_like(gkv)
    for h in range(H):
        win = slice(WIN[h], WIN[h] + 256)
        mk = head_mask(h)
        mkb = half(mk)
        qw, gw, kw, vw = gq_o[:, win], mix_o[:, win], kd[:, win], vd[:, win]
        s = dot_nt(qw * mkb, kw) * SCALE
        p = jnp.exp(s - jnp.max(s, axis=-1, keepdims=True))
        p = p / jnp.sum(p, axis=-1, keepdims=True)
        pb = half(p)
        dacc[:, win] += dot(pb, vw) * mk
        dp = dot_nt(gw * mkb, vw)
        ds = half(p * (dp - jnp.sum(p * dp, axis=-1, keepdims=True)))
        gq[:, win] += dot(ds, kw) * mk
        gkv[0, :, win] += dot_tn(ds, qw) * mk
        gkv[1, :, win] += dot_tn(pb, gw) * mk
    pay[:, 0:D] = half(gkv[0] * SCALE)
    pay[:, D : 2 * D] = half(gkv[1])
    mix = half(dacc[...])
    mix_o[...] = mix
    res[...] = half(x + dot(mix, wd))
    gqb = half(gq[...] * SCALE)
    gq_o[...] = gqb
    gin, gg = norm_back(dot_nt(gqb, wq), bg[1:2, :], n, inv)
    gqin[...] = cot[...].astype(F32) + gin
    gain_o[...] = gg
    for c in saves:
        c.wait()


def prepare_body(lg, z_h, h_h, a_h, n_h, i_h, s_h, act_h, p_h, zs, hs, qs, ns, vs, ss, acts, ps, sem, osem):
    loads = {}
    for k in range(4):
        loads["z", k] = pltpu.make_async_copy(z_h.at[k], zs.at[k], sem.at[k])
    for k in range(2):
        loads["h", k] = pltpu.make_async_copy(h_h.at[k], hs.at[k], sem.at[4 + k])
    loads["q"] = pltpu.make_async_copy(a_h.at[0:2], qs, sem.at[6])
    for c in loads.values():
        c.start()
    saves = []

    def save(src, dst):
        c = pltpu.make_async_copy(src, dst, osem.at[len(saves)])
        c.start()
        saves.append(c)

    for k, a in ((3, 0), (2, 2), (1, 1), (0, 4)):
        loads["z", k].wait()
        n, inv = norm(zs[k].astype(F32))
        ns[k] = half(n)
        save(ns.at[k], n_h.at[k])
        vs[k] = jnp.broadcast_to(inv, (R, 128))
        acts[a] = half(n * lg[k + 1 : k + 2, :])
        save(acts.at[a], act_h.at[a])
    save(vs, i_h)
    for k, a in ((1, 3), (0, 5)):
        loads["h", k].wait()
        x = hs[k].astype(F32)
        t = jnp.tanh(C0 * (x + C1 * x * x * x))
        acts[a] = half(0.5 * x * (1.0 + t))
        save(acts.at[a], act_h.at[a])
        ss[k] = 0.5 * (1.0 + t) + 0.5 * x * (1.0 - t * t) * (C0 * (1.0 + 3.0 * C1 * x * x))
        save(ss.at[k], s_h.at[k])
    loads["q"].wait()
    for h in range(H):
        win = slice(WIN[h], WIN[h] + 256)
        s = dot_nt(qs[0, :, win] * half(head_mask(h)), qs[1, :, win]) * SCALE
        p = jnp.exp(s - jnp.max(s, axis=-1, keepdims=True))
        ps[h] = half(p / jnp.sum(p, axis=-1, keepdims=True))
    save(ps, p_h)
    for c in saves:
        c.wait()


def lat_backward_body(
    sc, gin, lg, w, e_h, n_h, i_h, s_h, act_h, a_h, p_h, gmix, pack_o, g1c_o, gains_o,
    slots, ns, vs, ss, acts, qs, ps, acc, acc2, acc3, gh, gw, wsem, lsem,
):
    order = [8, 7, 6, 3, 4, 5, 2, 1, 0]
    ring = Ring(w, slots, wsem, order)
    todo = [
        (i_h, vs),
        (act_h.at[0], acts.at[0]),
        (s_h.at[1], ss.at[1]),
        (act_h.at[3], acts.at[1]),
        (n_h.at[2], ns.at[2]),
        (act_h.at[2], acts.at[3]),
        (a_h.at[3], acts.at[4]),
        (p_h, ps),
        (a_h.at[0:3], qs.at[0:3]),
        (n_h.at[1], ns.at[1]),
        (act_h.at[1], acts.at[2]),
        (s_h.at[0], ss.at[0]),
        (act_h.at[5], acts.at[5]),
        (n_h.at[0], ns.at[0]),
        (act_h.at[4], acts.at[6]),
        (e_h.at[:, 0:D], acts.at[7]),
    ]
    loads = [pltpu.make_async_copy(a, b, lsem.at[k]) for k, (a, b) in enumerate(todo)]
    after = {8: (4, 5, 6), 7: (7, 8), 6: (9, 10, 11, 12), 3: (13, 14, 15)}
    ring.start(8)
    for c in loads[:4]:
        c.start()
    for m in order[1 : ring.n]:
        ring.start(m)

    def ready(*ks):
        for k in ks:
            loads[k].wait()

    src = sc[1] * 80
    start = pl.multiple_of(jnp.minimum((src >> 7) * 128, 1024), 128)
    offset = src - start
    lane = lanes(256)

    def put(ref, to):
        v = pltpu.roll(ref[:, pl.ds(start, 256)].astype(F32), (to - offset + 256) & 255, 1)
        return jnp.where((lane >= to) & (lane < to + 80), v, 0.0)

    def weight_grad(window, first, count):
        a = acts[first : first + count].reshape(count * R, D)
        pack_o[:, 256 * window : 256 * window + 256] = half(dot_tn(a, gw[first : first + count].reshape(count * R, 256)))

    def mul(g_b, m):
        out = dot_nt(g_b, ring.get(m))
        ring.done(m)
        for k in after.get(m, ()):
            loads[k].start()
        return out

    gain_rows = []

    def back(g, k):
        out, gg = norm_back(g, lg[k + 1 : k + 2, :], ns[k].astype(F32), vs[k][:, 0:1])
        for t in range(10):
            gain_rows.append((10 * k + t, gg[:, 128 * t : 128 * t + 128]))
        return out

    for t in range(10):
        acc[:, 128 * t : 128 * t + 128] = gin[:, 16 * t : 16 * t + 16, :].reshape(R, 128).astype(F32)
    tile = lanes(128)
    values = pltpu.roll(gin[:, 176:192, :].reshape(R, 128).astype(F32), 80, 1)
    gw[0, :, 0:128] = half(jnp.where(tile < 80, gin[:, 160:176, :].reshape(R, 128).astype(F32), values))
    gw[0, :, 128:256] = half(jnp.where(tile < 32, values, 0.0))
    gw[1] = half(put(acc, 160))
    ready(0, 1, 2, 3)
    gh[...] = half(mul(half(acc[...]), 8) * ss[1])
    weight_grad(0, 0, 2)
    ready(4)
    gw[3] = half(put(gh, 0))
    acc[...] += back(mul(gh[...], 7), 2)
    gw[4] = half(put(acc, 80))
    qs[3] = half(mul(half(acc[...]), 6))
    acc2[...] = jnp.zeros_like(acc2)
    acc3[...] = jnp.zeros_like(acc3)
    ready(5, 6, 7, 8)
    for h in range(H):
        win = slice(WIN[h], WIN[h] + 256)
        mk = head_mask(h)
        pb = ps[h]
        p = pb.astype(F32)
        dp = dot_nt(qs[3, :, win] * half(mk), qs[2, :, win])
        ds = half(p * (dp - jnp.sum(p * dp, axis=-1, keepdims=True)) * SCALE)
        acc2[:, win] += dot(ds, qs[1, :, win]) * mk
        acc3[0, :, win] += dot_tn(ds, qs[0, :, win]) * mk
        acc3[1, :, win] += dot_tn(pb, qs[3, :, win]) * mk
    gw[2] = half(put(acc2, 0) + put(acc3.at[0], 80) + put(acc3.at[1], 160))
    gn = mul(half(acc2[...]), 3)
    gn = gn + mul(half(acc3[0]), 4)
    gn = gn + mul(half(acc3[1]), 5)
    ready(9, 10)
    weight_grad(1, 2, 1)
    acc[...] += back(gn, 1)
    gw[5] = half(put(acc, 160))
    ready(11, 12)
    gh[...] = half(mul(half(acc[...]), 2) * ss[0])
    weight_grad(2, 3, 3)
    gw[6] = half(put(gh, 0))
    ready(13, 14, 15)
    acc[...] += back(mul(gh[...], 1), 0)
    gw[7] = half(put(acc, 80))
    g1c_o[...] = half(put(acc, 0)[:, 0:128])
    gmix[...] = half(mul(half(acc[...]), 0))
    weight_grad(3, 6, 2)
    gains_o[...] = as_rows(gain_rows, 32)


def key_value_back_body(sc, rcv, lg, n_h, i_h, w, out, gain_o, wbuf, nbuf, ibuf, sem):
    rows = pl.ds(pl.multiple_of(sc[1] * 16, 16), 16)
    copies = []
    for k, m in enumerate((9, 10)):
        for i, r0, d0, n in pieces(80 * m, 80):
            copies.append((w.at[i, :, r0 : r0 + n, :], wbuf.at[k, :, d0 : d0 + n, :]))
    copies += [(n_h.at[3, rows, :], nbuf), (i_h.at[3, rows, :], ibuf)]
    copies = [pltpu.make_async_copy(a, b, sem.at[k]) for k, (a, b) in enumerate(copies)]
    for c in copies:
        c.start()
    s = half(jnp.sum(rcv[...].astype(F32), axis=0))
    for j in range(NJ):
        base = min(128 * (80 * j // 128), 1024)
        for k in range(2):
            v = s[:, D * k + base : D * k + base + 256].astype(F32)
            if 80 * j > base:
                v = pltpu.roll(v, 256 - (80 * j - base), 1)
            out[j, 160 + 16 * k : 176 + 16 * k, :] = half(v[:, 0:128])
    for c in copies:
        c.wait()
    gn = dot_nt(s[:, 0:D], wbuf[0].reshape(D, D)) + dot_nt(s[:, D : 2 * D], wbuf[1].reshape(D, D))
    g, gg = norm_back(gn, lg[4:5, :], nbuf[...].astype(F32), ibuf[:, 0:1])
    gain_o[...] = gg
    g = jnp.concatenate([half(g[:, 128 * t : 128 * t + 128]) for t in range(10)], axis=0)
    for j in range(NJ):
        out[j, 0:160, :] = g


def dec_weights_body(mix, cot, nd, gq, out, buf, sem):
    g = half(dot_tn(mix[...], cot[...]))
    for i in range(NI):
        for t in range(6):
            buf[i, 160 * t : 160 * t + 160, :] = g[160 * i : 160 * i + 160, 128 * t : 128 * t + 128]
    one = pltpu.make_async_copy(buf.at[:, 0:960, :], out.at[:, 0:960, :], sem.at[0])
    one.start()
    g = half(dot_tn(nd[...], gq[...]))
    for i in range(NI):
        for t in range(10):
            r = 960 + 96 * t
            buf[i, r : r + 96, :] = g[96 * i : 96 * i + 96, 128 * t : 128 * t + 128]
    two = pltpu.make_async_copy(buf.at[:, 960:1920, :], out.at[:, 960:1920, :], sem.at[1])
    two.start()
    one.wait()
    two.wait()


def spread(chunk, pay, td, tb):
    fill = jnp.zeros((96, 128), F32)
    for t in range(6):
        v = jnp.concatenate([chunk[160 * t : 160 * t + 160, :].astype(F32), fill], axis=0)
        td[128 * t : 128 * t + 128, :] = v.T
    fill = jnp.zeros((32, 128), F32)
    for t in range(10):
        v = jnp.concatenate([chunk[960 + 96 * t : 960 + 96 * t + 96, :].astype(F32), fill], axis=0)
        tb[128 * t : 128 * t + 128, :] = v.T
    for j in range(NJ):
        tail = pltpu.roll(td[48 * j : 48 * j + 48, 128:256], 96, 1)
        pay[j, 512:560, :] = half(tb[80 * j : 80 * j + 48, :] + tail)
        pay[j, 560:592, :] = half(tb[80 * j + 48 : 80 * j + 80, :])
        pay[j, 592:640, :] = half(td[48 * j : 48 * j + 48, 0:128])


def enc_back_body(
    sc, x_in, bg, lg, gd, gc, gmix_h, e_h, q_h, k_h, v_h, g_all, dw_h, gin_o, pay,
    gmix, e, q, k, v, wkv, gq, gkt, gvt, dw, td, tb, sem,
):
    pairs = [(gmix_h, gmix), (q_h, q), (k_h, k), (v_h, v), (e_h, e), (g_all, wkv), (dw_h, dw)]
    loads = [pltpu.make_async_copy(a, b, sem.at[n]) for n, (a, b) in enumerate(pairs)]
    for c in loads:
        c.start()
    for c in loads[:5]:
        c.wait()
    lse = unpack3(e[:, D : D + 128].astype(F32), 1)
    valid = lanes(N) + sc[1] * N < sc[5]
    gq[...] = jnp.zeros_like(gq)
    for h in range(H):
        win = slice(WIN[h], WIN[h] + 256)
        mk = head_mask(h)
        mkb = half(mk)
        qw, gw, kw, vw = q[:, win], gmix[:, win], k[:, win], v[:, win]
        rd = jnp.sum(gw.astype(F32) * e[:, win].astype(F32) * mk, axis=-1, keepdims=True)
        s = dot_nt(qw * mkb, kw) * SCALE
        p = jnp.where(valid, jnp.exp(jnp.where(valid, s, -1e30) - lse[:, h : h + 1]), 0.0)
        dp = dot_nt(gw * mkb, vw)
        ds = half(p * (dp - rd))
        gq[:, win] += dot(ds, kw) * mk
        o = OFF[h]
        gkt[E * h : E * h + E, :] = half(dot_tn(qw, ds)[o : o + E, :] * SCALE)
        gvt[E * h : E * h + E, :] = half(dot_tn(gw, half(p))[o : o + E, :])
    pay[:, 320:400, :] = gkt[...].reshape(NJ, 80, 128)
    pay[:, 400:480, :] = gvt[...].reshape(NJ, 80, 128)
    loads[5].wait()
    gqs = gq[...] * SCALE
    gqt = half(gqs.T)
    pay[:, 160:240, :] = gqt[:, 0:128].reshape(NJ, 80, 128)
    pay[:, 240:320, :] = gqt[:, 128:256].reshape(NJ, 80, 128)
    n, inv = norm(wkv[:, 176:192, :].reshape(R, D).astype(F32))
    gz, g0 = norm_back(dot_nt(half(gqs), wkv[:, 96:176, :].reshape(D, D)), lg[0:1, :], n, inv)
    gzt = half(gz.T)
    pay[:, 0:80, :] = gzt[:, 0:128].reshape(NJ, 80, 128)
    pay[:, 80:160, :] = gzt[:, 128:256].reshape(NJ, 80, 128)
    n, inv = norm(x_in[...].astype(F32))
    gnt = dot(wkv[:, 0:48, :].reshape(DI, D), gkt[...]) + dot(wkv[:, 48:96, :].reshape(DI, D), gvt[...])
    gin, gg = norm_back(gnt.T, bg[0:1, :], n, inv)
    gin_o[...] = gin
    rows = [(t, gg[:, 128 * t : 128 * t + 128]) for t in range(6)]
    rows += [(6 + t, gd[:, 128 * t : 128 * t + 128]) for t in range(6)]
    rows += [(12 + t, g0[:, 128 * t : 128 * t + 128]) for t in range(10)]
    rows += [(22 + t, gc[:, 128 * t : 128 * t + 128]) for t in range(10)]
    g = half(as_rows(rows, 32))
    for j in range(NJ):
        pay[j, 480:512, :] = g
    loads[6].wait()
    spread(dw, pay, td, tb)


def tail_one_body(rcv, nf_h, g_all, lg, lat_gain, g1c, out, dec_o, bq_o, nf, z0b, left, sem):
    loads = [
        pltpu.make_async_copy(nf_h, nf, sem.at[0]),
        pltpu.make_async_copy(g_all.at[:, 176:192, :], z0b, sem.at[1]),
    ]
    for c in loads:
        c.start()
    sums = jnp.sum(rcv[:, 0:320, :].astype(F32), axis=0)
    fill = jnp.zeros((48, 128), F32)
    left[...] = jnp.zeros_like(left)
    for s in range(NJ):
        left[0:80, 128 * s : 128 * s + 128] = rcv[s, 320:400, :]
        left[128:208, 128 * s : 128 * s + 128] = rcv[s, 400:480, :]
    loads[1].wait()
    nq = half(norm(z0b[...].reshape(R, D).astype(F32))[0] * lg[0:1, :])
    a = jnp.concatenate([sums[160:240], fill], axis=0).T
    b = jnp.concatenate([sums[240:320], fill], axis=0).T
    w0 = dot_tn(nq, half(jnp.concatenate([a, b], axis=0)))
    a = jnp.concatenate([sums[0:80], fill], axis=0).T
    b = jnp.concatenate([sums[80:160], fill], axis=0).T
    gz = half(jnp.concatenate([a, b], axis=0) + g1c[...].astype(F32))
    gains = jnp.sum(rcv[:, 480:512, :].astype(F32), axis=0)
    gains = half(jnp.concatenate([gains, lat_gain[...]], axis=0))
    loads[0].wait()
    wt = dot(left[...], nf[...]).T
    lane = lanes(128)
    key, value = wt[:, 0:128], wt[:, 128:256]
    one = half(jnp.where(lane < 80, key, pltpu.roll(value, 80, 1)))
    other = pltpu.roll(value, 32, 1)
    for i in range(NI):
        r = 96 * i
        beside = jnp.concatenate([other[r : r + 96, :], jnp.zeros((64, 128), F32)], axis=0)
        out[i, 0:160, :] = half(jnp.where(lane < 80, w0[160 * i : 160 * i + 160, :], beside))
        out[i, 160:192, :] = gz[32 * i : 32 * i + 32, :]
        out[i, 192:288, :] = one[r : r + 96, :]
        out[i, 288:352, :] = gains
    s = jnp.sum(rcv[:, 512:640, :].astype(F32), axis=0)
    bq_o[...] = s[0:80, 0:96]
    dec_o[:, 0:128] = s[80:128]
    dec_o[:, 128:160] = pltpu.roll(s[0:48], 32, 1)[:, 0:32]


def tail_two_body(rcv, pack, bq, arr_o, lm_o, om_o, bm_o, lat_o, byte_o):
    sums = jnp.sum(rcv[...].astype(F32), axis=0)
    lm_o[0] = sums[0:160, 0:80]
    arr_o[...] = sums[160:192, 0:80]
    lane = lanes(128)
    value = jnp.where(lane < 48, pltpu.roll(sums[192:288], 48, 1), pltpu.roll(sums[0:96], 96, 1))
    fill = jnp.zeros((32, 128), F32)
    bm_o[0] = jnp.concatenate([sums[192:288], fill], axis=0).T[0:80, 0:96]
    bm_o[1] = jnp.concatenate([value, fill], axis=0).T[0:80, 0:96]
    bm_o[2] = bq[...]
    g = sums[288:352]
    for t in range(6):
        for b in range(2):
            byte_o[b : b + 1, 128 * t : 128 * t + 128] = g[6 * b + t : 6 * b + t + 1, :]
    for t in range(10):
        for b in range(5):
            r = {0: 12, 1: 32, 2: 42, 3: 52, 4: 22}[b] + t
            lat_o[b : b + 1, 128 * t : 128 * t + 128] = g[r : r + 1, :]
    for m, (kind, n) in enumerate(SQUARE):
        window, o = PLACE[m]
        v = pack[:, 256 * window : 256 * window + 256].astype(F32)
        if o:
            v = pltpu.roll(v, 256 - o, 1)
        if kind == "l":
            lm_o[n] = v[:, 0:80]
        else:
            om_o[n] = v[:, 0:80]


def line(y, c, x, z):
    return ((y % 4) * 2 + c) * NJ + (x % 4) * NZ + (z % 4)


EVERY = [(y, c, x, z) for y in range(4) for c in range(2) for x in range(NX) for z in range(NZ)]


def along(stage, d):
    out = []
    for y, c, x, z in EVERY:
        on_x = (c == 0) == (stage == 0)
        out.append((line(y, c, x, z), line(y, c, x + d, z) if on_x else line(y, c, x, z + d)))
    return out


SWAP = [(line(y, c, x, z), line(y, 1 - c, x, z)) for y, c, x, z in EVERY]


def exchange(v, axes):
    flat = v.reshape(v.shape[0] * v.shape[1], v.shape[2])
    return lax.all_to_all(flat, axes, split_axis=0, concat_axis=0, tiled=True).reshape(v.shape)


def shards(inputs, queries, lengths, latent_array, latent_mats, out_mats, byte_mats, dec_out, lg, bg, cotangent):
    y, core, x, z = (lax.axis_index(a) for a in AXES)
    i, j = y * 2 + core, x * NZ + z
    sc = jnp.stack([i, j, x, z, core, lengths[0]]).astype(jnp.int32)
    xin, qin, cot = inputs[0], queries[0], cotangent[0]

    g0, wsh = call(
        pack_body,
        [((192, 640), BF, "v"), ((ROWS_I, D), BF, "h")],
        [(sc, "s"), (latent_mats, "h"), (out_mats, "h"), (byte_mats, "h"), (dec_out, "h"), (latent_array, "h")],
        [pltpu.VMEM((ROWS_I, D), BF), DMA((13,))],
        vmem=60,
        name="pack",
    )
    w = lax.all_gather(wsh, AXES, axis=0, tiled=True).reshape(NI, NJ, ROWS_I, D)

    def step(v, stage):
        return [lax.ppermute(v, AXES, along(stage, d)) for d in (1, 2, 3)]

    s0 = jnp.stack([g0] + step(g0, 0))
    own = [s0] + step(s0, 1)
    sib = [lax.ppermute(v, AXES, SWAP) for v in own]
    g_all, nb, k_b, v_b, q_b, pay = call(
        enc_body,
        [
            ((NJ, 192, D), BF, "h"),
            ((N, DI), BF, "v"),
            ((N, D), BF, "v"),
            ((N, D), BF, "v"),
            ((R, D), BF, "v"),
            ((R, D + 128), BF, "v"),
        ],
        [(sc, "s")] + [(v, "a") for v in own + sib] + [(xin, "v"), (bg, "v"), (lg, "v")],
        [pltpu.VMEM((NJ, 192, D), BF), pltpu.VMEM((R, D), F32), DMA((33,))],
        vmem=60,
        flops=3e9,
        name="enc",
    )
    rcv = exchange(pay.reshape(NJ, 16, D + 128), BLK)
    (mine,) = call(combine_body, [((16, D + 128), BF, "v")], [(rcv, "v")], name="combine")
    e = lax.all_gather(mine, BLK, axis=0, tiled=True)

    big = (NJ, 80, D)
    res, gqin, gd, dpay, mix, nd, gq, z_h, h_h, a_h = call(
        forward_body,
        [
            ((N, DI), BF, "v"),
            ((N, DI), F32, "v"),
            ((1, DI), F32, "v"),
            ((R, 2 * D), BF, "v"),
            ((N, D), BF, "v"),
            ((N, DI), BF, "v"),
            ((N, D), BF, "v"),
            ((4, R, D), BF, "h"),
            ((2, R, D), BF, "h"),
            ((4, R, D), BF, "h"),
        ],
        [(qin, "v"), (cot, "v"), (bg, "v"), (lg, "v"), (e, "h"), (g_all, "h"), (w, "h")],
        [
            pltpu.VMEM((4,) + big, BF),
            pltpu.VMEM((R, D), BF),
            pltpu.VMEM((NJ, 16, D), BF),
            pltpu.VMEM((4, R, D), F32),
            pltpu.VMEM((4, R, D), BF),
            pltpu.VMEM((2, R, D), BF),
            pltpu.VMEM((4, R, D), BF),
            pltpu.VMEM((R, D), F32),
            pltpu.VMEM((R, D), BF),
            pltpu.VMEM((R, D), BF),
            pltpu.VMEM((NJ, 80, DI), BF),
            pltpu.VMEM((NJ, 48, D), BF),
            pltpu.VMEM((N, D), F32),
            pltpu.VMEM((N, D), F32),
            pltpu.VMEM((2, R, D), F32),
            DMA((4, 2)),
            DMA((10,)),
            DMA((5,)),
        ],
        vmem=54,
        flops=1.5e10,
        name="forward",
    )
    rows = exchange(dpay.reshape(NJ, 16, 2 * D), BLK)
    n_h, i_h, s_h, act_h, p_h = call(
        prepare_body,
        [
            ((4, R, D), BF, "h"),
            ((4, R, 128), F32, "h"),
            ((2, R, D), F32, "h"),
            ((6, R, D), BF, "h"),
            ((H, R, R), BF, "h"),
        ],
        [(lg, "v"), (z_h, "h"), (h_h, "h"), (a_h, "h")],
        [
            pltpu.VMEM((4, R, D), BF),
            pltpu.VMEM((2, R, D), BF),
            pltpu.VMEM((2, R, D), BF),
            pltpu.VMEM((4, R, D), BF),
            pltpu.VMEM((4, R, 128), F32),
            pltpu.VMEM((2, R, D), F32),
            pltpu.VMEM((6, R, D), BF),
            pltpu.VMEM((H, R, R), BF),
            DMA((7,)),
            DMA((14,)),
        ],
        vmem=58,
        flops=5e9,
        name="prepare",
    )
    (dw,) = call(
        dec_weights_body,
        [((NI, 1920, 128), BF, "h")],
        [(mix, "v"), (cot, "v"), (nd, "v"), (gq, "v")],
        [pltpu.VMEM((NI, 1920, 128), BF), DMA((2,))],
        vmem=60,
        flops=4e9,
        name="dec_weights",
    )
    kv, gc = call(
        key_value_back_body,
        [((NJ, 192, 128), BF, "v"), ((1, D), F32, "v")],
        [(sc, "s"), (rows, "v"), (lg, "v"), (n_h, "h"), (i_h, "h"), (w, "h")],
        [pltpu.VMEM((2,) + big, BF), pltpu.VMEM((16, D), BF), pltpu.VMEM((16, 128), F32), DMA((6,))],
        vmem=58,
        flops=1e8,
        name="key_value_back",
    )
    gin4 = exchange(kv, BLK)
    nb, _ = lax.optimization_barrier((nb, gin4))
    nf = lax.all_gather(nb, BLK, axis=0, tiled=True)
    dw = lax.psum_scatter(dw.reshape(NI * 1920, 128), BATCH, scatter_dimension=0, tiled=True)

    gmix, pack, g1c, lat_gain = call(
        lat_backward_body,
        [((R, D), BF, "v"), ((D, 1024), BF, "v"), ((R, 128), BF, "v"), ((32, 128), F32, "v")],
        [(sc, "s"), (gin4, "v"), (lg, "v")] + [(v, "h") for v in (w, e, n_h, i_h, s_h, act_h, a_h, p_h)],
        [
            pltpu.VMEM((5,) + big, BF),
            pltpu.VMEM((4, R, D), BF),
            pltpu.VMEM((4, R, 128), F32),
            pltpu.VMEM((2, R, D), F32),
            pltpu.VMEM((8, R, D), BF),
            pltpu.VMEM((4, R, D), BF),
            pltpu.VMEM((H, R, R), BF),
            pltpu.VMEM((R, D), F32),
            pltpu.VMEM((R, D), F32),
            pltpu.VMEM((2, R, D), F32),
            pltpu.VMEM((R, D), BF),
            pltpu.VMEM((8, R, 256), BF),
            DMA((5, 2)),
            DMA((16,)),
        ],
        vmem=60,
        flops=8e10,
        name="lat_backward",
    )
    pack = lax.psum_scatter(pack, BATCH, scatter_dimension=0, tiled=True)
    gin, epay = call(
        enc_back_body,
        [((N, DI), F32, "v"), ((NJ, 640, 128), BF, "v")],
        [(sc, "s"), (xin, "v"), (bg, "v"), (lg, "v"), (gd, "v"), (gc, "v")]
        + [(v, "h") for v in (gmix, e, q_b, k_b, v_b, g_all, dw)],
        [
            pltpu.VMEM((R, D), BF),
            pltpu.VMEM((R, D + 128), BF),
            pltpu.VMEM((R, D), BF),
            pltpu.VMEM((N, D), BF),
            pltpu.VMEM((N, D), BF),
            pltpu.VMEM((NJ, 192, D), BF),
            pltpu.VMEM((R, D), F32),
            pltpu.VMEM((D, N), BF),
            pltpu.VMEM((D, N), BF),
            pltpu.VMEM((1920, 128), BF),
            pltpu.VMEM((DI, 256), F32),
            pltpu.VMEM((D, 128), F32),
            DMA((7,)),
        ],
        vmem=58,
        flops=3e9,
        name="enc_back",
    )
    r1 = exchange(epay, BLK)
    p2, dec_grad, bq_grad = call(
        tail_one_body,
        [((NI, 352, 128), BF, "v"), ((48, 160), F32, "v"), ((80, 96), F32, "v")],
        [(r1, "v"), (nf, "h"), (g_all, "h"), (lg, "v"), (lat_gain, "v"), (g1c, "v")],
        [pltpu.VMEM((NJ * N, DI), BF), pltpu.VMEM((NJ, 16, D), BF), pltpu.VMEM((256, 2048), BF), DMA((2,))],
        name="tail_one",
    )
    r2 = exchange(p2, BATCH)
    arr, lm, om, byte_grads, lat_gains, byte_gain = call(
        tail_two_body,
        [
            ((32, 80), F32, "v"),
            ((10, 160, 80), F32, "v"),
            ((2, 160, 80), F32, "v"),
            ((3, 80, 96), F32, "v"),
            ((5, D), F32, "v"),
            ((2, DI), F32, "v"),
        ],
        [(r2, "v"), (pack, "v"), (bq_grad, "v")],
        name="tail_two",
    )
    byte_grads = jnp.swapaxes(byte_grads, 1, 2)
    return (res[None], gin[None], gqin[None], arr, lm, om, byte_grads, dec_grad.T, lat_gains, byte_gain)


def solution(mesh):
    grid = Mesh(mesh.devices.reshape(4, 2, NX, NZ), AXES)
    return jax.shard_map(
        shards,
        mesh=grid,
        in_specs=(
            P(BATCH, BLK, None),
            P(BATCH, BLK, None),
            P(BATCH),
            P(BLK, None),
            P(None, BLK, None),
            P(None, BLK, None),
            P(None, BLK, None),
            P(BLK, None),
            P(),
            P(),
            P(BATCH, BLK, None),
        ),
        out_specs=(
            P(BATCH, BLK, None),
            P(BATCH, BLK, None),
            P(BATCH, BLK, None),
            P(BATCH, BLK),
            P(None, BATCH, BLK),
            P(None, BATCH, BLK),
            P(None, BATCH, BLK),
            P(BATCH, BLK),
            P(),
            P(),
        ),
        check_vma=False,
    )
```

```python
import jax
import jax.numpy as jnp
from jax import lax
from jax.experimental import pallas as pl
from jax.experimental.pallas import tpu as pltpu
from jax.sharding import Mesh, PartitionSpec as P

F32, BF = jnp.float32, jnp.bfloat16
D, DI, R, N, H, E = 1280, 768, 256, 128, 8, 160
NX, NZ, NJ, NI = 4, 4, 16, 8
SCALE = E**-0.5
EPS = 1e-5
MIB = 1 << 20
AXES = ("y", "core", "x", "z")
BATCH = ("y", "core")
BLK = ("x", "z")
WIN = [128 * (E * h // 128) for h in range(H)]
OFF = [E * h - WIN[h] for h in range(H)]
SQUARE = [("o", 0), ("l", 1), ("l", 2), ("l", 3), ("l", 4), ("l", 5), ("o", 1), ("l", 6), ("l", 7), ("l", 8), ("l", 9)]
ROWS_I = 128
DEC_ROW, BQ_ROW = 880, 960
PLACE = {9: (0, 0), 10: (0, 80), 8: (0, 160), 3: (1, 0), 4: (1, 80), 5: (1, 160), 7: (2, 0), 6: (2, 80), 2: (2, 160), 1: (3, 0), 0: (3, 80)}


def dot(a, b, ca=1, cb=0):
    return lax.dot_general(a, b, (((ca,), (cb,)), ((), ())), preferred_element_type=F32)


def dot_nt(a, b):
    return dot(a, b, 1, 1)


def dot_tn(a, b):
    return dot(a, b, 0, 0)


def half(v):
    return v.astype(BF)


def norm(v):
    c = v - jnp.mean(v, axis=-1, keepdims=True)
    inv = lax.rsqrt(jnp.mean(c * c, axis=-1, keepdims=True) + EPS)
    return c * inv, inv


def norm_back(g, gain, n, inv):
    gg = jnp.sum(g * n, axis=0, keepdims=True)
    inner = g * gain
    m1 = jnp.mean(inner, axis=-1, keepdims=True)
    m2 = jnp.mean(inner * n, axis=-1, keepdims=True)
    return inv * (inner - m1 - n * m2), gg


C0, C1 = 0.7978845608028654, 0.044715


def gelu(x):
    return 0.5 * x * (1.0 + jnp.tanh(C0 * (x + C1 * x * x * x)))


def gelu_slope(x):
    t = jnp.tanh(C0 * (x + C1 * x * x * x))
    return 0.5 * (1.0 + t) + 0.5 * x * (1.0 - t * t) * (C0 * (1.0 + 3.0 * C1 * x * x))


def lanes(width):
    return lax.broadcasted_iota(jnp.int32, (1, width), 1)


def head_mask(h):
    lane = lanes(256)
    return jnp.where((lane >= OFF[h]) & (lane < OFF[h] + E), 1.0, 0.0).astype(F32)


def pieces(row, count):
    out = []
    done = 0
    while done < count:
        i, r0 = divmod(row + done, ROWS_I)
        n = min(count - done, ROWS_I - r0)
        out.append((i, r0, done, n))
        done += n
    return out


def split3(v):
    hi = half(v).astype(F32)
    mid = half(v - hi).astype(F32)
    lo = half(v - hi - mid).astype(F32)
    return hi, mid, lo


def pack3(v):
    hi, mid, lo = split3(v)
    return half(hi + pltpu.roll(mid, 16, 1) + pltpu.roll(lo, 32, 1))


def unpack3(v, axis):
    return v + pltpu.roll(v, 112, axis) + pltpu.roll(v, 96, axis)


def as_rows(parts, count):
    row = lax.broadcasted_iota(jnp.int32, (count, 128), 0)
    out = jnp.zeros((count, 128), F32)
    for r, part in parts:
        out = jnp.where(row == r, part, out)
    return out


def call(body, outs, args, scratch=(), vmem=48, flops=0, name=None):
    spaces = {"v": pltpu.VMEM, "a": pl.ANY, "s": pltpu.SMEM, "h": pltpu.HBM}
    return pl.pallas_call(
        body,
        out_shape=[jax.ShapeDtypeStruct(s, t) for s, t, _ in outs],
        in_specs=[pl.BlockSpec(memory_space=spaces[m]) for _, m in args],
        out_specs=[pl.BlockSpec(memory_space=spaces[m]) for _, _, m in outs],
        scratch_shapes=list(scratch),
        compiler_params=pltpu.CompilerParams(vmem_limit_bytes=vmem * MIB),
        cost_estimate=pl.CostEstimate(flops=int(flops), bytes_accessed=4 * MIB, transcendentals=0),
        name=name,
    )(*[a for a, _ in args])


DMA = pltpu.SemaphoreType.DMA


def pack_body(sc, lm, om, bm, do, la, g0, wsh, buf, sem):
    i, core = sc[0], sc[4]
    cols = pl.ds(pl.multiple_of(core * 640, 128), 640)
    first = [
        (bm.at[0, :, cols], g0.at[0:48, :]),
        (bm.at[1, :, cols], g0.at[48:96, :]),
        (lm.at[0, :, cols], g0.at[96:176, :]),
        (la.at[:, cols], g0.at[176:192, :]),
    ]
    first = [pltpu.make_async_copy(a, b, sem.at[8 + k]) for k, (a, b) in enumerate(first)]
    for c in first:
        c.start()
    blocks = [(80 * k, 80, (om if s == "o" else lm), n, D) for k, (s, n) in enumerate(SQUARE)]
    blocks += [(DEC_ROW, 80, do, None, DI), (BQ_ROW, 48, bm, 2, D)]
    for k in range(NI):
        lo, hi = ROWS_I * k, ROWS_I * (k + 1)

        @pl.when(i == k)
        def _(lo=lo, hi=hi):
            cs = []
            for row, count, ref, n, width in blocks:
                a, b = max(lo, row), min(hi, row + count)
                if a < b:
                    src = ref.at[a - row : b - row, :] if n is None else ref.at[n, a - row : b - row, :]
                    dst = buf.at[a - lo : b - lo, :] if width == D else buf.at[a - lo : b - lo, 0:width]
                    cs.append(pltpu.make_async_copy(src, dst, sem.at[len(cs)]))
            for c in cs:
                c.start()
            for c in cs:
                c.wait()

    out = pltpu.make_async_copy(buf, wsh, sem.at[12])
    out.start()
    for c in first:
        c.wait()
    out.wait()


def pieces_from(sc, groups):
    x, z, core = sc[2], sc[3], sc[4]
    out = []
    for side in range(2):
        c = core if side == 0 else 1 - core
        col = pl.ds(pl.multiple_of(c * 640, 128), 640)
        for e in range(4):
            for d in range(4):
                xs = jnp.where(c == 0, (x + 4 - d) & 3, (x + 4 - e) & 3)
                zs = jnp.where(c == 0, (z + 4 - e) & 3, (z + 4 - d) & 3)
                out.append((xs * 4 + zs, col, groups[4 * side + e].at[d]))
    return out


def enc_body(sc, t0, t1, t2, t3, u0, u1, u2, u3, x_in, bg, lg, g_out, nb_o, k_o, v_o, q_o, pay, gs, acc, sem):
    copies = [
        pltpu.make_async_copy(src, gs.at[pos, :, col], sem.at[k])
        for k, (pos, col, src) in enumerate(pieces_from(sc, (t0, t1, t2, t3, u0, u1, u2, u3)))
    ]
    for c in copies:
        c.start()
    n_in, _ = norm(x_in[...].astype(F32))
    nb = half(n_in * bg[0:1, :])
    nb_o[...] = nb
    for c in copies:
        c.wait()
    save = pltpu.make_async_copy(gs, g_out, sem.at[32])
    save.start()
    k_o[...] = half(dot(nb, gs[:, 0:48, :].reshape(DI, D)))
    v_o[...] = half(dot(nb, gs[:, 48:96, :].reshape(DI, D)))
    z0b = gs[:, 176:192, :].reshape(R, D)
    nq, _ = norm(z0b.astype(F32))
    q_o[...] = half(dot(half(nq * lg[0:1, :]), gs[:, 96:176, :].reshape(D, D)))
    acc[...] = jnp.zeros_like(acc)
    valid = lanes(N) + sc[1] * N < sc[5]
    lane = lanes(128)
    stats = jnp.zeros((R, 128), F32)
    for h in range(H):
        w = slice(WIN[h], WIN[h] + 256)
        mk = head_mask(h)
        s = dot_nt(q_o[:, w] * half(mk), k_o[:, w]) * SCALE
        s = jnp.where(valid, s, -1e30)
        m = jnp.max(s, axis=-1, keepdims=True)
        p = jnp.exp(s - m)
        acc[:, w] += dot(half(p), v_o[:, w]) * mk
        stats = jnp.where(lane == h, m, stats)
        stats = jnp.where(lane == 8 + h, jnp.sum(p, axis=-1, keepdims=True), stats)
    pay[:, 0:D] = half(acc[...])
    pay[:, D : D + 128] = pack3(stats)
    save.wait()


def combine_body(rcv, out):
    st = unpack3(rcv[:, :, D : D + 128].astype(F32), 2)
    peak = jnp.max(st, axis=0, keepdims=True)
    w = jnp.exp(st - peak)
    total = jnp.sum(w * pltpu.roll(st, 120, 2), axis=0, keepdims=True)
    coef = w / total
    lane = lax.broadcasted_iota(jnp.int32, (1, 1, 128), 2)
    for t in range(10):
        h0, h1 = 128 * t // E, (128 * t + 127) // E
        c = coef[:, :, h0 : h0 + 1]
        if h1 != h0:
            c = jnp.where(lane >= E * h1 - 128 * t, coef[:, :, h1 : h1 + 1], c)
        o = jnp.sum(rcv[:, :, 128 * t : 128 * t + 128].astype(F32) * c, axis=0)
        out[:, 128 * t : 128 * t + 128] = half(o)
    lse = jnp.where(lanes(128) < 8, (peak + jnp.log(total))[0], 0.0)
    out[:, D : D + 128] = pack3(lse)


class Ring:
    def __init__(self, w, slots, sem, order):
        self.w, self.slots, self.sem, self.order = w, slots, sem, order
        self.n = slots.shape[0]
        self.pos = {m: k for k, m in enumerate(order)}

    def copies(self, m):
        s = self.pos[m] % self.n
        return [
            pltpu.make_async_copy(
                self.w.at[i, :, r0 : r0 + n, :], self.slots.at[s, :, d0 : d0 + n, :], self.sem.at[s, k]
            )
            for k, (i, r0, d0, n) in enumerate(pieces(80 * m, 80))
        ]

    def start(self, m):
        for c in self.copies(m):
            c.start()

    def begin(self):
        for m in self.order[: self.n]:
            self.start(m)

    def get(self, m):
        for c in self.copies(m):
            c.wait()
        return self.slots[self.pos[m] % self.n].reshape(D, D)

    def done(self, m):
        k = self.pos[m] + self.n
        if k < len(self.order):
            self.start(self.order[k])


def forward_body(
    qin, cot, bg, lg, e_h, g_all, w,
    res, gqin, gain_o, pay, mix_o, nd_o, gq_o, z_h, h_h, a_h,
    slots, e, z0b, zs, zb, hs, qs, acc, kd, vd, dec, bq, dacc, gq, gkv, wsem, ssem, lsem,
):
    first = [
        pltpu.make_async_copy(e_h.at[:, 0:D], e, lsem.at[3]),
        pltpu.make_async_copy(g_all.at[:, 176:192, :], z0b, lsem.at[4]),
    ]
    for c in first:
        c.start()
    ring = Ring(w, slots, wsem, list(range(11)))
    ring.begin()
    copies = []
    for i, r0, d0, n in pieces(BQ_ROW, 48):
        copies.append(pltpu.make_async_copy(w.at[i, :, r0 : r0 + n, :], bq.at[:, d0 : d0 + n, :], lsem.at[0]))
    for i, r0, d0, n in pieces(DEC_ROW, 80):
        copies.append(
            pltpu.make_async_copy(w.at[i, :, r0 : r0 + n, 0:DI], dec.at[:, d0 : d0 + n, :], lsem.at[len(copies)])
        )
    for c in copies:
        c.start()
    saves = []

    def save(src, dst):
        c = pltpu.make_async_copy(src, dst, ssem.at[len(saves)])
        c.start()
        saves.append(c)

    def keep(k):
        zb[k] = half(zs[k])
        save(zb.at[k], z_h.at[k])

    def mul(a, m):
        out = dot(a, ring.get(m))
        ring.done(m)
        return out

    for c in first:
        c.wait()
    z1 = z0b[...].reshape(R, D).astype(F32) + mul(e[...], 0)
    zs[0] = z1
    keep(0)
    h1 = mul(half(norm(z1)[0] * lg[1:2, :]), 1)
    hs[0] = half(h1)
    save(hs.at[0], h_h.at[0])
    zs[1] = zs[0] + mul(half(gelu(h1)), 2)
    keep(1)
    s_b = half(norm(zs[1])[0] * lg[2:3, :])
    for k in range(3):
        qs[k] = half(mul(s_b, 3 + k))
        save(qs.at[k], a_h.at[k])
    acc[...] = jnp.zeros_like(acc)
    for h in range(H):
        win = slice(WIN[h], WIN[h] + 256)
        mk = head_mask(h)
        s = dot_nt(qs[0, :, win] * half(mk), qs[1, :, win]) * SCALE
        p = jnp.exp(s - jnp.max(s, axis=-1, keepdims=True))
        p = p / jnp.sum(p, axis=-1, keepdims=True)
        acc[:, win] += dot(half(p), qs[2, :, win]) * mk
    qs[3] = half(acc[...])
    save(qs.at[3], a_h.at[3])
    zs[2] = zs[1] + mul(qs[3], 6)
    keep(2)
    h2 = mul(half(norm(zs[2])[0] * lg[3:4, :]), 7)
    hs[1] = half(h2)
    save(hs.at[1], h_h.at[1])
    zs[3] = zs[2] + mul(half(gelu(h2)), 8)
    keep(3)
    c_b = half(norm(zs[3])[0] * lg[4:5, :])
    kd[...] = half(mul(c_b, 9))
    vd[...] = half(mul(c_b, 10))

    x = qin[...].astype(F32)
    n, inv = norm(x)
    nd = half(n * bg[1:2, :])
    nd_o[...] = nd
    for c in copies:
        c.wait()
    wq = bq[...].reshape(DI, D)
    wd = dec[...].reshape(D, DI)
    gq_o[...] = half(dot(nd, wq))
    mix_o[...] = half(dot_nt(cot[...], wd))
    dacc[...] = jnp.zeros_like(dacc)
    gq[...] = jnp.zeros_like(gq)
    gkv[...] = jnp.zeros_like(gkv)
    for h in range(H):
        win = slice(WIN[h], WIN[h] + 256)
        mk = head_mask(h)
        mkb = half(mk)
        qw, gw, kw, vw = gq_o[:, win], mix_o[:, win], kd[:, win], vd[:, win]
        s = dot_nt(qw * mkb, kw) * SCALE
        p = jnp.exp(s - jnp.max(s, axis=-1, keepdims=True))
        p = p / jnp.sum(p, axis=-1, keepdims=True)
        pb = half(p)
        dacc[:, win] += dot(pb, vw) * mk
        dp = dot_nt(gw * mkb, vw)
        ds = half(p * (dp - jnp.sum(p * dp, axis=-1, keepdims=True)))
        gq[:, win] += dot(ds, kw) * mk
        gkv[0, :, win] += dot_tn(ds, qw) * mk
        gkv[1, :, win] += dot_tn(pb, gw) * mk
    pay[:, 0:D] = half(gkv[0] * SCALE)
    pay[:, D : 2 * D] = half(gkv[1])
    mix = half(dacc[...])
    mix_o[...] = mix
    res[...] = half(x + dot(mix, wd))
    gqb = half(gq[...] * SCALE)
    gq_o[...] = gqb
    gin, gg = norm_back(dot_nt(gqb, wq), bg[1:2, :], n, inv)
    gqin[...] = cot[...].astype(F32) + gin
    gain_o[...] = gg
    for c in saves:
        c.wait()


def prepare_body(lg, z_h, h_h, a_h, n_h, i_h, s_h, act_h, p_h, zs, hs, qs, ns, vs, ss, acts, ps, sem, osem):
    loads = {}
    for k in range(4):
        loads["z", k] = pltpu.make_async_copy(z_h.at[k], zs.at[k], sem.at[k])
    for k in range(2):
        loads["h", k] = pltpu.make_async_copy(h_h.at[k], hs.at[k], sem.at[4 + k])
    loads["q"] = pltpu.make_async_copy(a_h.at[0:2], qs, sem.at[6])
    for c in loads.values():
        c.start()
    saves = []

    def save(src, dst):
        c = pltpu.make_async_copy(src, dst, osem.at[len(saves)])
        c.start()
        saves.append(c)

    for k, a in ((3, 0), (2, 2), (1, 1), (0, 4)):
        loads["z", k].wait()
        n, inv = norm(zs[k].astype(F32))
        ns[k] = half(n)
        save(ns.at[k], n_h.at[k])
        vs[k] = jnp.broadcast_to(inv, (R, 128))
        acts[a] = half(n * lg[k + 1 : k + 2, :])
        save(acts.at[a], act_h.at[a])
    save(vs, i_h)
    for k, a in ((1, 3), (0, 5)):
        loads["h", k].wait()
        x = hs[k].astype(F32)
        t = jnp.tanh(C0 * (x + C1 * x * x * x))
        acts[a] = half(0.5 * x * (1.0 + t))
        save(acts.at[a], act_h.at[a])
        ss[k] = 0.5 * (1.0 + t) + 0.5 * x * (1.0 - t * t) * (C0 * (1.0 + 3.0 * C1 * x * x))
        save(ss.at[k], s_h.at[k])
    loads["q"].wait()
    for h in range(H):
        win = slice(WIN[h], WIN[h] + 256)
        s = dot_nt(qs[0, :, win] * half(head_mask(h)), qs[1, :, win]) * SCALE
        p = jnp.exp(s - jnp.max(s, axis=-1, keepdims=True))
        ps[h] = half(p / jnp.sum(p, axis=-1, keepdims=True))
    save(ps, p_h)
    for c in saves:
        c.wait()


def lat_backward_body(
    sc, gin, lg, w, e_h, n_h, i_h, s_h, act_h, a_h, p_h, nf, gmix, pack_o, g1c_o, gains_o,
    slots, ns, vs, ss, acts, qs, ps, acc, acc2, acc3, gh, gw, wsem, lsem,
):
    order = [8, 7, 6, 3, 4, 5, 2, 1, 0]
    ring = Ring(w, slots, wsem, order)
    todo = [
        (i_h, vs),
        (act_h.at[0], acts.at[0]),
        (s_h.at[1], ss.at[1]),
        (act_h.at[3], acts.at[1]),
        (n_h.at[2], ns.at[2]),
        (act_h.at[2], acts.at[3]),
        (a_h.at[3], acts.at[4]),
        (p_h, ps),
        (a_h.at[0:3], qs.at[0:3]),
        (n_h.at[1], ns.at[1]),
        (act_h.at[1], acts.at[2]),
        (s_h.at[0], ss.at[0]),
        (act_h.at[5], acts.at[5]),
        (n_h.at[0], ns.at[0]),
        (act_h.at[4], acts.at[6]),
        (e_h.at[:, 0:D], acts.at[7]),
    ]
    loads = [pltpu.make_async_copy(a, b, lsem.at[k]) for k, (a, b) in enumerate(todo)]
    after = {8: (4, 5, 6), 7: (7, 8), 6: (9, 10, 11, 12), 3: (13, 14, 15)}
    ring.start(8)
    for c in loads[:4]:
        c.start()
    for m in order[1 : ring.n]:
        ring.start(m)

    def ready(*ks):
        for k in ks:
            loads[k].wait()

    src = sc[1] * 80
    start = pl.multiple_of(jnp.minimum((src >> 7) * 128, 1024), 128)
    offset = src - start
    lane = lanes(256)

    def put(ref, to):
        v = pltpu.roll(ref[:, pl.ds(start, 256)].astype(F32), (to - offset + 256) & 255, 1)
        return jnp.where((lane >= to) & (lane < to + 80), v, 0.0)

    def weight_grad(window, first, count):
        a = acts[first : first + count].reshape(count * R, D)
        pack_o[:, 256 * window : 256 * window + 256] = half(dot_tn(a, gw[first : first + count].reshape(count * R, 256)))

    def mul(g_b, m):
        out = dot_nt(g_b, ring.get(m))
        ring.done(m)
        for k in after.get(m, ()):
            loads[k].start()
        return out

    gain_rows = []

    def back(g, k):
        out, gg = norm_back(g, lg[k + 1 : k + 2, :], ns[k].astype(F32), vs[k][:, 0:1])
        for t in range(10):
            gain_rows.append((10 * k + t, gg[:, 128 * t : 128 * t + 128]))
        return out

    for t in range(10):
        acc[:, 128 * t : 128 * t + 128] = gin[:, 16 * t : 16 * t + 16, :].reshape(R, 128).astype(F32)
    tile = lanes(128)
    values = pltpu.roll(gin[:, 176:192, :].reshape(R, 128).astype(F32), 80, 1)
    gw[0, :, 0:128] = half(jnp.where(tile < 80, gin[:, 160:176, :].reshape(R, 128).astype(F32), values))
    gw[0, :, 128:256] = half(jnp.where(tile < 32, values, 0.0))
    gw[1] = half(put(acc, 160))
    ready(0, 1, 2, 3)
    gh[...] = half(mul(half(acc[...]), 8) * ss[1])
    weight_grad(0, 0, 2)
    ready(4)
    gw[3] = half(put(gh, 0))
    acc[...] += back(mul(gh[...], 7), 2)
    gw[4] = half(put(acc, 80))
    qs[3] = half(mul(half(acc[...]), 6))
    acc2[...] = jnp.zeros_like(acc2)
    acc3[...] = jnp.zeros_like(acc3)
    ready(5, 6, 7, 8)
    for h in range(H):
        win = slice(WIN[h], WIN[h] + 256)
        mk = head_mask(h)
        pb = ps[h]
        p = pb.astype(F32)
        dp = dot_nt(qs[3, :, win] * half(mk), qs[2, :, win])
        ds = half(p * (dp - jnp.sum(p * dp, axis=-1, keepdims=True)) * SCALE)
        acc2[:, win] += dot(ds, qs[1, :, win]) * mk
        acc3[0, :, win] += dot_tn(ds, qs[0, :, win]) * mk
        acc3[1, :, win] += dot_tn(pb, qs[3, :, win]) * mk
    gw[2] = half(put(acc2, 0) + put(acc3.at[0], 80) + put(acc3.at[1], 160))
    gn = mul(half(acc2[...]), 3)
    gn = gn + mul(half(acc3[0]), 4)
    gn = gn + mul(half(acc3[1]), 5)
    ready(9, 10)
    weight_grad(1, 2, 1)
    acc[...] += back(gn, 1)
    gw[5] = half(put(acc, 160))
    ready(11, 12)
    gh[...] = half(mul(half(acc[...]), 2) * ss[0])
    weight_grad(2, 3, 3)
    gw[6] = half(put(gh, 0))
    ready(13, 14, 15)
    acc[...] += back(mul(gh[...], 1), 0)
    gw[7] = half(put(acc, 80))
    g1c_o[...] = half(put(acc, 0)[:, 0:128])
    gmix[...] = half(mul(half(acc[...]), 0))
    weight_grad(3, 6, 2)
    gains_o[...] = as_rows(gain_rows, 32)


def key_value_back_body(sc, rcv, lg, n_h, i_h, w, mark, out, gain_o, wbuf, nbuf, ibuf, sem):
    rows = pl.ds(pl.multiple_of(sc[1] * 16, 16), 16)
    copies = []
    for k, m in enumerate((9, 10)):
        for i, r0, d0, n in pieces(80 * m, 80):
            copies.append((w.at[i, :, r0 : r0 + n, :], wbuf.at[k, :, d0 : d0 + n, :]))
    copies += [(n_h.at[3, rows, :], nbuf), (i_h.at[3, rows, :], ibuf)]
    copies = [pltpu.make_async_copy(a, b, sem.at[k]) for k, (a, b) in enumerate(copies)]
    for c in copies:
        c.start()
    s = half(jnp.sum(rcv[...].astype(F32), axis=0))
    for j in range(NJ):
        base = min(128 * (80 * j // 128), 1024)
        for k in range(2):
            v = s[:, D * k + base : D * k + base + 256].astype(F32)
            if 80 * j > base:
                v = pltpu.roll(v, 256 - (80 * j - base), 1)
            out[j, 160 + 16 * k : 176 + 16 * k, :] = half(v[:, 0:128])
    for c in copies:
        c.wait()
    gn = dot_nt(s[:, 0:D], wbuf[0].reshape(D, D)) + dot_nt(s[:, D : 2 * D], wbuf[1].reshape(D, D))
    g, gg = norm_back(gn, lg[4:5, :], nbuf[...].astype(F32), ibuf[:, 0:1])
    gain_o[...] = gg
    g = jnp.concatenate([half(g[:, 128 * t : 128 * t + 128]) for t in range(10)], axis=0)
    for j in range(NJ):
        out[j, 0:160, :] = g


def dec_weights_body(mix, cot, nd, gq, after, out, mark, buf, sem):
    g = half(dot_tn(mix[...], cot[...]))
    for i in range(NI):
        for t in range(6):
            buf[i, 160 * t : 160 * t + 160, :] = g[160 * i : 160 * i + 160, 128 * t : 128 * t + 128]
    one = pltpu.make_async_copy(buf.at[:, 0:960, :], out.at[:, 0:960, :], sem.at[0])
    one.start()
    g = half(dot_tn(nd[...], gq[...]))
    for i in range(NI):
        for t in range(10):
            r = 960 + 96 * t
            buf[i, r : r + 96, :] = g[96 * i : 96 * i + 96, 128 * t : 128 * t + 128]
    two = pltpu.make_async_copy(buf.at[:, 960:1920, :], out.at[:, 960:1920, :], sem.at[1])
    two.start()
    mark[...] = jnp.zeros_like(mark)
    one.wait()
    two.wait()


def spread(chunk, pay, td, tb):
    fill = jnp.zeros((96, 128), F32)
    for t in range(6):
        v = jnp.concatenate([chunk[160 * t : 160 * t + 160, :].astype(F32), fill], axis=0)
        td[128 * t : 128 * t + 128, :] = v.T
    fill = jnp.zeros((32, 128), F32)
    for t in range(10):
        v = jnp.concatenate([chunk[960 + 96 * t : 960 + 96 * t + 96, :].astype(F32), fill], axis=0)
        tb[128 * t : 128 * t + 128, :] = v.T
    for j in range(NJ):
        tail = pltpu.roll(td[48 * j : 48 * j + 48, 128:256], 96, 1)
        pay[j, 512:560, :] = half(tb[80 * j : 80 * j + 48, :] + tail)
        pay[j, 560:592, :] = half(tb[80 * j + 48 : 80 * j + 80, :])
        pay[j, 592:640, :] = half(td[48 * j : 48 * j + 48, 0:128])


def enc_back_body(
    sc, x_in, bg, lg, gd, gc, gmix_h, e_h, q_h, k_h, v_h, g_all, dw_h, gin_o, pay,
    gmix, e, q, k, v, wkv, gq, gkt, gvt, dw, td, tb, sem,
):
    pairs = [(gmix_h, gmix), (q_h, q), (k_h, k), (v_h, v), (e_h, e), (g_all, wkv), (dw_h, dw)]
    loads = [pltpu.make_async_copy(a, b, sem.at[n]) for n, (a, b) in enumerate(pairs)]
    for c in loads:
        c.start()
    for c in loads[:5]:
        c.wait()
    lse = unpack3(e[:, D : D + 128].astype(F32), 1)
    valid = lanes(N) + sc[1] * N < sc[5]
    gq[...] = jnp.zeros_like(gq)
    for h in range(H):
        win = slice(WIN[h], WIN[h] + 256)
        mk = head_mask(h)
        mkb = half(mk)
        qw, gw, kw, vw = q[:, win], gmix[:, win], k[:, win], v[:, win]
        rd = jnp.sum(gw.astype(F32) * e[:, win].astype(F32) * mk, axis=-1, keepdims=True)
        s = dot_nt(qw * mkb, kw) * SCALE
        p = jnp.where(valid, jnp.exp(jnp.where(valid, s, -1e30) - lse[:, h : h + 1]), 0.0)
        dp = dot_nt(gw * mkb, vw)
        ds = half(p * (dp - rd))
        gq[:, win] += dot(ds, kw) * mk
        o = OFF[h]
        gkt[E * h : E * h + E, :] = half(dot_tn(qw, ds)[o : o + E, :] * SCALE)
        gvt[E * h : E * h + E, :] = half(dot_tn(gw, half(p))[o : o + E, :])
    pay[:, 320:400, :] = gkt[...].reshape(NJ, 80, 128)
    pay[:, 400:480, :] = gvt[...].reshape(NJ, 80, 128)
    loads[5].wait()
    gqs = gq[...] * SCALE
    gqt = half(gqs.T)
    pay[:, 160:240, :] = gqt[:, 0:128].reshape(NJ, 80, 128)
    pay[:, 240:320, :] = gqt[:, 128:256].reshape(NJ, 80, 128)
    n, inv = norm(wkv[:, 176:192, :].reshape(R, D).astype(F32))
    gz, g0 = norm_back(dot_nt(half(gqs), wkv[:, 96:176, :].reshape(D, D)), lg[0:1, :], n, inv)
    gzt = half(gz.T)
    pay[:, 0:80, :] = gzt[:, 0:128].reshape(NJ, 80, 128)
    pay[:, 80:160, :] = gzt[:, 128:256].reshape(NJ, 80, 128)
    n, inv = norm(x_in[...].astype(F32))
    gnt = dot(wkv[:, 0:48, :].reshape(DI, D), gkt[...]) + dot(wkv[:, 48:96, :].reshape(DI, D), gvt[...])
    gin, gg = norm_back(gnt.T, bg[0:1, :], n, inv)
    gin_o[...] = gin
    rows = [(t, gg[:, 128 * t : 128 * t + 128]) for t in range(6)]
    rows += [(6 + t, gd[:, 128 * t : 128 * t + 128]) for t in range(6)]
    rows += [(12 + t, g0[:, 128 * t : 128 * t + 128]) for t in range(10)]
    rows += [(22 + t, gc[:, 128 * t : 128 * t + 128]) for t in range(10)]
    g = half(as_rows(rows, 32))
    for j in range(NJ):
        pay[j, 480:512, :] = g
    loads[6].wait()
    spread(dw, pay, td, tb)


def tail_one_body(rcv, nf_h, g_all, lg, lat_gain, g1c, out, dec_o, bq_o, nf, z0b, left, sem):
    loads = [
        pltpu.make_async_copy(nf_h, nf, sem.at[0]),
        pltpu.make_async_copy(g_all.at[:, 176:192, :], z0b, sem.at[1]),
    ]
    for c in loads:
        c.start()
    sums = jnp.sum(rcv[:, 0:320, :].astype(F32), axis=0)
    fill = jnp.zeros((48, 128), F32)
    left[...] = jnp.zeros_like(left)
    for s in range(NJ):
        left[0:80, 128 * s : 128 * s + 128] = rcv[s, 320:400, :]
        left[128:208, 128 * s : 128 * s + 128] = rcv[s, 400:480, :]
    loads[1].wait()
    nq = half(norm(z0b[...].reshape(R, D).astype(F32))[0] * lg[0:1, :])
    a = jnp.concatenate([sums[160:240], fill], axis=0).T
    b = jnp.concatenate([sums[240:320], fill], axis=0).T
    w0 = dot_tn(nq, half(jnp.concatenate([a, b], axis=0)))
    a = jnp.concatenate([sums[0:80], fill], axis=0).T
    b = jnp.concatenate([sums[80:160], fill], axis=0).T
    gz = half(jnp.concatenate([a, b], axis=0) + g1c[...].astype(F32))
    gains = jnp.sum(rcv[:, 480:512, :].astype(F32), axis=0)
    gains = half(jnp.concatenate([gains, lat_gain[...]], axis=0))
    loads[0].wait()
    wt = dot(left[...], nf[...]).T
    lane = lanes(128)
    key, value = wt[:, 0:128], wt[:, 128:256]
    one = half(jnp.where(lane < 80, key, pltpu.roll(value, 80, 1)))
    other = pltpu.roll(value, 32, 1)
    for i in range(NI):
        r = 96 * i
        beside = jnp.concatenate([other[r : r + 96, :], jnp.zeros((64, 128), F32)], axis=0)
        out[i, 0:160, :] = half(jnp.where(lane < 80, w0[160 * i : 160 * i + 160, :], beside))
        out[i, 160:192, :] = gz[32 * i : 32 * i + 32, :]
        out[i, 192:288, :] = one[r : r + 96, :]
        out[i, 288:352, :] = gains
    s = jnp.sum(rcv[:, 512:640, :].astype(F32), axis=0)
    bq_o[...] = s[0:80, 0:96]
    dec_o[:, 0:128] = s[80:128]
    dec_o[:, 128:160] = pltpu.roll(s[0:48], 32, 1)[:, 0:32]


def tail_two_body(rcv, pack, bq, arr_o, lm_o, om_o, bm_o, lat_o, byte_o):
    sums = jnp.sum(rcv[...].astype(F32), axis=0)
    lm_o[0] = sums[0:160, 0:80]
    arr_o[...] = sums[160:192, 0:80]
    lane = lanes(128)
    value = jnp.where(lane < 48, pltpu.roll(sums[192:288], 48, 1), pltpu.roll(sums[0:96], 96, 1))
    fill = jnp.zeros((32, 128), F32)
    bm_o[0] = jnp.concatenate([sums[192:288], fill], axis=0).T[0:80, 0:96]
    bm_o[1] = jnp.concatenate([value, fill], axis=0).T[0:80, 0:96]
    bm_o[2] = bq[...]
    g = sums[288:352]
    for t in range(6):
        for b in range(2):
            byte_o[b : b + 1, 128 * t : 128 * t + 128] = g[6 * b + t : 6 * b + t + 1, :]
    for t in range(10):
        for b in range(5):
            r = {0: 12, 1: 32, 2: 42, 3: 52, 4: 22}[b] + t
            lat_o[b : b + 1, 128 * t : 128 * t + 128] = g[r : r + 1, :]
    for m, (kind, n) in enumerate(SQUARE):
        window, o = PLACE[m]
        v = pack[:, 256 * window : 256 * window + 256].astype(F32)
        if o:
            v = pltpu.roll(v, 256 - o, 1)
        if kind == "l":
            lm_o[n] = v[:, 0:80]
        else:
            om_o[n] = v[:, 0:80]


def line(y, c, x, z):
    return ((y % 4) * 2 + c) * NJ + (x % 4) * NZ + (z % 4)


EVERY = [(y, c, x, z) for y in range(4) for c in range(2) for x in range(NX) for z in range(NZ)]


def along(stage, d):
    out = []
    for y, c, x, z in EVERY:
        on_x = (c == 0) == (stage == 0)
        out.append((line(y, c, x, z), line(y, c, x + d, z) if on_x else line(y, c, x, z + d)))
    return out


SWAP = [(line(y, c, x, z), line(y, 1 - c, x, z)) for y, c, x, z in EVERY]


def exchange(v, axes):
    flat = v.reshape(v.shape[0] * v.shape[1], v.shape[2])
    return lax.all_to_all(flat, axes, split_axis=0, concat_axis=0, tiled=True).reshape(v.shape)


def shards(inputs, queries, lengths, latent_array, latent_mats, out_mats, byte_mats, dec_out, lg, bg, cotangent):
    y, core, x, z = (lax.axis_index(a) for a in AXES)
    i, j = y * 2 + core, x * NZ + z
    sc = jnp.stack([i, j, x, z, core, lengths[0]]).astype(jnp.int32)
    xin, qin, cot = inputs[0], queries[0], cotangent[0]

    g0, wsh = call(
        pack_body,
        [((192, 640), BF, "v"), ((ROWS_I, D), BF, "h")],
        [(sc, "s"), (latent_mats, "h"), (out_mats, "h"), (byte_mats, "h"), (dec_out, "h"), (latent_array, "h")],
        [pltpu.VMEM((ROWS_I, D), BF), DMA((13,))],
        vmem=60,
        name="pack",
    )
    w = lax.all_gather(wsh, AXES, axis=0, tiled=True).reshape(NI, NJ, ROWS_I, D)

    def step(v, stage):
        return [lax.ppermute(v, AXES, along(stage, d)) for d in (1, 2, 3)]

    s0 = jnp.stack([g0] + step(g0, 0))
    own = [s0] + step(s0, 1)
    sib = [lax.ppermute(v, AXES, SWAP) for v in own]
    g_all, nb, k_b, v_b, q_b, pay = call(
        enc_body,
        [
            ((NJ, 192, D), BF, "h"),
            ((N, DI), BF, "v"),
            ((N, D), BF, "v"),
            ((N, D), BF, "v"),
            ((R, D), BF, "v"),
            ((R, D + 128), BF, "v"),
        ],
        [(sc, "s")] + [(v, "a") for v in own + sib] + [(xin, "v"), (bg, "v"), (lg, "v")],
        [pltpu.VMEM((NJ, 192, D), BF), pltpu.VMEM((R, D), F32), DMA((33,))],
        vmem=60,
        flops=3e9,
        name="enc",
    )
    rcv = exchange(pay.reshape(NJ, 16, D + 128), BLK)
    (mine,) = call(combine_body, [((16, D + 128), BF, "v")], [(rcv, "v")], name="combine")
    e = lax.all_gather(mine, BLK, axis=0, tiled=True)
    nf = lax.all_gather(nb, BLK, axis=0, tiled=True)

    big = (NJ, 80, D)
    res, gqin, gd, dpay, mix, nd, gq, z_h, h_h, a_h = call(
        forward_body,
        [
            ((N, DI), BF, "v"),
            ((N, DI), F32, "v"),
            ((1, DI), F32, "v"),
            ((R, 2 * D), BF, "v"),
            ((N, D), BF, "v"),
            ((N, DI), BF, "v"),
            ((N, D), BF, "v"),
            ((4, R, D), BF, "h"),
            ((2, R, D), BF, "h"),
            ((4, R, D), BF, "h"),
        ],
        [(qin, "v"), (cot, "v"), (bg, "v"), (lg, "v"), (e, "h"), (g_all, "h"), (w, "h")],
        [
            pltpu.VMEM((4,) + big, BF),
            pltpu.VMEM((R, D), BF),
            pltpu.VMEM((NJ, 16, D), BF),
            pltpu.VMEM((4, R, D), F32),
            pltpu.VMEM((4, R, D), BF),
            pltpu.VMEM((2, R, D), BF),
            pltpu.VMEM((4, R, D), BF),
            pltpu.VMEM((R, D), F32),
            pltpu.VMEM((R, D), BF),
            pltpu.VMEM((R, D), BF),
            pltpu.VMEM((NJ, 80, DI), BF),
            pltpu.VMEM((NJ, 48, D), BF),
            pltpu.VMEM((N, D), F32),
            pltpu.VMEM((N, D), F32),
            pltpu.VMEM((2, R, D), F32),
            DMA((4, 2)),
            DMA((10,)),
            DMA((5,)),
        ],
        vmem=54,
        flops=1.5e10,
        name="forward",
    )
    rows = exchange(dpay.reshape(NJ, 16, 2 * D), BLK)
    n_h, i_h, s_h, act_h, p_h = call(
        prepare_body,
        [
            ((4, R, D), BF, "h"),
            ((4, R, 128), F32, "h"),
            ((2, R, D), F32, "h"),
            ((6, R, D), BF, "h"),
            ((H, R, R), BF, "h"),
        ],
        [(lg, "v"), (z_h, "h"), (h_h, "h"), (a_h, "h")],
        [
            pltpu.VMEM((4, R, D), BF),
            pltpu.VMEM((2, R, D), BF),
            pltpu.VMEM((2, R, D), BF),
            pltpu.VMEM((4, R, D), BF),
            pltpu.VMEM((4, R, 128), F32),
            pltpu.VMEM((2, R, D), F32),
            pltpu.VMEM((6, R, D), BF),
            pltpu.VMEM((H, R, R), BF),
            DMA((7,)),
            DMA((14,)),
        ],
        vmem=58,
        flops=5e9,
        name="prepare",
    )
    dw, mark = call(
        dec_weights_body,
        [((NI, 1920, 128), BF, "h"), ((8, 128), F32, "v")],
        [(mix, "v"), (cot, "v"), (nd, "v"), (gq, "v"), (i_h, "h")],
        [pltpu.VMEM((NI, 1920, 128), BF), DMA((2,))],
        vmem=60,
        flops=4e9,
        name="dec_weights",
    )
    kv, gc = call(
        key_value_back_body,
        [((NJ, 192, 128), BF, "v"), ((1, D), F32, "v")],
        [(sc, "s"), (rows, "v"), (lg, "v"), (n_h, "h"), (i_h, "h"), (w, "h"), (mark, "v")],
        [pltpu.VMEM((2,) + big, BF), pltpu.VMEM((16, D), BF), pltpu.VMEM((16, 128), F32), DMA((6,))],
        vmem=16,
        flops=1e8,
        name="key_value_back",
    )
    gin4 = exchange(kv, BLK)
    dw = lax.psum_scatter(dw.reshape(NI * 1920, 128), BATCH, scatter_dimension=0, tiled=True)

    gmix, pack, g1c, lat_gain = call(
        lat_backward_body,
        [((R, D), BF, "v"), ((D, 1024), BF, "v"), ((R, 128), BF, "v"), ((32, 128), F32, "v")],
        [(sc, "s"), (gin4, "v"), (lg, "v")] + [(v, "h") for v in (w, e, n_h, i_h, s_h, act_h, a_h, p_h, nf)],
        [
            pltpu.VMEM((5,) + big, BF),
            pltpu.VMEM((4, R, D), BF),
            pltpu.VMEM((4, R, 128), F32),
            pltpu.VMEM((2, R, D), F32),
            pltpu.VMEM((8, R, D), BF),
            pltpu.VMEM((4, R, D), BF),
            pltpu.VMEM((H, R, R), BF),
            pltpu.VMEM((R, D), F32),
            pltpu.VMEM((R, D), F32),
            pltpu.VMEM((2, R, D), F32),
            pltpu.VMEM((R, D), BF),
            pltpu.VMEM((8, R, 256), BF),
            DMA((5, 2)),
            DMA((16,)),
        ],
        vmem=60,
        flops=8e10,
        name="lat_backward",
    )
    pack = lax.psum_scatter(pack, BATCH, scatter_dimension=0, tiled=True)
    gin, epay = call(
        enc_back_body,
        [((N, DI), F32, "v"), ((NJ, 640, 128), BF, "v")],
        [(sc, "s"), (xin, "v"), (bg, "v"), (lg, "v"), (gd, "v"), (gc, "v")]
        + [(v, "h") for v in (gmix, e, q_b, k_b, v_b, g_all, dw)],
        [
            pltpu.VMEM((R, D), BF),
            pltpu.VMEM((R, D + 128), BF),
            pltpu.VMEM((R, D), BF),
            pltpu.VMEM((N, D), BF),
            pltpu.VMEM((N, D), BF),
            pltpu.VMEM((NJ, 192, D), BF),
            pltpu.VMEM((R, D), F32),
            pltpu.VMEM((D, N), BF),
            pltpu.VMEM((D, N), BF),
            pltpu.VMEM((1920, 128), BF),
            pltpu.VMEM((DI, 256), F32),
            pltpu.VMEM((D, 128), F32),
            DMA((7,)),
        ],
        vmem=58,
        flops=3e9,
        name="enc_back",
    )
    r1 = exchange(epay, BLK)
    p2, dec_grad, bq_grad = call(
        tail_one_body,
        [((NI, 352, 128), BF, "v"), ((48, 160), F32, "v"), ((80, 96), F32, "v")],
        [(r1, "v"), (nf, "h"), (g_all, "h"), (lg, "v"), (lat_gain, "v"), (g1c, "v")],
        [pltpu.VMEM((NJ * N, DI), BF), pltpu.VMEM((NJ, 16, D), BF), pltpu.VMEM((256, 2048), BF), DMA((2,))],
        name="tail_one",
    )
    r2 = exchange(p2, BATCH)
    arr, lm, om, byte_grads, lat_gains, byte_gain = call(
        tail_two_body,
        [
            ((32, 80), F32, "v"),
            ((10, 160, 80), F32, "v"),
            ((2, 160, 80), F32, "v"),
            ((3, 80, 96), F32, "v"),
            ((5, D), F32, "v"),
            ((2, DI), F32, "v"),
        ],
        [(r2, "v"), (pack, "v"), (bq_grad, "v")],
        name="tail_two",
    )
    byte_grads = jnp.swapaxes(byte_grads, 1, 2)
    return (res[None], gin[None], gqin[None], arr, lm, om, byte_grads, dec_grad.T, lat_gains, byte_gain)


def solution(mesh):
    grid = Mesh(mesh.devices.reshape(4, 2, NX, NZ), AXES)
    return jax.shard_map(
        shards,
        mesh=grid,
        in_specs=(
            P(BATCH, BLK, None),
            P(BATCH, BLK, None),
            P(BATCH),
            P(BLK, None),
            P(None, BLK, None),
            P(None, BLK, None),
            P(None, BLK, None),
            P(BLK, None),
            P(),
            P(),
            P(BATCH, BLK, None),
        ),
        out_specs=(
            P(BATCH, BLK, None),
            P(BATCH, BLK, None),
            P(BATCH, BLK, None),
            P(BATCH, BLK),
            P(None, BATCH, BLK),
            P(None, BATCH, BLK),
            P(None, BATCH, BLK),
            P(BATCH, BLK),
            P(),
            P(),
        ),
        check_vma=False,
    )
```

```python
import jax
import jax.numpy as jnp
from jax import lax
from jax.experimental import pallas as pl
from jax.experimental.pallas import tpu as pltpu
from jax.sharding import Mesh, PartitionSpec as P

F32, BF = jnp.float32, jnp.bfloat16
D, DI, R, N, H, E = 1280, 768, 256, 128, 8, 160
NX, NZ, NJ, NI = 4, 4, 16, 8
SCALE = E**-0.5
EPS = 1e-5
MIB = 1 << 20
AXES = ("y", "core", "x", "z")
BATCH = ("y", "core")
BLK = ("x", "z")
WIN = [128 * (E * h // 128) for h in range(H)]
OFF = [E * h - WIN[h] for h in range(H)]
SQUARE = [("o", 0), ("l", 1), ("l", 2), ("l", 3), ("l", 4), ("l", 5), ("o", 1), ("l", 6), ("l", 7), ("l", 8), ("l", 9)]
ROWS_I = 128
DEC_ROW, BQ_ROW = 880, 960
PLACE = {9: (0, 0), 10: (0, 80), 8: (0, 160), 3: (1, 0), 4: (1, 80), 5: (1, 160), 7: (2, 0), 6: (2, 80), 2: (2, 160), 1: (3, 0), 0: (3, 80)}


def dot(a, b, ca=1, cb=0):
    return lax.dot_general(a, b, (((ca,), (cb,)), ((), ())), preferred_element_type=F32)


def dot_nt(a, b):
    return dot(a, b, 1, 1)


def dot_tn(a, b):
    return dot(a, b, 0, 0)


def half(v):
    return v.astype(BF)


def norm(v):
    c = v - jnp.mean(v, axis=-1, keepdims=True)
    inv = lax.rsqrt(jnp.mean(c * c, axis=-1, keepdims=True) + EPS)
    return c * inv, inv


def norm_back(g, gain, n, inv):
    gg = jnp.sum(g * n, axis=0, keepdims=True)
    inner = g * gain
    m1 = jnp.mean(inner, axis=-1, keepdims=True)
    m2 = jnp.mean(inner * n, axis=-1, keepdims=True)
    return inv * (inner - m1 - n * m2), gg


C0, C1 = 0.7978845608028654, 0.044715


def gelu(x):
    return 0.5 * x * (1.0 + jnp.tanh(C0 * (x + C1 * x * x * x)))


def gelu_slope(x):
    t = jnp.tanh(C0 * (x + C1 * x * x * x))
    return 0.5 * (1.0 + t) + 0.5 * x * (1.0 - t * t) * (C0 * (1.0 + 3.0 * C1 * x * x))


def lanes(width):
    return lax.broadcasted_iota(jnp.int32, (1, width), 1)


def head_mask(h):
    lane = lanes(256)
    return jnp.where((lane >= OFF[h]) & (lane < OFF[h] + E), 1.0, 0.0).astype(F32)


def pieces(row, count):
    out = []
    done = 0
    while done < count:
        i, r0 = divmod(row + done, ROWS_I)
        n = min(count - done, ROWS_I - r0)
        out.append((i, r0, done, n))
        done += n
    return out


def split3(v):
    hi = half(v).astype(F32)
    mid = half(v - hi).astype(F32)
    lo = half(v - hi - mid).astype(F32)
    return hi, mid, lo


def pack3(v):
    hi, mid, lo = split3(v)
    return half(hi + pltpu.roll(mid, 16, 1) + pltpu.roll(lo, 32, 1))


def unpack3(v, axis):
    return v + pltpu.roll(v, 112, axis) + pltpu.roll(v, 96, axis)


def as_rows(parts, count):
    row = lax.broadcasted_iota(jnp.int32, (count, 128), 0)
    out = jnp.zeros((count, 128), F32)
    for r, part in parts:
        out = jnp.where(row == r, part, out)
    return out


def call(body, outs, args, scratch=(), vmem=48, flops=0, name=None):
    spaces = {"v": pltpu.VMEM, "a": pl.ANY, "s": pltpu.SMEM, "h": pltpu.HBM}
    return pl.pallas_call(
        body,
        out_shape=[jax.ShapeDtypeStruct(s, t) for s, t, _ in outs],
        in_specs=[pl.BlockSpec(memory_space=spaces[m]) for _, m in args],
        out_specs=[pl.BlockSpec(memory_space=spaces[m]) for _, _, m in outs],
        scratch_shapes=list(scratch),
        compiler_params=pltpu.CompilerParams(vmem_limit_bytes=vmem * MIB),
        cost_estimate=pl.CostEstimate(flops=int(flops), bytes_accessed=4 * MIB, transcendentals=0),
        name=name,
    )(*[a for a, _ in args])


DMA = pltpu.SemaphoreType.DMA


def pack_early_body(sc, lm, bm, la, g0, sem):
    cols = pl.ds(pl.multiple_of(sc[4] * 640, 128), 640)
    copies = [
        (bm.at[0, :, cols], g0.at[0:48, :]),
        (bm.at[1, :, cols], g0.at[48:96, :]),
        (lm.at[0, :, cols], g0.at[96:176, :]),
        (la.at[:, cols], g0.at[176:192, :]),
    ]
    copies = [pltpu.make_async_copy(a, b, sem.at[k]) for k, (a, b) in enumerate(copies)]
    for c in copies:
        c.start()
    for c in copies:
        c.wait()


def pack_body(sc, lm, om, bm, do, wsh, buf, sem):
    i = sc[0]
    blocks = [(80 * k, 80, (om if s == "o" else lm), n, D) for k, (s, n) in enumerate(SQUARE)]
    blocks += [(DEC_ROW, 80, do, None, DI), (BQ_ROW, 48, bm, 2, D)]
    for k in range(NI):
        lo, hi = ROWS_I * k, ROWS_I * (k + 1)

        @pl.when(i == k)
        def _(lo=lo, hi=hi):
            cs = []
            for row, count, ref, n, width in blocks:
                a, b = max(lo, row), min(hi, row + count)
                if a < b:
                    src = ref.at[a - row : b - row, :] if n is None else ref.at[n, a - row : b - row, :]
                    dst = buf.at[a - lo : b - lo, :] if width == D else buf.at[a - lo : b - lo, 0:width]
                    cs.append(pltpu.make_async_copy(src, dst, sem.at[len(cs)]))
            for c in cs:
                c.start()
            for c in cs:
                c.wait()

    out = pltpu.make_async_copy(buf, wsh, sem.at[8])
    out.start()
    out.wait()


def pieces_from(sc, own, sib):
    x, z, core = sc[2], sc[3], sc[4]
    out = []
    for side, (t0, t1, t2a, t2b, t3) in enumerate((own, sib)):
        c = core if side == 0 else 1 - core
        col = pl.ds(pl.multiple_of(c * 640, 128), 640)
        for e in range(4):
            for d in range(4):
                xs = jnp.where(c == 0, (x + 4 - d) & 3, (x + 4 - e) & 3)
                zs = jnp.where(c == 0, (z + 4 - e) & 3, (z + 4 - d) & 3)
                ref = (t0, t1, None, t3)[e] if e != 2 else (t2a, t2b)[d // 2]
                out.append((xs * 4 + zs, col, ref.at[d % 2 if e == 2 else d]))
    return out


def enc_body(
    sc, a0, a1, a2, a3, a4, b0, b1, b2, b3, b4, x_in, bg, lg, g_out, nb_o, k_o, v_o, q_o, pay, n_o, i_o, gs, acc, sem
):
    copies = [
        pltpu.make_async_copy(src, gs.at[pos, :, col], sem.at[k])
        for k, (pos, col, src) in enumerate(pieces_from(sc, (a0, a1, a2, a3, a4), (b0, b1, b2, b3, b4)))
    ]
    for c in copies:
        c.start()
    n_in, _ = norm(x_in[...].astype(F32))
    nb = half(n_in * bg[0:1, :])
    nb_o[...] = nb
    for c in copies:
        c.wait()
    save = pltpu.make_async_copy(gs, g_out, sem.at[32])
    save.start()
    k_o[...] = half(dot(nb, gs[:, 0:48, :].reshape(DI, D)))
    v_o[...] = half(dot(nb, gs[:, 48:96, :].reshape(DI, D)))
    z0b = gs[:, 176:192, :].reshape(R, D)
    nq, inv = norm(z0b.astype(F32))
    n_o[...] = half(nq)
    i_o[...] = jnp.broadcast_to(inv, (R, 128))
    q_o[...] = half(dot(half(nq * lg[0:1, :]), gs[:, 96:176, :].reshape(D, D)))
    acc[...] = jnp.zeros_like(acc)
    valid = lanes(N) + sc[1] * N < sc[5]
    lane = lanes(128)
    stats = jnp.zeros((R, 128), F32)
    for h in range(H):
        w = slice(WIN[h], WIN[h] + 256)
        mk = head_mask(h)
        s = dot_nt(q_o[:, w] * half(mk), k_o[:, w]) * SCALE
        s = jnp.where(valid, s, -1e30)
        m = jnp.max(s, axis=-1, keepdims=True)
        p = jnp.exp(s - m)
        acc[:, w] += dot(half(p), v_o[:, w]) * mk
        stats = jnp.where(lane == h, m, stats)
        stats = jnp.where(lane == 8 + h, jnp.sum(p, axis=-1, keepdims=True), stats)
    pay[:, 0:D] = half(acc[...])
    pay[:, D : D + 128] = pack3(stats)
    save.wait()


def combine_body(rcv, out):
    st = unpack3(rcv[:, :, D : D + 128].astype(F32), 2)
    peak = jnp.max(st, axis=0, keepdims=True)
    w = jnp.exp(st - peak)
    total = jnp.sum(w * pltpu.roll(st, 120, 2), axis=0, keepdims=True)
    coef = w / total
    lane = lax.broadcasted_iota(jnp.int32, (1, 1, 128), 2)
    for t in range(10):
        h0, h1 = 128 * t // E, (128 * t + 127) // E
        c = coef[:, :, h0 : h0 + 1]
        if h1 != h0:
            c = jnp.where(lane >= E * h1 - 128 * t, coef[:, :, h1 : h1 + 1], c)
        o = jnp.sum(rcv[:, :, 128 * t : 128 * t + 128].astype(F32) * c, axis=0)
        out[:, 128 * t : 128 * t + 128] = half(o)
    lse = jnp.where(lanes(128) < 8, (peak + jnp.log(total))[0], 0.0)
    out[:, D : D + 128] = pack3(lse)


class Ring:
    def __init__(self, w, slots, sem, order):
        self.w, self.slots, self.sem, self.order = w, slots, sem, order
        self.n = slots.shape[0]
        self.pos = {m: k for k, m in enumerate(order)}

    def copies(self, m):
        s = self.pos[m] % self.n
        return [
            pltpu.make_async_copy(
                self.w.at[i, :, r0 : r0 + n, :], self.slots.at[s, :, d0 : d0 + n, :], self.sem.at[s, k]
            )
            for k, (i, r0, d0, n) in enumerate(pieces(80 * m, 80))
        ]

    def start(self, m):
        for c in self.copies(m):
            c.start()

    def begin(self):
        for m in self.order[: self.n]:
            self.start(m)

    def get(self, m):
        for c in self.copies(m):
            c.wait()
        return self.slots[self.pos[m] % self.n].reshape(D, D)

    def done(self, m):
        k = self.pos[m] + self.n
        if k < len(self.order):
            self.start(self.order[k])


def forward_body(
    qin, cot, bg, lg, e_h, g_all, w,
    res, gqin, gain_o, pay, mix_o, nd_o, gq_o, z_h, h_h, a_h,
    slots, e, z0b, zs, zb, hs, qs, acc, kd, vd, dec, bq, dacc, gq, gkv, wsem, ssem, lsem,
):
    first = [
        pltpu.make_async_copy(e_h.at[:, 0:D], e, lsem.at[3]),
        pltpu.make_async_copy(g_all.at[:, 176:192, :], z0b, lsem.at[4]),
    ]
    for c in first:
        c.start()
    ring = Ring(w, slots, wsem, list(range(11)))
    ring.begin()
    copies = []
    for i, r0, d0, n in pieces(BQ_ROW, 48):
        copies.append(pltpu.make_async_copy(w.at[i, :, r0 : r0 + n, :], bq.at[:, d0 : d0 + n, :], lsem.at[0]))
    for i, r0, d0, n in pieces(DEC_ROW, 80):
        copies.append(
            pltpu.make_async_copy(w.at[i, :, r0 : r0 + n, 0:DI], dec.at[:, d0 : d0 + n, :], lsem.at[len(copies)])
        )
    for c in copies:
        c.start()
    saves = []

    def save(src, dst):
        c = pltpu.make_async_copy(src, dst, ssem.at[len(saves)])
        c.start()
        saves.append(c)

    def keep(k):
        zb[k] = half(zs[k])
        save(zb.at[k], z_h.at[k])

    def mul(a, m):
        out = dot(a, ring.get(m))
        ring.done(m)
        return out

    for c in first:
        c.wait()
    z1 = z0b[...].reshape(R, D).astype(F32) + mul(e[...], 0)
    zs[0] = z1
    keep(0)
    h1 = mul(half(norm(z1)[0] * lg[1:2, :]), 1)
    hs[0] = half(h1)
    save(hs.at[0], h_h.at[0])
    zs[1] = zs[0] + mul(half(gelu(h1)), 2)
    keep(1)
    s_b = half(norm(zs[1])[0] * lg[2:3, :])
    for k in range(3):
        qs[k] = half(mul(s_b, 3 + k))
        save(qs.at[k], a_h.at[k])
    acc[...] = jnp.zeros_like(acc)
    for h in range(H):
        win = slice(WIN[h], WIN[h] + 256)
        mk = head_mask(h)
        s = dot_nt(qs[0, :, win] * half(mk), qs[1, :, win]) * SCALE
        p = jnp.exp(s - jnp.max(s, axis=-1, keepdims=True))
        p = p / jnp.sum(p, axis=-1, keepdims=True)
        acc[:, win] += dot(half(p), qs[2, :, win]) * mk
    qs[3] = half(acc[...])
    save(qs.at[3], a_h.at[3])
    zs[2] = zs[1] + mul(qs[3], 6)
    keep(2)
    h2 = mul(half(norm(zs[2])[0] * lg[3:4, :]), 7)
    hs[1] = half(h2)
    save(hs.at[1], h_h.at[1])
    zs[3] = zs[2] + mul(half(gelu(h2)), 8)
    keep(3)
    c_b = half(norm(zs[3])[0] * lg[4:5, :])
    kd[...] = half(mul(c_b, 9))
    vd[...] = half(mul(c_b, 10))

    x = qin[...].astype(F32)
    n, inv = norm(x)
    nd = half(n * bg[1:2, :])
    nd_o[...] = nd
    for c in copies:
        c.wait()
    wq = bq[...].reshape(DI, D)
    wd = dec[...].reshape(D, DI)
    gq_o[...] = half(dot(nd, wq))
    mix_o[...] = half(dot_nt(cot[...], wd))
    dacc[...] = jnp.zeros_like(dacc)
    gq[...] = jnp.zeros_like(gq)
    gkv[...] = jnp.zeros_like(gkv)
    for h in range(H):
        win = slice(WIN[h], WIN[h] + 256)
        mk = head_mask(h)
        mkb = half(mk)
        qw, gw, kw, vw = gq_o[:, win], mix_o[:, win], kd[:, win], vd[:, win]
        s = dot_nt(qw * mkb, kw) * SCALE
        p = jnp.exp(s - jnp.max(s, axis=-1, keepdims=True))
        p = p / jnp.sum(p, axis=-1, keepdims=True)
        pb = half(p)
        dacc[:, win] += dot(pb, vw) * mk
        dp = dot_nt(gw * mkb, vw)
        ds = half(p * (dp - jnp.sum(p * dp, axis=-1, keepdims=True)))
        gq[:, win] += dot(ds, kw) * mk
        gkv[0, :, win] += dot_tn(ds, qw) * mk
        gkv[1, :, win] += dot_tn(pb, gw) * mk
    pay[:, 0:D] = half(gkv[0] * SCALE)
    pay[:, D : 2 * D] = half(gkv[1])
    mix = half(dacc[...])
    mix_o[...] = mix
    res[...] = half(x + dot(mix, wd))
    gqb = half(gq[...] * SCALE)
    gq_o[...] = gqb
    gin, gg = norm_back(dot_nt(gqb, wq), bg[1:2, :], n, inv)
    gqin[...] = cot[...].astype(F32) + gin
    gain_o[...] = gg
    for c in saves:
        c.wait()


def prepare_body(lg, z_h, h_h, a_h, n_h, i_h, s_h, act_h, p_h, zs, hs, qs, ns, vs, ss, acts, ps, sem, osem):
    loads = {}
    for k in range(4):
        loads["z", k] = pltpu.make_async_copy(z_h.at[k], zs.at[k], sem.at[k])
    for k in range(2):
        loads["h", k] = pltpu.make_async_copy(h_h.at[k], hs.at[k], sem.at[4 + k])
    loads["q"] = pltpu.make_async_copy(a_h.at[0:2], qs, sem.at[6])
    for c in loads.values():
        c.start()
    saves = []

    def save(src, dst):
        c = pltpu.make_async_copy(src, dst, osem.at[len(saves)])
        c.start()
        saves.append(c)

    for k, a in ((3, 0), (2, 2), (1, 1), (0, 4)):
        loads["z", k].wait()
        n, inv = norm(zs[k].astype(F32))
        ns[k] = half(n)
        save(ns.at[k], n_h.at[k])
        vs[k] = jnp.broadcast_to(inv, (R, 128))
        acts[a] = half(n * lg[k + 1 : k + 2, :])
        save(acts.at[a], act_h.at[a])
    save(vs, i_h)
    for k, a in ((1, 3), (0, 5)):
        loads["h", k].wait()
        x = hs[k].astype(F32)
        t = jnp.tanh(C0 * (x + C1 * x * x * x))
        acts[a] = half(0.5 * x * (1.0 + t))
        save(acts.at[a], act_h.at[a])
        ss[k] = 0.5 * (1.0 + t) + 0.5 * x * (1.0 - t * t) * (C0 * (1.0 + 3.0 * C1 * x * x))
        save(ss.at[k], s_h.at[k])
    loads["q"].wait()
    for h in range(H):
        win = slice(WIN[h], WIN[h] + 256)
        s = dot_nt(qs[0, :, win] * half(head_mask(h)), qs[1, :, win]) * SCALE
        p = jnp.exp(s - jnp.max(s, axis=-1, keepdims=True))
        ps[h] = half(p / jnp.sum(p, axis=-1, keepdims=True))
    save(ps, p_h)
    for c in saves:
        c.wait()


def lat_backward_body(
    sc, gin, lg, w, e_h, n_h, i_h, s_h, act_h, a_h, p_h, gmix, pack_o, g1c_o, gains_o,
    slots, ns, vs, ss, acts, qs, ps, acc, acc2, acc3, gh, gw, wsem, lsem,
):
    order = [8, 7, 6, 3, 4, 5, 2, 1, 0]
    ring = Ring(w, slots, wsem, order)
    todo = [
        (i_h, vs),
        (act_h.at[0], acts.at[0]),
        (s_h.at[1], ss.at[1]),
        (act_h.at[3], acts.at[1]),
        (n_h.at[2], ns.at[2]),
        (act_h.at[2], acts.at[3]),
        (a_h.at[3], acts.at[4]),
        (p_h, ps),
        (a_h.at[0:3], qs.at[0:3]),
        (n_h.at[1], ns.at[1]),
        (act_h.at[1], acts.at[2]),
        (s_h.at[0], ss.at[0]),
        (act_h.at[5], acts.at[5]),
        (n_h.at[0], ns.at[0]),
        (act_h.at[4], acts.at[6]),
        (e_h.at[:, 0:D], acts.at[7]),
    ]
    loads = [pltpu.make_async_copy(a, b, lsem.at[k]) for k, (a, b) in enumerate(todo)]
    after = {8: (4, 5, 6), 7: (7, 8), 6: (9, 10, 11, 12), 3: (13, 14, 15)}
    ring.start(8)
    for c in loads[:4]:
        c.start()
    for m in order[1 : ring.n]:
        ring.start(m)

    def ready(*ks):
        for k in ks:
            loads[k].wait()

    src = sc[1] * 80
    start = pl.multiple_of(jnp.minimum((src >> 7) * 128, 1024), 128)
    offset = src - start
    lane = lanes(256)

    def put(ref, to):
        v = pltpu.roll(ref[:, pl.ds(start, 256)].astype(F32), (to - offset + 256) & 255, 1)
        return jnp.where((lane >= to) & (lane < to + 80), v, 0.0)

    def weight_grad(window, first, count):
        a = acts[first : first + count].reshape(count * R, D)
        pack_o[:, 256 * window : 256 * window + 256] = half(dot_tn(a, gw[first : first + count].reshape(count * R, 256)))

    def mul(g_b, m):
        out = dot_nt(g_b, ring.get(m))
        ring.done(m)
        for k in after.get(m, ()):
            loads[k].start()
        return out

    gain_rows = []

    def back(g, k):
        out, gg = norm_back(g, lg[k + 1 : k + 2, :], ns[k].astype(F32), vs[k][:, 0:1])
        for t in range(10):
            gain_rows.append((10 * k + t, gg[:, 128 * t : 128 * t + 128]))
        return out

    for t in range(10):
        acc[:, 128 * t : 128 * t + 128] = gin[:, 16 * t : 16 * t + 16, :].reshape(R, 128).astype(F32)
    tile = lanes(128)
    values = pltpu.roll(gin[:, 176:192, :].reshape(R, 128).astype(F32), 80, 1)
    gw[0, :, 0:128] = half(jnp.where(tile < 80, gin[:, 160:176, :].reshape(R, 128).astype(F32), values))
    gw[0, :, 128:256] = half(jnp.where(tile < 32, values, 0.0))
    gw[1] = half(put(acc, 160))
    ready(0, 1, 2, 3)
    gh[...] = half(mul(half(acc[...]), 8) * ss[1])
    weight_grad(0, 0, 2)
    ready(4)
    gw[3] = half(put(gh, 0))
    acc[...] += back(mul(gh[...], 7), 2)
    gw[4] = half(put(acc, 80))
    qs[3] = half(mul(half(acc[...]), 6))
    acc2[...] = jnp.zeros_like(acc2)
    acc3[...] = jnp.zeros_like(acc3)
    ready(5, 6, 7, 8)
    for h in range(H):
        win = slice(WIN[h], WIN[h] + 256)
        mk = head_mask(h)
        pb = ps[h]
        p = pb.astype(F32)
        dp = dot_nt(qs[3, :, win] * half(mk), qs[2, :, win])
        ds = half(p * (dp - jnp.sum(p * dp, axis=-1, keepdims=True)) * SCALE)
        acc2[:, win] += dot(ds, qs[1, :, win]) * mk
        acc3[0, :, win] += dot_tn(ds, qs[0, :, win]) * mk
        acc3[1, :, win] += dot_tn(pb, qs[3, :, win]) * mk
    gw[2] = half(put(acc2, 0) + put(acc3.at[0], 80) + put(acc3.at[1], 160))
    gn = mul(half(acc2[...]), 3)
    gn = gn + mul(half(acc3[0]), 4)
    gn = gn + mul(half(acc3[1]), 5)
    ready(9, 10)
    weight_grad(1, 2, 1)
    acc[...] += back(gn, 1)
    gw[5] = half(put(acc, 160))
    ready(11, 12)
    gh[...] = half(mul(half(acc[...]), 2) * ss[0])
    weight_grad(2, 3, 3)
    gw[6] = half(put(gh, 0))
    ready(13, 14, 15)
    acc[...] += back(mul(gh[...], 1), 0)
    gw[7] = half(put(acc, 80))
    g1c_o[...] = half(put(acc, 0)[:, 0:128])
    gmix[...] = half(mul(half(acc[...]), 0))
    weight_grad(3, 6, 2)
    gains_o[...] = as_rows(gain_rows, 32)


def key_value_back_body(sc, rcv, lg, n_h, i_h, w, out, gain_o, wbuf, nbuf, ibuf, sem):
    rows = pl.ds(pl.multiple_of(sc[1] * 16, 16), 16)
    copies = []
    for k, m in enumerate((9, 10)):
        for i, r0, d0, n in pieces(80 * m, 80):
            copies.append((w.at[i, :, r0 : r0 + n, :], wbuf.at[k, :, d0 : d0 + n, :]))
    copies += [(n_h.at[3, rows, :], nbuf), (i_h.at[3, rows, :], ibuf)]
    copies = [pltpu.make_async_copy(a, b, sem.at[k]) for k, (a, b) in enumerate(copies)]
    for c in copies:
        c.start()
    s = half(jnp.sum(rcv[...].astype(F32), axis=0))
    for j in range(NJ):
        base = min(128 * (80 * j // 128), 1024)
        for k in range(2):
            v = s[:, D * k + base : D * k + base + 256].astype(F32)
            if 80 * j > base:
                v = pltpu.roll(v, 256 - (80 * j - base), 1)
            out[j, 160 + 16 * k : 176 + 16 * k, :] = half(v[:, 0:128])
    for c in copies:
        c.wait()
    gn = dot_nt(s[:, 0:D], wbuf[0].reshape(D, D)) + dot_nt(s[:, D : 2 * D], wbuf[1].reshape(D, D))
    g, gg = norm_back(gn, lg[4:5, :], nbuf[...].astype(F32), ibuf[:, 0:1])
    gain_o[...] = gg
    g = jnp.concatenate([half(g[:, 128 * t : 128 * t + 128]) for t in range(10)], axis=0)
    for j in range(NJ):
        out[j, 0:160, :] = g


def dec_weights_body(mix, cot, nd, gq, out, buf, sem):
    g = half(dot_tn(mix[...], cot[...]))
    for i in range(NI):
        for t in range(6):
            buf[i, 160 * t : 160 * t + 160, :] = g[160 * i : 160 * i + 160, 128 * t : 128 * t + 128]
    one = pltpu.make_async_copy(buf.at[:, 0:960, :], out.at[:, 0:960, :], sem.at[0])
    one.start()
    g = half(dot_tn(nd[...], gq[...]))
    for i in range(NI):
        for t in range(10):
            r = 960 + 96 * t
            buf[i, r : r + 96, :] = g[96 * i : 96 * i + 96, 128 * t : 128 * t + 128]
    two = pltpu.make_async_copy(buf.at[:, 960:1920, :], out.at[:, 960:1920, :], sem.at[1])
    two.start()
    one.wait()
    two.wait()


def spread(chunk, pay, td, tb):
    fill = jnp.zeros((96, 128), F32)
    for t in range(6):
        v = jnp.concatenate([chunk[160 * t : 160 * t + 160, :].astype(F32), fill], axis=0)
        td[128 * t : 128 * t + 128, :] = v.T
    fill = jnp.zeros((32, 128), F32)
    for t in range(10):
        v = jnp.concatenate([chunk[960 + 96 * t : 960 + 96 * t + 96, :].astype(F32), fill], axis=0)
        tb[128 * t : 128 * t + 128, :] = v.T
    for j in range(NJ):
        tail = pltpu.roll(td[48 * j : 48 * j + 48, 128:256], 96, 1)
        pay[j, 512:560, :] = half(tb[80 * j : 80 * j + 48, :] + tail)
        pay[j, 560:592, :] = half(tb[80 * j + 48 : 80 * j + 80, :])
        pay[j, 592:640, :] = half(td[48 * j : 48 * j + 48, 0:128])


def enc_back_body(
    sc, x_in, bg, lg, gd, gc, gmix_h, e_h, q_h, k_h, v_h, g_all, dw_h, n0_h, i0_h, gin_o, pay,
    gmix, e, q, k, v, wkv, n0, i0, gq, gkt, gvt, dw, td, tb, sem,
):
    pairs = [(gmix_h, gmix), (q_h, q), (k_h, k), (v_h, v), (e_h, e), (g_all, wkv), (dw_h, dw), (n0_h, n0), (i0_h, i0)]
    loads = [pltpu.make_async_copy(a, b, sem.at[n]) for n, (a, b) in enumerate(pairs)]
    for c in loads:
        c.start()
    for c in loads[:5]:
        c.wait()
    lse = unpack3(e[:, D : D + 128].astype(F32), 1)
    valid = lanes(N) + sc[1] * N < sc[5]
    gq[...] = jnp.zeros_like(gq)
    for h in range(H):
        win = slice(WIN[h], WIN[h] + 256)
        mk = head_mask(h)
        mkb = half(mk)
        qw, gw, kw, vw = q[:, win], gmix[:, win], k[:, win], v[:, win]
        rd = jnp.sum(gw.astype(F32) * e[:, win].astype(F32) * mk, axis=-1, keepdims=True)
        s = dot_nt(qw * mkb, kw) * SCALE
        p = jnp.where(valid, jnp.exp(jnp.where(valid, s, -1e30) - lse[:, h : h + 1]), 0.0)
        dp = dot_nt(gw * mkb, vw)
        ds = half(p * (dp - rd))
        gq[:, win] += dot(ds, kw) * mk
        o = OFF[h]
        gkt[E * h : E * h + E, :] = half(dot_tn(qw, ds)[o : o + E, :] * SCALE)
        gvt[E * h : E * h + E, :] = half(dot_tn(gw, half(p))[o : o + E, :])
    pay[:, 320:400, :] = gkt[...].reshape(NJ, 80, 128)
    pay[:, 400:480, :] = gvt[...].reshape(NJ, 80, 128)
    loads[5].wait()
    gqs = gq[...] * SCALE
    gqt = half(gqs.T)
    pay[:, 160:240, :] = gqt[:, 0:128].reshape(NJ, 80, 128)
    pay[:, 240:320, :] = gqt[:, 128:256].reshape(NJ, 80, 128)
    loads[7].wait()
    loads[8].wait()
    gz, g0 = norm_back(dot_nt(half(gqs), wkv[:, 96:176, :].reshape(D, D)), lg[0:1, :], n0[...].astype(F32), i0[:, 0:1])
    gzt = half(gz.T)
    pay[:, 0:80, :] = gzt[:, 0:128].reshape(NJ, 80, 128)
    pay[:, 80:160, :] = gzt[:, 128:256].reshape(NJ, 80, 128)
    n, inv = norm(x_in[...].astype(F32))
    gnt = dot(wkv[:, 0:48, :].reshape(DI, D), gkt[...]) + dot(wkv[:, 48:96, :].reshape(DI, D), gvt[...])
    gin, gg = norm_back(gnt.T, bg[0:1, :], n, inv)
    gin_o[...] = gin
    rows = [(t, gg[:, 128 * t : 128 * t + 128]) for t in range(6)]
    rows += [(6 + t, gd[:, 128 * t : 128 * t + 128]) for t in range(6)]
    rows += [(12 + t, g0[:, 128 * t : 128 * t + 128]) for t in range(10)]
    rows += [(22 + t, gc[:, 128 * t : 128 * t + 128]) for t in range(10)]
    g = half(as_rows(rows, 32))
    for j in range(NJ):
        pay[j, 480:512, :] = g
    loads[6].wait()
    spread(dw, pay, td, tb)


def tail_one_body(rcv, nf_h, n0_h, lg, lat_gain, g1c, out, dec_o, bq_o, nf, n0, left, sem):
    loads = [
        pltpu.make_async_copy(nf_h, nf, sem.at[0]),
        pltpu.make_async_copy(n0_h, n0, sem.at[1]),
    ]
    for c in loads:
        c.start()
    sums = jnp.sum(rcv[:, 0:320, :].astype(F32), axis=0)
    fill = jnp.zeros((48, 128), F32)
    left[...] = jnp.zeros_like(left)
    for s in range(NJ):
        left[0:80, 128 * s : 128 * s + 128] = rcv[s, 320:400, :]
        left[128:208, 128 * s : 128 * s + 128] = rcv[s, 400:480, :]
    loads[1].wait()
    nq = half(n0[...].astype(F32) * lg[0:1, :])
    a = jnp.concatenate([sums[160:240], fill], axis=0).T
    b = jnp.concatenate([sums[240:320], fill], axis=0).T
    w0 = dot_tn(nq, half(jnp.concatenate([a, b], axis=0)))
    a = jnp.concatenate([sums[0:80], fill], axis=0).T
    b = jnp.concatenate([sums[80:160], fill], axis=0).T
    gz = half(jnp.concatenate([a, b], axis=0) + g1c[...].astype(F32))
    gains = jnp.sum(rcv[:, 480:512, :].astype(F32), axis=0)
    gains = half(jnp.concatenate([gains, lat_gain[...]], axis=0))
    loads[0].wait()
    wt = dot(left[...], nf[...]).T
    lane = lanes(128)
    key, value = wt[:, 0:128], wt[:, 128:256]
    one = half(jnp.where(lane < 80, key, pltpu.roll(value, 80, 1)))
    other = pltpu.roll(value, 32, 1)
    for i in range(NI):
        r = 96 * i
        beside = jnp.concatenate([other[r : r + 96, :], jnp.zeros((64, 128), F32)], axis=0)
        out[i, 0:160, :] = half(jnp.where(lane < 80, w0[160 * i : 160 * i + 160, :], beside))
        out[i, 160:192, :] = gz[32 * i : 32 * i + 32, :]
        out[i, 192:288, :] = one[r : r + 96, :]
        out[i, 288:352, :] = gains
    s = jnp.sum(rcv[:, 512:640, :].astype(F32), axis=0)
    bq_o[...] = s[0:80, 0:96]
    dec_o[:, 0:128] = s[80:128]
    dec_o[:, 128:160] = pltpu.roll(s[0:48], 32, 1)[:, 0:32]


def tail_two_body(rcv, pack_h, bq, arr_o, lm_o, om_o, bm_o, lat_o, byte_o, pack, sem):
    load = pltpu.make_async_copy(pack_h, pack, sem)
    load.start()
    sums = jnp.sum(rcv[...].astype(F32), axis=0)
    lm_o[0] = sums[0:160, 0:80]
    arr_o[...] = sums[160:192, 0:80]
    lane = lanes(128)
    value = jnp.where(lane < 48, pltpu.roll(sums[192:288], 48, 1), pltpu.roll(sums[0:96], 96, 1))
    fill = jnp.zeros((32, 128), F32)
    bm_o[0] = jnp.concatenate([sums[192:288], fill], axis=0).T[0:80, 0:96]
    bm_o[1] = jnp.concatenate([value, fill], axis=0).T[0:80, 0:96]
    bm_o[2] = bq[...]
    g = sums[288:352]
    for t in range(6):
        for b in range(2):
            byte_o[b : b + 1, 128 * t : 128 * t + 128] = g[6 * b + t : 6 * b + t + 1, :]
    for t in range(10):
        for b in range(5):
            r = {0: 12, 1: 32, 2: 42, 3: 52, 4: 22}[b] + t
            lat_o[b : b + 1, 128 * t : 128 * t + 128] = g[r : r + 1, :]
    load.wait()
    for m, (kind, n) in enumerate(SQUARE):
        window, o = PLACE[m]
        v = pack[:, 256 * window : 256 * window + 256].astype(F32)
        if o:
            v = pltpu.roll(v, 256 - o, 1)
        if kind == "l":
            lm_o[n] = v[:, 0:80]
        else:
            om_o[n] = v[:, 0:80]


def line(y, c, x, z):
    return ((y % 4) * 2 + c) * NJ + (x % 4) * NZ + (z % 4)


EVERY = [(y, c, x, z) for y in range(4) for c in range(2) for x in range(NX) for z in range(NZ)]


def along(stage, d):
    out = []
    for y, c, x, z in EVERY:
        on_x = (c == 0) == (stage == 0)
        out.append((line(y, c, x, z), line(y, c, x + d, z) if on_x else line(y, c, x, z + d)))
    return out


SWAP = [(line(y, c, x, z), line(y, 1 - c, x, z)) for y, c, x, z in EVERY]


def exchange(v, axes):
    flat = v.reshape(v.shape[0] * v.shape[1], v.shape[2])
    return lax.all_to_all(flat, axes, split_axis=0, concat_axis=0, tiled=True).reshape(v.shape)


def shards(inputs, queries, lengths, latent_array, latent_mats, out_mats, byte_mats, dec_out, lg, bg, cotangent):
    y, core, x, z = (lax.axis_index(a) for a in AXES)
    i, j = y * 2 + core, x * NZ + z
    sc = jnp.stack([i, j, x, z, core, lengths[0]]).astype(jnp.int32)
    xin, qin, cot = inputs[0], queries[0], cotangent[0]

    (wsh,) = call(
        pack_body,
        [((ROWS_I, D), BF, "h")],
        [(sc, "s"), (latent_mats, "h"), (out_mats, "h"), (byte_mats, "h"), (dec_out, "h")],
        [pltpu.VMEM((ROWS_I, D), BF), DMA((9,))],
        vmem=60,
        name="pack",
    )
    (g0,) = call(
        pack_early_body,
        [((192, 640), BF, "v")],
        [(sc, "s"), (latent_mats, "h"), (byte_mats, "h"), (latent_array, "h")],
        [DMA((4,))],
        vmem=60,
        name="pack_early",
    )
    w = lax.all_gather(wsh, AXES, axis=0, tiled=True).reshape(NI, NJ, ROWS_I, D)

    s0 = jnp.stack([g0] + [lax.ppermute(g0, AXES, along(0, d)) for d in (1, 2, 3)])
    t1, t3 = (lax.ppermute(s0, AXES, along(1, d)) for d in (1, 3))
    t2a, t2b = lax.ppermute(t1[0:2], AXES, along(1, 1)), lax.ppermute(t3[2:4], AXES, along(1, 3))
    own = [s0, t1, t2a, t2b, t3]
    sib = [lax.ppermute(v, AXES, SWAP) for v in own]
    g_all, nb, k_b, v_b, q_b, pay, n0, i0 = call(
        enc_body,
        [
            ((NJ, 192, D), BF, "h"),
            ((N, DI), BF, "v"),
            ((N, D), BF, "v"),
            ((N, D), BF, "v"),
            ((R, D), BF, "v"),
            ((R, D + 128), BF, "v"),
            ((R, D), BF, "v"),
            ((R, 128), F32, "v"),
        ],
        [(sc, "s")] + [(v, "a") for v in own + sib] + [(xin, "v"), (bg, "v"), (lg, "v")],
        [pltpu.VMEM((NJ, 192, D), BF), pltpu.VMEM((R, D), F32), DMA((33,))],
        vmem=60,
        flops=3e9,
        name="enc",
    )
    rcv = exchange(pay.reshape(NJ, 16, D + 128), BLK)
    (mine,) = call(combine_body, [((16, D + 128), BF, "v")], [(rcv, "v")], name="combine")
    e = lax.all_gather(mine, BLK, axis=0, tiled=True)

    big = (NJ, 80, D)
    res, gqin, gd, dpay, mix, nd, gq, z_h, h_h, a_h = call(
        forward_body,
        [
            ((N, DI), BF, "v"),
            ((N, DI), F32, "v"),
            ((1, DI), F32, "v"),
            ((R, 2 * D), BF, "v"),
            ((N, D), BF, "v"),
            ((N, DI), BF, "v"),
            ((N, D), BF, "v"),
            ((4, R, D), BF, "h"),
            ((2, R, D), BF, "h"),
            ((4, R, D), BF, "h"),
        ],
        [(qin, "v"), (cot, "v"), (bg, "v"), (lg, "v"), (e, "h"), (g_all, "h"), (w, "h")],
        [
            pltpu.VMEM((3,) + big, BF),
            pltpu.VMEM((R, D), BF),
            pltpu.VMEM((NJ, 16, D), BF),
            pltpu.VMEM((4, R, D), F32),
            pltpu.VMEM((4, R, D), BF),
            pltpu.VMEM((2, R, D), BF),
            pltpu.VMEM((4, R, D), BF),
            pltpu.VMEM((R, D), F32),
            pltpu.VMEM((R, D), BF),
            pltpu.VMEM((R, D), BF),
            pltpu.VMEM((NJ, 80, DI), BF),
            pltpu.VMEM((NJ, 48, D), BF),
            pltpu.VMEM((N, D), F32),
            pltpu.VMEM((N, D), F32),
            pltpu.VMEM((2, R, D), F32),
            DMA((3, 2)),
            DMA((10,)),
            DMA((5,)),
        ],
        vmem=54,
        flops=1.5e10,
        name="forward",
    )
    rows = exchange(dpay.reshape(NJ, 16, 2 * D), BLK)
    n_h, i_h, s_h, act_h, p_h = call(
        prepare_body,
        [
            ((4, R, D), BF, "h"),
            ((4, R, 128), F32, "h"),
            ((2, R, D), F32, "h"),
            ((6, R, D), BF, "h"),
            ((H, R, R), BF, "h"),
        ],
        [(lg, "v"), (z_h, "h"), (h_h, "h"), (a_h, "h")],
        [
            pltpu.VMEM((4, R, D), BF),
            pltpu.VMEM((2, R, D), BF),
            pltpu.VMEM((2, R, D), BF),
            pltpu.VMEM((4, R, D), BF),
            pltpu.VMEM((4, R, 128), F32),
            pltpu.VMEM((2, R, D), F32),
            pltpu.VMEM((6, R, D), BF),
            pltpu.VMEM((H, R, R), BF),
            DMA((7,)),
            DMA((14,)),
        ],
        vmem=58,
        flops=5e9,
        name="prepare",
    )
    (dw,) = call(
        dec_weights_body,
        [((NI, 1920, 128), BF, "h")],
        [(mix, "v"), (cot, "v"), (nd, "v"), (gq, "v")],
        [pltpu.VMEM((NI, 1920, 128), BF), DMA((2,))],
        vmem=60,
        flops=4e9,
        name="dec_weights",
    )
    kv, gc = call(
        key_value_back_body,
        [((NJ, 192, 128), BF, "v"), ((1, D), F32, "v")],
        [(sc, "s"), (rows, "v"), (lg, "v"), (n_h, "h"), (i_h, "h"), (w, "h")],
        [pltpu.VMEM((2,) + big, BF), pltpu.VMEM((16, D), BF), pltpu.VMEM((16, 128), F32), DMA((6,))],
        vmem=58,
        flops=1e8,
        name="key_value_back",
    )
    gin4 = exchange(kv, BLK)
    nb, _ = lax.optimization_barrier((nb, gin4))
    nf = lax.all_gather(nb, BLK, axis=0, tiled=True)
    dw = lax.psum_scatter(dw.reshape(NI * 1920, 128), BATCH, scatter_dimension=0, tiled=True)

    gmix, pack, g1c, lat_gain = call(
        lat_backward_body,
        [((R, D), BF, "v"), ((D, 1024), BF, "v"), ((R, 128), BF, "v"), ((32, 128), F32, "v")],
        [(sc, "s"), (gin4, "v"), (lg, "v")] + [(v, "h") for v in (w, e, n_h, i_h, s_h, act_h, a_h, p_h)],
        [
            pltpu.VMEM((2,) + big, BF),
            pltpu.VMEM((4, R, D), BF),
            pltpu.VMEM((4, R, 128), F32),
            pltpu.VMEM((2, R, D), F32),
            pltpu.VMEM((8, R, D), BF),
            pltpu.VMEM((4, R, D), BF),
            pltpu.VMEM((H, R, R), BF),
            pltpu.VMEM((R, D), F32),
            pltpu.VMEM((R, D), F32),
            pltpu.VMEM((2, R, D), F32),
            pltpu.VMEM((R, D), BF),
            pltpu.VMEM((8, R, 256), BF),
            DMA((2, 2)),
            DMA((16,)),
        ],
        vmem=60,
        flops=8e10,
        name="lat_backward",
    )
    pack = lax.psum_scatter(pack, BATCH, scatter_dimension=0, tiled=True)
    gin, epay = call(
        enc_back_body,
        [((N, DI), F32, "v"), ((NJ, 640, 128), BF, "v")],
        [(sc, "s"), (xin, "v"), (bg, "v"), (lg, "v"), (gd, "v"), (gc, "v")]
        + [(v, "h") for v in (gmix, e, q_b, k_b, v_b, g_all, dw, n0, i0)],
        [
            pltpu.VMEM((R, D), BF),
            pltpu.VMEM((R, D + 128), BF),
            pltpu.VMEM((R, D), BF),
            pltpu.VMEM((N, D), BF),
            pltpu.VMEM((N, D), BF),
            pltpu.VMEM((NJ, 192, D), BF),
            pltpu.VMEM((R, D), BF),
            pltpu.VMEM((R, 128), F32),
            pltpu.VMEM((R, D), F32),
            pltpu.VMEM((D, N), BF),
            pltpu.VMEM((D, N), BF),
            pltpu.VMEM((1920, 128), BF),
            pltpu.VMEM((DI, 256), F32),
            pltpu.VMEM((D, 128), F32),
            DMA((9,)),
        ],
        vmem=58,
        flops=3e9,
        name="enc_back",
    )
    r1 = exchange(epay, BLK)
    p2, dec_grad, bq_grad = call(
        tail_one_body,
        [((NI, 352, 128), BF, "v"), ((48, 160), F32, "v"), ((80, 96), F32, "v")],
        [(r1, "v"), (nf, "h"), (n0, "h"), (lg, "v"), (lat_gain, "v"), (g1c, "v")],
        [pltpu.VMEM((NJ * N, DI), BF), pltpu.VMEM((R, D), BF), pltpu.VMEM((256, 2048), BF), DMA((2,))],
        vmem=52,
        name="tail_one",
    )
    r2 = exchange(p2, BATCH)
    arr, lm, om, byte_grads, lat_gains, byte_gain = call(
        tail_two_body,
        [
            ((32, 80), F32, "v"),
            ((10, 160, 80), F32, "v"),
            ((2, 160, 80), F32, "v"),
            ((3, 80, 96), F32, "v"),
            ((5, D), F32, "v"),
            ((2, DI), F32, "v"),
        ],
        [(r2, "v"), (pack, "h"), (bq_grad, "v")],
        [pltpu.VMEM((160, 1024), BF), DMA],
        name="tail_two",
    )
    byte_grads = jnp.swapaxes(byte_grads, 1, 2)
    return (res[None], gin[None], gqin[None], arr, lm, om, byte_grads, dec_grad.T, lat_gains, byte_gain)


def solution(mesh):
    grid = Mesh(mesh.devices.reshape(4, 2, NX, NZ), AXES)
    return jax.shard_map(
        shards,
        mesh=grid,
        in_specs=(
            P(BATCH, BLK, None),
            P(BATCH, BLK, None),
            P(BATCH),
            P(BLK, None),
            P(None, BLK, None),
            P(None, BLK, None),
            P(None, BLK, None),
            P(BLK, None),
            P(),
            P(),
            P(BATCH, BLK, None),
        ),
        out_specs=(
            P(BATCH, BLK, None),
            P(BATCH, BLK, None),
            P(BATCH, BLK, None),
            P(BATCH, BLK),
            P(None, BATCH, BLK),
            P(None, BATCH, BLK),
            P(None, BATCH, BLK),
            P(BATCH, BLK),
            P(),
            P(),
        ),
        check_vma=False,
    )
```

```python
import jax
import jax.numpy as jnp
from jax import lax
from jax.experimental import pallas as pl
from jax.experimental.pallas import tpu as pltpu
from jax.sharding import Mesh, PartitionSpec as P

F32, BF = jnp.float32, jnp.bfloat16
D, DI, R, N, H, E = 1280, 768, 256, 128, 8, 160
NX, NZ, NJ, NI = 4, 4, 16, 8
SCALE = E**-0.5
EPS = 1e-5
MIB = 1 << 20
AXES = ("y", "core", "x", "z")
BATCH = ("y", "core")
BLK = ("x", "z")
WIN = [128 * (E * h // 128) for h in range(H)]
OFF = [E * h - WIN[h] for h in range(H)]
SQUARE = [("o", 0), ("l", 1), ("l", 2), ("l", 3), ("l", 4), ("l", 5), ("o", 1), ("l", 6), ("l", 7), ("l", 8), ("l", 9)]
ROWS_I = 128
DEC_ROW, BQ_ROW = 880, 960
PLACE = {9: (0, 0), 10: (0, 80), 8: (0, 160), 3: (1, 0), 4: (1, 80), 5: (1, 160), 7: (2, 0), 6: (2, 80), 2: (2, 160), 1: (3, 0), 0: (3, 80)}


def dot(a, b, ca=1, cb=0):
    return lax.dot_general(a, b, (((ca,), (cb,)), ((), ())), preferred_element_type=F32)


def dot_nt(a, b):
    return dot(a, b, 1, 1)


def dot_tn(a, b):
    return dot(a, b, 0, 0)


def half(v):
    return v.astype(BF)


def norm(v):
    c = v - jnp.mean(v, axis=-1, keepdims=True)
    inv = lax.rsqrt(jnp.mean(c * c, axis=-1, keepdims=True) + EPS)
    return c * inv, inv


def norm_back(g, gain, n, inv):
    gg = jnp.sum(g * n, axis=0, keepdims=True)
    inner = g * gain
    m1 = jnp.mean(inner, axis=-1, keepdims=True)
    m2 = jnp.mean(inner * n, axis=-1, keepdims=True)
    return inv * (inner - m1 - n * m2), gg


C0, C1 = 0.7978845608028654, 0.044715


def gelu(x):
    return 0.5 * x * (1.0 + jnp.tanh(C0 * (x + C1 * x * x * x)))


def gelu_slope(x):
    t = jnp.tanh(C0 * (x + C1 * x * x * x))
    return 0.5 * (1.0 + t) + 0.5 * x * (1.0 - t * t) * (C0 * (1.0 + 3.0 * C1 * x * x))


def lanes(width):
    return lax.broadcasted_iota(jnp.int32, (1, width), 1)


def head_mask(h):
    lane = lanes(256)
    return jnp.where((lane >= OFF[h]) & (lane < OFF[h] + E), 1.0, 0.0).astype(F32)


def pieces(row, count):
    out = []
    done = 0
    while done < count:
        i, r0 = divmod(row + done, ROWS_I)
        n = min(count - done, ROWS_I - r0)
        out.append((i, r0, done, n))
        done += n
    return out


def split3(v):
    hi = half(v).astype(F32)
    mid = half(v - hi).astype(F32)
    lo = half(v - hi - mid).astype(F32)
    return hi, mid, lo


def pack3(v):
    hi, mid, lo = split3(v)
    return half(hi + pltpu.roll(mid, 16, 1) + pltpu.roll(lo, 32, 1))


def unpack3(v, axis):
    return v + pltpu.roll(v, 112, axis) + pltpu.roll(v, 96, axis)


def as_rows(parts, count):
    row = lax.broadcasted_iota(jnp.int32, (count, 128), 0)
    out = jnp.zeros((count, 128), F32)
    for r, part in parts:
        out = jnp.where(row == r, part, out)
    return out


def call(body, outs, args, scratch=(), vmem=48, flops=0, name=None):
    spaces = {"v": pltpu.VMEM, "a": pl.ANY, "s": pltpu.SMEM, "h": pltpu.HBM}
    return pl.pallas_call(
        body,
        out_shape=[jax.ShapeDtypeStruct(s, t) for s, t, _ in outs],
        in_specs=[pl.BlockSpec(memory_space=spaces[m]) for _, m in args],
        out_specs=[pl.BlockSpec(memory_space=spaces[m]) for _, _, m in outs],
        scratch_shapes=list(scratch),
        compiler_params=pltpu.CompilerParams(vmem_limit_bytes=vmem * MIB),
        cost_estimate=pl.CostEstimate(flops=int(flops), bytes_accessed=4 * MIB, transcendentals=0),
        name=name,
    )(*[a for a, _ in args])


DMA = pltpu.SemaphoreType.DMA


def pack_early_body(sc, lm, bm, la, g0, sem):
    cols = pl.ds(pl.multiple_of(sc[4] * 640, 128), 640)
    copies = [
        (bm.at[0, :, cols], g0.at[0:48, :]),
        (bm.at[1, :, cols], g0.at[48:96, :]),
        (lm.at[0, :, cols], g0.at[96:176, :]),
        (la.at[:, cols], g0.at[176:192, :]),
    ]
    copies = [pltpu.make_async_copy(a, b, sem.at[k]) for k, (a, b) in enumerate(copies)]
    for c in copies:
        c.start()
    for c in copies:
        c.wait()


def pack_body(sc, lm, om, bm, do, wsh, buf, sem):
    i = sc[0]
    blocks = [(80 * k, 80, (om if s == "o" else lm), n, D) for k, (s, n) in enumerate(SQUARE)]
    blocks += [(DEC_ROW, 80, do, None, DI), (BQ_ROW, 48, bm, 2, D)]
    for k in range(NI):
        lo, hi = ROWS_I * k, ROWS_I * (k + 1)

        @pl.when(i == k)
        def _(lo=lo, hi=hi):
            cs = []
            for row, count, ref, n, width in blocks:
                a, b = max(lo, row), min(hi, row + count)
                if a < b:
                    src = ref.at[a - row : b - row, :] if n is None else ref.at[n, a - row : b - row, :]
                    dst = buf.at[a - lo : b - lo, :] if width == D else buf.at[a - lo : b - lo, 0:width]
                    cs.append(pltpu.make_async_copy(src, dst, sem.at[len(cs)]))
            for c in cs:
                c.start()
            for c in cs:
                c.wait()

    out = pltpu.make_async_copy(buf, wsh, sem.at[8])
    out.start()
    out.wait()


def pieces_from(sc, own, sib):
    x, z, core = sc[2], sc[3], sc[4]
    out = []
    for side, (t0, t1, t2a, t2b, t3) in enumerate((own, sib)):
        c = core if side == 0 else 1 - core
        col = pl.ds(pl.multiple_of(c * 640, 128), 640)
        for e in range(4):
            for d in range(4):
                xs = jnp.where(c == 0, (x + 4 - d) & 3, (x + 4 - e) & 3)
                zs = jnp.where(c == 0, (z + 4 - e) & 3, (z + 4 - d) & 3)
                ref = (t0, t1, None, t3)[e] if e != 2 else (t2a, t2b)[d // 2]
                out.append((xs * 4 + zs, col, ref.at[d % 2 if e == 2 else d]))
    return out


def enc_body(
    sc, a0, a1, a2, a3, a4, b0, b1, b2, b3, b4, x_in, bg, lg, g_out, nb_o, k_o, v_o, q_o, pay, n_o, i_o, gs, acc, sem
):
    copies = [
        pltpu.make_async_copy(src, gs.at[pos, :, col], sem.at[k])
        for k, (pos, col, src) in enumerate(pieces_from(sc, (a0, a1, a2, a3, a4), (b0, b1, b2, b3, b4)))
    ]
    for c in copies:
        c.start()
    n_in, _ = norm(x_in[...].astype(F32))
    nb = half(n_in * bg[0:1, :])
    nb_o[...] = nb
    for c in copies:
        c.wait()
    save = pltpu.make_async_copy(gs, g_out, sem.at[32])
    save.start()
    k_o[...] = half(dot(nb, gs[:, 0:48, :].reshape(DI, D)))
    v_o[...] = half(dot(nb, gs[:, 48:96, :].reshape(DI, D)))
    z0b = gs[:, 176:192, :].reshape(R, D)
    nq, inv = norm(z0b.astype(F32))
    n_o[...] = half(nq)
    i_o[...] = jnp.broadcast_to(inv, (R, 128))
    q_o[...] = half(dot(half(nq * lg[0:1, :]), gs[:, 96:176, :].reshape(D, D)))
    acc[...] = jnp.zeros_like(acc)
    valid = lanes(N) + sc[1] * N < sc[5]
    lane = lanes(128)
    stats = jnp.zeros((R, 128), F32)
    for h in range(H):
        w = slice(WIN[h], WIN[h] + 256)
        mk = head_mask(h)
        s = dot_nt(q_o[:, w] * half(mk), k_o[:, w]) * SCALE
        s = jnp.where(valid, s, -1e30)
        m = jnp.max(s, axis=-1, keepdims=True)
        p = jnp.exp(s - m)
        acc[:, w] += dot(half(p), v_o[:, w]) * mk
        stats = jnp.where(lane == h, m, stats)
        stats = jnp.where(lane == 8 + h, jnp.sum(p, axis=-1, keepdims=True), stats)
    pay[:, 0:D] = half(acc[...])
    pay[:, D : D + 128] = pack3(stats)
    save.wait()


def combine_body(rcv, out):
    st = unpack3(rcv[:, :, D : D + 128].astype(F32), 2)
    peak = jnp.max(st, axis=0, keepdims=True)
    w = jnp.exp(st - peak)
    total = jnp.sum(w * pltpu.roll(st, 120, 2), axis=0, keepdims=True)
    coef = w / total
    lane = lax.broadcasted_iota(jnp.int32, (1, 1, 128), 2)
    for t in range(10):
        h0, h1 = 128 * t // E, (128 * t + 127) // E
        c = coef[:, :, h0 : h0 + 1]
        if h1 != h0:
            c = jnp.where(lane >= E * h1 - 128 * t, coef[:, :, h1 : h1 + 1], c)
        o = jnp.sum(rcv[:, :, 128 * t : 128 * t + 128].astype(F32) * c, axis=0)
        out[:, 128 * t : 128 * t + 128] = half(o)
    lse = jnp.where(lanes(128) < 8, (peak + jnp.log(total))[0], 0.0)
    out[:, D : D + 128] = pack3(lse)


class Ring:
    def __init__(self, w, slots, sem, order):
        self.w, self.slots, self.sem, self.order = w, slots, sem, order
        self.n = slots.shape[0]
        self.pos = {m: k for k, m in enumerate(order)}

    def copies(self, m):
        s = self.pos[m] % self.n
        return [
            pltpu.make_async_copy(
                self.w.at[i, :, r0 : r0 + n, :], self.slots.at[s, :, d0 : d0 + n, :], self.sem.at[s, k]
            )
            for k, (i, r0, d0, n) in enumerate(pieces(80 * m, 80))
        ]

    def start(self, m):
        for c in self.copies(m):
            c.start()

    def begin(self):
        for m in self.order[: self.n]:
            self.start(m)

    def get(self, m):
        for c in self.copies(m):
            c.wait()
        return self.slots[self.pos[m] % self.n].reshape(D, D)

    def done(self, m):
        k = self.pos[m] + self.n
        if k < len(self.order):
            self.start(self.order[k])


def forward_body(
    qin, cot, bg, lg, e_h, g_all, w,
    res, gqin, gain_o, pay, mix_o, nd_o, gq_o, z_h, h_h, a_h,
    slots, e, z0b, zs, zb, hs, qs, acc, kd, vd, dec, bq, dacc, gq, gkv, wsem, ssem, lsem,
):
    first = [
        pltpu.make_async_copy(e_h.at[:, 0:D], e, lsem.at[3]),
        pltpu.make_async_copy(g_all.at[:, 176:192, :], z0b, lsem.at[4]),
    ]
    for c in first:
        c.start()
    ring = Ring(w, slots, wsem, list(range(11)))
    ring.begin()
    copies = []
    for i, r0, d0, n in pieces(BQ_ROW, 48):
        copies.append(pltpu.make_async_copy(w.at[i, :, r0 : r0 + n, :], bq.at[:, d0 : d0 + n, :], lsem.at[0]))
    for i, r0, d0, n in pieces(DEC_ROW, 80):
        copies.append(
            pltpu.make_async_copy(w.at[i, :, r0 : r0 + n, 0:DI], dec.at[:, d0 : d0 + n, :], lsem.at[len(copies)])
        )
    for c in copies:
        c.start()
    saves = []

    def save(src, dst):
        c = pltpu.make_async_copy(src, dst, ssem.at[len(saves)])
        c.start()
        saves.append(c)

    def keep(k):
        zb[k] = half(zs[k])
        save(zb.at[k], z_h.at[k])

    def mul(a, m):
        out = dot(a, ring.get(m))
        ring.done(m)
        return out

    for c in first:
        c.wait()
    z1 = z0b[...].reshape(R, D).astype(F32) + mul(e[...], 0)
    zs[0] = z1
    keep(0)
    h1 = mul(half(norm(z1)[0] * lg[1:2, :]), 1)
    hs[0] = half(h1)
    save(hs.at[0], h_h.at[0])
    zs[1] = zs[0] + mul(half(gelu(h1)), 2)
    keep(1)
    s_b = half(norm(zs[1])[0] * lg[2:3, :])
    for k in range(3):
        qs[k] = half(mul(s_b, 3 + k))
        save(qs.at[k], a_h.at[k])
    acc[...] = jnp.zeros_like(acc)
    for h in range(H):
        win = slice(WIN[h], WIN[h] + 256)
        mk = head_mask(h)
        s = dot_nt(qs[0, :, win] * half(mk), qs[1, :, win]) * SCALE
        p = jnp.exp(s - jnp.max(s, axis=-1, keepdims=True))
        p = p / jnp.sum(p, axis=-1, keepdims=True)
        acc[:, win] += dot(half(p), qs[2, :, win]) * mk
    qs[3] = half(acc[...])
    save(qs.at[3], a_h.at[3])
    zs[2] = zs[1] + mul(qs[3], 6)
    keep(2)
    h2 = mul(half(norm(zs[2])[0] * lg[3:4, :]), 7)
    hs[1] = half(h2)
    save(hs.at[1], h_h.at[1])
    zs[3] = zs[2] + mul(half(gelu(h2)), 8)
    keep(3)
    c_b = half(norm(zs[3])[0] * lg[4:5, :])
    kd[...] = half(mul(c_b, 9))
    vd[...] = half(mul(c_b, 10))

    x = qin[...].astype(F32)
    n, inv = norm(x)
    nd = half(n * bg[1:2, :])
    nd_o[...] = nd
    for c in copies:
        c.wait()
    wq = bq[...].reshape(DI, D)
    wd = dec[...].reshape(D, DI)
    gq_o[...] = half(dot(nd, wq))
    mix_o[...] = half(dot_nt(cot[...], wd))
    dacc[...] = jnp.zeros_like(dacc)
    gq[...] = jnp.zeros_like(gq)
    gkv[...] = jnp.zeros_like(gkv)
    for h in range(H):
        win = slice(WIN[h], WIN[h] + 256)
        mk = head_mask(h)
        mkb = half(mk)
        qw, gw, kw, vw = gq_o[:, win], mix_o[:, win], kd[:, win], vd[:, win]
        s = dot_nt(qw * mkb, kw) * SCALE
        p = jnp.exp(s - jnp.max(s, axis=-1, keepdims=True))
        p = p / jnp.sum(p, axis=-1, keepdims=True)
        pb = half(p)
        dacc[:, win] += dot(pb, vw) * mk
        dp = dot_nt(gw * mkb, vw)
        ds = half(p * (dp - jnp.sum(p * dp, axis=-1, keepdims=True)))
        gq[:, win] += dot(ds, kw) * mk
        gkv[0, :, win] += dot_tn(ds, qw) * mk
        gkv[1, :, win] += dot_tn(pb, gw) * mk
    pay[:, 0:D] = half(gkv[0] * SCALE)
    pay[:, D : 2 * D] = half(gkv[1])
    mix = half(dacc[...])
    mix_o[...] = mix
    res[...] = half(x + dot(mix, wd))
    gqb = half(gq[...] * SCALE)
    gq_o[...] = gqb
    gin, gg = norm_back(dot_nt(gqb, wq), bg[1:2, :], n, inv)
    gqin[...] = cot[...].astype(F32) + gin
    gain_o[...] = gg
    for c in saves:
        c.wait()


def prepare_body(lg, z_h, h_h, a_h, n_h, i_h, s_h, act_h, p_h, zs, hs, qs, ns, vs, ss, acts, ps, sem, osem):
    loads = {}
    for k in range(4):
        loads["z", k] = pltpu.make_async_copy(z_h.at[k], zs.at[k], sem.at[k])
    for k in range(2):
        loads["h", k] = pltpu.make_async_copy(h_h.at[k], hs.at[k], sem.at[4 + k])
    loads["q"] = pltpu.make_async_copy(a_h.at[0:2], qs, sem.at[6])
    for c in loads.values():
        c.start()
    saves = []

    def save(src, dst):
        c = pltpu.make_async_copy(src, dst, osem.at[len(saves)])
        c.start()
        saves.append(c)

    for k, a in ((3, 0), (2, 2), (1, 1), (0, 4)):
        loads["z", k].wait()
        n, inv = norm(zs[k].astype(F32))
        ns[k] = half(n)
        save(ns.at[k], n_h.at[k])
        vs[k] = jnp.broadcast_to(inv, (R, 128))
        acts[a] = half(n * lg[k + 1 : k + 2, :])
        save(acts.at[a], act_h.at[a])
    save(vs, i_h)
    for k, a in ((1, 3), (0, 5)):
        loads["h", k].wait()
        x = hs[k].astype(F32)
        t = jnp.tanh(C0 * (x + C1 * x * x * x))
        acts[a] = half(0.5 * x * (1.0 + t))
        save(acts.at[a], act_h.at[a])
        ss[k] = 0.5 * (1.0 + t) + 0.5 * x * (1.0 - t * t) * (C0 * (1.0 + 3.0 * C1 * x * x))
        save(ss.at[k], s_h.at[k])
    loads["q"].wait()
    for h in range(H):
        win = slice(WIN[h], WIN[h] + 256)
        s = dot_nt(qs[0, :, win] * half(head_mask(h)), qs[1, :, win]) * SCALE
        p = jnp.exp(s - jnp.max(s, axis=-1, keepdims=True))
        ps[h] = half(p / jnp.sum(p, axis=-1, keepdims=True))
    save(ps, p_h)
    for c in saves:
        c.wait()


def lat_backward_body(
    sc, gin, lg, w, e_h, n_h, i_h, s_h, act_h, a_h, p_h, gmix, pack_o, g1c_o, gains_o,
    slots, ns, vs, ss, acts, qs, ps, acc, acc2, acc3, gh, gw, wsem, lsem,
):
    order = [8, 7, 6, 3, 4, 5, 2, 1, 0]
    ring = Ring(w, slots, wsem, order)
    todo = [
        (i_h, vs),
        (act_h.at[0], acts.at[0]),
        (s_h.at[1], ss.at[1]),
        (act_h.at[3], acts.at[1]),
        (n_h.at[2], ns.at[2]),
        (act_h.at[2], acts.at[3]),
        (a_h.at[3], acts.at[4]),
        (p_h, ps),
        (a_h.at[0:3], qs.at[0:3]),
        (n_h.at[1], ns.at[1]),
        (act_h.at[1], acts.at[2]),
        (s_h.at[0], ss.at[0]),
        (act_h.at[5], acts.at[5]),
        (n_h.at[0], ns.at[0]),
        (act_h.at[4], acts.at[6]),
        (e_h.at[:, 0:D], acts.at[7]),
    ]
    loads = [pltpu.make_async_copy(a, b, lsem.at[k]) for k, (a, b) in enumerate(todo)]
    after = {8: (4, 5, 6), 7: (7, 8), 6: (9, 10, 11, 12), 3: (13, 14, 15)}
    ring.start(8)
    for c in loads[:4]:
        c.start()
    for m in order[1 : ring.n]:
        ring.start(m)

    def ready(*ks):
        for k in ks:
            loads[k].wait()

    src = sc[1] * 80
    start = pl.multiple_of(jnp.minimum((src >> 7) * 128, 1024), 128)
    offset = src - start
    lane = lanes(256)

    def put(ref, to):
        v = pltpu.roll(ref[:, pl.ds(start, 256)].astype(F32), (to - offset + 256) & 255, 1)
        return jnp.where((lane >= to) & (lane < to + 80), v, 0.0)

    def weight_grad(window, first, count):
        a = acts[first : first + count].reshape(count * R, D)
        pack_o[:, 256 * window : 256 * window + 256] = half(dot_tn(a, gw[first : first + count].reshape(count * R, 256)))

    def mul(g_b, m):
        out = dot_nt(g_b, ring.get(m))
        ring.done(m)
        for k in after.get(m, ()):
            loads[k].start()
        return out

    gain_rows = []

    def back(g, k):
        out, gg = norm_back(g, lg[k + 1 : k + 2, :], ns[k].astype(F32), vs[k][:, 0:1])
        for t in range(10):
            gain_rows.append((10 * k + t, gg[:, 128 * t : 128 * t + 128]))
        return out

    for t in range(10):
        acc[:, 128 * t : 128 * t + 128] = gin[:, 16 * t : 16 * t + 16, :].reshape(R, 128).astype(F32)
    tile = lanes(128)
    values = pltpu.roll(gin[:, 176:192, :].reshape(R, 128).astype(F32), 80, 1)
    gw[0, :, 0:128] = half(jnp.where(tile < 80, gin[:, 160:176, :].reshape(R, 128).astype(F32), values))
    gw[0, :, 128:256] = half(jnp.where(tile < 32, values, 0.0))
    gw[1] = half(put(acc, 160))
    ready(0, 1, 2, 3)
    gh[...] = half(mul(half(acc[...]), 8) * ss[1])
    weight_grad(0, 0, 2)
    ready(4)
    gw[3] = half(put(gh, 0))
    acc[...] += back(mul(gh[...], 7), 2)
    gw[4] = half(put(acc, 80))
    qs[3] = half(mul(half(acc[...]), 6))
    acc2[...] = jnp.zeros_like(acc2)
    acc3[...] = jnp.zeros_like(acc3)
    ready(5, 6, 7, 8)
    for h in range(H):
        win = slice(WIN[h], WIN[h] + 256)
        mk = head_mask(h)
        pb = ps[h]
        p = pb.astype(F32)
        dp = dot_nt(qs[3, :, win] * half(mk), qs[2, :, win])
        ds = half(p * (dp - jnp.sum(p * dp, axis=-1, keepdims=True)) * SCALE)
        acc2[:, win] += dot(ds, qs[1, :, win]) * mk
        acc3[0, :, win] += dot_tn(ds, qs[0, :, win]) * mk
        acc3[1, :, win] += dot_tn(pb, qs[3, :, win]) * mk
    gw[2] = half(put(acc2, 0) + put(acc3.at[0], 80) + put(acc3.at[1], 160))
    gn = mul(half(acc2[...]), 3)
    gn = gn + mul(half(acc3[0]), 4)
    gn = gn + mul(half(acc3[1]), 5)
    ready(9, 10)
    weight_grad(1, 2, 1)
    acc[...] += back(gn, 1)
    gw[5] = half(put(acc, 160))
    ready(11, 12)
    gh[...] = half(mul(half(acc[...]), 2) * ss[0])
    weight_grad(2, 3, 3)
    gw[6] = half(put(gh, 0))
    ready(13, 14, 15)
    acc[...] += back(mul(gh[...], 1), 0)
    gw[7] = half(put(acc, 80))
    g1c_o[...] = half(put(acc, 0)[:, 0:128])
    gmix[...] = half(mul(half(acc[...]), 0))
    weight_grad(3, 6, 2)
    gains_o[...] = as_rows(gain_rows, 32)


def key_value_back_body(sc, rcv, lg, n_h, i_h, w, out, gain_o, wbuf, nbuf, ibuf, sem):
    rows = pl.ds(pl.multiple_of(sc[1] * 16, 16), 16)
    copies = []
    for k, m in enumerate((9, 10)):
        for i, r0, d0, n in pieces(80 * m, 80):
            copies.append((w.at[i, :, r0 : r0 + n, :], wbuf.at[k, :, d0 : d0 + n, :]))
    copies += [(n_h.at[3, rows, :], nbuf), (i_h.at[3, rows, :], ibuf)]
    copies = [pltpu.make_async_copy(a, b, sem.at[k]) for k, (a, b) in enumerate(copies)]
    for c in copies:
        c.start()
    s = half(jnp.sum(rcv[...].astype(F32), axis=0))
    for j in range(NJ):
        base = min(128 * (80 * j // 128), 1024)
        for k in range(2):
            v = s[:, D * k + base : D * k + base + 256].astype(F32)
            if 80 * j > base:
                v = pltpu.roll(v, 256 - (80 * j - base), 1)
            out[j, 160 + 16 * k : 176 + 16 * k, :] = half(v[:, 0:128])
    for c in copies:
        c.wait()
    gn = dot_nt(s[:, 0:D], wbuf[0].reshape(D, D)) + dot_nt(s[:, D : 2 * D], wbuf[1].reshape(D, D))
    g, gg = norm_back(gn, lg[4:5, :], nbuf[...].astype(F32), ibuf[:, 0:1])
    gain_o[...] = gg
    g = jnp.concatenate([half(g[:, 128 * t : 128 * t + 128]) for t in range(10)], axis=0)
    for j in range(NJ):
        out[j, 0:160, :] = g


def dec_weights_body(mix, cot, nd, gq, out, buf, sem):
    g = half(dot_tn(mix[...], cot[...]))
    for i in range(NI):
        for t in range(6):
            buf[i, 160 * t : 160 * t + 160, :] = g[160 * i : 160 * i + 160, 128 * t : 128 * t + 128]
    one = pltpu.make_async_copy(buf.at[:, 0:960, :], out.at[:, 0:960, :], sem.at[0])
    one.start()
    g = half(dot_tn(nd[...], gq[...]))
    for i in range(NI):
        for t in range(10):
            r = 960 + 96 * t
            buf[i, r : r + 96, :] = g[96 * i : 96 * i + 96, 128 * t : 128 * t + 128]
    two = pltpu.make_async_copy(buf.at[:, 960:1920, :], out.at[:, 960:1920, :], sem.at[1])
    two.start()
    one.wait()
    two.wait()


def spread(chunk, pay, td, tb):
    fill = jnp.zeros((96, 128), F32)
    for t in range(6):
        v = jnp.concatenate([chunk[160 * t : 160 * t + 160, :].astype(F32), fill], axis=0)
        td[128 * t : 128 * t + 128, :] = v.T
    fill = jnp.zeros((32, 128), F32)
    for t in range(10):
        v = jnp.concatenate([chunk[960 + 96 * t : 960 + 96 * t + 96, :].astype(F32), fill], axis=0)
        tb[128 * t : 128 * t + 128, :] = v.T
    for j in range(NJ):
        tail = pltpu.roll(td[48 * j : 48 * j + 48, 128:256], 96, 1)
        pay[j, 512:560, :] = half(tb[80 * j : 80 * j + 48, :] + tail)
        pay[j, 560:592, :] = half(tb[80 * j + 48 : 80 * j + 80, :])
        pay[j, 592:640, :] = half(td[48 * j : 48 * j + 48, 0:128])


def enc_back_body(
    sc, x_in, bg, lg, gd, gc, gmix_h, e_h, q_h, k_h, v_h, g_all, dw_h, n0_h, i0_h, gin_o, pay,
    gmix, e, q, k, v, wkv, n0, i0, gq, gkt, gvt, dw, td, tb, sem,
):
    pairs = [(gmix_h, gmix), (q_h, q), (k_h, k), (v_h, v), (e_h, e), (g_all, wkv), (dw_h, dw), (n0_h, n0), (i0_h, i0)]
    loads = [pltpu.make_async_copy(a, b, sem.at[n]) for n, (a, b) in enumerate(pairs)]
    for c in loads:
        c.start()
    for c in loads[:5]:
        c.wait()
    lse = unpack3(e[:, D : D + 128].astype(F32), 1)
    valid = lanes(N) + sc[1] * N < sc[5]
    gq[...] = jnp.zeros_like(gq)
    for h in range(H):
        win = slice(WIN[h], WIN[h] + 256)
        mk = head_mask(h)
        mkb = half(mk)
        qw, gw, kw, vw = q[:, win], gmix[:, win], k[:, win], v[:, win]
        rd = jnp.sum(gw.astype(F32) * e[:, win].astype(F32) * mk, axis=-1, keepdims=True)
        s = dot_nt(qw * mkb, kw) * SCALE
        p = jnp.where(valid, jnp.exp(jnp.where(valid, s, -1e30) - lse[:, h : h + 1]), 0.0)
        dp = dot_nt(gw * mkb, vw)
        ds = half(p * (dp - rd))
        gq[:, win] += dot(ds, kw) * mk
        o = OFF[h]
        gkt[E * h : E * h + E, :] = half(dot_tn(qw, ds)[o : o + E, :] * SCALE)
        gvt[E * h : E * h + E, :] = half(dot_tn(gw, half(p))[o : o + E, :])
    pay[:, 320:400, :] = gkt[...].reshape(NJ, 80, 128)
    pay[:, 400:480, :] = gvt[...].reshape(NJ, 80, 128)
    loads[5].wait()
    gqs = gq[...] * SCALE
    gqt = half(gqs.T)
    pay[:, 160:240, :] = gqt[:, 0:128].reshape(NJ, 80, 128)
    pay[:, 240:320, :] = gqt[:, 128:256].reshape(NJ, 80, 128)
    loads[7].wait()
    loads[8].wait()
    gz, g0 = norm_back(dot_nt(half(gqs), wkv[:, 96:176, :].reshape(D, D)), lg[0:1, :], n0[...].astype(F32), i0[:, 0:1])
    gzt = half(gz.T)
    pay[:, 0:80, :] = gzt[:, 0:128].reshape(NJ, 80, 128)
    pay[:, 80:160, :] = gzt[:, 128:256].reshape(NJ, 80, 128)
    n, inv = norm(x_in[...].astype(F32))
    gnt = dot(wkv[:, 0:48, :].reshape(DI, D), gkt[...]) + dot(wkv[:, 48:96, :].reshape(DI, D), gvt[...])
    gin, gg = norm_back(gnt.T, bg[0:1, :], n, inv)
    gin_o[...] = gin
    rows = [(t, gg[:, 128 * t : 128 * t + 128]) for t in range(6)]
    rows += [(6 + t, gd[:, 128 * t : 128 * t + 128]) for t in range(6)]
    rows += [(12 + t, g0[:, 128 * t : 128 * t + 128]) for t in range(10)]
    rows += [(22 + t, gc[:, 128 * t : 128 * t + 128]) for t in range(10)]
    g = half(as_rows(rows, 32))
    for j in range(NJ):
        pay[j, 480:512, :] = g
    loads[6].wait()
    spread(dw, pay, td, tb)


def tail_one_body(rcv, nf_h, n0_h, lg, lat_gain, g1c, out, dec_o, bq_o, nf, n0, left, sem):
    loads = [
        pltpu.make_async_copy(nf_h, nf, sem.at[0]),
        pltpu.make_async_copy(n0_h, n0, sem.at[1]),
    ]
    for c in loads:
        c.start()
    sums = jnp.sum(rcv[:, 0:320, :].astype(F32), axis=0)
    fill = jnp.zeros((48, 128), F32)
    left[...] = jnp.zeros_like(left)
    for s in range(NJ):
        left[0:80, 128 * s : 128 * s + 128] = rcv[s, 320:400, :]
        left[128:208, 128 * s : 128 * s + 128] = rcv[s, 400:480, :]
    loads[1].wait()
    nq = half(n0[...].astype(F32) * lg[0:1, :])
    a = jnp.concatenate([sums[160:240], fill], axis=0).T
    b = jnp.concatenate([sums[240:320], fill], axis=0).T
    w0 = dot_tn(nq, half(jnp.concatenate([a, b], axis=0)))
    a = jnp.concatenate([sums[0:80], fill], axis=0).T
    b = jnp.concatenate([sums[80:160], fill], axis=0).T
    gz = half(jnp.concatenate([a, b], axis=0) + g1c[...].astype(F32))
    gains = jnp.sum(rcv[:, 480:512, :].astype(F32), axis=0)
    gains = half(jnp.concatenate([gains, lat_gain[...]], axis=0))
    loads[0].wait()
    wt = dot(left[...], nf[...]).T
    lane = lanes(128)
    key, value = wt[:, 0:128], wt[:, 128:256]
    one = half(jnp.where(lane < 80, key, pltpu.roll(value, 80, 1)))
    other = pltpu.roll(value, 32, 1)
    for i in range(NI):
        r = 96 * i
        beside = jnp.concatenate([other[r : r + 96, :], jnp.zeros((64, 128), F32)], axis=0)
        out[i, 0:160, :] = half(jnp.where(lane < 80, w0[160 * i : 160 * i + 160, :], beside))
        out[i, 160:192, :] = gz[32 * i : 32 * i + 32, :]
        out[i, 192:288, :] = one[r : r + 96, :]
        out[i, 288:352, :] = gains
    s = jnp.sum(rcv[:, 512:640, :].astype(F32), axis=0)
    bq_o[...] = s[0:80, 0:96]
    dec_o[:, 0:128] = s[80:128]
    dec_o[:, 128:160] = pltpu.roll(s[0:48], 32, 1)[:, 0:32]


def tail_two_body(rcv, pack_h, bq, arr_o, lm_o, om_o, bm_o, lat_o, byte_o, pack, sem):
    load = pltpu.make_async_copy(pack_h, pack, sem)
    load.start()
    sums = jnp.sum(rcv[...].astype(F32), axis=0)
    lm_o[0] = sums[0:160, 0:80]
    arr_o[...] = sums[160:192, 0:80]
    lane = lanes(128)
    value = jnp.where(lane < 48, pltpu.roll(sums[192:288], 48, 1), pltpu.roll(sums[0:96], 96, 1))
    fill = jnp.zeros((32, 128), F32)
    bm_o[0] = jnp.concatenate([sums[192:288], fill], axis=0).T[0:80, 0:96]
    bm_o[1] = jnp.concatenate([value, fill], axis=0).T[0:80, 0:96]
    bm_o[2] = bq[...]
    g = sums[288:352]
    for t in range(6):
        for b in range(2):
            byte_o[b : b + 1, 128 * t : 128 * t + 128] = g[6 * b + t : 6 * b + t + 1, :]
    for t in range(10):
        for b in range(5):
            r = {0: 12, 1: 32, 2: 42, 3: 52, 4: 22}[b] + t
            lat_o[b : b + 1, 128 * t : 128 * t + 128] = g[r : r + 1, :]
    load.wait()
    for m, (kind, n) in enumerate(SQUARE):
        window, o = PLACE[m]
        v = pack[:, 256 * window : 256 * window + 256].astype(F32)
        if o:
            v = pltpu.roll(v, 256 - o, 1)
        if kind == "l":
            lm_o[n] = v[:, 0:80]
        else:
            om_o[n] = v[:, 0:80]


def line(y, c, x, z):
    return ((y % 4) * 2 + c) * NJ + (x % 4) * NZ + (z % 4)


EVERY = [(y, c, x, z) for y in range(4) for c in range(2) for x in range(NX) for z in range(NZ)]


def along(stage, d):
    out = []
    for y, c, x, z in EVERY:
        on_x = (c == 0) == (stage == 0)
        out.append((line(y, c, x, z), line(y, c, x + d, z) if on_x else line(y, c, x, z + d)))
    return out


SWAP = [(line(y, c, x, z), line(y, 1 - c, x, z)) for y, c, x, z in EVERY]


def exchange(v, axes):
    flat = v.reshape(v.shape[0] * v.shape[1], v.shape[2])
    return lax.all_to_all(flat, axes, split_axis=0, concat_axis=0, tiled=True).reshape(v.shape)


def shards(inputs, queries, lengths, latent_array, latent_mats, out_mats, byte_mats, dec_out, lg, bg, cotangent):
    y, core, x, z = (lax.axis_index(a) for a in AXES)
    i, j = y * 2 + core, x * NZ + z
    sc = jnp.stack([i, j, x, z, core, lengths[0]]).astype(jnp.int32)
    xin, qin, cot = inputs[0], queries[0], cotangent[0]

    (wsh,) = call(
        pack_body,
        [((ROWS_I, D), BF, "h")],
        [(sc, "s"), (latent_mats, "h"), (out_mats, "h"), (byte_mats, "h"), (dec_out, "h")],
        [pltpu.VMEM((ROWS_I, D), BF), DMA((9,))],
        vmem=60,
        name="pack",
    )
    (g0,) = call(
        pack_early_body,
        [((192, 640), BF, "v")],
        [(sc, "s"), (latent_mats, "h"), (byte_mats, "h"), (latent_array, "h")],
        [DMA((4,))],
        vmem=60,
        name="pack_early",
    )
    w = lax.all_gather(wsh, AXES, axis=0, tiled=True).reshape(NI, NJ, ROWS_I, D)

    s0 = jnp.stack([g0] + [lax.ppermute(g0, AXES, along(0, d)) for d in (1, 2, 3)])
    t1, t3 = (lax.ppermute(s0, AXES, along(1, d)) for d in (1, 3))
    t2a, t2b = lax.ppermute(t1[0:2], AXES, along(1, 1)), lax.ppermute(t3[2:4], AXES, along(1, 3))
    own = [s0, t1, t2a, t2b, t3]
    sib = [lax.ppermute(v, AXES, SWAP) for v in own]
    g_all, nb, k_b, v_b, q_b, pay, n0, i0 = call(
        enc_body,
        [
            ((NJ, 192, D), BF, "h"),
            ((N, DI), BF, "v"),
            ((N, D), BF, "v"),
            ((N, D), BF, "v"),
            ((R, D), BF, "v"),
            ((R, D + 128), BF, "v"),
            ((R, D), BF, "v"),
            ((R, 128), F32, "v"),
        ],
        [(sc, "s")] + [(v, "a") for v in own + sib] + [(xin, "v"), (bg, "v"), (lg, "v")],
        [pltpu.VMEM((NJ, 192, D), BF), pltpu.VMEM((R, D), F32), DMA((33,))],
        vmem=60,
        flops=3e9,
        name="enc",
    )
    rcv = exchange(pay.reshape(NJ, 16, D + 128), BLK)
    (mine,) = call(combine_body, [((16, D + 128), BF, "v")], [(rcv, "v")], name="combine")
    e = lax.all_gather(mine, BLK, axis=0, tiled=True)

    big = (NJ, 80, D)
    res, gqin, gd, dpay, mix, nd, gq, z_h, h_h, a_h = call(
        forward_body,
        [
            ((N, DI), BF, "v"),
            ((N, DI), F32, "v"),
            ((1, DI), F32, "v"),
            ((R, 2 * D), BF, "v"),
            ((N, D), BF, "v"),
            ((N, DI), BF, "v"),
            ((N, D), BF, "v"),
            ((4, R, D), BF, "h"),
            ((2, R, D), BF, "h"),
            ((4, R, D), BF, "h"),
        ],
        [(qin, "v"), (cot, "v"), (bg, "v"), (lg, "v"), (e, "h"), (g_all, "h"), (w, "h")],
        [
            pltpu.VMEM((3,) + big, BF),
            pltpu.VMEM((R, D), BF),
            pltpu.VMEM((NJ, 16, D), BF),
            pltpu.VMEM((4, R, D), F32),
            pltpu.VMEM((4, R, D), BF),
            pltpu.VMEM((2, R, D), BF),
            pltpu.VMEM((4, R, D), BF),
            pltpu.VMEM((R, D), F32),
            pltpu.VMEM((R, D), BF),
            pltpu.VMEM((R, D), BF),
            pltpu.VMEM((NJ, 80, DI), BF),
            pltpu.VMEM((NJ, 48, D), BF),
            pltpu.VMEM((N, D), F32),
            pltpu.VMEM((N, D), F32),
            pltpu.VMEM((2, R, D), F32),
            DMA((3, 2)),
            DMA((10,)),
            DMA((5,)),
        ],
        vmem=54,
        flops=1.5e10,
        name="forward",
    )
    rows = exchange(dpay.reshape(NJ, 16, 2 * D), BLK)
    n_h, i_h, s_h, act_h, p_h = call(
        prepare_body,
        [
            ((4, R, D), BF, "h"),
            ((4, R, 128), F32, "h"),
            ((2, R, D), F32, "h"),
            ((6, R, D), BF, "h"),
            ((H, R, R), BF, "h"),
        ],
        [(lg, "v"), (z_h, "h"), (h_h, "h"), (a_h, "h")],
        [
            pltpu.VMEM((4, R, D), BF),
            pltpu.VMEM((2, R, D), BF),
            pltpu.VMEM((2, R, D), BF),
            pltpu.VMEM((4, R, D), BF),
            pltpu.VMEM((4, R, 128), F32),
            pltpu.VMEM((2, R, D), F32),
            pltpu.VMEM((6, R, D), BF),
            pltpu.VMEM((H, R, R), BF),
            DMA((7,)),
            DMA((14,)),
        ],
        vmem=58,
        flops=5e9,
        name="prepare",
    )
    (dw,) = call(
        dec_weights_body,
        [((NI, 1920, 128), BF, "h")],
        [(mix, "v"), (cot, "v"), (nd, "v"), (gq, "v")],
        [pltpu.VMEM((NI, 1920, 128), BF), DMA((2,))],
        vmem=60,
        flops=4e9,
        name="dec_weights",
    )
    kv, gc = call(
        key_value_back_body,
        [((NJ, 192, 128), BF, "v"), ((1, D), F32, "v")],
        [(sc, "s"), (rows, "v"), (lg, "v"), (n_h, "h"), (i_h, "h"), (w, "h")],
        [pltpu.VMEM((2,) + big, BF), pltpu.VMEM((16, D), BF), pltpu.VMEM((16, 128), F32), DMA((6,))],
        vmem=58,
        flops=1e8,
        name="key_value_back",
    )
    gin4 = exchange(kv, BLK)
    nb, _ = lax.optimization_barrier((nb, gc))
    nf = lax.all_gather(nb, BLK, axis=0, tiled=True)
    dw = lax.psum_scatter(dw.reshape(NI * 1920, 128), BATCH, scatter_dimension=0, tiled=True)

    gmix, pack, g1c, lat_gain = call(
        lat_backward_body,
        [((R, D), BF, "v"), ((D, 1024), BF, "v"), ((R, 128), BF, "v"), ((32, 128), F32, "v")],
        [(sc, "s"), (gin4, "v"), (lg, "v")] + [(v, "h") for v in (w, e, n_h, i_h, s_h, act_h, a_h, p_h)],
        [
            pltpu.VMEM((2,) + big, BF),
            pltpu.VMEM((4, R, D), BF),
            pltpu.VMEM((4, R, 128), F32),
            pltpu.VMEM((2, R, D), F32),
            pltpu.VMEM((8, R, D), BF),
            pltpu.VMEM((4, R, D), BF),
            pltpu.VMEM((H, R, R), BF),
            pltpu.VMEM((R, D), F32),
            pltpu.VMEM((R, D), F32),
            pltpu.VMEM((2, R, D), F32),
            pltpu.VMEM((R, D), BF),
            pltpu.VMEM((8, R, 256), BF),
            DMA((2, 2)),
            DMA((16,)),
        ],
        vmem=60,
        flops=8e10,
        name="lat_backward",
    )
    pack = lax.psum_scatter(pack, BATCH, scatter_dimension=0, tiled=True)
    gin, epay = call(
        enc_back_body,
        [((N, DI), F32, "v"), ((NJ, 640, 128), BF, "v")],
        [(sc, "s"), (xin, "v"), (bg, "v"), (lg, "v"), (gd, "v"), (gc, "v")]
        + [(v, "h") for v in (gmix, e, q_b, k_b, v_b, g_all, dw, n0, i0)],
        [
            pltpu.VMEM((R, D), BF),
            pltpu.VMEM((R, D + 128), BF),
            pltpu.VMEM((R, D), BF),
            pltpu.VMEM((N, D), BF),
            pltpu.VMEM((N, D), BF),
            pltpu.VMEM((NJ, 192, D), BF),
            pltpu.VMEM((R, D), BF),
            pltpu.VMEM((R, 128), F32),
            pltpu.VMEM((R, D), F32),
            pltpu.VMEM((D, N), BF),
            pltpu.VMEM((D, N), BF),
            pltpu.VMEM((1920, 128), BF),
            pltpu.VMEM((DI, 256), F32),
            pltpu.VMEM((D, 128), F32),
            DMA((9,)),
        ],
        vmem=58,
        flops=3e9,
        name="enc_back",
    )
    r1 = exchange(epay, BLK)
    p2, dec_grad, bq_grad = call(
        tail_one_body,
        [((NI, 352, 128), BF, "v"), ((48, 160), F32, "v"), ((80, 96), F32, "v")],
        [(r1, "v"), (nf, "h"), (n0, "h"), (lg, "v"), (lat_gain, "v"), (g1c, "v")],
        [pltpu.VMEM((NJ * N, DI), BF), pltpu.VMEM((R, D), BF), pltpu.VMEM((256, 2048), BF), DMA((2,))],
        name="tail_one",
    )
    r2 = exchange(p2, BATCH)
    arr, lm, om, byte_grads, lat_gains, byte_gain = call(
        tail_two_body,
        [
            ((32, 80), F32, "v"),
            ((10, 160, 80), F32, "v"),
            ((2, 160, 80), F32, "v"),
            ((3, 80, 96), F32, "v"),
            ((5, D), F32, "v"),
            ((2, DI), F32, "v"),
        ],
        [(r2, "v"), (pack, "h"), (bq_grad, "v")],
        [pltpu.VMEM((160, 1024), BF), DMA],
        name="tail_two",
    )
    byte_grads = jnp.swapaxes(byte_grads, 1, 2)
    return (res[None], gin[None], gqin[None], arr, lm, om, byte_grads, dec_grad.T, lat_gains, byte_gain)


def solution(mesh):
    grid = Mesh(mesh.devices.reshape(4, 2, NX, NZ), AXES)
    return jax.shard_map(
        shards,
        mesh=grid,
        in_specs=(
            P(BATCH, BLK, None),
            P(BATCH, BLK, None),
            P(BATCH),
            P(BLK, None),
            P(None, BLK, None),
            P(None, BLK, None),
            P(None, BLK, None),
            P(BLK, None),
            P(),
            P(),
            P(BATCH, BLK, None),
        ),
        out_specs=(
            P(BATCH, BLK, None),
            P(BATCH, BLK, None),
            P(BATCH, BLK, None),
            P(BATCH, BLK),
            P(None, BATCH, BLK),
            P(None, BATCH, BLK),
            P(None, BATCH, BLK),
            P(BATCH, BLK),
            P(),
            P(),
        ),
        check_vma=False,
    )
```

```python
import jax
import jax.numpy as jnp
from jax import lax
from jax.experimental import pallas as pl
from jax.experimental.pallas import tpu as pltpu
from jax.sharding import Mesh, PartitionSpec as P

F32, BF = jnp.float32, jnp.bfloat16
D, DI, R, N, H, E = 1280, 768, 256, 128, 8, 160
NX, NZ, NJ, NI = 4, 4, 16, 8
SCALE = E**-0.5
EPS = 1e-5
MIB = 1 << 20
AXES = ("y", "core", "x", "z")
BATCH = ("y", "core")
BLK = ("x", "z")
WIN = [128 * (E * h // 128) for h in range(H)]
OFF = [E * h - WIN[h] for h in range(H)]
SQUARE = [("o", 0), ("l", 1), ("l", 2), ("l", 3), ("l", 4), ("l", 5), ("o", 1), ("l", 6), ("l", 7), ("l", 8), ("l", 9)]
ROWS_I = 128
DEC_ROW, BQ_ROW = 880, 960
PLACE = {9: (0, 0), 10: (0, 80), 8: (0, 160), 3: (1, 0), 4: (1, 80), 5: (1, 160), 7: (2, 0), 6: (2, 80), 2: (2, 160), 1: (3, 0), 0: (3, 80)}


def dot(a, b, ca=1, cb=0):
    return lax.dot_general(a, b, (((ca,), (cb,)), ((), ())), preferred_element_type=F32)


def dot_nt(a, b):
    return dot(a, b, 1, 1)


def dot_tn(a, b):
    return dot(a, b, 0, 0)


def half(v):
    return v.astype(BF)


def norm(v):
    c = v - jnp.mean(v, axis=-1, keepdims=True)
    inv = lax.rsqrt(jnp.mean(c * c, axis=-1, keepdims=True) + EPS)
    return c * inv, inv


def norm_back(g, gain, n, inv):
    gg = jnp.sum(g * n, axis=0, keepdims=True)
    inner = g * gain
    m1 = jnp.mean(inner, axis=-1, keepdims=True)
    m2 = jnp.mean(inner * n, axis=-1, keepdims=True)
    return inv * (inner - m1 - n * m2), gg


C0, C1 = 0.7978845608028654, 0.044715


def gelu(x):
    return 0.5 * x * (1.0 + jnp.tanh(C0 * (x + C1 * x * x * x)))


def gelu_slope(x):
    t = jnp.tanh(C0 * (x + C1 * x * x * x))
    return 0.5 * (1.0 + t) + 0.5 * x * (1.0 - t * t) * (C0 * (1.0 + 3.0 * C1 * x * x))


def lanes(width):
    return lax.broadcasted_iota(jnp.int32, (1, width), 1)


def head_mask(h):
    lane = lanes(256)
    return jnp.where((lane >= OFF[h]) & (lane < OFF[h] + E), 1.0, 0.0).astype(F32)


def pieces(row, count):
    out = []
    done = 0
    while done < count:
        i, r0 = divmod(row + done, ROWS_I)
        n = min(count - done, ROWS_I - r0)
        out.append((i, r0, done, n))
        done += n
    return out


def split3(v):
    hi = half(v).astype(F32)
    mid = half(v - hi).astype(F32)
    lo = half(v - hi - mid).astype(F32)
    return hi, mid, lo


def pack3(v):
    hi, mid, lo = split3(v)
    return half(hi + pltpu.roll(mid, 16, 1) + pltpu.roll(lo, 32, 1))


def unpack3(v, axis):
    return v + pltpu.roll(v, 112, axis) + pltpu.roll(v, 96, axis)


def as_rows(parts, count):
    row = lax.broadcasted_iota(jnp.int32, (count, 128), 0)
    out = jnp.zeros((count, 128), F32)
    for r, part in parts:
        out = jnp.where(row == r, part, out)
    return out


def call(body, outs, args, scratch=(), vmem=48, flops=0, name=None):
    spaces = {"v": pltpu.VMEM, "a": pl.ANY, "s": pltpu.SMEM, "h": pltpu.HBM}
    return pl.pallas_call(
        body,
        out_shape=[jax.ShapeDtypeStruct(s, t) for s, t, _ in outs],
        in_specs=[pl.BlockSpec(memory_space=spaces[m]) for _, m in args],
        out_specs=[pl.BlockSpec(memory_space=spaces[m]) for _, _, m in outs],
        scratch_shapes=list(scratch),
        compiler_params=pltpu.CompilerParams(vmem_limit_bytes=vmem * MIB),
        cost_estimate=pl.CostEstimate(flops=int(flops), bytes_accessed=4 * MIB, transcendentals=0),
        name=name,
    )(*[a for a, _ in args])


DMA = pltpu.SemaphoreType.DMA


def pack_early_body(sc, lm, bm, la, g0, sem):
    cols = pl.ds(pl.multiple_of(sc[4] * 640, 128), 640)
    copies = [
        (bm.at[0, :, cols], g0.at[0:48, :]),
        (bm.at[1, :, cols], g0.at[48:96, :]),
        (lm.at[0, :, cols], g0.at[96:176, :]),
        (la.at[:, cols], g0.at[176:192, :]),
    ]
    copies = [pltpu.make_async_copy(a, b, sem.at[k]) for k, (a, b) in enumerate(copies)]
    for c in copies:
        c.start()
    for c in copies:
        c.wait()


def pack_body(sc, lm, om, bm, do, wsh, buf, sem):
    i = sc[0]
    blocks = [(80 * k, 80, (om if s == "o" else lm), n, D) for k, (s, n) in enumerate(SQUARE)]
    blocks += [(DEC_ROW, 80, do, None, DI), (BQ_ROW, 48, bm, 2, D)]
    for k in range(NI):
        lo, hi = ROWS_I * k, ROWS_I * (k + 1)

        @pl.when(i == k)
        def _(lo=lo, hi=hi):
            cs = []
            for row, count, ref, n, width in blocks:
                a, b = max(lo, row), min(hi, row + count)
                if a < b:
                    src = ref.at[a - row : b - row, :] if n is None else ref.at[n, a - row : b - row, :]
                    dst = buf.at[a - lo : b - lo, :] if width == D else buf.at[a - lo : b - lo, 0:width]
                    cs.append(pltpu.make_async_copy(src, dst, sem.at[len(cs)]))
            for c in cs:
                c.start()
            for c in cs:
                c.wait()

    out = pltpu.make_async_copy(buf, wsh, sem.at[8])
    out.start()
    out.wait()


def pieces_from(sc, own, sib):
    x, z, core = sc[2], sc[3], sc[4]
    out = []
    for side, (t0, t1, t2a, t2b, t3) in enumerate((own, sib)):
        c = core if side == 0 else 1 - core
        col = pl.ds(pl.multiple_of(c * 640, 128), 640)
        for e in range(4):
            for d in range(4):
                xs = jnp.where(c == 0, (x + 4 - d) & 3, (x + 4 - e) & 3)
                zs = jnp.where(c == 0, (z + 4 - e) & 3, (z + 4 - d) & 3)
                ref = (t0, t1, None, t3)[e] if e != 2 else (t2a, t2b)[d // 2]
                out.append((xs * 4 + zs, col, ref.at[d % 2 if e == 2 else d]))
    return out


def enc_body(
    sc, a0, a1, a2, a3, a4, b0, b1, b2, b3, b4, x_in, bg, lg, g_out, nb_o, k_o, v_o, q_o, pay, n_o, i_o, gs, acc, sem
):
    copies = [
        pltpu.make_async_copy(src, gs.at[pos, :, col], sem.at[k])
        for k, (pos, col, src) in enumerate(pieces_from(sc, (a0, a1, a2, a3, a4), (b0, b1, b2, b3, b4)))
    ]
    for c in copies:
        c.start()
    n_in, _ = norm(x_in[...].astype(F32))
    nb = half(n_in * bg[0:1, :])
    nb_o[...] = nb
    for c in copies:
        c.wait()
    save = pltpu.make_async_copy(gs, g_out, sem.at[32])
    save.start()
    k_o[...] = half(dot(nb, gs[:, 0:48, :].reshape(DI, D)))
    v_o[...] = half(dot(nb, gs[:, 48:96, :].reshape(DI, D)))
    z0b = gs[:, 176:192, :].reshape(R, D)
    nq, inv = norm(z0b.astype(F32))
    n_o[...] = half(nq)
    i_o[...] = jnp.broadcast_to(inv, (R, 128))
    q_o[...] = half(dot(half(nq * lg[0:1, :]), gs[:, 96:176, :].reshape(D, D)))
    acc[...] = jnp.zeros_like(acc)
    valid = lanes(N) + sc[1] * N < sc[5]
    lane = lanes(128)
    stats = jnp.zeros((R, 128), F32)
    for h in range(H):
        w = slice(WIN[h], WIN[h] + 256)
        mk = head_mask(h)
        s = dot_nt(q_o[:, w] * half(mk), k_o[:, w]) * SCALE
        s = jnp.where(valid, s, -1e30)
        m = jnp.max(s, axis=-1, keepdims=True)
        p = jnp.exp(s - m)
        acc[:, w] += dot(half(p), v_o[:, w]) * mk
        stats = jnp.where(lane == h, m, stats)
        stats = jnp.where(lane == 8 + h, jnp.sum(p, axis=-1, keepdims=True), stats)
    pay[:, 0:D] = half(acc[...])
    pay[:, D : D + 128] = pack3(stats)
    save.wait()


def combine_body(rcv, out):
    st = unpack3(rcv[:, :, D : D + 128].astype(F32), 2)
    peak = jnp.max(st, axis=0, keepdims=True)
    w = jnp.exp(st - peak)
    total = jnp.sum(w * pltpu.roll(st, 120, 2), axis=0, keepdims=True)
    coef = w / total
    lane = lax.broadcasted_iota(jnp.int32, (1, 1, 128), 2)
    for t in range(10):
        h0, h1 = 128 * t // E, (128 * t + 127) // E
        c = coef[:, :, h0 : h0 + 1]
        if h1 != h0:
            c = jnp.where(lane >= E * h1 - 128 * t, coef[:, :, h1 : h1 + 1], c)
        o = jnp.sum(rcv[:, :, 128 * t : 128 * t + 128].astype(F32) * c, axis=0)
        out[:, 128 * t : 128 * t + 128] = half(o)
    lse = jnp.where(lanes(128) < 8, (peak + jnp.log(total))[0], 0.0)
    out[:, D : D + 128] = pack3(lse)


class Ring:
    def __init__(self, w, slots, sem, order):
        self.w, self.slots, self.sem, self.order = w, slots, sem, order
        self.n = slots.shape[0]
        self.pos = {m: k for k, m in enumerate(order)}

    def copies(self, m):
        s = self.pos[m] % self.n
        return [
            pltpu.make_async_copy(
                self.w.at[i, :, r0 : r0 + n, :], self.slots.at[s, :, d0 : d0 + n, :], self.sem.at[s, k]
            )
            for k, (i, r0, d0, n) in enumerate(pieces(80 * m, 80))
        ]

    def start(self, m):
        for c in self.copies(m):
            c.start()

    def begin(self):
        for m in self.order[: self.n]:
            self.start(m)

    def get(self, m):
        for c in self.copies(m):
            c.wait()
        return self.slots[self.pos[m] % self.n].reshape(D, D)

    def done(self, m):
        k = self.pos[m] + self.n
        if k < len(self.order):
            self.start(self.order[k])


def forward_body(
    qin, cot, bg, lg, e_h, g_all, w,
    res, gqin, gain_o, pay, mix_o, nd_o, gq_o, z_h, h_h, a_h,
    slots, e, z0b, zs, zb, hs, qs, acc, kd, vd, dec, bq, dacc, gq, gkv, wsem, ssem, lsem,
):
    first = [
        pltpu.make_async_copy(e_h.at[:, 0:D], e, lsem.at[3]),
        pltpu.make_async_copy(g_all.at[:, 176:192, :], z0b, lsem.at[4]),
    ]
    for c in first:
        c.start()
    ring = Ring(w, slots, wsem, list(range(11)))
    ring.begin()
    copies = []
    for i, r0, d0, n in pieces(BQ_ROW, 48):
        copies.append(pltpu.make_async_copy(w.at[i, :, r0 : r0 + n, :], bq.at[:, d0 : d0 + n, :], lsem.at[0]))
    for i, r0, d0, n in pieces(DEC_ROW, 80):
        copies.append(
            pltpu.make_async_copy(w.at[i, :, r0 : r0 + n, 0:DI], dec.at[:, d0 : d0 + n, :], lsem.at[len(copies)])
        )
    for c in copies:
        c.start()
    saves = []

    def save(src, dst):
        c = pltpu.make_async_copy(src, dst, ssem.at[len(saves)])
        c.start()
        saves.append(c)

    def keep(k):
        zb[k] = half(zs[k])
        save(zb.at[k], z_h.at[k])

    def mul(a, m):
        out = dot(a, ring.get(m))
        ring.done(m)
        return out

    for c in first:
        c.wait()
    z1 = z0b[...].reshape(R, D).astype(F32) + mul(e[...], 0)
    zs[0] = z1
    keep(0)
    h1 = mul(half(norm(z1)[0] * lg[1:2, :]), 1)
    hs[0] = half(h1)
    save(hs.at[0], h_h.at[0])
    zs[1] = zs[0] + mul(half(gelu(h1)), 2)
    keep(1)
    s_b = half(norm(zs[1])[0] * lg[2:3, :])
    for k in range(3):
        qs[k] = half(mul(s_b, 3 + k))
        save(qs.at[k], a_h.at[k])
    acc[...] = jnp.zeros_like(acc)
    for h in range(H):
        win = slice(WIN[h], WIN[h] + 256)
        mk = head_mask(h)
        s = dot_nt(qs[0, :, win] * half(mk), qs[1, :, win]) * SCALE
        p = jnp.exp(s - jnp.max(s, axis=-1, keepdims=True))
        p = p / jnp.sum(p, axis=-1, keepdims=True)
        acc[:, win] += dot(half(p), qs[2, :, win]) * mk
    qs[3] = half(acc[...])
    save(qs.at[3], a_h.at[3])
    zs[2] = zs[1] + mul(qs[3], 6)
    keep(2)
    h2 = mul(half(norm(zs[2])[0] * lg[3:4, :]), 7)
    hs[1] = half(h2)
    save(hs.at[1], h_h.at[1])
    zs[3] = zs[2] + mul(half(gelu(h2)), 8)
    keep(3)
    c_b = half(norm(zs[3])[0] * lg[4:5, :])
    kd[...] = half(mul(c_b, 9))
    vd[...] = half(mul(c_b, 10))

    x = qin[...].astype(F32)
    n, inv = norm(x)
    nd = half(n * bg[1:2, :])
    nd_o[...] = nd
    for c in copies:
        c.wait()
    wq = bq[...].reshape(DI, D)
    wd = dec[...].reshape(D, DI)
    gq_o[...] = half(dot(nd, wq))
    mix_o[...] = half(dot_nt(cot[...], wd))
    dacc[...] = jnp.zeros_like(dacc)
    gq[...] = jnp.zeros_like(gq)
    gkv[...] = jnp.zeros_like(gkv)
    for h in range(H):
        win = slice(WIN[h], WIN[h] + 256)
        mk = head_mask(h)
        mkb = half(mk)
        qw, gw, kw, vw = gq_o[:, win], mix_o[:, win], kd[:, win], vd[:, win]
        s = dot_nt(qw * mkb, kw) * SCALE
        p = jnp.exp(s - jnp.max(s, axis=-1, keepdims=True))
        p = p / jnp.sum(p, axis=-1, keepdims=True)
        pb = half(p)
        dacc[:, win] += dot(pb, vw) * mk
        dp = dot_nt(gw * mkb, vw)
        ds = half(p * (dp - jnp.sum(p * dp, axis=-1, keepdims=True)))
        gq[:, win] += dot(ds, kw) * mk
        gkv[0, :, win] += dot_tn(ds, qw) * mk
        gkv[1, :, win] += dot_tn(pb, gw) * mk
    pay[:, 0:D] = half(gkv[0] * SCALE)
    pay[:, D : 2 * D] = half(gkv[1])
    mix = half(dacc[...])
    mix_o[...] = mix
    res[...] = half(x + dot(mix, wd))
    gqb = half(gq[...] * SCALE)
    gq_o[...] = gqb
    gin, gg = norm_back(dot_nt(gqb, wq), bg[1:2, :], n, inv)
    gqin[...] = cot[...].astype(F32) + gin
    gain_o[...] = gg
    for c in saves:
        c.wait()


def prepare_body(lg, z_h, h_h, a_h, n_h, i_h, s_h, act_h, p_h, n3_h, i3_h, zs, hs, qs, ns, vs, ss, acts, ps, sem, osem):
    loads = {}
    for k in range(4):
        loads["z", k] = pltpu.make_async_copy(z_h.at[k], zs.at[k], sem.at[k])
    for k in range(2):
        loads["h", k] = pltpu.make_async_copy(h_h.at[k], hs.at[k], sem.at[4 + k])
    loads["q"] = pltpu.make_async_copy(a_h.at[0:2], qs, sem.at[6])
    for c in loads.values():
        c.start()
    saves = []

    def save(src, dst):
        c = pltpu.make_async_copy(src, dst, osem.at[len(saves)])
        c.start()
        saves.append(c)

    for k, a in ((3, 0), (2, 2), (1, 1), (0, 4)):
        loads["z", k].wait()
        n, inv = norm(zs[k].astype(F32))
        ns[k] = half(n)
        save(ns.at[k], n3_h if k == 3 else n_h.at[k])
        vs[k] = jnp.broadcast_to(inv, (R, 128))
        acts[a] = half(n * lg[k + 1 : k + 2, :])
        save(acts.at[a], act_h.at[a])
    save(vs.at[0:3], i_h)
    save(vs.at[3], i3_h)
    for k, a in ((1, 3), (0, 5)):
        loads["h", k].wait()
        x = hs[k].astype(F32)
        t = jnp.tanh(C0 * (x + C1 * x * x * x))
        acts[a] = half(0.5 * x * (1.0 + t))
        save(acts.at[a], act_h.at[a])
        ss[k] = 0.5 * (1.0 + t) + 0.5 * x * (1.0 - t * t) * (C0 * (1.0 + 3.0 * C1 * x * x))
        save(ss.at[k], s_h.at[k])
    loads["q"].wait()
    for h in range(H):
        win = slice(WIN[h], WIN[h] + 256)
        s = dot_nt(qs[0, :, win] * half(head_mask(h)), qs[1, :, win]) * SCALE
        p = jnp.exp(s - jnp.max(s, axis=-1, keepdims=True))
        ps[h] = half(p / jnp.sum(p, axis=-1, keepdims=True))
    save(ps, p_h)
    for c in saves:
        c.wait()


def lat_backward_body(
    sc, gin, lg, w, e_h, n_h, i_h, s_h, act_h, a_h, p_h, gmix, pack_h, g1c_o, gains_o,
    slots, ns, vs, ss, acts, qs, ps, acc, acc2, acc3, gh, gw, pack, wsem, lsem, osem,
):
    order = [8, 7, 6, 3, 4, 5, 2, 1, 0]
    ring = Ring(w, slots, wsem, order)
    todo = [
        (i_h, vs),
        (act_h.at[0], acts.at[0]),
        (s_h.at[1], ss.at[1]),
        (act_h.at[3], acts.at[1]),
        (n_h.at[2], ns.at[2]),
        (act_h.at[2], acts.at[3]),
        (a_h.at[3], acts.at[4]),
        (p_h, ps),
        (a_h.at[0:3], qs.at[0:3]),
        (n_h.at[1], ns.at[1]),
        (act_h.at[1], acts.at[2]),
        (s_h.at[0], ss.at[0]),
        (act_h.at[5], acts.at[5]),
        (n_h.at[0], ns.at[0]),
        (act_h.at[4], acts.at[6]),
        (e_h.at[:, 0:D], acts.at[7]),
    ]
    loads = [pltpu.make_async_copy(a, b, lsem.at[k]) for k, (a, b) in enumerate(todo)]
    after = {8: (4, 5, 6), 7: (7, 8), 6: (9, 10, 11, 12), 3: (13, 14, 15)}
    ring.start(8)
    for c in loads[:4]:
        c.start()
    for m in order[1 : ring.n]:
        ring.start(m)

    def ready(*ks):
        for k in ks:
            loads[k].wait()

    src = sc[1] * 80
    start = pl.multiple_of(jnp.minimum((src >> 7) * 128, 1024), 128)
    offset = src - start
    lane = lanes(256)

    def put(ref, to):
        v = pltpu.roll(ref[:, pl.ds(start, 256)].astype(F32), (to - offset + 256) & 255, 1)
        return jnp.where((lane >= to) & (lane < to + 80), v, 0.0)

    leaves = [
        pltpu.make_async_copy(pack.at[k], pack_h.at[:, 256 * k : 256 * k + 256], osem.at[k]) for k in range(4)
    ]

    def weight_grad(window, first, count):
        a = acts[first : first + count].reshape(count * R, D)
        pack[window] = half(dot_tn(a, gw[first : first + count].reshape(count * R, 256)))
        leaves[window].start()

    def mul(g_b, m):
        out = dot_nt(g_b, ring.get(m))
        ring.done(m)
        for k in after.get(m, ()):
            loads[k].start()
        return out

    gain_rows = []

    def back(g, k):
        out, gg = norm_back(g, lg[k + 1 : k + 2, :], ns[k].astype(F32), vs[k][:, 0:1])
        for t in range(10):
            gain_rows.append((10 * k + t, gg[:, 128 * t : 128 * t + 128]))
        return out

    for t in range(10):
        acc[:, 128 * t : 128 * t + 128] = gin[:, 16 * t : 16 * t + 16, :].reshape(R, 128).astype(F32)
    tile = lanes(128)
    values = pltpu.roll(gin[:, 176:192, :].reshape(R, 128).astype(F32), 80, 1)
    gw[0, :, 0:128] = half(jnp.where(tile < 80, gin[:, 160:176, :].reshape(R, 128).astype(F32), values))
    gw[0, :, 128:256] = half(jnp.where(tile < 32, values, 0.0))
    gw[1] = half(put(acc, 160))
    ready(0, 1, 2, 3)
    gh[...] = half(mul(half(acc[...]), 8) * ss[1])
    weight_grad(0, 0, 2)
    ready(4)
    gw[3] = half(put(gh, 0))
    acc[...] += back(mul(gh[...], 7), 2)
    gw[4] = half(put(acc, 80))
    qs[3] = half(mul(half(acc[...]), 6))
    acc2[...] = jnp.zeros_like(acc2)
    acc3[...] = jnp.zeros_like(acc3)
    ready(5, 6, 7, 8)
    for h in range(H):
        win = slice(WIN[h], WIN[h] + 256)
        mk = head_mask(h)
        pb = ps[h]
        p = pb.astype(F32)
        dp = dot_nt(qs[3, :, win] * half(mk), qs[2, :, win])
        ds = half(p * (dp - jnp.sum(p * dp, axis=-1, keepdims=True)) * SCALE)
        acc2[:, win] += dot(ds, qs[1, :, win]) * mk
        acc3[0, :, win] += dot_tn(ds, qs[0, :, win]) * mk
        acc3[1, :, win] += dot_tn(pb, qs[3, :, win]) * mk
    gw[2] = half(put(acc2, 0) + put(acc3.at[0], 80) + put(acc3.at[1], 160))
    gn = mul(half(acc2[...]), 3)
    gn = gn + mul(half(acc3[0]), 4)
    gn = gn + mul(half(acc3[1]), 5)
    ready(9, 10)
    weight_grad(1, 2, 1)
    acc[...] += back(gn, 1)
    gw[5] = half(put(acc, 160))
    ready(11, 12)
    gh[...] = half(mul(half(acc[...]), 2) * ss[0])
    weight_grad(2, 3, 3)
    gw[6] = half(put(gh, 0))
    ready(13, 14, 15)
    acc[...] += back(mul(gh[...], 1), 0)
    gw[7] = half(put(acc, 80))
    g1c_o[...] = half(put(acc, 0)[:, 0:128])
    gmix[...] = half(mul(half(acc[...]), 0))
    weight_grad(3, 6, 2)
    gains_o[...] = as_rows(gain_rows, 32)
    for c in leaves:
        c.wait()


def key_value_back_body(sc, rcv, lg, n3_h, i3_h, w, out, gain_o, wbuf, nbuf, ibuf, sem):
    rows = pl.ds(pl.multiple_of(sc[1] * 16, 16), 16)
    copies = []
    for k, m in enumerate((9, 10)):
        for i, r0, d0, n in pieces(80 * m, 80):
            copies.append((w.at[i, :, r0 : r0 + n, :], wbuf.at[k, :, d0 : d0 + n, :]))
    copies += [(n3_h.at[rows, :], nbuf), (i3_h.at[rows, :], ibuf)]
    copies = [pltpu.make_async_copy(a, b, sem.at[k]) for k, (a, b) in enumerate(copies)]
    for c in copies:
        c.start()
    s = half(jnp.sum(rcv[...].astype(F32), axis=0))
    for j in range(NJ):
        base = min(128 * (80 * j // 128), 1024)
        for k in range(2):
            v = s[:, D * k + base : D * k + base + 256].astype(F32)
            if 80 * j > base:
                v = pltpu.roll(v, 256 - (80 * j - base), 1)
            out[j, 160 + 16 * k : 176 + 16 * k, :] = half(v[:, 0:128])
    for c in copies:
        c.wait()
    gn = dot_nt(s[:, 0:D], wbuf[0].reshape(D, D)) + dot_nt(s[:, D : 2 * D], wbuf[1].reshape(D, D))
    g, gg = norm_back(gn, lg[4:5, :], nbuf[...].astype(F32), ibuf[:, 0:1])
    gain_o[...] = gg
    g = jnp.concatenate([half(g[:, 128 * t : 128 * t + 128]) for t in range(10)], axis=0)
    for j in range(NJ):
        out[j, 0:160, :] = g


def dec_weights_body(mix, cot, nd, gq, out, buf, sem):
    g = half(dot_tn(mix[...], cot[...]))
    for i in range(NI):
        for t in range(6):
            buf[i, 160 * t : 160 * t + 160, :] = g[160 * i : 160 * i + 160, 128 * t : 128 * t + 128]
    one = pltpu.make_async_copy(buf.at[:, 0:960, :], out.at[:, 0:960, :], sem.at[0])
    one.start()
    g = half(dot_tn(nd[...], gq[...]))
    for i in range(NI):
        for t in range(10):
            r = 960 + 96 * t
            buf[i, r : r + 96, :] = g[96 * i : 96 * i + 96, 128 * t : 128 * t + 128]
    two = pltpu.make_async_copy(buf.at[:, 960:1920, :], out.at[:, 960:1920, :], sem.at[1])
    two.start()
    one.wait()
    two.wait()


def spread(chunk, pay, td, tb):
    fill = jnp.zeros((96, 128), F32)
    for t in range(6):
        v = jnp.concatenate([chunk[160 * t : 160 * t + 160, :].astype(F32), fill], axis=0)
        td[128 * t : 128 * t + 128, :] = v.T
    fill = jnp.zeros((32, 128), F32)
    for t in range(10):
        v = jnp.concatenate([chunk[960 + 96 * t : 960 + 96 * t + 96, :].astype(F32), fill], axis=0)
        tb[128 * t : 128 * t + 128, :] = v.T
    for j in range(NJ):
        tail = pltpu.roll(td[48 * j : 48 * j + 48, 128:256], 96, 1)
        pay[j, 512:560, :] = half(tb[80 * j : 80 * j + 48, :] + tail)
        pay[j, 560:592, :] = half(tb[80 * j + 48 : 80 * j + 80, :])
        pay[j, 592:640, :] = half(td[48 * j : 48 * j + 48, 0:128])


def enc_back_body(
    sc, x_in, bg, lg, gd, gc, gmix_h, e_h, q_h, k_h, v_h, g_all, dw_h, n0_h, i0_h, gin_o, pay,
    gmix, e, q, k, v, wkv, n0, i0, gq, gkt, gvt, dw, td, tb, sem,
):
    pairs = [(gmix_h, gmix), (q_h, q), (k_h, k), (v_h, v), (e_h, e), (g_all, wkv), (dw_h, dw), (n0_h, n0), (i0_h, i0)]
    loads = [pltpu.make_async_copy(a, b, sem.at[n]) for n, (a, b) in enumerate(pairs)]
    for c in loads[:5]:
        c.start()
    for c in loads[:5]:
        c.wait()
    for c in loads[5:]:
        c.start()
    lse = unpack3(e[:, D : D + 128].astype(F32), 1)
    valid = lanes(N) + sc[1] * N < sc[5]
    gq[...] = jnp.zeros_like(gq)
    for h in range(H):
        win = slice(WIN[h], WIN[h] + 256)
        mk = head_mask(h)
        mkb = half(mk)
        qw, gw, kw, vw = q[:, win], gmix[:, win], k[:, win], v[:, win]
        rd = jnp.sum(gw.astype(F32) * e[:, win].astype(F32) * mk, axis=-1, keepdims=True)
        s = dot_nt(qw * mkb, kw) * SCALE
        p = jnp.where(valid, jnp.exp(jnp.where(valid, s, -1e30) - lse[:, h : h + 1]), 0.0)
        dp = dot_nt(gw * mkb, vw)
        ds = half(p * (dp - rd))
        gq[:, win] += dot(ds, kw) * mk
        o = OFF[h]
        gkt[E * h : E * h + E, :] = half(dot_tn(qw, ds)[o : o + E, :] * SCALE)
        gvt[E * h : E * h + E, :] = half(dot_tn(gw, half(p))[o : o + E, :])
    pay[:, 320:400, :] = gkt[...].reshape(NJ, 80, 128)
    pay[:, 400:480, :] = gvt[...].reshape(NJ, 80, 128)
    loads[5].wait()
    gqs = gq[...] * SCALE
    gqt = half(gqs.T)
    pay[:, 160:240, :] = gqt[:, 0:128].reshape(NJ, 80, 128)
    pay[:, 240:320, :] = gqt[:, 128:256].reshape(NJ, 80, 128)
    loads[7].wait()
    loads[8].wait()
    gz, g0 = norm_back(dot_nt(half(gqs), wkv[:, 96:176, :].reshape(D, D)), lg[0:1, :], n0[...].astype(F32), i0[:, 0:1])
    gzt = half(gz.T)
    pay[:, 0:80, :] = gzt[:, 0:128].reshape(NJ, 80, 128)
    pay[:, 80:160, :] = gzt[:, 128:256].reshape(NJ, 80, 128)
    n, inv = norm(x_in[...].astype(F32))
    gnt = dot(wkv[:, 0:48, :].reshape(DI, D), gkt[...]) + dot(wkv[:, 48:96, :].reshape(DI, D), gvt[...])
    gin, gg = norm_back(gnt.T, bg[0:1, :], n, inv)
    gin_o[...] = gin
    rows = [(t, gg[:, 128 * t : 128 * t + 128]) for t in range(6)]
    rows += [(6 + t, gd[:, 128 * t : 128 * t + 128]) for t in range(6)]
    rows += [(12 + t, g0[:, 128 * t : 128 * t + 128]) for t in range(10)]
    rows += [(22 + t, gc[:, 128 * t : 128 * t + 128]) for t in range(10)]
    g = half(as_rows(rows, 32))
    for j in range(NJ):
        pay[j, 480:512, :] = g
    loads[6].wait()
    spread(dw, pay, td, tb)


def tail_one_body(rcv, nf_h, n0_h, lg, lat_gain, g1c, out, dec_o, bq_o, nf, n0, left, sem):
    loads = [
        pltpu.make_async_copy(nf_h, nf, sem.at[0]),
        pltpu.make_async_copy(n0_h, n0, sem.at[1]),
    ]
    for c in loads:
        c.start()
    sums = jnp.sum(rcv[:, 0:320, :].astype(F32), axis=0)
    fill = jnp.zeros((48, 128), F32)
    left[...] = jnp.zeros_like(left)
    for s in range(NJ):
        left[0:80, 128 * s : 128 * s + 128] = rcv[s, 320:400, :]
        left[128:208, 128 * s : 128 * s + 128] = rcv[s, 400:480, :]
    loads[1].wait()
    nq = half(n0[...].astype(F32) * lg[0:1, :])
    a = jnp.concatenate([sums[160:240], fill], axis=0).T
    b = jnp.concatenate([sums[240:320], fill], axis=0).T
    w0 = dot_tn(nq, half(jnp.concatenate([a, b], axis=0)))
    a = jnp.concatenate([sums[0:80], fill], axis=0).T
    b = jnp.concatenate([sums[80:160], fill], axis=0).T
    gz = half(jnp.concatenate([a, b], axis=0) + g1c[...].astype(F32))
    gains = jnp.sum(rcv[:, 480:512, :].astype(F32), axis=0)
    gains = half(jnp.concatenate([gains, lat_gain[...]], axis=0))
    loads[0].wait()
    wt = dot(left[...], nf[...]).T
    lane = lanes(128)
    key, value = wt[:, 0:128], wt[:, 128:256]
    one = half(jnp.where(lane < 80, key, pltpu.roll(value, 80, 1)))
    other = pltpu.roll(value, 32, 1)
    for i in range(NI):
        r = 96 * i
        beside = jnp.concatenate([other[r : r + 96, :], jnp.zeros((64, 128), F32)], axis=0)
        out[i, 0:160, :] = half(jnp.where(lane < 80, w0[160 * i : 160 * i + 160, :], beside))
        out[i, 160:192, :] = gz[32 * i : 32 * i + 32, :]
        out[i, 192:288, :] = one[r : r + 96, :]
        out[i, 288:352, :] = gains
    s = jnp.sum(rcv[:, 512:640, :].astype(F32), axis=0)
    bq_o[...] = s[0:80, 0:96]
    dec_o[:, 0:128] = s[80:128]
    dec_o[:, 128:160] = pltpu.roll(s[0:48], 32, 1)[:, 0:32]


def tail_two_body(rcv, pack_h, bq, arr_o, lm_o, om_o, bm_o, lat_o, byte_o, pack, sem):
    load = pltpu.make_async_copy(pack_h, pack, sem)
    load.start()
    sums = jnp.sum(rcv[...].astype(F32), axis=0)
    lm_o[0] = sums[0:160, 0:80]
    arr_o[...] = sums[160:192, 0:80]
    lane = lanes(128)
    value = jnp.where(lane < 48, pltpu.roll(sums[192:288], 48, 1), pltpu.roll(sums[0:96], 96, 1))
    fill = jnp.zeros((32, 128), F32)
    bm_o[0] = jnp.concatenate([sums[192:288], fill], axis=0).T[0:80, 0:96]
    bm_o[1] = jnp.concatenate([value, fill], axis=0).T[0:80, 0:96]
    bm_o[2] = bq[...]
    g = sums[288:352]
    for t in range(6):
        for b in range(2):
            byte_o[b : b + 1, 128 * t : 128 * t + 128] = g[6 * b + t : 6 * b + t + 1, :]
    for t in range(10):
        for b in range(5):
            r = {0: 12, 1: 32, 2: 42, 3: 52, 4: 22}[b] + t
            lat_o[b : b + 1, 128 * t : 128 * t + 128] = g[r : r + 1, :]
    load.wait()
    for m, (kind, n) in enumerate(SQUARE):
        window, o = PLACE[m]
        v = pack[:, 256 * window : 256 * window + 256].astype(F32)
        if o:
            v = pltpu.roll(v, 256 - o, 1)
        if kind == "l":
            lm_o[n] = v[:, 0:80]
        else:
            om_o[n] = v[:, 0:80]


def line(y, c, x, z):
    return ((y % 4) * 2 + c) * NJ + (x % 4) * NZ + (z % 4)


EVERY = [(y, c, x, z) for y in range(4) for c in range(2) for x in range(NX) for z in range(NZ)]


def along(stage, d):
    out = []
    for y, c, x, z in EVERY:
        on_x = (c == 0) == (stage == 0)
        out.append((line(y, c, x, z), line(y, c, x + d, z) if on_x else line(y, c, x, z + d)))
    return out


SWAP = [(line(y, c, x, z), line(y, 1 - c, x, z)) for y, c, x, z in EVERY]


def exchange(v, axes):
    flat = v.reshape(v.shape[0] * v.shape[1], v.shape[2])
    return lax.all_to_all(flat, axes, split_axis=0, concat_axis=0, tiled=True).reshape(v.shape)


def shards(inputs, queries, lengths, latent_array, latent_mats, out_mats, byte_mats, dec_out, lg, bg, cotangent):
    y, core, x, z = (lax.axis_index(a) for a in AXES)
    i, j = y * 2 + core, x * NZ + z
    sc = jnp.stack([i, j, x, z, core, lengths[0]]).astype(jnp.int32)
    xin, qin, cot = inputs[0], queries[0], cotangent[0]

    (wsh,) = call(
        pack_body,
        [((ROWS_I, D), BF, "h")],
        [(sc, "s"), (latent_mats, "h"), (out_mats, "h"), (byte_mats, "h"), (dec_out, "h")],
        [pltpu.VMEM((ROWS_I, D), BF), DMA((9,))],
        vmem=60,
        name="pack",
    )
    (g0,) = call(
        pack_early_body,
        [((192, 640), BF, "v")],
        [(sc, "s"), (latent_mats, "h"), (byte_mats, "h"), (latent_array, "h")],
        [DMA((4,))],
        vmem=60,
        name="pack_early",
    )
    w = lax.all_gather(wsh, AXES, axis=0, tiled=True).reshape(NI, NJ, ROWS_I, D)

    s0 = jnp.stack([g0] + [lax.ppermute(g0, AXES, along(0, d)) for d in (1, 2, 3)])
    t1, t3 = (lax.ppermute(s0, AXES, along(1, d)) for d in (1, 3))
    t2a, t2b = lax.ppermute(t1[0:2], AXES, along(1, 1)), lax.ppermute(t3[2:4], AXES, along(1, 3))
    own = [s0, t1, t2a, t2b, t3]
    sib = [lax.ppermute(v, AXES, SWAP) for v in own]
    g_all, nb, k_b, v_b, q_b, pay, n0, i0 = call(
        enc_body,
        [
            ((NJ, 192, D), BF, "h"),
            ((N, DI), BF, "v"),
            ((N, D), BF, "v"),
            ((N, D), BF, "v"),
            ((R, D), BF, "v"),
            ((R, D + 128), BF, "v"),
            ((R, D), BF, "v"),
            ((R, 128), F32, "v"),
        ],
        [(sc, "s")] + [(v, "a") for v in own + sib] + [(xin, "v"), (bg, "v"), (lg, "v")],
        [pltpu.VMEM((NJ, 192, D), BF), pltpu.VMEM((R, D), F32), DMA((33,))],
        vmem=60,
        flops=3e9,
        name="enc",
    )
    rcv = exchange(pay.reshape(NJ, 16, D + 128), BLK)
    (mine,) = call(combine_body, [((16, D + 128), BF, "v")], [(rcv, "v")], name="combine")
    e = lax.all_gather(mine, BLK, axis=0, tiled=True)

    big = (NJ, 80, D)
    res, gqin, gd, dpay, mix, nd, gq, z_h, h_h, a_h = call(
        forward_body,
        [
            ((N, DI), BF, "v"),
            ((N, DI), F32, "v"),
            ((1, DI), F32, "v"),
            ((R, 2 * D), BF, "v"),
            ((N, D), BF, "v"),
            ((N, DI), BF, "v"),
            ((N, D), BF, "v"),
            ((4, R, D), BF, "h"),
            ((2, R, D), BF, "h"),
            ((4, R, D), BF, "h"),
        ],
        [(qin, "v"), (cot, "v"), (bg, "v"), (lg, "v"), (e, "h"), (g_all, "h"), (w, "h")],
        [
            pltpu.VMEM((3,) + big, BF),
            pltpu.VMEM((R, D), BF),
            pltpu.VMEM((NJ, 16, D), BF),
            pltpu.VMEM((4, R, D), F32),
            pltpu.VMEM((4, R, D), BF),
            pltpu.VMEM((2, R, D), BF),
            pltpu.VMEM((4, R, D), BF),
            pltpu.VMEM((R, D), F32),
            pltpu.VMEM((R, D), BF),
            pltpu.VMEM((R, D), BF),
            pltpu.VMEM((NJ, 80, DI), BF),
            pltpu.VMEM((NJ, 48, D), BF),
            pltpu.VMEM((N, D), F32),
            pltpu.VMEM((N, D), F32),
            pltpu.VMEM((2, R, D), F32),
            DMA((3, 2)),
            DMA((10,)),
            DMA((5,)),
        ],
        vmem=54,
        flops=1.5e10,
        name="forward",
    )
    rows = exchange(dpay.reshape(NJ, 16, 2 * D), BLK)
    n_h, i_h, s_h, act_h, p_h, n3, i3 = call(
        prepare_body,
        [
            ((3, R, D), BF, "h"),
            ((3, R, 128), F32, "h"),
            ((2, R, D), F32, "h"),
            ((6, R, D), BF, "h"),
            ((H, R, R), BF, "h"),
            ((R, D), BF, "h"),
            ((R, 128), F32, "h"),
        ],
        [(lg, "v"), (z_h, "h"), (h_h, "h"), (a_h, "h")],
        [
            pltpu.VMEM((4, R, D), BF),
            pltpu.VMEM((2, R, D), BF),
            pltpu.VMEM((2, R, D), BF),
            pltpu.VMEM((4, R, D), BF),
            pltpu.VMEM((4, R, 128), F32),
            pltpu.VMEM((2, R, D), F32),
            pltpu.VMEM((6, R, D), BF),
            pltpu.VMEM((H, R, R), BF),
            DMA((7,)),
            DMA((15,)),
        ],
        vmem=58,
        flops=5e9,
        name="prepare",
    )
    (dw,) = call(
        dec_weights_body,
        [((NI, 1920, 128), BF, "h")],
        [(mix, "v"), (cot, "v"), (nd, "v"), (gq, "v")],
        [pltpu.VMEM((NI, 1920, 128), BF), DMA((2,))],
        vmem=60,
        flops=4e9,
        name="dec_weights",
    )
    kv, gc = call(
        key_value_back_body,
        [((NJ, 192, 128), BF, "v"), ((1, D), F32, "v")],
        [(sc, "s"), (rows, "v"), (lg, "v"), (n3, "h"), (i3, "h"), (w, "h")],
        [pltpu.VMEM((2,) + big, BF), pltpu.VMEM((16, D), BF), pltpu.VMEM((16, 128), F32), DMA((6,))],
        vmem=18,
        flops=1e8,
        name="key_value_back",
    )
    gin4 = exchange(kv, BLK)
    nb, _ = lax.optimization_barrier((nb, gc))
    nf = lax.all_gather(nb, BLK, axis=0, tiled=True)
    dw = lax.psum_scatter(dw.reshape(NI * 1920, 128), BATCH, scatter_dimension=0, tiled=True)

    gmix, pack, g1c, lat_gain = call(
        lat_backward_body,
        [((R, D), BF, "v"), ((D, 1024), BF, "h"), ((R, 128), BF, "v"), ((32, 128), F32, "v")],
        [(sc, "s"), (gin4, "v"), (lg, "v")] + [(v, "h") for v in (w, e, n_h, i_h, s_h, act_h, a_h, p_h)],
        [
            pltpu.VMEM((2,) + big, BF),
            pltpu.VMEM((3, R, D), BF),
            pltpu.VMEM((3, R, 128), F32),
            pltpu.VMEM((2, R, D), F32),
            pltpu.VMEM((8, R, D), BF),
            pltpu.VMEM((4, R, D), BF),
            pltpu.VMEM((H, R, R), BF),
            pltpu.VMEM((R, D), F32),
            pltpu.VMEM((R, D), F32),
            pltpu.VMEM((2, R, D), F32),
            pltpu.VMEM((R, D), BF),
            pltpu.VMEM((8, R, 256), BF),
            pltpu.VMEM((4, D, 256), BF),
            DMA((2, 2)),
            DMA((16,)),
            DMA((4,)),
        ],
        vmem=57,
        flops=8e10,
        name="lat_backward",
    )
    pack = lax.psum_scatter(pack, BATCH, scatter_dimension=0, tiled=True)
    gin, epay = call(
        enc_back_body,
        [((N, DI), F32, "v"), ((NJ, 640, 128), BF, "v")],
        [(sc, "s"), (xin, "v"), (bg, "v"), (lg, "v"), (gd, "v"), (gc, "v")]
        + [(v, "h") for v in (gmix, e, q_b, k_b, v_b, g_all, dw, n0, i0)],
        [
            pltpu.VMEM((R, D), BF),
            pltpu.VMEM((R, D + 128), BF),
            pltpu.VMEM((R, D), BF),
            pltpu.VMEM((N, D), BF),
            pltpu.VMEM((N, D), BF),
            pltpu.VMEM((NJ, 192, D), BF),
            pltpu.VMEM((R, D), BF),
            pltpu.VMEM((R, 128), F32),
            pltpu.VMEM((R, D), F32),
            pltpu.VMEM((D, N), BF),
            pltpu.VMEM((D, N), BF),
            pltpu.VMEM((1920, 128), BF),
            pltpu.VMEM((DI, 256), F32),
            pltpu.VMEM((D, 128), F32),
            DMA((9,)),
        ],
        vmem=58,
        flops=3e9,
        name="enc_back",
    )
    r1 = exchange(epay, BLK)
    p2, dec_grad, bq_grad = call(
        tail_one_body,
        [((NI, 352, 128), BF, "v"), ((48, 160), F32, "v"), ((80, 96), F32, "v")],
        [(r1, "v"), (nf, "h"), (n0, "h"), (lg, "v"), (lat_gain, "v"), (g1c, "v")],
        [pltpu.VMEM((NJ * N, DI), BF), pltpu.VMEM((R, D), BF), pltpu.VMEM((256, 2048), BF), DMA((2,))],
        name="tail_one",
    )
    r2 = exchange(p2, BATCH)
    arr, lm, om, byte_grads, lat_gains, byte_gain = call(
        tail_two_body,
        [
            ((32, 80), F32, "v"),
            ((10, 160, 80), F32, "v"),
            ((2, 160, 80), F32, "v"),
            ((3, 80, 96), F32, "v"),
            ((5, D), F32, "v"),
            ((2, DI), F32, "v"),
        ],
        [(r2, "v"), (pack, "h"), (bq_grad, "v")],
        [pltpu.VMEM((160, 1024), BF), DMA],
        name="tail_two",
    )
    byte_grads = jnp.swapaxes(byte_grads, 1, 2)
    return (res[None], gin[None], gqin[None], arr, lm, om, byte_grads, dec_grad.T, lat_gains, byte_gain)


def solution(mesh):
    grid = Mesh(mesh.devices.reshape(4, 2, NX, NZ), AXES)
    return jax.shard_map(
        shards,
        mesh=grid,
        in_specs=(
            P(BATCH, BLK, None),
            P(BATCH, BLK, None),
            P(BATCH),
            P(BLK, None),
            P(None, BLK, None),
            P(None, BLK, None),
            P(None, BLK, None),
            P(BLK, None),
            P(),
            P(),
            P(BATCH, BLK, None),
        ),
        out_specs=(
            P(BATCH, BLK, None),
            P(BATCH, BLK, None),
            P(BATCH, BLK, None),
            P(BATCH, BLK),
            P(None, BATCH, BLK),
            P(None, BATCH, BLK),
            P(None, BATCH, BLK),
            P(BATCH, BLK),
            P(),
            P(),
        ),
        check_vma=False,
    )
```

```python
import jax
import jax.numpy as jnp
from jax import lax
from jax.experimental import pallas as pl
from jax.experimental.pallas import tpu as pltpu
from jax.sharding import Mesh, PartitionSpec as P

F32, BF = jnp.float32, jnp.bfloat16
D, DI, R, N, H, E = 1280, 768, 256, 128, 8, 160
NX, NZ, NJ, NI = 4, 4, 16, 8
SCALE = E**-0.5
EPS = 1e-5
MIB = 1 << 20
AXES = ("y", "core", "x", "z")
BATCH = ("y", "core")
BLK = ("x", "z")
WIN = [128 * (E * h // 128) for h in range(H)]
OFF = [E * h - WIN[h] for h in range(H)]
SQUARE = [("o", 0), ("l", 1), ("l", 2), ("l", 3), ("l", 4), ("l", 5), ("o", 1), ("l", 6), ("l", 7), ("l", 8), ("l", 9)]
ROWS_I = 128
DEC_ROW, BQ_ROW = 880, 960
PLACE = {9: (0, 0), 10: (0, 80), 8: (0, 160), 3: (1, 0), 4: (1, 80), 5: (1, 160), 7: (2, 0), 6: (2, 80), 2: (2, 160), 1: (3, 0), 0: (3, 80)}


def dot(a, b, ca=1, cb=0):
    return lax.dot_general(a, b, (((ca,), (cb,)), ((), ())), preferred_element_type=F32)


def dot_nt(a, b):
    return dot(a, b, 1, 1)


def dot_tn(a, b):
    return dot(a, b, 0, 0)


def half(v):
    return v.astype(BF)


def norm(v):
    c = v - jnp.mean(v, axis=-1, keepdims=True)
    inv = lax.rsqrt(jnp.mean(c * c, axis=-1, keepdims=True) + EPS)
    return c * inv, inv


def norm_back(g, gain, n, inv):
    gg = jnp.sum(g * n, axis=0, keepdims=True)
    inner = g * gain
    m1 = jnp.mean(inner, axis=-1, keepdims=True)
    m2 = jnp.mean(inner * n, axis=-1, keepdims=True)
    return inv * (inner - m1 - n * m2), gg


C0, C1 = 0.7978845608028654, 0.044715


def gelu(x):
    return 0.5 * x * (1.0 + jnp.tanh(C0 * (x + C1 * x * x * x)))


def gelu_slope(x):
    t = jnp.tanh(C0 * (x + C1 * x * x * x))
    return 0.5 * (1.0 + t) + 0.5 * x * (1.0 - t * t) * (C0 * (1.0 + 3.0 * C1 * x * x))


def lanes(width):
    return lax.broadcasted_iota(jnp.int32, (1, width), 1)


def head_mask(h):
    lane = lanes(256)
    return jnp.where((lane >= OFF[h]) & (lane < OFF[h] + E), 1.0, 0.0).astype(F32)


def pieces(row, count):
    out = []
    done = 0
    while done < count:
        i, r0 = divmod(row + done, ROWS_I)
        n = min(count - done, ROWS_I - r0)
        out.append((i, r0, done, n))
        done += n
    return out


def split3(v):
    hi = half(v).astype(F32)
    mid = half(v - hi).astype(F32)
    lo = half(v - hi - mid).astype(F32)
    return hi, mid, lo


def pack3(v):
    hi, mid, lo = split3(v)
    return half(hi + pltpu.roll(mid, 16, 1) + pltpu.roll(lo, 32, 1))


def unpack3(v, axis):
    return v + pltpu.roll(v, 112, axis) + pltpu.roll(v, 96, axis)


def as_rows(parts, count):
    row = lax.broadcasted_iota(jnp.int32, (count, 128), 0)
    out = jnp.zeros((count, 128), F32)
    for r, part in parts:
        out = jnp.where(row == r, part, out)
    return out


def call(body, outs, args, scratch=(), vmem=48, flops=0, name=None):
    spaces = {"v": pltpu.VMEM, "a": pl.ANY, "s": pltpu.SMEM, "h": pltpu.HBM}
    return pl.pallas_call(
        body,
        out_shape=[jax.ShapeDtypeStruct(s, t) for s, t, _ in outs],
        in_specs=[pl.BlockSpec(memory_space=spaces[m]) for _, m in args],
        out_specs=[pl.BlockSpec(memory_space=spaces[m]) for _, _, m in outs],
        scratch_shapes=list(scratch),
        compiler_params=pltpu.CompilerParams(vmem_limit_bytes=vmem * MIB),
        cost_estimate=pl.CostEstimate(flops=int(flops), bytes_accessed=4 * MIB, transcendentals=0),
        name=name,
    )(*[a for a, _ in args])


DMA = pltpu.SemaphoreType.DMA


def pack_early_body(sc, lm, bm, la, g0, sem):
    cols = pl.ds(pl.multiple_of(sc[4] * 640, 128), 640)
    copies = [
        (bm.at[0, :, cols], g0.at[0:48, :]),
        (bm.at[1, :, cols], g0.at[48:96, :]),
        (lm.at[0, :, cols], g0.at[96:176, :]),
        (la.at[:, cols], g0.at[176:192, :]),
    ]
    copies = [pltpu.make_async_copy(a, b, sem.at[k]) for k, (a, b) in enumerate(copies)]
    for c in copies:
        c.start()
    for c in copies:
        c.wait()


def pack_body(sc, lm, om, bm, do, wsh, buf, sem):
    i = sc[0]
    blocks = [(80 * k, 80, (om if s == "o" else lm), n, D) for k, (s, n) in enumerate(SQUARE)]
    blocks += [(DEC_ROW, 80, do, None, DI), (BQ_ROW, 48, bm, 2, D)]
    for k in range(NI):
        lo, hi = ROWS_I * k, ROWS_I * (k + 1)

        @pl.when(i == k)
        def _(lo=lo, hi=hi):
            cs = []
            for row, count, ref, n, width in blocks:
                a, b = max(lo, row), min(hi, row + count)
                if a < b:
                    src = ref.at[a - row : b - row, :] if n is None else ref.at[n, a - row : b - row, :]
                    dst = buf.at[a - lo : b - lo, :] if width == D else buf.at[a - lo : b - lo, 0:width]
                    cs.append(pltpu.make_async_copy(src, dst, sem.at[len(cs)]))
            for c in cs:
                c.start()
            for c in cs:
                c.wait()

    out = pltpu.make_async_copy(buf, wsh, sem.at[8])
    out.start()
    out.wait()


def pieces_from(sc, own, sib):
    x, z, core = sc[2], sc[3], sc[4]
    out = []
    for side, (t0, t1, t2a, t2b, t3) in enumerate((own, sib)):
        c = core if side == 0 else 1 - core
        col = pl.ds(pl.multiple_of(c * 640, 128), 640)
        for e in range(4):
            for d in range(4):
                xs = jnp.where(c == 0, (x + 4 - d) & 3, (x + 4 - e) & 3)
                zs = jnp.where(c == 0, (z + 4 - e) & 3, (z + 4 - d) & 3)
                ref = (t0, t1, None, t3)[e] if e != 2 else (t2a, t2b)[d // 2]
                out.append((xs * 4 + zs, col, ref.at[d % 2 if e == 2 else d]))
    return out


def enc_body(
    sc, a0, a1, a2, a3, a4, b0, b1, b2, b3, b4, x_in, bg, lg, g_out, nb_o, k_o, v_o, q_o, pay, n_o, i_o, gs, acc, sem
):
    copies = [
        pltpu.make_async_copy(src, gs.at[pos, :, col], sem.at[k])
        for k, (pos, col, src) in enumerate(pieces_from(sc, (a0, a1, a2, a3, a4), (b0, b1, b2, b3, b4)))
    ]
    for c in copies:
        c.start()
    n_in, _ = norm(x_in[...].astype(F32))
    nb = half(n_in * bg[0:1, :])
    nb_o[...] = nb
    for c in copies:
        c.wait()
    save = pltpu.make_async_copy(gs, g_out, sem.at[32])
    save.start()
    k_o[...] = half(dot(nb, gs[:, 0:48, :].reshape(DI, D)))
    v_o[...] = half(dot(nb, gs[:, 48:96, :].reshape(DI, D)))
    z0b = gs[:, 176:192, :].reshape(R, D)
    nq, inv = norm(z0b.astype(F32))
    n_o[...] = half(nq)
    i_o[...] = jnp.broadcast_to(inv, (R, 128))
    q_o[...] = half(dot(half(nq * lg[0:1, :]), gs[:, 96:176, :].reshape(D, D)))
    acc[...] = jnp.zeros_like(acc)
    valid = lanes(N) + sc[1] * N < sc[5]
    lane = lanes(128)
    stats = jnp.zeros((R, 128), F32)
    for h in range(H):
        w = slice(WIN[h], WIN[h] + 256)
        mk = head_mask(h)
        s = dot_nt(q_o[:, w] * half(mk), k_o[:, w]) * SCALE
        s = jnp.where(valid, s, -1e30)
        m = jnp.max(s, axis=-1, keepdims=True)
        p = jnp.exp(s - m)
        acc[:, w] += dot(half(p), v_o[:, w]) * mk
        stats = jnp.where(lane == h, m, stats)
        stats = jnp.where(lane == 8 + h, jnp.sum(p, axis=-1, keepdims=True), stats)
    pay[:, 0:D] = half(acc[...])
    pay[:, D : D + 128] = pack3(stats)
    save.wait()


def combine_body(rcv, out):
    st = unpack3(rcv[:, :, D : D + 128].astype(F32), 2)
    peak = jnp.max(st, axis=0, keepdims=True)
    w = jnp.exp(st - peak)
    total = jnp.sum(w * pltpu.roll(st, 120, 2), axis=0, keepdims=True)
    coef = w / total
    lane = lax.broadcasted_iota(jnp.int32, (1, 1, 128), 2)
    for t in range(10):
        h0, h1 = 128 * t // E, (128 * t + 127) // E
        c = coef[:, :, h0 : h0 + 1]
        if h1 != h0:
            c = jnp.where(lane >= E * h1 - 128 * t, coef[:, :, h1 : h1 + 1], c)
        o = jnp.sum(rcv[:, :, 128 * t : 128 * t + 128].astype(F32) * c, axis=0)
        out[:, 128 * t : 128 * t + 128] = half(o)
    lse = jnp.where(lanes(128) < 8, (peak + jnp.log(total))[0], 0.0)
    out[:, D : D + 128] = pack3(lse)


class Ring:
    def __init__(self, w, slots, sem, order):
        self.w, self.slots, self.sem, self.order = w, slots, sem, order
        self.n = slots.shape[0]
        self.pos = {m: k for k, m in enumerate(order)}

    def copies(self, m):
        s = self.pos[m] % self.n
        return [
            pltpu.make_async_copy(
                self.w.at[i, :, r0 : r0 + n, :], self.slots.at[s, :, d0 : d0 + n, :], self.sem.at[s, k]
            )
            for k, (i, r0, d0, n) in enumerate(pieces(80 * m, 80))
        ]

    def start(self, m):
        for c in self.copies(m):
            c.start()

    def begin(self):
        for m in self.order[: self.n]:
            self.start(m)

    def get(self, m):
        for c in self.copies(m):
            c.wait()
        return self.slots[self.pos[m] % self.n].reshape(D, D)

    def done(self, m):
        k = self.pos[m] + self.n
        if k < len(self.order):
            self.start(self.order[k])


def forward_body(
    qin, cot, bg, lg, e_h, g_all, w,
    res, gqin, gain_o, pay, mix_o, nd_o, gq_o, z_h, h_h, a_h,
    slots, e, z0b, zs, zb, hs, qs, acc, kd, vd, dec, bq, dacc, gq, gkv, wsem, ssem, lsem,
):
    first = [
        pltpu.make_async_copy(e_h.at[:, 0:D], e, lsem.at[3]),
        pltpu.make_async_copy(g_all.at[:, 176:192, :], z0b, lsem.at[4]),
    ]
    for c in first:
        c.start()
    ring = Ring(w, slots, wsem, list(range(11)))
    ring.begin()
    copies = []
    for i, r0, d0, n in pieces(BQ_ROW, 48):
        copies.append(pltpu.make_async_copy(w.at[i, :, r0 : r0 + n, :], bq.at[:, d0 : d0 + n, :], lsem.at[0]))
    for i, r0, d0, n in pieces(DEC_ROW, 80):
        copies.append(
            pltpu.make_async_copy(w.at[i, :, r0 : r0 + n, 0:DI], dec.at[:, d0 : d0 + n, :], lsem.at[len(copies)])
        )
    for c in copies:
        c.start()
    saves = []

    def save(src, dst):
        c = pltpu.make_async_copy(src, dst, ssem.at[len(saves)])
        c.start()
        saves.append(c)

    def keep(k):
        zb[k] = half(zs[k])
        save(zb.at[k], z_h.at[k])

    def mul(a, m):
        out = dot(a, ring.get(m))
        ring.done(m)
        return out

    for c in first:
        c.wait()
    z1 = z0b[...].reshape(R, D).astype(F32) + mul(e[...], 0)
    zs[0] = z1
    keep(0)
    h1 = mul(half(norm(z1)[0] * lg[1:2, :]), 1)
    hs[0] = half(h1)
    save(hs.at[0], h_h.at[0])
    zs[1] = zs[0] + mul(half(gelu(h1)), 2)
    keep(1)
    s_b = half(norm(zs[1])[0] * lg[2:3, :])
    for k in range(3):
        qs[k] = half(mul(s_b, 3 + k))
        save(qs.at[k], a_h.at[k])
    acc[...] = jnp.zeros_like(acc)
    for h in range(H):
        win = slice(WIN[h], WIN[h] + 256)
        mk = head_mask(h)
        s = dot_nt(qs[0, :, win] * half(mk), qs[1, :, win]) * SCALE
        p = jnp.exp(s - jnp.max(s, axis=-1, keepdims=True))
        p = p / jnp.sum(p, axis=-1, keepdims=True)
        acc[:, win] += dot(half(p), qs[2, :, win]) * mk
    qs[3] = half(acc[...])
    save(qs.at[3], a_h.at[3])
    zs[2] = zs[1] + mul(qs[3], 6)
    keep(2)
    h2 = mul(half(norm(zs[2])[0] * lg[3:4, :]), 7)
    hs[1] = half(h2)
    save(hs.at[1], h_h.at[1])
    zs[3] = zs[2] + mul(half(gelu(h2)), 8)
    keep(3)
    c_b = half(norm(zs[3])[0] * lg[4:5, :])
    kd[...] = half(mul(c_b, 9))
    vd[...] = half(mul(c_b, 10))

    x = qin[...].astype(F32)
    n, inv = norm(x)
    nd = half(n * bg[1:2, :])
    nd_o[...] = nd
    for c in copies:
        c.wait()
    wq = bq[...].reshape(DI, D)
    wd = dec[...].reshape(D, DI)
    gq_o[...] = half(dot(nd, wq))
    mix_o[...] = half(dot_nt(cot[...], wd))
    dacc[...] = jnp.zeros_like(dacc)
    gq[...] = jnp.zeros_like(gq)
    gkv[...] = jnp.zeros_like(gkv)
    for h in range(H):
        win = slice(WIN[h], WIN[h] + 256)
        mk = head_mask(h)
        mkb = half(mk)
        qw, gw, kw, vw = gq_o[:, win], mix_o[:, win], kd[:, win], vd[:, win]
        s = dot_nt(qw * mkb, kw) * SCALE
        p = jnp.exp(s - jnp.max(s, axis=-1, keepdims=True))
        p = p / jnp.sum(p, axis=-1, keepdims=True)
        pb = half(p)
        dacc[:, win] += dot(pb, vw) * mk
        dp = dot_nt(gw * mkb, vw)
        ds = half(p * (dp - jnp.sum(p * dp, axis=-1, keepdims=True)))
        gq[:, win] += dot(ds, kw) * mk
        gkv[0, :, win] += dot_tn(ds, qw) * mk
        gkv[1, :, win] += dot_tn(pb, gw) * mk
    pay[:, 0:D] = half(gkv[0] * SCALE)
    pay[:, D : 2 * D] = half(gkv[1])
    mix = half(dacc[...])
    mix_o[...] = mix
    res[...] = half(x + dot(mix, wd))
    gqb = half(gq[...] * SCALE)
    gq_o[...] = gqb
    gin, gg = norm_back(dot_nt(gqb, wq), bg[1:2, :], n, inv)
    gqin[...] = cot[...].astype(F32) + gin
    gain_o[...] = gg
    for c in saves:
        c.wait()


def prepare_body(lg, z_h, h_h, a_h, n_h, i_h, s_h, act_h, p_h, zs, hs, qs, ns, vs, ss, acts, ps, sem, osem):
    loads = {}
    for k in range(4):
        loads["z", k] = pltpu.make_async_copy(z_h.at[k], zs.at[k], sem.at[k])
    for k in range(2):
        loads["h", k] = pltpu.make_async_copy(h_h.at[k], hs.at[k], sem.at[4 + k])
    loads["q"] = pltpu.make_async_copy(a_h.at[0:2], qs, sem.at[6])
    for c in loads.values():
        c.start()
    saves = []

    def save(src, dst):
        c = pltpu.make_async_copy(src, dst, osem.at[len(saves)])
        c.start()
        saves.append(c)

    for k, a in ((3, 0), (2, 2), (1, 1), (0, 4)):
        loads["z", k].wait()
        n, inv = norm(zs[k].astype(F32))
        ns[k] = half(n)
        save(ns.at[k], n_h.at[k])
        vs[k] = jnp.broadcast_to(inv, (R, 128))
        acts[a] = half(n * lg[k + 1 : k + 2, :])
        save(acts.at[a], act_h.at[a])
    save(vs, i_h)
    for k, a in ((1, 3), (0, 5)):
        loads["h", k].wait()
        x = hs[k].astype(F32)
        t = jnp.tanh(C0 * (x + C1 * x * x * x))
        acts[a] = half(0.5 * x * (1.0 + t))
        save(acts.at[a], act_h.at[a])
        ss[k] = 0.5 * (1.0 + t) + 0.5 * x * (1.0 - t * t) * (C0 * (1.0 + 3.0 * C1 * x * x))
        save(ss.at[k], s_h.at[k])
    loads["q"].wait()
    for h in range(H):
        win = slice(WIN[h], WIN[h] + 256)
        s = dot_nt(qs[0, :, win] * half(head_mask(h)), qs[1, :, win]) * SCALE
        p = jnp.exp(s - jnp.max(s, axis=-1, keepdims=True))
        ps[h] = half(p / jnp.sum(p, axis=-1, keepdims=True))
    save(ps, p_h)
    for c in saves:
        c.wait()


def lat_backward_body(
    sc, gin, lg, w, e_h, n_h, i_h, s_h, act_h, a_h, p_h, gmix, pack_o, g1c_o, gains_o,
    slots, ns, vs, ss, acts, qs, ps, acc, acc2, acc3, gh, gw, wsem, lsem,
):
    order = [8, 7, 6, 3, 4, 5, 2, 1, 0]
    ring = Ring(w, slots, wsem, order)
    todo = [
        (i_h, vs),
        (act_h.at[0], acts.at[0]),
        (s_h.at[1], ss.at[1]),
        (act_h.at[3], acts.at[1]),
        (n_h.at[2], ns.at[2]),
        (act_h.at[2], acts.at[3]),
        (a_h.at[3], acts.at[4]),
        (p_h, ps),
        (a_h.at[0:3], qs.at[0:3]),
        (n_h.at[1], ns.at[1]),
        (act_h.at[1], acts.at[2]),
        (s_h.at[0], ss.at[0]),
        (act_h.at[5], acts.at[5]),
        (n_h.at[0], ns.at[0]),
        (act_h.at[4], acts.at[6]),
        (e_h.at[:, 0:D], acts.at[7]),
    ]
    loads = [pltpu.make_async_copy(a, b, lsem.at[k]) for k, (a, b) in enumerate(todo)]
    after = {8: (4, 5, 6), 7: (7, 8), 6: (9, 10, 11, 12), 3: (13, 14, 15)}
    ring.start(8)
    for c in loads[:4]:
        c.start()
    for m in order[1 : ring.n]:
        ring.start(m)

    def ready(*ks):
        for k in ks:
            loads[k].wait()

    src = sc[1] * 80
    start = pl.multiple_of(jnp.minimum((src >> 7) * 128, 1024), 128)
    offset = src - start
    lane = lanes(256)

    def put(ref, to):
        v = pltpu.roll(ref[:, pl.ds(start, 256)].astype(F32), (to - offset + 256) & 255, 1)
        return jnp.where((lane >= to) & (lane < to + 80), v, 0.0)

    def weight_grad(window, first, count):
        a = acts[first : first + count].reshape(count * R, D)
        pack_o[:, 256 * window : 256 * window + 256] = half(dot_tn(a, gw[first : first + count].reshape(count * R, 256)))

    def mul(g_b, m):
        out = dot_nt(g_b, ring.get(m))
        ring.done(m)
        for k in after.get(m, ()):
            loads[k].start()
        return out

    gain_rows = []

    def back(g, k):
        out, gg = norm_back(g, lg[k + 1 : k + 2, :], ns[k].astype(F32), vs[k][:, 0:1])
        for t in range(10):
            gain_rows.append((10 * k + t, gg[:, 128 * t : 128 * t + 128]))
        return out

    for t in range(10):
        acc[:, 128 * t : 128 * t + 128] = gin[:, 16 * t : 16 * t + 16, :].reshape(R, 128).astype(F32)
    tile = lanes(128)
    values = pltpu.roll(gin[:, 176:192, :].reshape(R, 128).astype(F32), 80, 1)
    gw[0, :, 0:128] = half(jnp.where(tile < 80, gin[:, 160:176, :].reshape(R, 128).astype(F32), values))
    gw[0, :, 128:256] = half(jnp.where(tile < 32, values, 0.0))
    gw[1] = half(put(acc, 160))
    ready(0, 1, 2, 3)
    gh[...] = half(mul(half(acc[...]), 8) * ss[1])
    weight_grad(0, 0, 2)
    ready(4)
    gw[3] = half(put(gh, 0))
    acc[...] += back(mul(gh[...], 7), 2)
    gw[4] = half(put(acc, 80))
    qs[3] = half(mul(half(acc[...]), 6))
    acc2[...] = jnp.zeros_like(acc2)
    acc3[...] = jnp.zeros_like(acc3)
    ready(5, 6, 7, 8)
    for h in range(H):
        win = slice(WIN[h], WIN[h] + 256)
        mk = head_mask(h)
        pb = ps[h]
        p = pb.astype(F32)
        dp = dot_nt(qs[3, :, win] * half(mk), qs[2, :, win])
        ds = half(p * (dp - jnp.sum(p * dp, axis=-1, keepdims=True)) * SCALE)
        acc2[:, win] += dot(ds, qs[1, :, win]) * mk
        acc3[0, :, win] += dot_tn(ds, qs[0, :, win]) * mk
        acc3[1, :, win] += dot_tn(pb, qs[3, :, win]) * mk
    gw[2] = half(put(acc2, 0) + put(acc3.at[0], 80) + put(acc3.at[1], 160))
    gn = mul(half(acc2[...]), 3)
    gn = gn + mul(half(acc3[0]), 4)
    gn = gn + mul(half(acc3[1]), 5)
    ready(9, 10)
    weight_grad(1, 2, 1)
    acc[...] += back(gn, 1)
    gw[5] = half(put(acc, 160))
    ready(11, 12)
    gh[...] = half(mul(half(acc[...]), 2) * ss[0])
    weight_grad(2, 3, 3)
    gw[6] = half(put(gh, 0))
    ready(13, 14, 15)
    acc[...] += back(mul(gh[...], 1), 0)
    gw[7] = half(put(acc, 80))
    g1c_o[...] = half(put(acc, 0)[:, 0:128])
    gmix[...] = half(mul(half(acc[...]), 0))
    weight_grad(3, 6, 2)
    gains_o[...] = as_rows(gain_rows, 32)


def key_value_back_body(sc, rcv, lg, n_h, i_h, w, out, gain_o, wbuf, nbuf, ibuf, sem):
    rows = pl.ds(pl.multiple_of(sc[1] * 16, 16), 16)
    copies = []
    for k, m in enumerate((9, 10)):
        for i, r0, d0, n in pieces(80 * m, 80):
            copies.append((w.at[i, :, r0 : r0 + n, :], wbuf.at[k, :, d0 : d0 + n, :]))
    copies += [(n_h.at[3, rows, :], nbuf), (i_h.at[3, rows, :], ibuf)]
    copies = [pltpu.make_async_copy(a, b, sem.at[k]) for k, (a, b) in enumerate(copies)]
    for c in copies:
        c.start()
    s = half(jnp.sum(rcv[...].astype(F32), axis=0))
    for j in range(NJ):
        base = min(128 * (80 * j // 128), 1024)
        for k in range(2):
            v = s[:, D * k + base : D * k + base + 256].astype(F32)
            if 80 * j > base:
                v = pltpu.roll(v, 256 - (80 * j - base), 1)
            out[j, 160 + 16 * k : 176 + 16 * k, :] = half(v[:, 0:128])
    for c in copies:
        c.wait()
    gn = dot_nt(s[:, 0:D], wbuf[0].reshape(D, D)) + dot_nt(s[:, D : 2 * D], wbuf[1].reshape(D, D))
    g, gg = norm_back(gn, lg[4:5, :], nbuf[...].astype(F32), ibuf[:, 0:1])
    gain_o[...] = gg
    g = jnp.concatenate([half(g[:, 128 * t : 128 * t + 128]) for t in range(10)], axis=0)
    for j in range(NJ):
        out[j, 0:160, :] = g


def dec_weights_body(mix, cot, nd, gq, out, buf, sem):
    g = half(dot_tn(mix[...], cot[...]))
    for i in range(NI):
        for t in range(6):
            buf[i, 160 * t : 160 * t + 160, :] = g[160 * i : 160 * i + 160, 128 * t : 128 * t + 128]
    one = pltpu.make_async_copy(buf.at[:, 0:960, :], out.at[:, 0:960, :], sem.at[0])
    one.start()
    g = half(dot_tn(nd[...], gq[...]))
    for i in range(NI):
        for t in range(10):
            r = 960 + 96 * t
            buf[i, r : r + 96, :] = g[96 * i : 96 * i + 96, 128 * t : 128 * t + 128]
    two = pltpu.make_async_copy(buf.at[:, 960:1920, :], out.at[:, 960:1920, :], sem.at[1])
    two.start()
    one.wait()
    two.wait()


def spread(chunk, pay, td, tb):
    fill = jnp.zeros((96, 128), F32)
    for t in range(6):
        v = jnp.concatenate([chunk[160 * t : 160 * t + 160, :].astype(F32), fill], axis=0)
        td[128 * t : 128 * t + 128, :] = v.T
    fill = jnp.zeros((32, 128), F32)
    for t in range(10):
        v = jnp.concatenate([chunk[960 + 96 * t : 960 + 96 * t + 96, :].astype(F32), fill], axis=0)
        tb[128 * t : 128 * t + 128, :] = v.T
    for j in range(NJ):
        tail = pltpu.roll(td[48 * j : 48 * j + 48, 128:256], 96, 1)
        pay[j, 512:560, :] = half(tb[80 * j : 80 * j + 48, :] + tail)
        pay[j, 560:592, :] = half(tb[80 * j + 48 : 80 * j + 80, :])
        pay[j, 592:640, :] = half(td[48 * j : 48 * j + 48, 0:128])


def enc_back_body(
    sc, x_in, bg, lg, gd, gc, gmix_h, e_h, q_h, k_h, v_h, g_all, dw_h, n0_h, i0_h, gin_o, pay,
    gmix, e, q, k, v, wkv, n0, i0, gq, gkt, gvt, dw, td, tb, sem,
):
    pairs = [(gmix_h, gmix), (q_h, q), (k_h, k), (v_h, v), (e_h, e), (g_all, wkv), (dw_h, dw), (n0_h, n0), (i0_h, i0)]
    loads = [pltpu.make_async_copy(a, b, sem.at[n]) for n, (a, b) in enumerate(pairs)]
    for c in loads:
        c.start()
    for c in loads[:5]:
        c.wait()
    lse = unpack3(e[:, D : D + 128].astype(F32), 1)
    valid = lanes(N) + sc[1] * N < sc[5]
    gq[...] = jnp.zeros_like(gq)
    for h in range(H):
        win = slice(WIN[h], WIN[h] + 256)
        mk = head_mask(h)
        mkb = half(mk)
        qw, gw, kw, vw = q[:, win], gmix[:, win], k[:, win], v[:, win]
        rd = jnp.sum(gw.astype(F32) * e[:, win].astype(F32) * mk, axis=-1, keepdims=True)
        s = dot_nt(qw * mkb, kw) * SCALE
        p = jnp.where(valid, jnp.exp(jnp.where(valid, s, -1e30) - lse[:, h : h + 1]), 0.0)
        dp = dot_nt(gw * mkb, vw)
        ds = half(p * (dp - rd))
        gq[:, win] += dot(ds, kw) * mk
        o = OFF[h]
        gkt[E * h : E * h + E, :] = half(dot_tn(qw, ds)[o : o + E, :] * SCALE)
        gvt[E * h : E * h + E, :] = half(dot_tn(gw, half(p))[o : o + E, :])
    pay[:, 320:400, :] = gkt[...].reshape(NJ, 80, 128)
    pay[:, 400:480, :] = gvt[...].reshape(NJ, 80, 128)
    loads[5].wait()
    gqs = gq[...] * SCALE
    gqt = half(gqs.T)
    pay[:, 160:240, :] = gqt[:, 0:128].reshape(NJ, 80, 128)
    pay[:, 240:320, :] = gqt[:, 128:256].reshape(NJ, 80, 128)
    loads[7].wait()
    loads[8].wait()
    gz, g0 = norm_back(dot_nt(half(gqs), wkv[:, 96:176, :].reshape(D, D)), lg[0:1, :], n0[...].astype(F32), i0[:, 0:1])
    gzt = half(gz.T)
    pay[:, 0:80, :] = gzt[:, 0:128].reshape(NJ, 80, 128)
    pay[:, 80:160, :] = gzt[:, 128:256].reshape(NJ, 80, 128)
    n, inv = norm(x_in[...].astype(F32))
    gnt = dot(wkv[:, 0:48, :].reshape(DI, D), gkt[...]) + dot(wkv[:, 48:96, :].reshape(DI, D), gvt[...])
    gin, gg = norm_back(gnt.T, bg[0:1, :], n, inv)
    gin_o[...] = gin
    rows = [(t, gg[:, 128 * t : 128 * t + 128]) for t in range(6)]
    rows += [(6 + t, gd[:, 128 * t : 128 * t + 128]) for t in range(6)]
    rows += [(12 + t, g0[:, 128 * t : 128 * t + 128]) for t in range(10)]
    rows += [(22 + t, gc[:, 128 * t : 128 * t + 128]) for t in range(10)]
    g = half(as_rows(rows, 32))
    for j in range(NJ):
        pay[j, 480:512, :] = g
    loads[6].wait()
    spread(dw, pay, td, tb)


def tail_one_body(sc, rcv, nf_h, n0_h, lg, lat_gain, g1c, keep, send, dec_o, bq_o, nf, n0, left, out, sem):
    loads = [
        pltpu.make_async_copy(nf_h, nf, sem.at[0]),
        pltpu.make_async_copy(n0_h, n0, sem.at[1]),
    ]
    for c in loads:
        c.start()
    sums = jnp.sum(rcv[:, 0:320, :].astype(F32), axis=0)
    fill = jnp.zeros((48, 128), F32)
    left[...] = jnp.zeros_like(left)
    for s in range(NJ):
        left[0:80, 128 * s : 128 * s + 128] = rcv[s, 320:400, :]
        left[128:208, 128 * s : 128 * s + 128] = rcv[s, 400:480, :]
    loads[1].wait()
    nq = half(n0[...].astype(F32) * lg[0:1, :])
    a = jnp.concatenate([sums[160:240], fill], axis=0).T
    b = jnp.concatenate([sums[240:320], fill], axis=0).T
    w0 = dot_tn(nq, half(jnp.concatenate([a, b], axis=0)))
    a = jnp.concatenate([sums[0:80], fill], axis=0).T
    b = jnp.concatenate([sums[80:160], fill], axis=0).T
    gz = half(jnp.concatenate([a, b], axis=0) + g1c[...].astype(F32))
    gains = jnp.sum(rcv[:, 480:512, :].astype(F32), axis=0)
    gains = half(jnp.concatenate([gains, lat_gain[...]], axis=0))
    loads[0].wait()
    wt = dot(left[...], nf[...]).T
    lane = lanes(128)
    key, value = wt[:, 0:128], wt[:, 128:256]
    one = half(jnp.where(lane < 80, key, pltpu.roll(value, 80, 1)))
    other = pltpu.roll(value, 32, 1)
    for i in range(NI):
        to = jnp.where(sc[4] == i % 2, 0, 1)
        r = 96 * i
        beside = jnp.concatenate([other[r : r + 96, :], jnp.zeros((64, 128), F32)], axis=0)
        out[to, i // 2, 0:160, :] = half(jnp.where(lane < 80, w0[160 * i : 160 * i + 160, :], beside))
        out[to, i // 2, 160:192, :] = gz[32 * i : 32 * i + 32, :]
        out[to, i // 2, 192:288, :] = one[r : r + 96, :]
        out[to, i // 2, 288:352, :] = gains
    s = jnp.sum(rcv[:, 512:640, :].astype(F32), axis=0)
    bq_o[...] = s[0:80, 0:96]
    dec_o[:, 0:128] = s[80:128]
    dec_o[:, 128:160] = pltpu.roll(s[0:48], 32, 1)[:, 0:32]
    keep[...] = out[0]
    send[...] = out[1]


def pair_sum_body(a, b, out):
    out[...] = half(a[...].astype(F32) + b[...].astype(F32))


def tail_two_body(rcv, pack_h, bq, arr_o, lm_o, om_o, bm_o, lat_o, byte_o, pack, sem):
    load = pltpu.make_async_copy(pack_h, pack, sem)
    load.start()
    sums = jnp.sum(rcv[...].astype(F32), axis=0)
    lm_o[0] = sums[0:160, 0:80]
    arr_o[...] = sums[160:192, 0:80]
    lane = lanes(128)
    value = jnp.where(lane < 48, pltpu.roll(sums[192:288], 48, 1), pltpu.roll(sums[0:96], 96, 1))
    fill = jnp.zeros((32, 128), F32)
    bm_o[0] = jnp.concatenate([sums[192:288], fill], axis=0).T[0:80, 0:96]
    bm_o[1] = jnp.concatenate([value, fill], axis=0).T[0:80, 0:96]
    bm_o[2] = bq[...]
    g = sums[288:352]
    for t in range(6):
        for b in range(2):
            byte_o[b : b + 1, 128 * t : 128 * t + 128] = g[6 * b + t : 6 * b + t + 1, :]
    for t in range(10):
        for b in range(5):
            r = {0: 12, 1: 32, 2: 42, 3: 52, 4: 22}[b] + t
            lat_o[b : b + 1, 128 * t : 128 * t + 128] = g[r : r + 1, :]
    load.wait()
    for m, (kind, n) in enumerate(SQUARE):
        window, o = PLACE[m]
        v = pack[:, 256 * window : 256 * window + 256].astype(F32)
        if o:
            v = pltpu.roll(v, 256 - o, 1)
        if kind == "l":
            lm_o[n] = v[:, 0:80]
        else:
            om_o[n] = v[:, 0:80]


def line(y, c, x, z):
    return ((y % 4) * 2 + c) * NJ + (x % 4) * NZ + (z % 4)


EVERY = [(y, c, x, z) for y in range(4) for c in range(2) for x in range(NX) for z in range(NZ)]


def along(stage, d):
    out = []
    for y, c, x, z in EVERY:
        on_x = (c == 0) == (stage == 0)
        out.append((line(y, c, x, z), line(y, c, x + d, z) if on_x else line(y, c, x, z + d)))
    return out


SWAP = [(line(y, c, x, z), line(y, 1 - c, x, z)) for y, c, x, z in EVERY]


def exchange(v, axes):
    flat = v.reshape(v.shape[0] * v.shape[1], v.shape[2])
    return lax.all_to_all(flat, axes, split_axis=0, concat_axis=0, tiled=True).reshape(v.shape)


def shards(inputs, queries, lengths, latent_array, latent_mats, out_mats, byte_mats, dec_out, lg, bg, cotangent):
    y, core, x, z = (lax.axis_index(a) for a in AXES)
    i, j = y * 2 + core, x * NZ + z
    sc = jnp.stack([i, j, x, z, core, lengths[0]]).astype(jnp.int32)
    xin, qin, cot = inputs[0], queries[0], cotangent[0]

    (wsh,) = call(
        pack_body,
        [((ROWS_I, D), BF, "h")],
        [(sc, "s"), (latent_mats, "h"), (out_mats, "h"), (byte_mats, "h"), (dec_out, "h")],
        [pltpu.VMEM((ROWS_I, D), BF), DMA((9,))],
        vmem=60,
        name="pack",
    )
    (g0,) = call(
        pack_early_body,
        [((192, 640), BF, "v")],
        [(sc, "s"), (latent_mats, "h"), (byte_mats, "h"), (latent_array, "h")],
        [DMA((4,))],
        vmem=60,
        name="pack_early",
    )
    w = lax.all_gather(wsh, AXES, axis=0, tiled=True).reshape(NI, NJ, ROWS_I, D)

    s0 = jnp.stack([g0] + [lax.ppermute(g0, AXES, along(0, d)) for d in (1, 2, 3)])
    t1, t3 = (lax.ppermute(s0, AXES, along(1, d)) for d in (1, 3))
    t2a, t2b = lax.ppermute(t1[0:2], AXES, along(1, 1)), lax.ppermute(t3[2:4], AXES, along(1, 3))
    own = [s0, t1, t2a, t2b, t3]
    sib = [lax.ppermute(v, AXES, SWAP) for v in own]
    g_all, nb, k_b, v_b, q_b, pay, n0, i0 = call(
        enc_body,
        [
            ((NJ, 192, D), BF, "h"),
            ((N, DI), BF, "v"),
            ((N, D), BF, "v"),
            ((N, D), BF, "v"),
            ((R, D), BF, "v"),
            ((R, D + 128), BF, "v"),
            ((R, D), BF, "v"),
            ((R, 128), F32, "v"),
        ],
        [(sc, "s")] + [(v, "a") for v in own + sib] + [(xin, "v"), (bg, "v"), (lg, "v")],
        [pltpu.VMEM((NJ, 192, D), BF), pltpu.VMEM((R, D), F32), DMA((33,))],
        vmem=60,
        flops=3e9,
        name="enc",
    )
    rcv = exchange(pay.reshape(NJ, 16, D + 128), BLK)
    (mine,) = call(combine_body, [((16, D + 128), BF, "v")], [(rcv, "v")], name="combine")
    e = lax.all_gather(mine, BLK, axis=0, tiled=True)

    big = (NJ, 80, D)
    res, gqin, gd, dpay, mix, nd, gq, z_h, h_h, a_h = call(
        forward_body,
        [
            ((N, DI), BF, "v"),
            ((N, DI), F32, "v"),
            ((1, DI), F32, "v"),
            ((R, 2 * D), BF, "v"),
            ((N, D), BF, "v"),
            ((N, DI), BF, "v"),
            ((N, D), BF, "v"),
            ((4, R, D), BF, "h"),
            ((2, R, D), BF, "h"),
            ((4, R, D), BF, "h"),
        ],
        [(qin, "v"), (cot, "v"), (bg, "v"), (lg, "v"), (e, "h"), (g_all, "h"), (w, "h")],
        [
            pltpu.VMEM((3,) + big, BF),
            pltpu.VMEM((R, D), BF),
            pltpu.VMEM((NJ, 16, D), BF),
            pltpu.VMEM((4, R, D), F32),
            pltpu.VMEM((4, R, D), BF),
            pltpu.VMEM((2, R, D), BF),
            pltpu.VMEM((4, R, D), BF),
            pltpu.VMEM((R, D), F32),
            pltpu.VMEM((R, D), BF),
            pltpu.VMEM((R, D), BF),
            pltpu.VMEM((NJ, 80, DI), BF),
            pltpu.VMEM((NJ, 48, D), BF),
            pltpu.VMEM((N, D), F32),
            pltpu.VMEM((N, D), F32),
            pltpu.VMEM((2, R, D), F32),
            DMA((3, 2)),
            DMA((10,)),
            DMA((5,)),
        ],
        vmem=54,
        flops=1.5e10,
        name="forward",
    )
    rows = exchange(dpay.reshape(NJ, 16, 2 * D), BLK)
    n_h, i_h, s_h, act_h, p_h = call(
        prepare_body,
        [
            ((4, R, D), BF, "h"),
            ((4, R, 128), F32, "h"),
            ((2, R, D), F32, "h"),
            ((6, R, D), BF, "h"),
            ((H, R, R), BF, "h"),
        ],
        [(lg, "v"), (z_h, "h"), (h_h, "h"), (a_h, "h")],
        [
            pltpu.VMEM((4, R, D), BF),
            pltpu.VMEM((2, R, D), BF),
            pltpu.VMEM((2, R, D), BF),
            pltpu.VMEM((4, R, D), BF),
            pltpu.VMEM((4, R, 128), F32),
            pltpu.VMEM((2, R, D), F32),
            pltpu.VMEM((6, R, D), BF),
            pltpu.VMEM((H, R, R), BF),
            DMA((7,)),
            DMA((14,)),
        ],
        vmem=58,
        flops=5e9,
        name="prepare",
    )
    (dw,) = call(
        dec_weights_body,
        [((NI, 1920, 128), BF, "h")],
        [(mix, "v"), (cot, "v"), (nd, "v"), (gq, "v")],
        [pltpu.VMEM((NI, 1920, 128), BF), DMA((2,))],
        vmem=60,
        flops=4e9,
        name="dec_weights",
    )
    kv, gc = call(
        key_value_back_body,
        [((NJ, 192, 128), BF, "v"), ((1, D), F32, "v")],
        [(sc, "s"), (rows, "v"), (lg, "v"), (n_h, "h"), (i_h, "h"), (w, "h")],
        [pltpu.VMEM((2,) + big, BF), pltpu.VMEM((16, D), BF), pltpu.VMEM((16, 128), F32), DMA((6,))],
        vmem=58,
        flops=1e8,
        name="key_value_back",
    )
    gin4 = exchange(kv, BLK)
    nb, _ = lax.optimization_barrier((nb, gc))
    nf = lax.all_gather(nb, BLK, axis=0, tiled=True)
    dw = lax.psum_scatter(dw.reshape(NI * 1920, 128), BATCH, scatter_dimension=0, tiled=True)

    gmix, pack, g1c, lat_gain = call(
        lat_backward_body,
        [((R, D), BF, "v"), ((D, 1024), BF, "v"), ((R, 128), BF, "v"), ((32, 128), F32, "v")],
        [(sc, "s"), (gin4, "v"), (lg, "v")] + [(v, "h") for v in (w, e, n_h, i_h, s_h, act_h, a_h, p_h)],
        [
            pltpu.VMEM((2,) + big, BF),
            pltpu.VMEM((4, R, D), BF),
            pltpu.VMEM((4, R, 128), F32),
            pltpu.VMEM((2, R, D), F32),
            pltpu.VMEM((8, R, D), BF),
            pltpu.VMEM((4, R, D), BF),
            pltpu.VMEM((H, R, R), BF),
            pltpu.VMEM((R, D), F32),
            pltpu.VMEM((R, D), F32),
            pltpu.VMEM((2, R, D), F32),
            pltpu.VMEM((R, D), BF),
            pltpu.VMEM((8, R, 256), BF),
            DMA((2, 2)),
            DMA((16,)),
        ],
        vmem=60,
        flops=8e10,
        name="lat_backward",
    )
    pack = lax.psum_scatter(pack, BATCH, scatter_dimension=0, tiled=True)
    gin, epay = call(
        enc_back_body,
        [((N, DI), F32, "v"), ((NJ, 640, 128), BF, "v")],
        [(sc, "s"), (xin, "v"), (bg, "v"), (lg, "v"), (gd, "v"), (gc, "v")]
        + [(v, "h") for v in (gmix, e, q_b, k_b, v_b, g_all, dw, n0, i0)],
        [
            pltpu.VMEM((R, D), BF),
            pltpu.VMEM((R, D + 128), BF),
            pltpu.VMEM((R, D), BF),
            pltpu.VMEM((N, D), BF),
            pltpu.VMEM((N, D), BF),
            pltpu.VMEM((NJ, 192, D), BF),
            pltpu.VMEM((R, D), BF),
            pltpu.VMEM((R, 128), F32),
            pltpu.VMEM((R, D), F32),
            pltpu.VMEM((D, N), BF),
            pltpu.VMEM((D, N), BF),
            pltpu.VMEM((1920, 128), BF),
            pltpu.VMEM((DI, 256), F32),
            pltpu.VMEM((D, 128), F32),
            DMA((9,)),
        ],
        vmem=58,
        flops=3e9,
        name="enc_back",
    )
    r1 = exchange(epay, BLK)
    keep, send, dec_grad, bq_grad = call(
        tail_one_body,
        [((4, 352, 128), BF, "v"), ((4, 352, 128), BF, "v"), ((48, 160), F32, "v"), ((80, 96), F32, "v")],
        [(sc, "s"), (r1, "v"), (nf, "h"), (n0, "h"), (lg, "v"), (lat_gain, "v"), (g1c, "v")],
        [pltpu.VMEM((NJ * N, DI), BF), pltpu.VMEM((R, D), BF), pltpu.VMEM((256, 2048), BF), pltpu.VMEM((2, 4, 352, 128), BF), DMA((2,))],
        name="tail_one",
    )
    (p2,) = call(
        pair_sum_body,
        [((4, 352, 128), BF, "v")],
        [(keep, "v"), (lax.ppermute(send, AXES, SWAP), "v")],
        vmem=12,
        name="pair_sum",
    )
    r2 = exchange(p2, ("y",))
    arr, lm, om, byte_grads, lat_gains, byte_gain = call(
        tail_two_body,
        [
            ((32, 80), F32, "v"),
            ((10, 160, 80), F32, "v"),
            ((2, 160, 80), F32, "v"),
            ((3, 80, 96), F32, "v"),
            ((5, D), F32, "v"),
            ((2, DI), F32, "v"),
        ],
        [(r2, "v"), (pack, "h"), (bq_grad, "v")],
        [pltpu.VMEM((160, 1024), BF), DMA],
        name="tail_two",
    )
    byte_grads = jnp.swapaxes(byte_grads, 1, 2)
    return (res[None], gin[None], gqin[None], arr, lm, om, byte_grads, dec_grad.T, lat_gains, byte_gain)


def solution(mesh):
    grid = Mesh(mesh.devices.reshape(4, 2, NX, NZ), AXES)
    return jax.shard_map(
        shards,
        mesh=grid,
        in_specs=(
            P(BATCH, BLK, None),
            P(BATCH, BLK, None),
            P(BATCH),
            P(BLK, None),
            P(None, BLK, None),
            P(None, BLK, None),
            P(None, BLK, None),
            P(BLK, None),
            P(),
            P(),
            P(BATCH, BLK, None),
        ),
        out_specs=(
            P(BATCH, BLK, None),
            P(BATCH, BLK, None),
            P(BATCH, BLK, None),
            P(BATCH, BLK),
            P(None, BATCH, BLK),
            P(None, BATCH, BLK),
            P(None, BATCH, BLK),
            P(BATCH, BLK),
            P(),
            P(),
        ),
        check_vma=False,
    )
```

```python
import jax
import jax.numpy as jnp
from jax import lax
from jax.experimental import pallas as pl
from jax.experimental.pallas import tpu as pltpu
from jax.sharding import Mesh, PartitionSpec as P

F32, BF = jnp.float32, jnp.bfloat16
D, DI, R, N, H, E = 1280, 768, 256, 128, 8, 160
NX, NZ, NJ, NI = 4, 4, 16, 8
SCALE = E**-0.5
EPS = 1e-5
MIB = 1 << 20
AXES = ("y", "core", "x", "z")
BATCH = ("y", "core")
BLK = ("x", "z")
WIN = [128 * (E * h // 128) for h in range(H)]
OFF = [E * h - WIN[h] for h in range(H)]
SQUARE = [("o", 0), ("l", 1), ("l", 2), ("l", 3), ("l", 4), ("l", 5), ("o", 1), ("l", 6), ("l", 7), ("l", 8), ("l", 9)]
ROWS_I = 128
DEC_ROW, BQ_ROW = 880, 960
PLACE = {9: (0, 0), 10: (0, 80), 8: (0, 160), 3: (1, 0), 4: (1, 80), 5: (1, 160), 7: (2, 0), 6: (2, 80), 2: (2, 160), 1: (3, 0), 0: (3, 80)}


def dot(a, b, ca=1, cb=0):
    return lax.dot_general(a, b, (((ca,), (cb,)), ((), ())), preferred_element_type=F32)


def dot_nt(a, b):
    return dot(a, b, 1, 1)


def dot_tn(a, b):
    return dot(a, b, 0, 0)


def half(v):
    return v.astype(BF)


def norm(v):
    c = v - jnp.mean(v, axis=-1, keepdims=True)
    inv = lax.rsqrt(jnp.mean(c * c, axis=-1, keepdims=True) + EPS)
    return c * inv, inv


def norm_back(g, gain, n, inv):
    gg = jnp.sum(g * n, axis=0, keepdims=True)
    inner = g * gain
    m1 = jnp.mean(inner, axis=-1, keepdims=True)
    m2 = jnp.mean(inner * n, axis=-1, keepdims=True)
    return inv * (inner - m1 - n * m2), gg


C0, C1 = 0.7978845608028654, 0.044715


def gelu(x):
    return 0.5 * x * (1.0 + jnp.tanh(C0 * (x + C1 * x * x * x)))


def gelu_slope(x):
    t = jnp.tanh(C0 * (x + C1 * x * x * x))
    return 0.5 * (1.0 + t) + 0.5 * x * (1.0 - t * t) * (C0 * (1.0 + 3.0 * C1 * x * x))


def lanes(width):
    return lax.broadcasted_iota(jnp.int32, (1, width), 1)


def head_mask(h):
    lane = lanes(256)
    return jnp.where((lane >= OFF[h]) & (lane < OFF[h] + E), 1.0, 0.0).astype(F32)


def pieces(row, count):
    out = []
    done = 0
    while done < count:
        i, r0 = divmod(row + done, ROWS_I)
        n = min(count - done, ROWS_I - r0)
        out.append((i, r0, done, n))
        done += n
    return out


def split3(v):
    hi = half(v).astype(F32)
    mid = half(v - hi).astype(F32)
    lo = half(v - hi - mid).astype(F32)
    return hi, mid, lo


def pack3(v):
    hi, mid, lo = split3(v)
    return half(hi + pltpu.roll(mid, 16, 1) + pltpu.roll(lo, 32, 1))


def unpack3(v, axis):
    return v + pltpu.roll(v, 112, axis) + pltpu.roll(v, 96, axis)


def as_rows(parts, count):
    row = lax.broadcasted_iota(jnp.int32, (count, 128), 0)
    out = jnp.zeros((count, 128), F32)
    for r, part in parts:
        out = jnp.where(row == r, part, out)
    return out


def call(body, outs, args, scratch=(), vmem=48, flops=0, name=None):
    spaces = {"v": pltpu.VMEM, "a": pl.ANY, "s": pltpu.SMEM, "h": pltpu.HBM}
    return pl.pallas_call(
        body,
        out_shape=[jax.ShapeDtypeStruct(s, t) for s, t, _ in outs],
        in_specs=[pl.BlockSpec(memory_space=spaces[m]) for _, m in args],
        out_specs=[pl.BlockSpec(memory_space=spaces[m]) for _, _, m in outs],
        scratch_shapes=list(scratch),
        compiler_params=pltpu.CompilerParams(vmem_limit_bytes=vmem * MIB),
        cost_estimate=pl.CostEstimate(flops=int(flops), bytes_accessed=4 * MIB, transcendentals=0),
        name=name,
    )(*[a for a, _ in args])


DMA = pltpu.SemaphoreType.DMA


def pack_early_body(sc, lm, bm, la, g0, sem):
    cols = pl.ds(pl.multiple_of(sc[4] * 640, 128), 640)
    copies = [
        (bm.at[0, :, cols], g0.at[0:48, :]),
        (bm.at[1, :, cols], g0.at[48:96, :]),
        (lm.at[0, :, cols], g0.at[96:176, :]),
        (la.at[:, cols], g0.at[176:192, :]),
    ]
    copies = [pltpu.make_async_copy(a, b, sem.at[k]) for k, (a, b) in enumerate(copies)]
    for c in copies:
        c.start()
    for c in copies:
        c.wait()


def pack_body(sc, lm, om, bm, do, wsh, buf, sem):
    i = sc[0]
    blocks = [(80 * k, 80, (om if s == "o" else lm), n, D) for k, (s, n) in enumerate(SQUARE)]
    blocks += [(DEC_ROW, 80, do, None, DI), (BQ_ROW, 48, bm, 2, D)]
    for k in range(NI):
        lo, hi = ROWS_I * k, ROWS_I * (k + 1)

        @pl.when(i == k)
        def _(lo=lo, hi=hi):
            cs = []
            for row, count, ref, n, width in blocks:
                a, b = max(lo, row), min(hi, row + count)
                if a < b:
                    src = ref.at[a - row : b - row, :] if n is None else ref.at[n, a - row : b - row, :]
                    dst = buf.at[a - lo : b - lo, :] if width == D else buf.at[a - lo : b - lo, 0:width]
                    cs.append(pltpu.make_async_copy(src, dst, sem.at[len(cs)]))
            for c in cs:
                c.start()
            for c in cs:
                c.wait()

    out = pltpu.make_async_copy(buf, wsh, sem.at[8])
    out.start()
    out.wait()


def pieces_from(sc, own, sib):
    x, z, core = sc[2], sc[3], sc[4]
    out = []
    for side, (t0, t1, t2a, t2b, t3) in enumerate((own, sib)):
        c = core if side == 0 else 1 - core
        col = pl.ds(pl.multiple_of(c * 640, 128), 640)
        for e in range(4):
            for d in range(4):
                xs = jnp.where(c == 0, (x + 4 - d) & 3, (x + 4 - e) & 3)
                zs = jnp.where(c == 0, (z + 4 - e) & 3, (z + 4 - d) & 3)
                ref = (t0, t1, None, t3)[e] if e != 2 else (t2a, t2b)[d // 2]
                out.append((xs * 4 + zs, col, ref.at[d % 2 if e == 2 else d]))
    return out


def enc_body(
    sc, a0, a1, a2, a3, a4, b0, b1, b2, b3, b4, x_in, bg, lg, g_out, nb_o, k_o, v_o, q_o, pay, n_o, i_o, gs, acc, sem
):
    copies = [
        pltpu.make_async_copy(src, gs.at[pos, :, col], sem.at[k])
        for k, (pos, col, src) in enumerate(pieces_from(sc, (a0, a1, a2, a3, a4), (b0, b1, b2, b3, b4)))
    ]
    for c in copies:
        c.start()
    n_in, _ = norm(x_in[...].astype(F32))
    nb = half(n_in * bg[0:1, :])
    nb_o[...] = nb
    for c in copies:
        c.wait()
    save = pltpu.make_async_copy(gs, g_out, sem.at[32])
    save.start()
    k_o[...] = half(dot(nb, gs[:, 0:48, :].reshape(DI, D)))
    v_o[...] = half(dot(nb, gs[:, 48:96, :].reshape(DI, D)))
    z0b = gs[:, 176:192, :].reshape(R, D)
    nq, inv = norm(z0b.astype(F32))
    n_o[...] = half(nq)
    i_o[...] = jnp.broadcast_to(inv, (R, 128))
    q_o[...] = half(dot(half(nq * lg[0:1, :]), gs[:, 96:176, :].reshape(D, D)))
    acc[...] = jnp.zeros_like(acc)
    valid = lanes(N) + sc[1] * N < sc[5]
    lane = lanes(128)
    stats = jnp.zeros((R, 128), F32)
    for h in range(H):
        w = slice(WIN[h], WIN[h] + 256)
        mk = head_mask(h)
        s = dot_nt(q_o[:, w] * half(mk), k_o[:, w]) * SCALE
        s = jnp.where(valid, s, -1e30)
        m = jnp.max(s, axis=-1, keepdims=True)
        p = jnp.exp(s - m)
        acc[:, w] += dot(half(p), v_o[:, w]) * mk
        stats = jnp.where(lane == h, m, stats)
        stats = jnp.where(lane == 8 + h, jnp.sum(p, axis=-1, keepdims=True), stats)
    pay[:, 0:D] = half(acc[...])
    pay[:, D : D + 128] = pack3(stats)
    save.wait()


def combine_body(rcv, out):
    st = unpack3(rcv[:, :, D : D + 128].astype(F32), 2)
    peak = jnp.max(st, axis=0, keepdims=True)
    w = jnp.exp(st - peak)
    total = jnp.sum(w * pltpu.roll(st, 120, 2), axis=0, keepdims=True)
    coef = w / total
    lane = lax.broadcasted_iota(jnp.int32, (1, 1, 128), 2)
    for t in range(10):
        h0, h1 = 128 * t // E, (128 * t + 127) // E
        c = coef[:, :, h0 : h0 + 1]
        if h1 != h0:
            c = jnp.where(lane >= E * h1 - 128 * t, coef[:, :, h1 : h1 + 1], c)
        o = jnp.sum(rcv[:, :, 128 * t : 128 * t + 128].astype(F32) * c, axis=0)
        out[:, 128 * t : 128 * t + 128] = half(o)
    lse = jnp.where(lanes(128) < 8, (peak + jnp.log(total))[0], 0.0)
    out[:, D : D + 128] = pack3(lse)


class Ring:
    def __init__(self, w, slots, sem, order):
        self.w, self.slots, self.sem, self.order = w, slots, sem, order
        self.n = slots.shape[0]
        self.pos = {m: k for k, m in enumerate(order)}

    def copies(self, m):
        s = self.pos[m] % self.n
        return [
            pltpu.make_async_copy(
                self.w.at[i, :, r0 : r0 + n, :], self.slots.at[s, :, d0 : d0 + n, :], self.sem.at[s, k]
            )
            for k, (i, r0, d0, n) in enumerate(pieces(80 * m, 80))
        ]

    def start(self, m):
        for c in self.copies(m):
            c.start()

    def begin(self):
        for m in self.order[: self.n]:
            self.start(m)

    def get(self, m):
        for c in self.copies(m):
            c.wait()
        return self.slots[self.pos[m] % self.n].reshape(D, D)

    def done(self, m):
        k = self.pos[m] + self.n
        if k < len(self.order):
            self.start(self.order[k])


def forward_body(
    qin, cot, bg, lg, e_h, g_all, w,
    res, gqin, gain_o, pay, mix_o, nd_o, gq_o, z_h, h_h, a_h,
    slots, e, z0b, zs, zb, hs, qs, acc, kd, vd, dec, bq, dacc, gq, gkv, wsem, ssem, lsem,
):
    first = [
        pltpu.make_async_copy(e_h.at[:, 0:D], e, lsem.at[3]),
        pltpu.make_async_copy(g_all.at[:, 176:192, :], z0b, lsem.at[4]),
    ]
    for c in first:
        c.start()
    ring = Ring(w, slots, wsem, list(range(11)))
    ring.begin()
    copies = []
    for i, r0, d0, n in pieces(BQ_ROW, 48):
        copies.append(pltpu.make_async_copy(w.at[i, :, r0 : r0 + n, :], bq.at[:, d0 : d0 + n, :], lsem.at[0]))
    for i, r0, d0, n in pieces(DEC_ROW, 80):
        copies.append(
            pltpu.make_async_copy(w.at[i, :, r0 : r0 + n, 0:DI], dec.at[:, d0 : d0 + n, :], lsem.at[len(copies)])
        )
    for c in copies:
        c.start()
    saves = []

    def save(src, dst):
        c = pltpu.make_async_copy(src, dst, ssem.at[len(saves)])
        c.start()
        saves.append(c)

    def keep(k):
        zb[k] = half(zs[k])
        save(zb.at[k], z_h.at[k])

    def mul(a, m):
        out = dot(a, ring.get(m))
        ring.done(m)
        return out

    for c in first:
        c.wait()
    z1 = z0b[...].reshape(R, D).astype(F32) + mul(e[...], 0)
    zs[0] = z1
    keep(0)
    h1 = mul(half(norm(z1)[0] * lg[1:2, :]), 1)
    hs[0] = half(h1)
    save(hs.at[0], h_h.at[0])
    zs[1] = zs[0] + mul(half(gelu(h1)), 2)
    keep(1)
    s_b = half(norm(zs[1])[0] * lg[2:3, :])
    for k in range(3):
        qs[k] = half(mul(s_b, 3 + k))
        save(qs.at[k], a_h.at[k])
    acc[...] = jnp.zeros_like(acc)
    for h in range(H):
        win = slice(WIN[h], WIN[h] + 256)
        mk = head_mask(h)
        s = dot_nt(qs[0, :, win] * half(mk), qs[1, :, win]) * SCALE
        p = jnp.exp(s - jnp.max(s, axis=-1, keepdims=True))
        p = p / jnp.sum(p, axis=-1, keepdims=True)
        acc[:, win] += dot(half(p), qs[2, :, win]) * mk
    qs[3] = half(acc[...])
    save(qs.at[3], a_h.at[3])
    zs[2] = zs[1] + mul(qs[3], 6)
    keep(2)
    h2 = mul(half(norm(zs[2])[0] * lg[3:4, :]), 7)
    hs[1] = half(h2)
    save(hs.at[1], h_h.at[1])
    zs[3] = zs[2] + mul(half(gelu(h2)), 8)
    keep(3)
    c_b = half(norm(zs[3])[0] * lg[4:5, :])
    kd[...] = half(mul(c_b, 9))
    vd[...] = half(mul(c_b, 10))

    x = qin[...].astype(F32)
    n, inv = norm(x)
    nd = half(n * bg[1:2, :])
    nd_o[...] = nd
    for c in copies:
        c.wait()
    wq = bq[...].reshape(DI, D)
    wd = dec[...].reshape(D, DI)
    gq_o[...] = half(dot(nd, wq))
    mix_o[...] = half(dot_nt(cot[...], wd))
    dacc[...] = jnp.zeros_like(dacc)
    gq[...] = jnp.zeros_like(gq)
    gkv[...] = jnp.zeros_like(gkv)
    for h in range(H):
        win = slice(WIN[h], WIN[h] + 256)
        mk = head_mask(h)
        mkb = half(mk)
        qw, gw, kw, vw = gq_o[:, win], mix_o[:, win], kd[:, win], vd[:, win]
        s = dot_nt(qw * mkb, kw) * SCALE
        p = jnp.exp(s - jnp.max(s, axis=-1, keepdims=True))
        p = p / jnp.sum(p, axis=-1, keepdims=True)
        pb = half(p)
        dacc[:, win] += dot(pb, vw) * mk
        dp = dot_nt(gw * mkb, vw)
        ds = half(p * (dp - jnp.sum(p * dp, axis=-1, keepdims=True)))
        gq[:, win] += dot(ds, kw) * mk
        gkv[0, :, win] += dot_tn(ds, qw) * mk
        gkv[1, :, win] += dot_tn(pb, gw) * mk
    pay[:, 0:D] = half(gkv[0] * SCALE)
    pay[:, D : 2 * D] = half(gkv[1])
    mix = half(dacc[...])
    mix_o[...] = mix
    res[...] = half(x + dot(mix, wd))
    gqb = half(gq[...] * SCALE)
    gq_o[...] = gqb
    gin, gg = norm_back(dot_nt(gqb, wq), bg[1:2, :], n, inv)
    gqin[...] = cot[...].astype(F32) + gin
    gain_o[...] = gg
    for c in saves:
        c.wait()


def prepare_body(lg, z_h, h_h, a_h, n_h, i_h, s_h, act_h, p_h, zs, hs, qs, ns, vs, ss, acts, ps, sem, osem):
    loads = {}
    for k in range(4):
        loads["z", k] = pltpu.make_async_copy(z_h.at[k], zs.at[k], sem.at[k])
    for k in range(2):
        loads["h", k] = pltpu.make_async_copy(h_h.at[k], hs.at[k], sem.at[4 + k])
    loads["q"] = pltpu.make_async_copy(a_h.at[0:2], qs, sem.at[6])
    for c in loads.values():
        c.start()
    saves = []

    def save(src, dst):
        c = pltpu.make_async_copy(src, dst, osem.at[len(saves)])
        c.start()
        saves.append(c)

    for k, a in ((3, 0), (2, 2), (1, 1), (0, 4)):
        loads["z", k].wait()
        n, inv = norm(zs[k].astype(F32))
        ns[k] = half(n)
        save(ns.at[k], n_h.at[k])
        vs[k] = jnp.broadcast_to(inv, (R, 128))
        acts[a] = half(n * lg[k + 1 : k + 2, :])
        save(acts.at[a], act_h.at[a])
    save(vs, i_h)
    for k, a in ((1, 3), (0, 5)):
        loads["h", k].wait()
        x = hs[k].astype(F32)
        t = jnp.tanh(C0 * (x + C1 * x * x * x))
        acts[a] = half(0.5 * x * (1.0 + t))
        save(acts.at[a], act_h.at[a])
        ss[k] = 0.5 * (1.0 + t) + 0.5 * x * (1.0 - t * t) * (C0 * (1.0 + 3.0 * C1 * x * x))
        save(ss.at[k], s_h.at[k])
    loads["q"].wait()
    for h in range(H):
        win = slice(WIN[h], WIN[h] + 256)
        s = dot_nt(qs[0, :, win] * half(head_mask(h)), qs[1, :, win]) * SCALE
        p = jnp.exp(s - jnp.max(s, axis=-1, keepdims=True))
        ps[h] = half(p / jnp.sum(p, axis=-1, keepdims=True))
    save(ps, p_h)
    for c in saves:
        c.wait()


def lat_backward_body(
    sc, gin, lg, w, e_h, n_h, i_h, s_h, act_h, a_h, p_h, dw, gmix, pack_o, g1c_o, gains_o,
    slots, ns, vs, ss, acts, qs, ps, acc, acc2, acc3, gh, gw, wsem, lsem,
):
    order = [8, 7, 6, 3, 4, 5, 2, 1, 0]
    ring = Ring(w, slots, wsem, order)
    todo = [
        (i_h, vs),
        (act_h.at[0], acts.at[0]),
        (s_h.at[1], ss.at[1]),
        (act_h.at[3], acts.at[1]),
        (n_h.at[2], ns.at[2]),
        (act_h.at[2], acts.at[3]),
        (a_h.at[3], acts.at[4]),
        (p_h, ps),
        (a_h.at[0:3], qs.at[0:3]),
        (n_h.at[1], ns.at[1]),
        (act_h.at[1], acts.at[2]),
        (s_h.at[0], ss.at[0]),
        (act_h.at[5], acts.at[5]),
        (n_h.at[0], ns.at[0]),
        (act_h.at[4], acts.at[6]),
        (e_h.at[:, 0:D], acts.at[7]),
    ]
    loads = [pltpu.make_async_copy(a, b, lsem.at[k]) for k, (a, b) in enumerate(todo)]
    after = {8: (4, 5, 6), 7: (7, 8), 6: (9, 10, 11, 12), 3: (13, 14, 15)}
    ring.start(8)
    for c in loads[:4]:
        c.start()
    for m in order[1 : ring.n]:
        ring.start(m)

    def ready(*ks):
        for k in ks:
            loads[k].wait()

    src = sc[1] * 80
    start = pl.multiple_of(jnp.minimum((src >> 7) * 128, 1024), 128)
    offset = src - start
    lane = lanes(256)

    def put(ref, to):
        v = pltpu.roll(ref[:, pl.ds(start, 256)].astype(F32), (to - offset + 256) & 255, 1)
        return jnp.where((lane >= to) & (lane < to + 80), v, 0.0)

    def weight_grad(window, first, count):
        a = acts[first : first + count].reshape(count * R, D)
        pack_o[:, 256 * window : 256 * window + 256] = half(dot_tn(a, gw[first : first + count].reshape(count * R, 256)))

    def mul(g_b, m):
        out = dot_nt(g_b, ring.get(m))
        ring.done(m)
        for k in after.get(m, ()):
            loads[k].start()
        return out

    gain_rows = []

    def back(g, k):
        out, gg = norm_back(g, lg[k + 1 : k + 2, :], ns[k].astype(F32), vs[k][:, 0:1])
        for t in range(10):
            gain_rows.append((10 * k + t, gg[:, 128 * t : 128 * t + 128]))
        return out

    for t in range(10):
        acc[:, 128 * t : 128 * t + 128] = gin[:, 16 * t : 16 * t + 16, :].reshape(R, 128).astype(F32)
    tile = lanes(128)
    values = pltpu.roll(gin[:, 176:192, :].reshape(R, 128).astype(F32), 80, 1)
    gw[0, :, 0:128] = half(jnp.where(tile < 80, gin[:, 160:176, :].reshape(R, 128).astype(F32), values))
    gw[0, :, 128:256] = half(jnp.where(tile < 32, values, 0.0))
    gw[1] = half(put(acc, 160))
    ready(0, 1, 2, 3)
    gh[...] = half(mul(half(acc[...]), 8) * ss[1])
    weight_grad(0, 0, 2)
    ready(4)
    gw[3] = half(put(gh, 0))
    acc[...] += back(mul(gh[...], 7), 2)
    gw[4] = half(put(acc, 80))
    qs[3] = half(mul(half(acc[...]), 6))
    acc2[...] = jnp.zeros_like(acc2)
    acc3[...] = jnp.zeros_like(acc3)
    ready(5, 6, 7, 8)
    for h in range(H):
        win = slice(WIN[h], WIN[h] + 256)
        mk = head_mask(h)
        pb = ps[h]
        p = pb.astype(F32)
        dp = dot_nt(qs[3, :, win] * half(mk), qs[2, :, win])
        ds = half(p * (dp - jnp.sum(p * dp, axis=-1, keepdims=True)) * SCALE)
        acc2[:, win] += dot(ds, qs[1, :, win]) * mk
        acc3[0, :, win] += dot_tn(ds, qs[0, :, win]) * mk
        acc3[1, :, win] += dot_tn(pb, qs[3, :, win]) * mk
    gw[2] = half(put(acc2, 0) + put(acc3.at[0], 80) + put(acc3.at[1], 160))
    gn = mul(half(acc2[...]), 3)
    gn = gn + mul(half(acc3[0]), 4)
    gn = gn + mul(half(acc3[1]), 5)
    ready(9, 10)
    weight_grad(1, 2, 1)
    acc[...] += back(gn, 1)
    gw[5] = half(put(acc, 160))
    ready(11, 12)
    gh[...] = half(mul(half(acc[...]), 2) * ss[0])
    weight_grad(2, 3, 3)
    gw[6] = half(put(gh, 0))
    ready(13, 14, 15)
    acc[...] += back(mul(gh[...], 1), 0)
    gw[7] = half(put(acc, 80))
    g1c_o[...] = half(put(acc, 0)[:, 0:128])
    gmix[...] = half(mul(half(acc[...]), 0))
    weight_grad(3, 6, 2)
    gains_o[...] = as_rows(gain_rows, 32)


def key_value_back_body(sc, rcv, lg, n_h, i_h, w, out, gain_o, wbuf, nbuf, ibuf, sem):
    rows = pl.ds(pl.multiple_of(sc[1] * 16, 16), 16)
    copies = []
    for k, m in enumerate((9, 10)):
        for i, r0, d0, n in pieces(80 * m, 80):
            copies.append((w.at[i, :, r0 : r0 + n, :], wbuf.at[k, :, d0 : d0 + n, :]))
    copies += [(n_h.at[3, rows, :], nbuf), (i_h.at[3, rows, :], ibuf)]
    copies = [pltpu.make_async_copy(a, b, sem.at[k]) for k, (a, b) in enumerate(copies)]
    for c in copies:
        c.start()
    s = half(jnp.sum(rcv[...].astype(F32), axis=0))
    for j in range(NJ):
        base = min(128 * (80 * j // 128), 1024)
        for k in range(2):
            v = s[:, D * k + base : D * k + base + 256].astype(F32)
            if 80 * j > base:
                v = pltpu.roll(v, 256 - (80 * j - base), 1)
            out[j, 160 + 16 * k : 176 + 16 * k, :] = half(v[:, 0:128])
    for c in copies:
        c.wait()
    gn = dot_nt(s[:, 0:D], wbuf[0].reshape(D, D)) + dot_nt(s[:, D : 2 * D], wbuf[1].reshape(D, D))
    g, gg = norm_back(gn, lg[4:5, :], nbuf[...].astype(F32), ibuf[:, 0:1])
    gain_o[...] = gg
    g = jnp.concatenate([half(g[:, 128 * t : 128 * t + 128]) for t in range(10)], axis=0)
    for j in range(NJ):
        out[j, 0:160, :] = g


def dec_weights_body(mix, cot, nd, gq, out, buf, sem):
    g = half(dot_tn(mix[...], cot[...]))
    for i in range(NI):
        for t in range(6):
            buf[i, 160 * t : 160 * t + 160, :] = g[160 * i : 160 * i + 160, 128 * t : 128 * t + 128]
    one = pltpu.make_async_copy(buf.at[:, 0:960, :], out.at[:, 0:960, :], sem.at[0])
    one.start()
    g = half(dot_tn(nd[...], gq[...]))
    for i in range(NI):
        for t in range(10):
            r = 960 + 96 * t
            buf[i, r : r + 96, :] = g[96 * i : 96 * i + 96, 128 * t : 128 * t + 128]
    two = pltpu.make_async_copy(buf.at[:, 960:1920, :], out.at[:, 960:1920, :], sem.at[1])
    two.start()
    one.wait()
    two.wait()


def dec_spread_body(chunk, pay, td, tb):
    fill = jnp.zeros((96, 128), F32)
    for t in range(6):
        v = jnp.concatenate([chunk[160 * t : 160 * t + 160, :].astype(F32), fill], axis=0)
        td[128 * t : 128 * t + 128, :] = v.T
    fill = jnp.zeros((32, 128), F32)
    for t in range(10):
        v = jnp.concatenate([chunk[960 + 96 * t : 960 + 96 * t + 96, :].astype(F32), fill], axis=0)
        tb[128 * t : 128 * t + 128, :] = v.T
    for j in range(NJ):
        tail = pltpu.roll(td[48 * j : 48 * j + 48, 128:256], 96, 1)
        pay[j, 0:48, :] = half(tb[80 * j : 80 * j + 48, :] + tail)
        pay[j, 48:80, :] = half(tb[80 * j + 48 : 80 * j + 80, :])
        pay[j, 80:128, :] = half(td[48 * j : 48 * j + 48, 0:128])


def enc_back_body(
    sc, x_in, bg, lg, gd, gc, gmix_h, e_h, q_h, k_h, v_h, g_all, dw_h, n0_h, i0_h, gin_o, pay,
    gmix, e, q, k, v, wkv, n0, i0, gq, gkt, gvt, sem,
):
    pairs = [(gmix_h, gmix), (q_h, q), (k_h, k), (v_h, v), (e_h, e), (g_all, wkv), (dw_h, pay.at[:, 512:640, :]), (n0_h, n0), (i0_h, i0)]
    loads = [pltpu.make_async_copy(a, b, sem.at[n]) for n, (a, b) in enumerate(pairs)]
    for c in loads:
        c.start()
    for c in loads[:5]:
        c.wait()
    lse = unpack3(e[:, D : D + 128].astype(F32), 1)
    valid = lanes(N) + sc[1] * N < sc[5]
    gq[...] = jnp.zeros_like(gq)
    for h in range(H):
        win = slice(WIN[h], WIN[h] + 256)
        mk = head_mask(h)
        mkb = half(mk)
        qw, gw, kw, vw = q[:, win], gmix[:, win], k[:, win], v[:, win]
        rd = jnp.sum(gw.astype(F32) * e[:, win].astype(F32) * mk, axis=-1, keepdims=True)
        s = dot_nt(qw * mkb, kw) * SCALE
        p = jnp.where(valid, jnp.exp(jnp.where(valid, s, -1e30) - lse[:, h : h + 1]), 0.0)
        dp = dot_nt(gw * mkb, vw)
        ds = half(p * (dp - rd))
        gq[:, win] += dot(ds, kw) * mk
        o = OFF[h]
        gkt[E * h : E * h + E, :] = half(dot_tn(qw, ds)[o : o + E, :] * SCALE)
        gvt[E * h : E * h + E, :] = half(dot_tn(gw, half(p))[o : o + E, :])
    pay[:, 320:400, :] = gkt[...].reshape(NJ, 80, 128)
    pay[:, 400:480, :] = gvt[...].reshape(NJ, 80, 128)
    loads[5].wait()
    gqs = gq[...] * SCALE
    gqt = half(gqs.T)
    pay[:, 160:240, :] = gqt[:, 0:128].reshape(NJ, 80, 128)
    pay[:, 240:320, :] = gqt[:, 128:256].reshape(NJ, 80, 128)
    loads[7].wait()
    loads[8].wait()
    gz, g0 = norm_back(dot_nt(half(gqs), wkv[:, 96:176, :].reshape(D, D)), lg[0:1, :], n0[...].astype(F32), i0[:, 0:1])
    gzt = half(gz.T)
    pay[:, 0:80, :] = gzt[:, 0:128].reshape(NJ, 80, 128)
    pay[:, 80:160, :] = gzt[:, 128:256].reshape(NJ, 80, 128)
    n, inv = norm(x_in[...].astype(F32))
    gnt = dot(wkv[:, 0:48, :].reshape(DI, D), gkt[...]) + dot(wkv[:, 48:96, :].reshape(DI, D), gvt[...])
    gin, gg = norm_back(gnt.T, bg[0:1, :], n, inv)
    gin_o[...] = gin
    rows = [(t, gg[:, 128 * t : 128 * t + 128]) for t in range(6)]
    rows += [(6 + t, gd[:, 128 * t : 128 * t + 128]) for t in range(6)]
    rows += [(12 + t, g0[:, 128 * t : 128 * t + 128]) for t in range(10)]
    rows += [(22 + t, gc[:, 128 * t : 128 * t + 128]) for t in range(10)]
    g = half(as_rows(rows, 32))
    for j in range(NJ):
        pay[j, 480:512, :] = g
    loads[6].wait()


def tail_one_body(sc, rcv, nf_h, n0_h, lg, lat_gain, g1c, keep, send, dec_o, bq_o, nf, n0, left, out, sem):
    loads = [
        pltpu.make_async_copy(nf_h, nf, sem.at[0]),
        pltpu.make_async_copy(n0_h, n0, sem.at[1]),
    ]
    for c in loads:
        c.start()
    sums = jnp.sum(rcv[:, 0:320, :].astype(F32), axis=0)
    fill = jnp.zeros((48, 128), F32)
    left[...] = jnp.zeros_like(left)
    for s in range(NJ):
        left[0:80, 128 * s : 128 * s + 128] = rcv[s, 320:400, :]
        left[128:208, 128 * s : 128 * s + 128] = rcv[s, 400:480, :]
    loads[1].wait()
    nq = half(n0[...].astype(F32) * lg[0:1, :])
    a = jnp.concatenate([sums[160:240], fill], axis=0).T
    b = jnp.concatenate([sums[240:320], fill], axis=0).T
    w0 = dot_tn(nq, half(jnp.concatenate([a, b], axis=0)))
    a = jnp.concatenate([sums[0:80], fill], axis=0).T
    b = jnp.concatenate([sums[80:160], fill], axis=0).T
    gz = half(jnp.concatenate([a, b], axis=0) + g1c[...].astype(F32))
    gains = jnp.sum(rcv[:, 480:512, :].astype(F32), axis=0)
    gains = half(jnp.concatenate([gains, lat_gain[...]], axis=0))
    loads[0].wait()
    wt = dot(left[...], nf[...]).T
    lane = lanes(128)
    key, value = wt[:, 0:128], wt[:, 128:256]
    one = half(jnp.where(lane < 80, key, pltpu.roll(value, 80, 1)))
    other = pltpu.roll(value, 32, 1)
    for i in range(NI):
        to = jnp.where(sc[4] == i % 2, 0, 1)
        r = 96 * i
        beside = jnp.concatenate([other[r : r + 96, :], jnp.zeros((64, 128), F32)], axis=0)
        out[to, i // 2, 0:160, :] = half(jnp.where(lane < 80, w0[160 * i : 160 * i + 160, :], beside))
        out[to, i // 2, 160:192, :] = gz[32 * i : 32 * i + 32, :]
        out[to, i // 2, 192:288, :] = one[r : r + 96, :]
        out[to, i // 2, 288:352, :] = gains
    s = jnp.sum(rcv[:, 512:640, :].astype(F32), axis=0)
    bq_o[...] = s[0:80, 0:96]
    dec_o[:, 0:128] = s[80:128]
    dec_o[:, 128:160] = pltpu.roll(s[0:48], 32, 1)[:, 0:32]
    keep[...] = out[0]
    send[...] = out[1]


def pair_sum_body(a, b, out):
    out[...] = half(a[...].astype(F32) + b[...].astype(F32))


def tail_two_body(rcv, pack_h, bq, arr_o, lm_o, om_o, bm_o, lat_o, byte_o, pack, sem):
    load = pltpu.make_async_copy(pack_h, pack, sem)
    load.start()
    sums = jnp.sum(rcv[...].astype(F32), axis=0)
    lm_o[0] = sums[0:160, 0:80]
    arr_o[...] = sums[160:192, 0:80]
    lane = lanes(128)
    value = jnp.where(lane < 48, pltpu.roll(sums[192:288], 48, 1), pltpu.roll(sums[0:96], 96, 1))
    fill = jnp.zeros((32, 128), F32)
    bm_o[0] = jnp.concatenate([sums[192:288], fill], axis=0).T[0:80, 0:96]
    bm_o[1] = jnp.concatenate([value, fill], axis=0).T[0:80, 0:96]
    bm_o[2] = bq[...]
    g = sums[288:352]
    for t in range(6):
        for b in range(2):
            byte_o[b : b + 1, 128 * t : 128 * t + 128] = g[6 * b + t : 6 * b + t + 1, :]
    for t in range(10):
        for b in range(5):
            r = {0: 12, 1: 32, 2: 42, 3: 52, 4: 22}[b] + t
            lat_o[b : b + 1, 128 * t : 128 * t + 128] = g[r : r + 1, :]
    load.wait()
    for m, (kind, n) in enumerate(SQUARE):
        window, o = PLACE[m]
        v = pack[:, 256 * window : 256 * window + 256].astype(F32)
        if o:
            v = pltpu.roll(v, 256 - o, 1)
        if kind == "l":
            lm_o[n] = v[:, 0:80]
        else:
            om_o[n] = v[:, 0:80]


def line(y, c, x, z):
    return ((y % 4) * 2 + c) * NJ + (x % 4) * NZ + (z % 4)


EVERY = [(y, c, x, z) for y in range(4) for c in range(2) for x in range(NX) for z in range(NZ)]


def along(stage, d):
    out = []
    for y, c, x, z in EVERY:
        on_x = (c == 0) == (stage == 0)
        out.append((line(y, c, x, z), line(y, c, x + d, z) if on_x else line(y, c, x, z + d)))
    return out


SWAP = [(line(y, c, x, z), line(y, 1 - c, x, z)) for y, c, x, z in EVERY]


def exchange(v, axes):
    flat = v.reshape(v.shape[0] * v.shape[1], v.shape[2])
    return lax.all_to_all(flat, axes, split_axis=0, concat_axis=0, tiled=True).reshape(v.shape)


def shards(inputs, queries, lengths, latent_array, latent_mats, out_mats, byte_mats, dec_out, lg, bg, cotangent):
    y, core, x, z = (lax.axis_index(a) for a in AXES)
    i, j = y * 2 + core, x * NZ + z
    sc = jnp.stack([i, j, x, z, core, lengths[0]]).astype(jnp.int32)
    xin, qin, cot = inputs[0], queries[0], cotangent[0]

    (wsh,) = call(
        pack_body,
        [((ROWS_I, D), BF, "h")],
        [(sc, "s"), (latent_mats, "h"), (out_mats, "h"), (byte_mats, "h"), (dec_out, "h")],
        [pltpu.VMEM((ROWS_I, D), BF), DMA((9,))],
        vmem=60,
        name="pack",
    )
    (g0,) = call(
        pack_early_body,
        [((192, 640), BF, "v")],
        [(sc, "s"), (latent_mats, "h"), (byte_mats, "h"), (latent_array, "h")],
        [DMA((4,))],
        vmem=60,
        name="pack_early",
    )
    w = lax.all_gather(wsh, AXES, axis=0, tiled=True).reshape(NI, NJ, ROWS_I, D)

    s0 = jnp.stack([g0] + [lax.ppermute(g0, AXES, along(0, d)) for d in (1, 2, 3)])
    t1, t3 = (lax.ppermute(s0, AXES, along(1, d)) for d in (1, 3))
    t2a, t2b = lax.ppermute(t1[0:2], AXES, along(1, 1)), lax.ppermute(t3[2:4], AXES, along(1, 3))
    own = [s0, t1, t2a, t2b, t3]
    sib = [lax.ppermute(v, AXES, SWAP) for v in own]
    g_all, nb, k_b, v_b, q_b, pay, n0, i0 = call(
        enc_body,
        [
            ((NJ, 192, D), BF, "h"),
            ((N, DI), BF, "v"),
            ((N, D), BF, "v"),
            ((N, D), BF, "v"),
            ((R, D), BF, "v"),
            ((R, D + 128), BF, "v"),
            ((R, D), BF, "v"),
            ((R, 128), F32, "v"),
        ],
        [(sc, "s")] + [(v, "a") for v in own + sib] + [(xin, "v"), (bg, "v"), (lg, "v")],
        [pltpu.VMEM((NJ, 192, D), BF), pltpu.VMEM((R, D), F32), DMA((33,))],
        vmem=60,
        flops=3e9,
        name="enc",
    )
    rcv = exchange(pay.reshape(NJ, 16, D + 128), BLK)
    (mine,) = call(combine_body, [((16, D + 128), BF, "v")], [(rcv, "v")], name="combine")
    e = lax.all_gather(mine, BLK, axis=0, tiled=True)

    big = (NJ, 80, D)
    res, gqin, gd, dpay, mix, nd, gq, z_h, h_h, a_h = call(
        forward_body,
        [
            ((N, DI), BF, "v"),
            ((N, DI), F32, "v"),
            ((1, DI), F32, "v"),
            ((R, 2 * D), BF, "v"),
            ((N, D), BF, "v"),
            ((N, DI), BF, "v"),
            ((N, D), BF, "v"),
            ((4, R, D), BF, "h"),
            ((2, R, D), BF, "h"),
            ((4, R, D), BF, "h"),
        ],
        [(qin, "v"), (cot, "v"), (bg, "v"), (lg, "v"), (e, "h"), (g_all, "h"), (w, "h")],
        [
            pltpu.VMEM((3,) + big, BF),
            pltpu.VMEM((R, D), BF),
            pltpu.VMEM((NJ, 16, D), BF),
            pltpu.VMEM((4, R, D), F32),
            pltpu.VMEM((4, R, D), BF),
            pltpu.VMEM((2, R, D), BF),
            pltpu.VMEM((4, R, D), BF),
            pltpu.VMEM((R, D), F32),
            pltpu.VMEM((R, D), BF),
            pltpu.VMEM((R, D), BF),
            pltpu.VMEM((NJ, 80, DI), BF),
            pltpu.VMEM((NJ, 48, D), BF),
            pltpu.VMEM((N, D), F32),
            pltpu.VMEM((N, D), F32),
            pltpu.VMEM((2, R, D), F32),
            DMA((3, 2)),
            DMA((10,)),
            DMA((5,)),
        ],
        vmem=54,
        flops=1.5e10,
        name="forward",
    )
    rows = exchange(dpay.reshape(NJ, 16, 2 * D), BLK)
    n_h, i_h, s_h, act_h, p_h = call(
        prepare_body,
        [
            ((4, R, D), BF, "h"),
            ((4, R, 128), F32, "h"),
            ((2, R, D), F32, "h"),
            ((6, R, D), BF, "h"),
            ((H, R, R), BF, "h"),
        ],
        [(lg, "v"), (z_h, "h"), (h_h, "h"), (a_h, "h")],
        [
            pltpu.VMEM((4, R, D), BF),
            pltpu.VMEM((2, R, D), BF),
            pltpu.VMEM((2, R, D), BF),
            pltpu.VMEM((4, R, D), BF),
            pltpu.VMEM((4, R, 128), F32),
            pltpu.VMEM((2, R, D), F32),
            pltpu.VMEM((6, R, D), BF),
            pltpu.VMEM((H, R, R), BF),
            DMA((7,)),
            DMA((14,)),
        ],
        vmem=58,
        flops=5e9,
        name="prepare",
    )
    (dw,) = call(
        dec_weights_body,
        [((NI, 1920, 128), BF, "h")],
        [(mix, "v"), (cot, "v"), (nd, "v"), (gq, "v")],
        [pltpu.VMEM((NI, 1920, 128), BF), DMA((2,))],
        vmem=60,
        flops=4e9,
        name="dec_weights",
    )
    kv, gc = call(
        key_value_back_body,
        [((NJ, 192, 128), BF, "v"), ((1, D), F32, "v")],
        [(sc, "s"), (rows, "v"), (lg, "v"), (n_h, "h"), (i_h, "h"), (w, "h")],
        [pltpu.VMEM((2,) + big, BF), pltpu.VMEM((16, D), BF), pltpu.VMEM((16, 128), F32), DMA((6,))],
        vmem=58,
        flops=1e8,
        name="key_value_back",
    )
    gin4 = exchange(kv, BLK)
    nb, _ = lax.optimization_barrier((nb, gc))
    nf = lax.all_gather(nb, BLK, axis=0, tiled=True)
    dw = lax.psum_scatter(dw.reshape(NI * 1920, 128), BATCH, scatter_dimension=0, tiled=True)

    (dw,) = call(
        dec_spread_body,
        [((NJ, 128, 128), BF, "v")],
        [(dw, "v")],
        [pltpu.VMEM((DI, 256), F32), pltpu.VMEM((D, 128), F32)],
        vmem=16,
        name="dec_spread",
    )
    gmix, pack, g1c, lat_gain = call(
        lat_backward_body,
        [((R, D), BF, "v"), ((D, 1024), BF, "v"), ((R, 128), BF, "v"), ((32, 128), F32, "v")],
        [(sc, "s"), (gin4, "v"), (lg, "v")] + [(v, "h") for v in (w, e, n_h, i_h, s_h, act_h, a_h, p_h, dw)],
        [
            pltpu.VMEM((2,) + big, BF),
            pltpu.VMEM((4, R, D), BF),
            pltpu.VMEM((4, R, 128), F32),
            pltpu.VMEM((2, R, D), F32),
            pltpu.VMEM((8, R, D), BF),
            pltpu.VMEM((4, R, D), BF),
            pltpu.VMEM((H, R, R), BF),
            pltpu.VMEM((R, D), F32),
            pltpu.VMEM((R, D), F32),
            pltpu.VMEM((2, R, D), F32),
            pltpu.VMEM((R, D), BF),
            pltpu.VMEM((8, R, 256), BF),
            DMA((2, 2)),
            DMA((16,)),
        ],
        vmem=60,
        flops=8e10,
        name="lat_backward",
    )
    pack = lax.psum_scatter(pack, BATCH, scatter_dimension=0, tiled=True)
    gin, epay = call(
        enc_back_body,
        [((N, DI), F32, "v"), ((NJ, 640, 128), BF, "v")],
        [(sc, "s"), (xin, "v"), (bg, "v"), (lg, "v"), (gd, "v"), (gc, "v")]
        + [(v, "h") for v in (gmix, e, q_b, k_b, v_b, g_all, dw, n0, i0)],
        [
            pltpu.VMEM((R, D), BF),
            pltpu.VMEM((R, D + 128), BF),
            pltpu.VMEM((R, D), BF),
            pltpu.VMEM((N, D), BF),
            pltpu.VMEM((N, D), BF),
            pltpu.VMEM((NJ, 192, D), BF),
            pltpu.VMEM((R, D), BF),
            pltpu.VMEM((R, 128), F32),
            pltpu.VMEM((R, D), F32),
            pltpu.VMEM((D, N), BF),
            pltpu.VMEM((D, N), BF),
            DMA((9,)),
        ],
        vmem=58,
        flops=3e9,
        name="enc_back",
    )
    r1 = exchange(epay, BLK)
    keep, send, dec_grad, bq_grad = call(
        tail_one_body,
        [((4, 352, 128), BF, "v"), ((4, 352, 128), BF, "v"), ((48, 160), F32, "v"), ((80, 96), F32, "v")],
        [(sc, "s"), (r1, "v"), (nf, "h"), (n0, "h"), (lg, "v"), (lat_gain, "v"), (g1c, "v")],
        [pltpu.VMEM((NJ * N, DI), BF), pltpu.VMEM((R, D), BF), pltpu.VMEM((256, 2048), BF), pltpu.VMEM((2, 4, 352, 128), BF), DMA((2,))],
        name="tail_one",
    )
    (p2,) = call(
        pair_sum_body,
        [((4, 352, 128), BF, "v")],
        [(keep, "v"), (lax.ppermute(send, AXES, SWAP), "v")],
        vmem=12,
        name="pair_sum",
    )
    r2 = exchange(p2, ("y",))
    arr, lm, om, byte_grads, lat_gains, byte_gain = call(
        tail_two_body,
        [
            ((32, 80), F32, "v"),
            ((10, 160, 80), F32, "v"),
            ((2, 160, 80), F32, "v"),
            ((3, 80, 96), F32, "v"),
            ((5, D), F32, "v"),
            ((2, DI), F32, "v"),
        ],
        [(r2, "v"), (pack, "h"), (bq_grad, "v")],
        [pltpu.VMEM((160, 1024), BF), DMA],
        name="tail_two",
    )
    byte_grads = jnp.swapaxes(byte_grads, 1, 2)
    return (res[None], gin[None], gqin[None], arr, lm, om, byte_grads, dec_grad.T, lat_gains, byte_gain)


def solution(mesh):
    grid = Mesh(mesh.devices.reshape(4, 2, NX, NZ), AXES)
    return jax.shard_map(
        shards,
        mesh=grid,
        in_specs=(
            P(BATCH, BLK, None),
            P(BATCH, BLK, None),
            P(BATCH),
            P(BLK, None),
            P(None, BLK, None),
            P(None, BLK, None),
            P(None, BLK, None),
            P(BLK, None),
            P(),
            P(),
            P(BATCH, BLK, None),
        ),
        out_specs=(
            P(BATCH, BLK, None),
            P(BATCH, BLK, None),
            P(BATCH, BLK, None),
            P(BATCH, BLK),
            P(None, BATCH, BLK),
            P(None, BATCH, BLK),
            P(None, BATCH, BLK),
            P(BATCH, BLK),
            P(),
            P(),
        ),
        check_vma=False,
    )
```
